32 devices in a mesh: seq: 4 (over y, x), fsdp: 8 (over z, core).
Axes of the slice: x: 2, y: 2, z: 4, core: 2. Of those that a mesh axis runs over, the one named last changes fastest.
Arguments:
- resid_in: float32 [16, 1024, 2048], P('fsdp', 'seq'), may hold values from -6 to 6
- qkv_weight: float32 [6144, 2048], P('fsdp'), may hold values from -0.125 to 0.125
- qkv_bias: float32 [6144], P('fsdp'), may hold values from -2 to 2
- out_weight: float32 [2048, 2048], P('fsdp'), may hold values from -1 to 1
- out_bias: float32 [2048], P('fsdp'), may hold values from -2 to 2
- up_weight: float32 [8192, 2048], P('fsdp'), may hold values from -0.125 to 0.125
- up_bias: float32 [8192], P('fsdp'), may hold values from -3 to 3
- down_weight: float32 [8192, 2048], P('fsdp'), may hold values from -0.0625 to 0.0625
- down_bias: float32 [2048], P('fsdp'), may hold values from -2 to 2
- attn_gain: float32 [2048], P('fsdp'), may hold values from 0.5 to 1.5
- attn_shift: float32 [2048], P('fsdp'), may hold values from -1.2 to 1.2
- mlp_gain: float32 [2048], P('fsdp'), may hold values from 0.5 to 1.5
- mlp_shift: float32 [2048], P('fsdp'), may hold values from -1.2 to 1.2
- block_ids: int32 [16, 1024], P('fsdp'), may hold values from 0 to 7, never falling along the last dimension, each value on 1 to 256 neighbouring positions
- offsets: int32 [16, 8], P('fsdp'), may hold values from 0 to 4095
- grad_out: float32 [16, 1024, 2048], P('fsdp', 'seq'), may hold values from -6 to 6
Outputs:
- resid_out: float32 [16, 1024, 2048], P('fsdp', 'seq')
- grad_in: float32 [16, 1024, 2048], P('fsdp', 'seq')
- qkv_weight_grad: float32 [6144, 2048], P('fsdp')
- qkv_bias_grad: float32 [4096], P('fsdp')
- value_bias_grad: float32 [2048], P('fsdp')
- out_weight_grad: float32 [2048, 2048], P('fsdp')
- out_bias_grad: float32 [2048], P('fsdp')
- up_weight_grad: float32 [8192, 2048], P('fsdp')
- up_bias_grad: float32 [8192], P('fsdp')
- down_weight_grad: float32 [8192, 2048], P('fsdp')
- down_bias_grad: float32 [2048], P('fsdp')
- attn_gain_grad: float32 [2048], P('fsdp')
- attn_shift_grad: float32 [2048], P('fsdp')
- mlp_gain_grad: float32 [2048], P('fsdp')
- mlp_shift_grad: float32 [2048], P('fsdp')
The draws below stay inside these ranges and needn't reach their ends.
Inputs may be any that keep to these rules, and one draw needn't show every extreme that they name: `block_ids`: along each sequence the block numbers never fall; every block holds 1 to 256 tokens and one block exactly 256.
All inputs are finite; a program needn't handle non-finite values.
Results may differ from the reference program's by a relative error of at most 0.012.
The reference program's roundings to bfloat16 on the way count: a program that leaves them out, or rounds other values in their place, can miss the bound.
Values may be sent and summed in bfloat16 or wider, within the bound.
A program may use at most 576 MiB of HBM per device.

```python
import math
import jax
import jax.numpy as jnp
import numpy as np
from jax import lax

D = 2048
HEADS = 8
HEAD_DIM = 256
ROT_DIM = 64
FF = 8192
SEQ_LEN = 1024
BLOCK = 256
NBLK = 8
SEQS = 16


def set_ends(drawn, key, least, top_value):
    spot = [jax.random.randint(jax.random.fold_in(key, axis), (), 0, length) for axis, length in enumerate(drawn.shape)]
    widest = drawn.shape.index(max(drawn.shape))
    beside = spot[:widest] + [(spot[widest] + 1) % drawn.shape[widest]] + spot[widest + 1:]
    return drawn.at[tuple(spot)].set(least).at[tuple(beside)].set(top_value)


def level_of(key, extent, shards, low, largest):
    level, own = 1.0, jax.random.fold_in(key, 6)
    for axis_at, blocks in shards:
        draws = jnp.exp(jax.random.uniform(jax.random.fold_in(own, axis_at), (blocks,), jnp.float32, low / len(shards), largest / len(shards)))
        level = level * jnp.repeat(draws, extent[axis_at] // blocks).reshape([-1 if axis == axis_at else 1 for axis in range(len(extent))])
    return level


def length_profile(number_of, total, limit, skew):
    loads = [(1 << 20) // math.isqrt(rank ** skew) + 1 for rank in range(2, number_of + 1)]
    rest, counts = total - limit - (number_of - 1), [1] * (number_of - 1)
    while rest > 0:
        candidates = [i for i in range(number_of - 1) if counts[i] < limit]
        pool, budget = sum([loads[i] for i in candidates]), rest
        for i in candidates:
            extra = min(limit - counts[i], max(1, budget * loads[i] // pool), rest)
            counts[i] = counts[i] + extra
            rest = rest - extra
    return np.array([limit] + counts)


def ragged(stream_key, number_of, total, limit, slope):
    if number_of == 2:
        one = jax.random.randint(stream_key, (), max(1, total - limit), min(limit, total - 1) + 1)
        return jnp.stack([one, total - one])
    lengths = jnp.asarray(length_profile(number_of, total, limit, slope), jnp.int32)
    couples = (number_of - 1) // 2
    source_of, taker = lengths[1:1 + 2 * couples:2], lengths[2:2 + 2 * couples:2]
    room = jnp.minimum(source_of - 1, limit - taker)
    shifted = jax.random.randint(jax.random.fold_in(stream_key, 1), (couples,), 0, 1 << 20) % (room + 1)
    lengths = lengths.at[1:1 + 2 * couples:2].set(source_of - shifted).at[2:2 + 2 * couples:2].set(taker + shifted)
    return lengths[jax.random.permutation(jax.random.fold_in(stream_key, 2), number_of)]


def centred(stream_key, extent, width, bound, shards=(), kind=jnp.bfloat16):
    drawn = jax.random.normal(stream_key, extent, jnp.float32) * width
    if len(shards) > 0:
        drawn = level_of(stream_key, extent, shards, -0.22, 0.18) * drawn
    return jnp.clip(drawn, min=-bound, max=bound).astype(kind)


def setup_inputs(seed: int = 0) -> dict:
    key_of = jax.random.split(jax.random.key(seed), 17)
    resid_in = centred(key_of[0], (SEQS, SEQ_LEN, D), 1.0, 6.0, ((0, 8), (1, 4)), jnp.float32)
    qkv_weight = centred(key_of[1], (3 * D, D), D ** -0.5, 0.125, ((0, 8),), jnp.float32)
    qkv_bias = centred(key_of[2], (3 * D,), 0.3, 2.0, ((0, 8),), jnp.float32)
    out_weight = centred(key_of[3], (D, D), (D // 64) ** -0.5, 1.0, ((0, 8),), jnp.float32)
    out_bias = centred(key_of[4], (D,), 0.3, 2.0, ((0, 8),), jnp.float32)
    up_weight = centred(key_of[5], (FF, D), D ** -0.5, 0.125, ((0, 8),), jnp.float32)
    up_bias = centred(key_of[6], (FF,), 0.5, 3.0, ((0, 8),), jnp.float32)
    down_weight = centred(key_of[7], (FF, D), FF ** -0.5, 0.0625, ((0, 8),), jnp.float32)
    down_bias = centred(key_of[8], (D,), 0.3, 2.0, ((0, 8),), jnp.float32)
    attn_gain = jnp.clip(1.0 + 0.1 * jax.random.normal(key_of[9], (D,), jnp.float32), 0.5, 1.5)
    attn_shift = centred(key_of[10], (D,), 0.2, 1.2, ((0, 8),), jnp.float32)
    mlp_gain = jnp.clip(1.0 + 0.1 * jax.random.normal(key_of[11], (D,), jnp.float32), 0.5, 1.5)
    mlp_shift = centred(key_of[12], (D,), 0.2, 1.2, ((0, 8),), jnp.float32)
    block_ids = jax.vmap(lambda own: jnp.searchsorted(jnp.cumsum(ragged(own, NBLK, SEQ_LEN, BLOCK, 0)), jnp.arange(SEQ_LEN), side="right"))(jax.random.split(key_of[13], SEQS)).reshape((SEQS, SEQ_LEN)).astype(jnp.int32)
    offsets = set_ends(jax.random.randint(key_of[14], (SEQS, NBLK), 0, 4096), jax.random.fold_in(key_of[14], 1), 0, 4095).astype(jnp.int32)
    grad_out = centred(key_of[15], (SEQS, SEQ_LEN, D), 1.0, 6.0, ((0, 8), (1, 4)), jnp.float32)
    return dict(resid_in=resid_in, qkv_weight=qkv_weight, qkv_bias=qkv_bias, out_weight=out_weight, out_bias=out_bias, up_weight=up_weight, up_bias=up_bias, down_weight=down_weight, down_bias=down_bias, attn_gain=attn_gain, attn_shift=attn_shift, mlp_gain=mlp_gain, mlp_shift=mlp_shift, block_ids=block_ids, offsets=offsets, grad_out=grad_out)


EPS = 1e-05
exact_prec = lax.Precision.HIGHEST

@jax.custom_vjp
def low(v):
    return lax.optimization_barrier(v.astype(jnp.bfloat16)).astype(jnp.float32)

@jax.custom_vjp
def low_back(v):
    return v

def low_keep(v):
    return (low(v), None)

def low_pass(kept, grad):
    return (grad,)

def back_keep(v):
    return (v, None)

def back_low(kept, grad):
    return (low(grad),)
low.defvjp(low_keep, low_pass)
low_back.defvjp(back_keep, back_low)

def matmul(left, right):
    return jnp.dot(left, right, precision=exact_prec, preferred_element_type=jnp.float32)

def layer_norm(values, gain, shift):
    center = values - lax.optimization_barrier(jnp.mean(values, axis=-1, keepdims=True))
    spread = lax.optimization_barrier(jnp.mean(center * center, axis=-1, keepdims=True))
    return center * lax.rsqrt(spread + EPS) * gain + shift

def rotary_tables(positions):
    half = ROT_DIM // 2
    inverse = jnp.exp(jnp.arange(half, dtype=jnp.float32) * (-2.0 * math.log(10000.0) / ROT_DIM))
    angles = positions.astype(jnp.float32)[..., None] * inverse
    return (jnp.cos(angles), jnp.sin(angles))

def block_offset(ids, starts):
    numbers = jnp.arange(starts.shape[1], dtype=jnp.int32)
    match = (ids[:, :, None] == numbers[None, None, :]).astype(jnp.int32)
    return lax.optimization_barrier(jnp.sum(match * starts[:, None, :], axis=-1)).astype(jnp.int32)

def rotate(values, cosine, sine):
    half = ROT_DIM // 2
    cosine = cosine[..., None, :]
    sine = sine[..., None, :]
    first = values[..., :half]
    second = values[..., half:ROT_DIM]
    return jnp.concatenate([first * cosine - second * sine, second * cosine + first * sine, values[..., ROT_DIM:]], axis=-1)

def attend(items):
    query, keys, values, ids = items
    allowed = ids[None, :] <= ids[:, None]
    scores = jnp.einsum('qhd,khd->hqk', query, keys, precision=exact_prec) * HEAD_DIM ** (-0.5)
    scores = low_back(scores)
    scores = jnp.where(allowed[None], scores, -1e+30)
    top = lax.optimization_barrier(jnp.max(scores, axis=-1, keepdims=True))
    weights = jnp.exp(scores - top)
    probs = low(weights / lax.optimization_barrier(jnp.sum(weights, axis=-1, keepdims=True)))
    return jnp.einsum('hqk,khd->qhd', probs, values, precision=exact_prec)

def forward(params, resid, ids, starts):
    qkv_w, qkv_b, out_w, out_b, up_w, up_b, down_w, down_b, gain_a, shift_a, gain_m, shift_m = params
    groups, length = (resid.shape[0], resid.shape[1])
    flat = resid.reshape(groups * length, D)
    normed_attn = low(layer_norm(flat, gain_a, shift_a))
    normed_mlp = low(layer_norm(flat, gain_m, shift_m))
    projected = low_back(matmul(normed_attn, low(qkv_w).T)) + qkv_b
    projected = projected.reshape(groups, length, 3, HEADS, HEAD_DIM)
    positions = block_offset(ids, starts) + jnp.arange(length, dtype=jnp.int32)[None, :]
    cosine, sine = rotary_tables(positions)
    query = low_back(low(rotate(projected[:, :, 0], cosine, sine)))
    keys = low_back(low(rotate(projected[:, :, 1], cosine, sine)))
    values = low_back(low(projected[:, :, 2]))
    mixed = lax.map(jax.checkpoint(attend), (query, keys, values, ids))
    mixed = low_back(low(mixed.reshape(groups * length, D)))
    attn_out = low_back(matmul(mixed, low(out_w))) + out_b
    hidden = low_back(matmul(normed_mlp, low(up_w).T)) + up_b
    active = low_back(low(jax.nn.gelu(hidden, approximate=False)))
    branch = low_back(matmul(active, low(down_w))) + down_b
    return (flat + attn_out + branch).reshape(resid.shape)

def reference(resid_in, qkv_weight, qkv_bias, out_weight, out_bias, up_weight, up_bias, down_weight, down_bias, attn_gain, attn_shift, mlp_gain, mlp_shift, block_ids, offsets, grad_out):
    params = (qkv_weight, qkv_bias, out_weight, out_bias, up_weight, up_bias, down_weight, down_bias, attn_gain, attn_shift, mlp_gain, mlp_shift)
    group = math.gcd(SEQS, 4)
    count = SEQS // group

    def split(array):
        return array.reshape((count, group) + array.shape[1:])

    def step(totals, items):
        resid, ids, starts, cotangent = items

        def apply(weights, inputs):
            return forward(weights, inputs, ids, starts)
        result, pullback = jax.vjp(apply, params, resid)
        weight_grads, input_grad = pullback(cotangent)
        return (jax.tree.map(jnp.add, totals, weight_grads), (result, input_grad))
    zeros = jax.tree.map(jnp.zeros_like, params)
    totals, (outputs, input_grads) = lax.scan(step, zeros, (split(resid_in), split(block_ids), split(offsets), split(grad_out)))
    bias_grad = totals[1]
    return (outputs.reshape(resid_in.shape), input_grads.reshape(resid_in.shape), totals[0], bias_grad[:2 * D], bias_grad[2 * D:], totals[2], totals[3], totals[4], totals[5], totals[6], totals[7], totals[8], totals[9], totals[10], totals[11])
```

```python
import math

import jax
import jax.numpy as jnp
from jax import lax
from jax.sharding import PartitionSpec as P

HEADS = 8
HEAD_DIM = 256
ROT_DIM = 64


EPS = 1e-05
NEG_FILL = -1e30


def layer_norm(values, gain, shift):
    center = values - jnp.mean(values, axis=-1, keepdims=True)
    spread = jnp.mean(center * center, axis=-1, keepdims=True)
    return center * lax.rsqrt(spread + EPS) * gain + shift


def rotary_tables(positions):
    half = ROT_DIM // 2
    inverse = jnp.exp(jnp.arange(half, dtype=jnp.float32) * (-2.0 * math.log(10000.0) / ROT_DIM))
    angles = positions.astype(jnp.float32)[..., None] * inverse
    return (jnp.cos(angles), jnp.sin(angles))


def block_offset(ids, starts):
    numbers = jnp.arange(starts.shape[1], dtype=jnp.int32)
    match = (ids[:, :, None] == numbers[None, None, :]).astype(jnp.int32)
    return jnp.sum(match * starts[:, None, :], axis=-1)


def rotate(values, cosine, sine):
    half = ROT_DIM // 2
    cosine = cosine[..., None, :]
    sine = sine[..., None, :]
    first = values[..., :half]
    second = values[..., half:ROT_DIM]
    return jnp.concatenate(
        [first * cosine - second * sine, second * cosine + first * sine, values[..., ROT_DIM:]],
        axis=-1,
    )


def gelu_exact(values):
    return jax.nn.gelu(values, approximate=False)


def contract_lead(left, right):
    return lax.dot_general(
        left, right, (((0,), (0,)), ((), ())), preferred_element_type=jnp.float32
    )


def contract_last(left, right):
    return lax.dot_general(
        left, right, (((1,), (1,)), ((), ())), preferred_element_type=jnp.float32
    )


def attend_forward(items):
    query, keys, values, ids = items
    allowed = ids[None, :] <= ids[:, None]
    scores = jnp.where(allowed, contract_last(query, keys) * HEAD_DIM ** (-0.5), NEG_FILL)
    top = jnp.max(scores, axis=1, keepdims=True)
    weights = jnp.exp(scores - top)
    total = jnp.sum(weights, axis=1, keepdims=True)
    probs = (weights / total).astype(jnp.bfloat16)
    mixed = jnp.dot(probs, values, preferred_element_type=jnp.float32).astype(jnp.bfloat16)
    return (mixed, (top + jnp.log(total))[:, 0])


def attend_backward(items):
    query, keys, values, ids, lse_row, grad_mix = items
    scale = HEAD_DIM ** (-0.5)
    allowed = ids[None, :] <= ids[:, None]
    scores = contract_last(query, keys) * scale
    probs = jnp.where(allowed, jnp.exp(scores - lse_row[:, None]), 0.0)
    grad_probs = contract_last(grad_mix, values)
    inner = jnp.sum(probs * grad_probs, axis=1, keepdims=True)
    grad_scores = (probs * (grad_probs - inner)).astype(jnp.bfloat16)
    grad_query = (jnp.dot(grad_scores, keys, preferred_element_type=jnp.float32) * scale).astype(
        jnp.bfloat16
    )
    grad_keys = (contract_lead(grad_scores, query) * scale).astype(jnp.bfloat16)
    grad_values = contract_lead(probs.astype(jnp.bfloat16), grad_mix).astype(jnp.bfloat16)
    return (grad_query, grad_keys, grad_values)


def body(
    resid_in,
    qkv_weight,
    qkv_bias,
    out_weight,
    out_bias,
    up_weight,
    up_bias,
    down_weight,
    down_bias,
    attn_gain,
    attn_shift,
    mlp_gain,
    mlp_shift,
    block_ids,
    offsets,
    grad_out,
):
    groups, piece, width = resid_in.shape
    tokens = groups * piece
    pieces = lax.axis_size("seq")
    length = piece * pieces
    rank = lax.axis_index("fsdp")
    heads_here = HEADS // pieces
    pairs = groups * heads_here
    flat = resid_in.reshape(tokens, width)
    gain_a, shift_a, gain_m, shift_m, proj_bias, attn_bias, hidden_bias, mlp_bias = (
        lax.all_gather(attn_gain, "fsdp", axis=0, tiled=True),
        lax.all_gather(attn_shift, "fsdp", axis=0, tiled=True),
        lax.all_gather(mlp_gain, "fsdp", axis=0, tiled=True),
        lax.all_gather(mlp_shift, "fsdp", axis=0, tiled=True),
        lax.all_gather(qkv_bias, "fsdp", axis=0, tiled=True),
        lax.all_gather(out_bias, "fsdp", axis=0, tiled=True),
        lax.all_gather(up_bias, "fsdp", axis=0, tiled=True),
        lax.all_gather(down_bias, "fsdp", axis=0, tiled=True),
    )
    qkv_low = qkv_weight.astype(jnp.bfloat16)
    out_low = out_weight.astype(jnp.bfloat16)
    up_low = up_weight.astype(jnp.bfloat16)
    down_low = down_weight.astype(jnp.bfloat16)
    qkv_full, out_full = (
        lax.all_gather(qkv_low, "fsdp", axis=0, tiled=True),
        lax.all_gather(out_low, "fsdp", axis=0, tiled=True),
    )
    normed_a32, norm_back_a = jax.vjp(layer_norm, flat, gain_a, shift_a)
    normed_m32, norm_back_m = jax.vjp(layer_norm, flat, gain_m, shift_m)
    normed_attn = normed_a32.astype(jnp.bfloat16)
    normed_mlp = normed_m32.astype(jnp.bfloat16)
    projected = (contract_last(normed_attn, qkv_full) + proj_bias).reshape(
        groups, piece, 3, HEADS, HEAD_DIM
    )
    first_pos = lax.axis_index("seq") * piece
    ids_piece = lax.dynamic_slice_in_dim(block_ids, first_pos, piece, 1)
    positions = (
        block_offset(ids_piece, offsets) + first_pos + jnp.arange(piece, dtype=jnp.int32)[None, :]
    )
    cosine, sine = rotary_tables(positions)
    query = rotate(projected[:, :, 0], cosine, sine)
    keys = rotate(projected[:, :, 1], cosine, sine)
    packed = jnp.stack([query, keys, projected[:, :, 2]], axis=2).astype(jnp.bfloat16)
    heads = lax.all_to_all(packed, "seq", split_axis=3, concat_axis=1, tiled=True)
    stacked = heads.transpose(2, 0, 3, 1, 4).reshape(3, pairs, length, HEAD_DIM)
    ids_pairs = jnp.repeat(block_ids, heads_here, axis=0)
    mixed_pairs, lse_pairs = lax.map(
        attend_forward, (stacked[0], stacked[1], stacked[2], ids_pairs)
    )
    back_heads = mixed_pairs.reshape(groups, heads_here, length, HEAD_DIM).transpose(0, 2, 1, 3)
    mixed_tok = lax.all_to_all(back_heads, "seq", split_axis=1, concat_axis=2, tiled=True).reshape(
        tokens, width
    )
    attn_part = jnp.dot(mixed_tok, out_full, preferred_element_type=jnp.float32) + attn_bias
    units_here = up_weight.shape[0]
    group_rows = lax.all_gather(normed_mlp, "fsdp", axis=0, tiled=True)
    local_bias = lax.dynamic_slice_in_dim(hidden_bias, rank * units_here, units_here)
    hidden = contract_last(group_rows, up_low) + local_bias
    active, gelu_back = jax.vjp(gelu_exact, hidden)
    active_low = active.astype(jnp.bfloat16)
    branch = (
        lax.psum_scatter(
            jnp.dot(active_low, down_low, preferred_element_type=jnp.float32).astype(jnp.bfloat16),
            "fsdp",
            scatter_dimension=0,
            tiled=True,
        ).astype(jnp.float32)
        + mlp_bias
    )
    result = flat + attn_part + branch
    grad_flat = grad_out.reshape(tokens, width)
    grad_low = grad_flat.astype(jnp.bfloat16)
    bias_sum = jnp.sum(grad_flat, axis=0)
    group_grad = lax.all_gather(grad_low, "fsdp", axis=0, tiled=True)
    grad_active = contract_last(group_grad, down_low).astype(jnp.bfloat16)
    grad_hidden = gelu_back(grad_active.astype(jnp.float32))[0]
    grad_hidden_low = grad_hidden.astype(jnp.bfloat16)
    grad_normed_m = lax.psum_scatter(
        jnp.dot(grad_hidden_low, up_low, preferred_element_type=jnp.float32),
        "fsdp",
        scatter_dimension=0,
        tiled=True,
    )
    up_grad_shard = contract_lead(grad_hidden_low, group_rows)
    down_grad_shard = contract_lead(active_low, group_grad)
    local_sum = jnp.sum(grad_hidden, axis=0)
    up_bias_term = lax.dynamic_update_slice_in_dim(
        jnp.zeros((hidden_bias.shape[0],), jnp.float32), local_sum, rank * units_here, 0
    )
    grad_mixed = contract_last(grad_low, out_full).astype(jnp.bfloat16)
    grad_heads = lax.all_to_all(
        grad_mixed.reshape(groups, piece, HEADS, HEAD_DIM),
        "seq",
        split_axis=2,
        concat_axis=1,
        tiled=True,
    )
    grad_pairs = grad_heads.transpose(0, 2, 1, 3).reshape(pairs, length, HEAD_DIM)
    grad_query, grad_keys, grad_values = lax.map(
        attend_backward, (stacked[0], stacked[1], stacked[2], ids_pairs, lse_pairs, grad_pairs)
    )
    grads_stack = (
        jnp.stack([grad_query, grad_keys, grad_values], axis=0)
        .reshape(3, groups, heads_here, length, HEAD_DIM)
        .transpose(1, 3, 0, 2, 4)
    )
    returned = lax.all_to_all(grads_stack, "seq", split_axis=1, concat_axis=3, tiled=True).astype(
        jnp.float32
    )
    grad_projected = jnp.stack(
        [
            rotate(returned[:, :, 0], cosine, -sine),
            rotate(returned[:, :, 1], cosine, -sine),
            returned[:, :, 2],
        ],
        axis=2,
    ).reshape(tokens, 3 * width)
    grad_projected_low = grad_projected.astype(jnp.bfloat16)
    proj_bias_term = jnp.sum(grad_projected, axis=0)
    qk_bias_term = proj_bias_term[: 2 * width]
    value_bias_term = proj_bias_term[2 * width :]
    grad_normed_a = jnp.dot(grad_projected_low, qkv_full, preferred_element_type=jnp.float32)
    grad_from_a, gain_a_term, shift_a_term = norm_back_a(grad_normed_a)
    grad_from_m, gain_m_term, shift_m_term = norm_back_m(grad_normed_m)
    grad_input = grad_flat + grad_from_a + grad_from_m
    qkv_term = contract_lead(grad_projected_low, normed_attn)
    out_term = contract_lead(mixed_tok, grad_low)
    (
        qkv_shard,
        out_shard,
        qk_bias_shard,
        value_bias_shard,
        bias_shard,
        up_bias_shard,
        gain_a_shard,
        shift_a_shard,
        gain_m_shard,
        shift_m_shard,
    ) = (
        lax.psum_scatter(qkv_term, "fsdp", scatter_dimension=0, tiled=True),
        lax.psum_scatter(out_term, "fsdp", scatter_dimension=0, tiled=True),
        lax.psum_scatter(qk_bias_term, "fsdp", scatter_dimension=0, tiled=True),
        lax.psum_scatter(value_bias_term, "fsdp", scatter_dimension=0, tiled=True),
        lax.psum_scatter(bias_sum, "fsdp", scatter_dimension=0, tiled=True),
        lax.psum_scatter(up_bias_term, "fsdp", scatter_dimension=0, tiled=True),
        lax.psum_scatter(gain_a_term, "fsdp", scatter_dimension=0, tiled=True),
        lax.psum_scatter(shift_a_term, "fsdp", scatter_dimension=0, tiled=True),
        lax.psum_scatter(gain_m_term, "fsdp", scatter_dimension=0, tiled=True),
        lax.psum_scatter(shift_m_term, "fsdp", scatter_dimension=0, tiled=True),
    )
    totals = lax.psum(
        (
            qkv_shard,
            out_shard,
            up_grad_shard,
            down_grad_shard,
            qk_bias_shard,
            value_bias_shard,
            bias_shard,
            up_bias_shard,
            gain_a_shard,
            shift_a_shard,
            gain_m_shard,
            shift_m_shard,
        ),
        "seq",
    )
    return (
        result.reshape(groups, piece, width),
        grad_input.reshape(groups, piece, width),
        totals[0],
        totals[4],
        totals[5],
        totals[1],
        totals[6],
        totals[2],
        totals[7],
        totals[3],
        totals[6],
        totals[8],
        totals[9],
        totals[10],
        totals[11],
    )


LANES = 128


def pick(slices, which):
    return lax.dynamic_index_in_dim(slices, which, 0, keepdims=False)


def swap_core(value):
    return lax.ppermute(value, "fsdp", [(i, i ^ 1) for i in range(8)])


def along_z(value, pairs):
    return lax.ppermute(value, "fsdp", [(2 * a + c, 2 * b + c) for a, b in pairs for c in range(2)])


def spread_pairs(step):
    pairs = []
    for source in range(4):
        part = (step + source) % 4
        for rank in range(8):
            pairs.append((source * 8 + rank, (2 * (rank % 2) + part // 2) * 8 + rank - rank % 2 + part % 2))
    return pairs


def gather_z(own, z):
    low_half = z < 2
    edge = (z == 0) | (z == 3)
    above = along_z(own, [(1, 0), (2, 1), (3, 2)])
    below = along_z(own, [(0, 1), (1, 2), (2, 3)])
    first = jnp.where(low_half, above, below)
    outer = jnp.where(low_half, below, above)
    inner = along_z(first, [(1, 0), (2, 3)])
    cross = along_z(outer, [(1, 2), (2, 1)])
    second = jnp.where(edge, inner, outer)
    third = jnp.where(edge, along_z(cross, [(1, 0), (2, 3)]), cross)
    return [own, first, second, third]


def scatter_z(parts, z):
    low = jnp.bfloat16
    low_half = z < 2
    far = along_z(parts[3].astype(low), [(0, 1), (3, 2)])
    cross = along_z((parts[3] + far.astype(jnp.float32)).astype(low), [(1, 2), (2, 1)])
    near = along_z(parts[2].astype(low), [(0, 1), (3, 2)])
    one = parts[1] + near.astype(jnp.float32)
    two = parts[2] + cross.astype(jnp.float32)
    up = jnp.where(low_half, one, two).astype(low)
    down = jnp.where(low_half, two, one).astype(low)
    from_below = along_z(up, [(0, 1), (1, 2), (2, 3)])
    from_above = along_z(down, [(1, 0), (2, 1), (3, 2)])
    return parts[0] + from_below.astype(jnp.float32) + from_above.astype(jnp.float32)


def swap_seq(value, bit):
    return lax.ppermute(value, "seq", [(i, i ^ bit) for i in range(4)])


def sum_seq(part, x, y):
    rows, columns = part.shape
    halves = part.reshape(2, 2, 2, rows // 8, columns)
    low = jnp.bfloat16
    outs = []
    for half, (bit_a, at_a), (bit_b, at_b) in ((0, (1, x), (2, y)), (1, (2, y), (1, x))):
        mine = halves[half]
        sent = swap_seq(pick(mine, 1 - at_a).astype(low), bit_a)
        kept = pick(mine, at_a) + sent.astype(jnp.float32)
        sent = swap_seq(pick(kept, 1 - at_b).astype(low), bit_b)
        outs.append((pick(kept, at_b) + sent.astype(jnp.float32)).astype(low))
    return outs


def spread_seq(pieces, x, y):
    outs = []
    for piece, (bit_a, at_a), (bit_b, at_b) in ((pieces[0], (1, x), (2, y)), (pieces[1], (2, y), (1, x))):
        other = swap_seq(piece, bit_b)
        both = jnp.where(at_b == 0, jnp.stack([piece, other]), jnp.stack([other, piece]))
        other = swap_seq(both, bit_a)
        outs.append(jnp.where(at_a == 0, jnp.stack([both, other]), jnp.stack([other, both])))
    rows, columns = pieces[0].shape
    return jnp.stack(outs).reshape(8 * rows, columns).astype(jnp.float32)


def split_body(
    resid_in,
    qkv_weight,
    qkv_bias,
    out_weight,
    out_bias,
    up_weight,
    up_bias,
    down_weight,
    down_bias,
    attn_gain,
    attn_shift,
    mlp_gain,
    mlp_shift,
    block_ids,
    offsets,
    grad_out,
):
    low = jnp.bfloat16
    f32 = jnp.float32
    groups, piece, width = resid_in.shape
    tokens = groups * piece
    s = lax.axis_index("seq")
    f = lax.axis_index("fsdp")
    z, c = f // 2, f % 2
    x, y = s % 2, s // 2
    both_axes = ("seq", "fsdp")
    units = up_weight.shape[0]

    packed = jnp.concatenate(
        [attn_gain, attn_shift, mlp_gain, mlp_shift, out_bias + down_bias, qkv_bias]
    )
    small = lax.all_gather(packed, "fsdp", axis=0)
    gain_a, shift_a, gain_m, shift_m, bias_out = (
        small[:, i * 256 : (i + 1) * 256].reshape(width) for i in range(5)
    )
    head_bias = small[:, 5 * 256 :].reshape(3, HEADS, HEAD_DIM)
    head_bias = lax.dynamic_index_in_dim(head_bias, f, 1, keepdims=False).reshape(3 * HEAD_DIM)
    ids_starts = lax.all_gather(
        jnp.concatenate([block_ids, offsets], axis=1), "fsdp", axis=0, tiled=True
    )
    ids_all = ids_starts[:, : block_ids.shape[1]]
    starts_all = ids_starts[:, block_ids.shape[1] :]

    flat = resid_in.reshape(tokens, width)
    center = flat - jnp.mean(flat, axis=-1, keepdims=True)
    inv = lax.rsqrt(jnp.mean(center * center, axis=-1, keepdims=True) + EPS)
    normal = center * inv
    grad_flat = grad_out.reshape(tokens, width)

    def plane_out(value):
        parts = value.reshape(4, tokens // 4, width)
        got = [
            lax.ppermute(pick(parts, (k + s) % 4), both_axes, spread_pairs(k)) for k in range(4)
        ]
        return jnp.concatenate(got, axis=0)

    def plane_back(value):
        parts = value.reshape(4, tokens // 4, width)
        got = jnp.stack(
            [
                lax.ppermute(parts[k], both_axes, [(b, a) for a, b in spread_pairs(k)])
                for k in range(4)
            ]
        )
        return jnp.concatenate([pick(got, (j - s + 4) % 4) for j in range(4)], axis=0)

    own_n = plane_out(normal.astype(low))
    own_g = plane_out(grad_flat.astype(low))

    quarter = HEAD_DIM // 4
    qkv_low = lax.dynamic_slice_in_dim(
        qkv_weight.reshape(3, HEAD_DIM, width), s * quarter, quarter, 1
    ).astype(low)
    came = jnp.stack(
        [
            lax.ppermute(qkv_low[i], "fsdp", [(r, (3 * r + i) % 8) for r in range(8)])
            for i in range(3)
        ]
    )

    def third_of(i):
        return (3 * ((3 * (f - i + 8)) % 8) + i) // 8

    slot_of = [
        sum(jnp.where(third_of(i) == kind, i, 0) for i in range(3)) for kind in range(3)
    ]
    came = jnp.stack([pick(came, slot_of[kind]) for kind in range(3)])
    head_w = lax.all_gather(came, "seq", axis=1, tiled=True).reshape(3 * HEAD_DIM, width)
    up_low = up_weight.astype(low)
    plain_w = jnp.concatenate([up_low, head_w], axis=0)
    gains = jnp.concatenate(
        [jnp.broadcast_to(gain_m, (units, width)), jnp.broadcast_to(gain_a, (768, width))], axis=0
    )
    shifts = jnp.concatenate(
        [jnp.broadcast_to(shift_m, (units, width)), jnp.broadcast_to(shift_a, (768, width))],
        axis=0,
    )
    w_in = (plain_w.astype(f32) * gains).astype(low)
    bias_in = jnp.concatenate([up_bias, head_bias]) + jnp.sum(
        plain_w.astype(f32) * shifts, axis=1
    )
    w_out = jnp.concatenate([down_weight, out_weight], axis=0).astype(low)

    halves = [(2 * (s % 2) + c, c), (2 * (s % 2) + 1 - c, 1 - c)]
    rows_at = [((part - k + 4) % 4) * 2 + core for part, core in halves for k in range(4)]
    blocks = [
        z,
        jnp.where(z % 2 == 0, 1, 2),
        jnp.where(z == 0, 2, jnp.where(z == 1, 0, jnp.where(z == 2, 3, 1))),
        jnp.where(z < 2, 3, 0),
    ]
    ids_rows = ids_all.reshape(16, 8, LANES)
    ids_slots = [pick(ids_rows, block * 4 + s) for block in blocks]
    ids_here = jnp.stack(
        [jnp.concatenate([pick(row, at) for at in rows_at]) for row in ids_slots]
    )
    starts_here = jnp.stack([pick(starts_all, block * 4 + s) for block in blocks])
    pos = (jnp.stack(rows_at)[:, None] * LANES + jnp.arange(LANES)[None, :]).reshape(1024)
    positions = block_offset(ids_here, starts_here) + pos[None, :]
    cosine, sine = rotary_tables(positions)

    slots_n = gather_z(own_n, z)
    own_g, _ = lax.optimization_barrier((own_g, slots_n[3]))
    slots_g = gather_z(own_g, z)

    full_n, kept_act, kept_slope, heads, outs = [], [], [], [], []
    parts = []
    for t in range(4):
        n_t = jnp.concatenate([slots_n[t], swap_core(slots_n[t])], axis=0)
        full_n.append(n_t)
        projected = contract_last(n_t, w_in) + bias_in
        hidden = projected[:, :units]
        cdf = 0.5 * (1.0 + lax.erf(hidden * (0.5**0.5)))
        act = (hidden * cdf).astype(low)
        slope = (cdf + hidden * jnp.exp(-0.5 * hidden * hidden) * (1.0 / math.sqrt(2.0 * math.pi))).astype(low)
        qkv = projected[:, units:].reshape(1024, 3, HEAD_DIM)
        query = rotate(qkv[:, None, 0], cosine[t], sine[t])[:, 0].astype(low)
        keys = rotate(qkv[:, None, 1], cosine[t], sine[t])[:, 0].astype(low)
        values = qkv[:, 2].astype(low)
        mixed, lse = attend_forward((query, keys, values, ids_here[t]))
        heads.append((query, keys, values, lse))
        a_t = jnp.concatenate([act, mixed], axis=1)
        outs.append(a_t)
        kept_slope.append(slope)
        p_own = jnp.dot(a_t[:512], w_out, preferred_element_type=f32)
        p_sib = jnp.dot(a_t[512:], w_out, preferred_element_type=f32).astype(low)
        parts.append(p_own + swap_core(p_sib).astype(f32))
    branch = plane_back(scatter_z(parts, z).astype(low))
    result = flat + branch.astype(f32) + bias_out

    full_g, backs, parts = [], [], []
    for t in range(4):
        g_t = jnp.concatenate([slots_g[t], swap_core(slots_g[t])], axis=0)
        full_g.append(g_t)
        grad_a = contract_last(g_t, w_out).astype(low)
        gh = (grad_a[:, :units].astype(f32) * kept_slope[t].astype(f32)).astype(low)
        query, keys, values, lse = heads[t]
        gq, gk, gv = attend_backward((query, keys, values, ids_here[t], lse, grad_a[:, units:]))
        gq = rotate(gq.astype(f32)[:, None], cosine[t], -sine[t])[:, 0].astype(low)
        gk = rotate(gk.astype(f32)[:, None], cosine[t], -sine[t])[:, 0].astype(low)
        b_t = jnp.concatenate([gh, gq, gk, gv], axis=1)
        backs.append(b_t)
        u_own = jnp.dot(b_t[:512], w_in, preferred_element_type=f32)
        u_sib = jnp.dot(b_t[512:], w_in, preferred_element_type=f32).astype(low)
        parts.append(u_own + swap_core(u_sib).astype(f32))
    u = plane_back(scatter_z(parts, z).astype(low)).astype(f32)
    grad_input = grad_flat + inv * (
        u - jnp.mean(u, axis=-1, keepdims=True) - normal * jnp.mean(u * normal, axis=-1, keepdims=True)
    )

    all_n, all_g = jnp.concatenate(full_n), jnp.concatenate(full_g)
    all_a, all_b = jnp.concatenate(outs), jnp.concatenate(backs)
    term_out = contract_lead(all_a, all_g)
    raw_in = contract_lead(all_b, all_n)
    sums = jnp.sum(all_b.astype(f32), axis=0)
    term_in = raw_in * gains + sums[:, None] * shifts
    gain_terms = raw_in * plain_w.astype(f32)
    shift_terms = sums[:, None] * plain_w.astype(f32)

    down_out = spread_seq(sum_seq(term_out, x, y), x, y)
    up_out = spread_seq(sum_seq(term_in[:units], x, y), x, y)
    qkv_quarter = sum_seq(term_in[units:].reshape(3, 2, 4, 32, width).transpose(1, 2, 0, 3, 4).reshape(768, width), x, y)
    qkv_quarter = jnp.stack(qkv_quarter).reshape(2, 3, 32, width)
    kinds = jnp.stack([pick(qkv_quarter.transpose(1, 0, 2, 3), third_of(i)) for i in range(3)])
    qkv_back = [
        lax.ppermute(kinds[i], "fsdp", [((3 * r + i) % 8, r) for r in range(8)]) for i in range(3)
    ]
    qkv_back = jnp.stack(qkv_back).transpose(1, 0, 2, 3).reshape(2, 96, width)
    qkv_out = spread_seq([qkv_back[0], qkv_back[1]], x, y)
    qkv_out = qkv_out.reshape(2, 4, 3, 32, width).transpose(2, 0, 1, 3, 4).reshape(768, width)

    slots = jnp.zeros((16, HEAD_DIM), f32)
    slots = lax.dynamic_update_slice(slots, sums[units : units + 256][None], (f, 0))
    slots = lax.dynamic_update_slice(slots, sums[units + 256 : units + 512][None], (8 + f, 0))
    spread = jnp.stack(
        [
            jnp.sum(gain_terms[units:], axis=0),
            jnp.sum(shift_terms[units:], axis=0),
            jnp.sum(gain_terms[:units], axis=0),
            jnp.sum(shift_terms[:units], axis=0),
            jnp.sum(grad_flat, axis=0),
        ]
    )
    wide = jnp.concatenate(
        [spread.reshape(5, 8, 256).transpose(1, 0, 2).reshape(8, 5 * 256), slots.reshape(8, 512)], axis=1
    )
    mine = lax.psum_scatter(wide, "fsdp", scatter_dimension=0, tiled=True)[0]
    mine = lax.psum(jnp.concatenate([mine, sums[:units], sums[units + 512 :]]), "seq")
    vectors = [mine[i * 256 : (i + 1) * 256] for i in range(5)]
    qk_grad = mine[1280:1792]
    up_bias_grad = mine[1792 : 1792 + units]
    value_grad = mine[1792 + units :]
    return (
        result.reshape(groups, piece, width),
        grad_input.reshape(groups, piece, width),
        qkv_out,
        qk_grad,
        value_grad,
        down_out[units:],
        vectors[4],
        up_out,
        up_bias_grad,
        down_out[:units],
        vectors[4],
        vectors[0],
        vectors[1],
        vectors[2],
        vectors[3],
    )


def solution(mesh):
    placed = (
        P("fsdp", "seq", None),
        P("fsdp", None),
        P("fsdp"),
        P("fsdp", None),
        P("fsdp"),
        P("fsdp", None),
        P("fsdp"),
        P("fsdp", None),
        P("fsdp"),
        P("fsdp"),
        P("fsdp"),
        P("fsdp"),
        P("fsdp"),
        P("fsdp", None),
        P("fsdp", None),
        P("fsdp", "seq", None),
    )
    return jax.shard_map(
        split_body if mesh.shape["fsdp"] == HEADS and mesh.shape["seq"] == 4 else body,
        mesh=mesh,
        in_specs=placed,
        out_specs=(
            P("fsdp", "seq", None),
            P("fsdp", "seq", None),
            P("fsdp", None),
            P("fsdp"),
            P("fsdp"),
            P("fsdp", None),
            P("fsdp"),
            P("fsdp", None),
            P("fsdp"),
            P("fsdp", None),
            P("fsdp"),
            P("fsdp"),
            P("fsdp"),
            P("fsdp"),
            P("fsdp"),
        ),
        check_vma=False,
    )
```

```python
import functools
import math

import jax
import jax.numpy as jnp
from jax import lax
from jax.experimental import pallas as pl
from jax.experimental.pallas import tpu as pltpu
from jax.sharding import PartitionSpec as P

HEADS = 8
HEAD_DIM = 256
ROT_DIM = 64


EPS = 1e-05
NEG_FILL = -1e30


def layer_norm(values, gain, shift):
    center = values - jnp.mean(values, axis=-1, keepdims=True)
    spread = jnp.mean(center * center, axis=-1, keepdims=True)
    return center * lax.rsqrt(spread + EPS) * gain + shift


def rotary_tables(positions):
    half = ROT_DIM // 2
    inverse = jnp.exp(jnp.arange(half, dtype=jnp.float32) * (-2.0 * math.log(10000.0) / ROT_DIM))
    angles = positions.astype(jnp.float32)[..., None] * inverse
    return (jnp.cos(angles), jnp.sin(angles))


def block_offset(ids, starts):
    numbers = jnp.arange(starts.shape[1], dtype=jnp.int32)
    match = (ids[:, :, None] == numbers[None, None, :]).astype(jnp.int32)
    return jnp.sum(match * starts[:, None, :], axis=-1)


def rotate(values, cosine, sine):
    half = ROT_DIM // 2
    cosine = cosine[..., None, :]
    sine = sine[..., None, :]
    first = values[..., :half]
    second = values[..., half:ROT_DIM]
    return jnp.concatenate(
        [first * cosine - second * sine, second * cosine + first * sine, values[..., ROT_DIM:]],
        axis=-1,
    )


def gelu_exact(values):
    return jax.nn.gelu(values, approximate=False)


def contract_lead(left, right):
    return lax.dot_general(
        left, right, (((0,), (0,)), ((), ())), preferred_element_type=jnp.float32
    )


def contract_last(left, right):
    return lax.dot_general(
        left, right, (((1,), (1,)), ((), ())), preferred_element_type=jnp.float32
    )


def attend_forward(items):
    query, keys, values, ids = items
    allowed = ids[None, :] <= ids[:, None]
    scores = jnp.where(allowed, contract_last(query, keys) * HEAD_DIM ** (-0.5), NEG_FILL)
    top = jnp.max(scores, axis=1, keepdims=True)
    weights = jnp.exp(scores - top)
    total = jnp.sum(weights, axis=1, keepdims=True)
    probs = (weights / total).astype(jnp.bfloat16)
    mixed = jnp.dot(probs, values, preferred_element_type=jnp.float32).astype(jnp.bfloat16)
    return (mixed, (top + jnp.log(total))[:, 0])


def attend_backward(items):
    query, keys, values, ids, lse_row, grad_mix = items
    scale = HEAD_DIM ** (-0.5)
    allowed = ids[None, :] <= ids[:, None]
    scores = contract_last(query, keys) * scale
    probs = jnp.where(allowed, jnp.exp(scores - lse_row[:, None]), 0.0)
    grad_probs = contract_last(grad_mix, values)
    inner = jnp.sum(probs * grad_probs, axis=1, keepdims=True)
    grad_scores = (probs * (grad_probs - inner)).astype(jnp.bfloat16)
    grad_query = (jnp.dot(grad_scores, keys, preferred_element_type=jnp.float32) * scale).astype(
        jnp.bfloat16
    )
    grad_keys = (contract_lead(grad_scores, query) * scale).astype(jnp.bfloat16)
    grad_values = contract_lead(probs.astype(jnp.bfloat16), grad_mix).astype(jnp.bfloat16)
    return (grad_query, grad_keys, grad_values)


def body(
    resid_in,
    qkv_weight,
    qkv_bias,
    out_weight,
    out_bias,
    up_weight,
    up_bias,
    down_weight,
    down_bias,
    attn_gain,
    attn_shift,
    mlp_gain,
    mlp_shift,
    block_ids,
    offsets,
    grad_out,
):
    groups, piece, width = resid_in.shape
    tokens = groups * piece
    pieces = lax.axis_size("seq")
    length = piece * pieces
    rank = lax.axis_index("fsdp")
    heads_here = HEADS // pieces
    pairs = groups * heads_here
    flat = resid_in.reshape(tokens, width)
    gain_a, shift_a, gain_m, shift_m, proj_bias, attn_bias, hidden_bias, mlp_bias = (
        lax.all_gather(attn_gain, "fsdp", axis=0, tiled=True),
        lax.all_gather(attn_shift, "fsdp", axis=0, tiled=True),
        lax.all_gather(mlp_gain, "fsdp", axis=0, tiled=True),
        lax.all_gather(mlp_shift, "fsdp", axis=0, tiled=True),
        lax.all_gather(qkv_bias, "fsdp", axis=0, tiled=True),
        lax.all_gather(out_bias, "fsdp", axis=0, tiled=True),
        lax.all_gather(up_bias, "fsdp", axis=0, tiled=True),
        lax.all_gather(down_bias, "fsdp", axis=0, tiled=True),
    )
    qkv_low = qkv_weight.astype(jnp.bfloat16)
    out_low = out_weight.astype(jnp.bfloat16)
    up_low = up_weight.astype(jnp.bfloat16)
    down_low = down_weight.astype(jnp.bfloat16)
    qkv_full, out_full = (
        lax.all_gather(qkv_low, "fsdp", axis=0, tiled=True),
        lax.all_gather(out_low, "fsdp", axis=0, tiled=True),
    )
    normed_a32, norm_back_a = jax.vjp(layer_norm, flat, gain_a, shift_a)
    normed_m32, norm_back_m = jax.vjp(layer_norm, flat, gain_m, shift_m)
    normed_attn = normed_a32.astype(jnp.bfloat16)
    normed_mlp = normed_m32.astype(jnp.bfloat16)
    projected = (contract_last(normed_attn, qkv_full) + proj_bias).reshape(
        groups, piece, 3, HEADS, HEAD_DIM
    )
    first_pos = lax.axis_index("seq") * piece
    ids_piece = lax.dynamic_slice_in_dim(block_ids, first_pos, piece, 1)
    positions = (
        block_offset(ids_piece, offsets) + first_pos + jnp.arange(piece, dtype=jnp.int32)[None, :]
    )
    cosine, sine = rotary_tables(positions)
    query = rotate(projected[:, :, 0], cosine, sine)
    keys = rotate(projected[:, :, 1], cosine, sine)
    packed = jnp.stack([query, keys, projected[:, :, 2]], axis=2).astype(jnp.bfloat16)
    heads = lax.all_to_all(packed, "seq", split_axis=3, concat_axis=1, tiled=True)
    stacked = heads.transpose(2, 0, 3, 1, 4).reshape(3, pairs, length, HEAD_DIM)
    ids_pairs = jnp.repeat(block_ids, heads_here, axis=0)
    mixed_pairs, lse_pairs = lax.map(
        attend_forward, (stacked[0], stacked[1], stacked[2], ids_pairs)
    )
    back_heads = mixed_pairs.reshape(groups, heads_here, length, HEAD_DIM).transpose(0, 2, 1, 3)
    mixed_tok = lax.all_to_all(back_heads, "seq", split_axis=1, concat_axis=2, tiled=True).reshape(
        tokens, width
    )
    attn_part = jnp.dot(mixed_tok, out_full, preferred_element_type=jnp.float32) + attn_bias
    units_here = up_weight.shape[0]
    group_rows = lax.all_gather(normed_mlp, "fsdp", axis=0, tiled=True)
    local_bias = lax.dynamic_slice_in_dim(hidden_bias, rank * units_here, units_here)
    hidden = contract_last(group_rows, up_low) + local_bias
    active, gelu_back = jax.vjp(gelu_exact, hidden)
    active_low = active.astype(jnp.bfloat16)
    branch = (
        lax.psum_scatter(
            jnp.dot(active_low, down_low, preferred_element_type=jnp.float32).astype(jnp.bfloat16),
            "fsdp",
            scatter_dimension=0,
            tiled=True,
        ).astype(jnp.float32)
        + mlp_bias
    )
    result = flat + attn_part + branch
    grad_flat = grad_out.reshape(tokens, width)
    grad_low = grad_flat.astype(jnp.bfloat16)
    bias_sum = jnp.sum(grad_flat, axis=0)
    group_grad = lax.all_gather(grad_low, "fsdp", axis=0, tiled=True)
    grad_active = contract_last(group_grad, down_low).astype(jnp.bfloat16)
    grad_hidden = gelu_back(grad_active.astype(jnp.float32))[0]
    grad_hidden_low = grad_hidden.astype(jnp.bfloat16)
    grad_normed_m = lax.psum_scatter(
        jnp.dot(grad_hidden_low, up_low, preferred_element_type=jnp.float32),
        "fsdp",
        scatter_dimension=0,
        tiled=True,
    )
    up_grad_shard = contract_lead(grad_hidden_low, group_rows)
    down_grad_shard = contract_lead(active_low, group_grad)
    local_sum = jnp.sum(grad_hidden, axis=0)
    up_bias_term = lax.dynamic_update_slice_in_dim(
        jnp.zeros((hidden_bias.shape[0],), jnp.float32), local_sum, rank * units_here, 0
    )
    grad_mixed = contract_last(grad_low, out_full).astype(jnp.bfloat16)
    grad_heads = lax.all_to_all(
        grad_mixed.reshape(groups, piece, HEADS, HEAD_DIM),
        "seq",
        split_axis=2,
        concat_axis=1,
        tiled=True,
    )
    grad_pairs = grad_heads.transpose(0, 2, 1, 3).reshape(pairs, length, HEAD_DIM)
    grad_query, grad_keys, grad_values = lax.map(
        attend_backward, (stacked[0], stacked[1], stacked[2], ids_pairs, lse_pairs, grad_pairs)
    )
    grads_stack = (
        jnp.stack([grad_query, grad_keys, grad_values], axis=0)
        .reshape(3, groups, heads_here, length, HEAD_DIM)
        .transpose(1, 3, 0, 2, 4)
    )
    returned = lax.all_to_all(grads_stack, "seq", split_axis=1, concat_axis=3, tiled=True).astype(
        jnp.float32
    )
    grad_projected = jnp.stack(
        [
            rotate(returned[:, :, 0], cosine, -sine),
            rotate(returned[:, :, 1], cosine, -sine),
            returned[:, :, 2],
        ],
        axis=2,
    ).reshape(tokens, 3 * width)
    grad_projected_low = grad_projected.astype(jnp.bfloat16)
    proj_bias_term = jnp.sum(grad_projected, axis=0)
    qk_bias_term = proj_bias_term[: 2 * width]
    value_bias_term = proj_bias_term[2 * width :]
    grad_normed_a = jnp.dot(grad_projected_low, qkv_full, preferred_element_type=jnp.float32)
    grad_from_a, gain_a_term, shift_a_term = norm_back_a(grad_normed_a)
    grad_from_m, gain_m_term, shift_m_term = norm_back_m(grad_normed_m)
    grad_input = grad_flat + grad_from_a + grad_from_m
    qkv_term = contract_lead(grad_projected_low, normed_attn)
    out_term = contract_lead(mixed_tok, grad_low)
    (
        qkv_shard,
        out_shard,
        qk_bias_shard,
        value_bias_shard,
        bias_shard,
        up_bias_shard,
        gain_a_shard,
        shift_a_shard,
        gain_m_shard,
        shift_m_shard,
    ) = (
        lax.psum_scatter(qkv_term, "fsdp", scatter_dimension=0, tiled=True),
        lax.psum_scatter(out_term, "fsdp", scatter_dimension=0, tiled=True),
        lax.psum_scatter(qk_bias_term, "fsdp", scatter_dimension=0, tiled=True),
        lax.psum_scatter(value_bias_term, "fsdp", scatter_dimension=0, tiled=True),
        lax.psum_scatter(bias_sum, "fsdp", scatter_dimension=0, tiled=True),
        lax.psum_scatter(up_bias_term, "fsdp", scatter_dimension=0, tiled=True),
        lax.psum_scatter(gain_a_term, "fsdp", scatter_dimension=0, tiled=True),
        lax.psum_scatter(shift_a_term, "fsdp", scatter_dimension=0, tiled=True),
        lax.psum_scatter(gain_m_term, "fsdp", scatter_dimension=0, tiled=True),
        lax.psum_scatter(shift_m_term, "fsdp", scatter_dimension=0, tiled=True),
    )
    totals = lax.psum(
        (
            qkv_shard,
            out_shard,
            up_grad_shard,
            down_grad_shard,
            qk_bias_shard,
            value_bias_shard,
            bias_shard,
            up_bias_shard,
            gain_a_shard,
            shift_a_shard,
            gain_m_shard,
            shift_m_shard,
        ),
        "seq",
    )
    return (
        result.reshape(groups, piece, width),
        grad_input.reshape(groups, piece, width),
        totals[0],
        totals[4],
        totals[5],
        totals[1],
        totals[6],
        totals[2],
        totals[7],
        totals[3],
        totals[6],
        totals[8],
        totals[9],
        totals[10],
        totals[11],
    )


bf, f32 = jnp.bfloat16, jnp.float32
TOK, HALF = 1024, 512
VM = 56 * 1024 * 1024


def nt(a, b):
    return lax.dot_general(a, b, (((1,), (1,)), ((), ())), preferred_element_type=f32)


def nn(a, b):
    return lax.dot_general(a, b, (((1,), (0,)), ((), ())), preferred_element_type=f32)


def tn(a, b):
    return lax.dot_general(a, b, (((0,), (0,)), ((), ())), preferred_element_type=f32)


def params(n=1, limit=VM):
    return pltpu.CompilerParams(dimension_semantics=("arbitrary",) * n, vmem_limit_bytes=limit)


def cost(flops, nbytes):
    return pl.CostEstimate(flops=int(flops), bytes_accessed=int(nbytes), transcendentals=0)


def turn(head, c, s):
    first = head[:, :128]
    lane = lax.broadcasted_iota(jnp.int32, first.shape, 1)
    partner = jnp.where(lane < 32, pltpu.roll(first, 96, 1), pltpu.roll(first, 32, 1))
    return jnp.concatenate([first * c + partner * s, head[:, 128:]], axis=1)


def gelu_pair(h):
    cdf = 0.5 * (1.0 + lax.erf(h * (0.5**0.5)))
    pdf = jnp.exp(-0.5 * (h * h)) * (1.0 / math.sqrt(2.0 * math.pi))
    return (h * cdf).astype(bf), (cdf + h * pdf).astype(bf)


def h_body(units_tiles, n0, n1, w, b, c, s, act, slope, qkv, x):
    j = pl.program_id(0)

    @pl.when(j == 0)
    def _():
        x[:HALF] = n0[...]
        x[HALF:] = n1[...]

    @pl.when(j < units_tiles)
    def _():
        act[...], slope[...] = gelu_pair(nt(x[...], w[...]) + b[...])

    @pl.when((j >= units_tiles) & (j < units_tiles + 2))
    def _():
        qkv[0] = turn(nt(x[...], w[...]) + b[...], c[0], s[0]).astype(bf)

    @pl.when(j == units_tiles + 2)
    def _():
        qkv[0] = (nt(x[...], w[...]) + b[...]).astype(bf)


def h_call(n0, n1, w, b, c, s, t):
    width = n0.shape[1]
    rows = w.shape[0]
    tile = 256
    units_tiles = (rows - 768) // tile
    full = lambda *shape: pl.BlockSpec(shape, lambda j: (0,) * len(shape))
    return pl.pallas_call(
        functools.partial(h_body, units_tiles),
        grid=(rows // tile,),
        in_specs=[
            full(HALF, width), full(HALF, width),
            pl.BlockSpec((tile, width), lambda j: (j, 0)),
            pl.BlockSpec((1, tile), lambda j: (0, j)),
            pl.BlockSpec((1, TOK, 128), lambda j: (t, 0, 0)), pl.BlockSpec((1, TOK, 128), lambda j: (t, 0, 0)),
        ],
        out_specs=[
            pl.BlockSpec((TOK, tile), lambda j: (0, jnp.minimum(j, units_tiles - 1))),
            pl.BlockSpec((TOK, tile), lambda j: (0, jnp.minimum(j, units_tiles - 1))),
            pl.BlockSpec((1, TOK, tile), lambda j: (jnp.maximum(j - units_tiles, 0), 0, 0)),
        ],
        out_shape=[
            jax.ShapeDtypeStruct((TOK, rows - 768), bf),
            jax.ShapeDtypeStruct((TOK, rows - 768), bf),
            jax.ShapeDtypeStruct((3, TOK, 256), bf),
        ],
        scratch_shapes=[pltpu.VMEM((TOK, width), bf)],
        compiler_params=params(),
        cost_estimate=cost(2 * TOK * width * rows, 24e6),
        name="project",
    )(n0, n1, w, b, c, s)


def attn_body(q, k, v, idq, idk, mixed, lse):
    scores = nt(q[0], k[0]) * (256 ** -0.5)
    allowed = idk[0] <= idq[0]
    scores = jnp.where(allowed, scores, -1e30)
    top = jnp.max(scores, axis=1, keepdims=True)
    weights = jnp.exp(scores - top)
    total = jnp.sum(weights, axis=1, keepdims=True)
    probs = (weights / total).astype(bf)
    mixed[...] = nn(probs, v[0]).astype(bf)
    lse[...] = top + jnp.log(total)


def attn_call(qkv, ids_col, ids_row, t):
    tile = 256
    return pl.pallas_call(
        attn_body,
        grid=(TOK // tile,),
        in_specs=[
            pl.BlockSpec((1, tile, 256), lambda i: (0, i, 0)),
            pl.BlockSpec((1, TOK, 256), lambda i: (1, 0, 0)),
            pl.BlockSpec((1, TOK, 256), lambda i: (2, 0, 0)),
            pl.BlockSpec((1, tile, 1), lambda i: (t, i, 0)),
            pl.BlockSpec((1, 1, TOK), lambda i: (t, 0, 0)),
        ],
        out_specs=[
            pl.BlockSpec((tile, 256), lambda i: (i, 0)),
            pl.BlockSpec((tile, 1), lambda i: (i, 0)),
        ],
        out_shape=[jax.ShapeDtypeStruct((TOK, 256), bf), jax.ShapeDtypeStruct((TOK, 1), f32)],
        compiler_params=params(),
        cost_estimate=cost(4 * TOK * TOK * 256, 4e6),
        name="attend",
    )(qkv, qkv, qkv, ids_col, ids_row)


def attn_back_body(q, k, v, g, idq, idk, lse, cq, sq, ck, sk, out_q, out_kv, sums, acc_k, acc_v, acc_s):
    i = pl.program_id(0)
    last = pl.num_programs(0) - 1
    scale = 256 ** -0.5

    @pl.when(i == 0)
    def _():
        acc_k[...] = jnp.zeros_like(acc_k)
        acc_v[...] = jnp.zeros_like(acc_v)
        acc_s[...] = jnp.zeros_like(acc_s)

    scores = nt(q[0], k[0]) * scale
    allowed = idk[0] <= idq[0]
    probs = jnp.where(allowed, jnp.exp(scores - lse[...]), 0.0)
    grad_probs = nt(g[...], v[0])
    inner = jnp.sum(probs * grad_probs, axis=1, keepdims=True)
    gs = (probs * (grad_probs - inner)).astype(bf)
    gq = (nn(gs, k[0]) * scale).astype(bf).astype(f32)
    gq = turn(gq, cq[0], -sq[0])
    acc_s[0:1, :] += jnp.sum(gq, axis=0, keepdims=True)
    out_q[0] = gq.astype(bf)
    acc_k[...] += tn(gs, q[0])
    acc_v[...] += tn(probs.astype(bf), g[...])

    @pl.when(i == last)
    def _():
        gk = (acc_k[...] * scale).astype(bf).astype(f32)
        gk = turn(gk, ck[0], -sk[0])
        out_kv[0] = gk.astype(bf)
        gv = acc_v[...].astype(bf)
        out_kv[1] = gv
        acc_s[1:2, :] = jnp.sum(gk, axis=0, keepdims=True)
        acc_s[2:3, :] = jnp.sum(gv.astype(f32), axis=0, keepdims=True)
        sums[...] = acc_s[...]


def attn_back_call(qkv, gmix, ids_col, ids_row, lse, c, s, t):
    tile = 256
    return pl.pallas_call(
        attn_back_body,
        grid=(TOK // tile,),
        in_specs=[
            pl.BlockSpec((1, tile, 256), lambda i: (0, i, 0)),
            pl.BlockSpec((1, TOK, 256), lambda i: (1, 0, 0)),
            pl.BlockSpec((1, TOK, 256), lambda i: (2, 0, 0)),
            pl.BlockSpec((tile, 256), lambda i: (i, 0)),
            pl.BlockSpec((1, tile, 1), lambda i: (t, i, 0)),
            pl.BlockSpec((1, 1, TOK), lambda i: (t, 0, 0)),
            pl.BlockSpec((tile, 1), lambda i: (i, 0)),
            pl.BlockSpec((1, tile, 128), lambda i: (t, i, 0)),
            pl.BlockSpec((1, tile, 128), lambda i: (t, i, 0)),
            pl.BlockSpec((1, TOK, 128), lambda i: (t, 0, 0)),
            pl.BlockSpec((1, TOK, 128), lambda i: (t, 0, 0)),
        ],
        out_specs=[
            pl.BlockSpec((1, tile, 256), lambda i: (0, i, 0)),
            pl.BlockSpec((2, TOK, 256), lambda i: (0, 0, 0)),
            pl.BlockSpec((8, 256), lambda i: (0, 0)),
        ],
        out_shape=[
            jax.ShapeDtypeStruct((1, TOK, 256), bf),
            jax.ShapeDtypeStruct((2, TOK, 256), bf),
            jax.ShapeDtypeStruct((8, 256), f32),
        ],
        scratch_shapes=[pltpu.VMEM((TOK, 256), f32), pltpu.VMEM((TOK, 256), f32), pltpu.VMEM((8, 256), f32)],
        compiler_params=params(),
        cost_estimate=cost(10 * TOK * TOK * 256, 6e6),
        name="attend_back",
    )(qkv, qkv, qkv, gmix, ids_col, ids_row, lse, c, s, c, s)


def p_body(act, mixed, wd, wo, own, sib):
    out = nn(act[...], wd[...]) + nn(mixed[...], wo[...])
    own[...] = out[:HALF]
    sib[...] = out[HALF:].astype(bf)


def p_call(act, mixed, w):
    units, width = act.shape[1], w.shape[1]
    tile = 256
    full = lambda *shape: pl.BlockSpec(shape, lambda j: (0,) * len(shape))
    return pl.pallas_call(
        p_body,
        grid=(width // tile,),
        in_specs=[
            full(TOK, units), full(TOK, 256),
            pl.BlockSpec((units, tile), lambda j: (0, j)),
            pl.BlockSpec((256, tile), lambda j: (units // 256, j)),
        ],
        out_specs=[pl.BlockSpec((HALF, tile), lambda j: (0, j))] * 2,
        out_shape=[jax.ShapeDtypeStruct((HALF, width), f32), jax.ShapeDtypeStruct((HALF, width), bf)],
        compiler_params=params(),
        cost_estimate=cost(2 * TOK * width * (units + 256), 16e6),
        name="combine",
    )(act, mixed, w, w)


def ga_body(units_tiles, g0, g1, w, slope, gh, gmix, x):
    j = pl.program_id(0)

    @pl.when(j == 0)
    def _():
        x[:HALF] = g0[...]
        x[HALF:] = g1[...]

    ga = nt(x[...], w[...]).astype(bf)

    @pl.when(j < units_tiles)
    def _():
        gh[...] = (ga.astype(f32) * slope[...].astype(f32)).astype(bf)

    @pl.when(j == units_tiles)
    def _():
        gmix[...] = ga


def ga_call(g0, g1, w, slope):
    width, rows = w.shape[1], w.shape[0]
    tile = 256
    units_tiles = rows // tile - 1
    full = lambda *shape: pl.BlockSpec(shape, lambda j: (0,) * len(shape))
    return pl.pallas_call(
        functools.partial(ga_body, units_tiles),
        grid=(rows // tile,),
        in_specs=[
            full(HALF, width), full(HALF, width),
            pl.BlockSpec((tile, width), lambda j: (j, 0)),
            pl.BlockSpec((TOK, tile), lambda j: (0, jnp.minimum(j, units_tiles - 1))),
        ],
        out_specs=[
            pl.BlockSpec((TOK, tile), lambda j: (0, jnp.minimum(j, units_tiles - 1))),
            full(TOK, 256),
        ],
        out_shape=[jax.ShapeDtypeStruct((TOK, rows - 256), bf), jax.ShapeDtypeStruct((TOK, 256), bf)],
        scratch_shapes=[pltpu.VMEM((TOK, width), bf)],
        compiler_params=params(),
        cost_estimate=cost(2 * TOK * width * rows, 16e6),
        name="pull",
    )(g0, g1, w, slope)


def u_body(gh, gq, gkv, wu, wq, own, sib):
    out = nn(gh[...], wu[...]) + nn(gq[0], wq[0:256]) + nn(gkv[0], wq[256:512]) + nn(gkv[1], wq[512:768])
    own[...] = out[:HALF]
    sib[...] = out[HALF:].astype(bf)


def u_call(gh, gq, gkv, w_up, w_qkv):
    units, width = gh.shape[1], w_up.shape[1]
    tile = 256
    full = lambda *shape: pl.BlockSpec(shape, lambda j: (0,) * len(shape))
    return pl.pallas_call(
        u_body,
        grid=(width // tile,),
        in_specs=[
            full(TOK, units), full(1, TOK, 256), full(2, TOK, 256),
            pl.BlockSpec((units, tile), lambda j: (0, j)),
            pl.BlockSpec((768, tile), lambda j: (0, j)),
        ],
        out_specs=[pl.BlockSpec((HALF, tile), lambda j: (0, j))] * 2,
        out_shape=[jax.ShapeDtypeStruct((HALF, width), f32), jax.ShapeDtypeStruct((HALF, width), bf)],
        compiler_params=params(),
        cost_estimate=cost(2 * TOK * width * (units + 768), 20e6),
        name="push",
    )(gh, gq, gkv, w_up, w_qkv)


def g2_body(acts, mixes, rights, term, acc, left, right, out, sems):
    units = acts.shape[2]
    rows = units + 256

    def copies(k):
        slot = k % 2
        pairs = [
            (acts.at[k], left.at[slot, :, pl.ds(0, units)]),
            (mixes.at[k], left.at[slot, :, pl.ds(units, 256)]),
            (rights.at[k], right.at[slot]),
        ]
        return [pltpu.make_async_copy(a, b, sems.at[slot, i]) for i, (a, b) in enumerate(pairs)]

    for cp in copies(0):
        cp.start()
    for k in range(4):
        if k < 3:
            for cp in copies(k + 1):
                cp.start()
        for cp in copies(k):
            cp.wait()
        slot = k % 2

        @pl.loop(0, rows // 256)
        def _(m):
            cols = pl.ds(pl.multiple_of(m * 256, 256), 256)
            part = tn(left[slot, :, cols], right[slot])
            if k == 0:
                acc[cols, :] = part
            elif k < 3:
                acc[cols, :] += part
            else:
                out[cols, :] = (acc[cols, :] + part).astype(bf)
    done = pltpu.make_async_copy(out, term, sems.at[0, 0])
    done.start()
    done.wait()


def g2_call(acts, mixes, rights):
    units, width = acts.shape[2], rights.shape[2]
    rows = units + 256
    return pl.pallas_call(
        g2_body,
        in_specs=[pl.BlockSpec(memory_space=pl.ANY)] * 3,
        out_specs=pl.BlockSpec(memory_space=pl.ANY),
        out_shape=jax.ShapeDtypeStruct((rows, width), bf),
        scratch_shapes=[
            pltpu.VMEM((rows, width), f32),
            pltpu.VMEM((2, TOK, rows), bf),
            pltpu.VMEM((2, TOK, width), bf),
            pltpu.VMEM((rows, width), bf),
            pltpu.SemaphoreType.DMA((2, 4)),
        ],
        compiler_params=pltpu.CompilerParams(vmem_limit_bytes=VM),
        cost_estimate=cost(2 * 4096 * width * rows, 40e6),
        name="grad_out_weights",
    )(acts, mixes, rights)


def g1_body(
    ghs, gps, rights, plain, gain, shift, term, sides, sums, acc, acc_s, left, right, out, w, sems, sem_w
):
    units = ghs.shape[2]
    rows = units + 768
    tiles = rows // 256

    def copies(k):
        slot = k % 2
        pairs = [(ghs.at[k], left.at[slot, :, pl.ds(0, units)])]
        pairs += [(gps.at[k, i], left.at[slot, :, pl.ds(units + 256 * i, 256)]) for i in range(3)]
        pairs += [(rights.at[k], right.at[slot])]
        return [pltpu.make_async_copy(a, b, sems.at[slot, i]) for i, (a, b) in enumerate(pairs)]

    weights = pltpu.make_async_copy(plain, w, sem_w)
    weights.start()
    for cp in copies(0):
        cp.start()
    ones = jnp.ones((TOK, 128), bf)
    sides[...] = jnp.zeros_like(sides)
    for k in range(4):
        if k < 3:
            for cp in copies(k + 1):
                cp.start()
        for cp in copies(k):
            cp.wait()
        slot = k % 2
        if k == 3:
            weights.wait()

        @pl.loop(0, tiles)
        def _(m):
            cols = pl.ds(pl.multiple_of(m * 256, 256), 256)
            piece = left[slot, :, cols]
            part = tn(piece, right[slot])
            part_s = tn(piece, ones)
            if k == 0:
                acc[cols, :] = part
                acc_s[cols, :] = part_s
            elif k < 3:
                acc[cols, :] += part
                acc_s[cols, :] += part_s
            else:
                raw = acc[cols, :] + part
                total = acc_s[cols, :] + part_s
                acc_s[cols, :] = total
                total = total[:, 0:1]
                which = (m >= units // 256).astype(jnp.int32)
                g = jnp.where(which == 0, gain[0:1, :], gain[1:2, :])
                s = jnp.where(which == 0, shift[0:1, :], shift[1:2, :])
                out[cols, :] = (raw * g + total * s).astype(bf)
                wt = w[cols, :].astype(f32)
                one = jnp.sum(wt * raw, axis=0, keepdims=True)
                two = jnp.sum(wt * total, axis=0, keepdims=True)

                @pl.when(which == 0)
                def _():
                    sides[0:1, :] += one
                    sides[1:2, :] += two

                @pl.when(which == 1)
                def _():
                    sides[2:3, :] += one
                    sides[3:4, :] += two

    done = pltpu.make_async_copy(out, term, sem_w)
    done.start()
    sums[...] = acc_s[...]
    done.wait()


def g1_call(ghs, gps, rights, plain, gain, shift):
    units, width = ghs.shape[2], rights.shape[2]
    rows = units + 768
    anys = pl.BlockSpec(memory_space=pl.ANY)
    vmem = pl.BlockSpec(memory_space=pltpu.VMEM)
    return pl.pallas_call(
        g1_body,
        in_specs=[anys] * 4 + [vmem] * 2,
        out_specs=[anys, vmem, vmem],
        out_shape=[
            jax.ShapeDtypeStruct((rows, width), bf),
            jax.ShapeDtypeStruct((8, width), f32),
            jax.ShapeDtypeStruct((rows, 128), f32),
        ],
        scratch_shapes=[
            pltpu.VMEM((rows, width), f32),
            pltpu.VMEM((rows, 128), f32),
            pltpu.VMEM((2, TOK, rows), bf),
            pltpu.VMEM((2, TOK, width), bf),
            pltpu.VMEM((rows, width), bf),
            pltpu.VMEM((rows, width), bf),
            pltpu.SemaphoreType.DMA((2, 6)),
            pltpu.SemaphoreType.DMA,
        ],
        compiler_params=pltpu.CompilerParams(vmem_limit_bytes=VM),
        cost_estimate=cost(2 * 4096 * width * rows, 50e6),
        name="grad_in_weights",
    )(ghs, gps, rights, plain, gain, shift)


LANES = 128


MESH = pl.DeviceIdType.MESH


def line_order(z, t):
    near = jnp.where(z < 2, z + 1, z - 1)
    mid = jnp.where(z == 0, 2, jnp.where(z == 1, 0, jnp.where(z == 2, 3, 1)))
    far = jnp.where(z < 2, 3, 0)
    return jnp.where(t == 0, z, jnp.where(t == 1, near, jnp.where(t == 2, mid, far)))


def remote(src, dst, send, recv, s, f):
    return pltpu.make_async_remote_copy(
        src_ref=src, dst_ref=dst, send_sem=send, recv_sem=recv, device_id=(s, f), device_id_type=MESH
    )


def line_barrier(s, f, z):
    barrier = pltpu.get_barrier_semaphore()

    @pl.when(z < 3)
    def _():
        pl.semaphore_signal(barrier, inc=1, device_id=(s, f + 2), device_id_type=MESH)

    @pl.when(z > 0)
    def _():
        pl.semaphore_signal(barrier, inc=1, device_id=(s, f - 2), device_id_type=MESH)

    pl.semaphore_signal(barrier, inc=1, device_id=(s, f + 1 - 2 * (f % 2)), device_id_type=MESH)

    @pl.when((z == 0) | (z == 3))
    def _():
        pl.semaphore_wait(barrier, 2)

    @pl.when((z == 1) | (z == 2))
    def _():
        pl.semaphore_wait(barrier, 3)


def line_step(buf, k, z, s, f, sems, held=None):
    send_up, recv_up, send_dn, recv_dn = sems
    own = pl.ds(0, HALF)

    @pl.when((z - k >= 0) & (z < 3))
    def _():
        ref = buf.at[z - k, own]
        remote(ref if held is None else held, ref, send_up.at[k], recv_up.at[k], s, f + 2).start()

    @pl.when((z + k <= 3) & (z > 0))
    def _():
        ref = buf.at[z + k, own]
        remote(ref if held is None else held, ref, send_dn.at[k], recv_dn.at[k], s, f - 2).start()


def line_arrive(buf, k, z, s, f, sems):
    send_up, recv_up, send_dn, recv_dn = sems
    own = pl.ds(0, HALF)

    @pl.when(z - 1 - k >= 0)
    def _():
        ref = buf.at[z - 1 - k, own]
        remote(ref, ref, send_up.at[k], recv_up.at[k], s, f - 2).wait_recv()

    @pl.when(z + 1 + k <= 3)
    def _():
        ref = buf.at[z + 1 + k, own]
        remote(ref, ref, send_dn.at[k], recv_dn.at[k], s, f + 2).wait_recv()


def line_sent(buf, k, z, s, f, sems):
    send_up, recv_up, send_dn, recv_dn = sems
    own = pl.ds(0, HALF)

    @pl.when((z - k >= 0) & (z < 3))
    def _():
        ref = buf.at[z - k, own]
        remote(ref, ref, send_up.at[k], recv_up.at[k], s, f + 2).wait_send()

    @pl.when((z + k <= 3) & (z > 0))
    def _():
        ref = buf.at[z + k, own]
        remote(ref, ref, send_dn.at[k], recv_dn.at[k], s, f - 2).wait_send()


def core_copy(buf, b, s, f, sems, held=None):
    send, recv = sems
    return remote(
        buf.at[b, pl.ds(0, HALF)] if held is None else held, buf.at[b, pl.ds(HALF, HALF)], send.at[b], recv.at[b], s, f + 1 - 2 * (f % 2)
    )


def new_blocks(k, z, act):
    if k == 0:
        act(z)
        return

    @pl.when(z - k >= 0)
    def _():
        act(z - k)

    @pl.when(z + k <= 3)
    def _():
        act(z + k)


def forward_body(
    own_n, own_g, w_in_h, w_out_h, bias, cos, sin, idc, idr,
    n_all, g_all, act_o, slope_o, qkv_o, mixed_o, lse_o, own_o, sib_o,
    w_in, w_out, x, act, slope, qkv, mixed, lse, p_own, p_sib,
    load, line_n0, line_n1, line_n2, line_n3, line_g0, line_g1, line_g2, line_g3,
    core_n0, core_n1, core_p0, core_p1, out_sems,
):
    s, f = lax.axis_index("seq"), lax.axis_index("fsdp")
    z = f // 2
    line_n, line_g = (line_n0, line_n1, line_n2, line_n3), (line_g0, line_g1, line_g2, line_g3)
    core_n, core_p = (core_n0, core_n1), (core_p0, core_p1)
    own, other = pl.ds(0, HALF), pl.ds(HALF, HALF)
    units = act.shape[1]
    first = [
        pltpu.make_async_copy(own_n, x.at[own], load.at[0]),
        pltpu.make_async_copy(own_g, p_sib, load.at[3]),
        pltpu.make_async_copy(w_in_h, w_in, load.at[1]),
        pltpu.make_async_copy(w_out_h, w_out, load.at[2]),
    ]
    keep = [
        pltpu.make_async_copy(x.at[own], n_all.at[z, own], load.at[0]),
        pltpu.make_async_copy(p_sib, g_all.at[z, own], load.at[3]),
    ]
    for copy in first:
        copy.start()
    line_barrier(s, f, z)

    def outs(b):
        return [
            pltpu.make_async_copy(src, dst.at[b], out_sems.at[i])
            for i, (src, dst) in enumerate(
                [(act, act_o), (slope, slope_o), (qkv, qkv_o), (mixed, mixed_o), (lse, lse_o), (p_own, own_o)]
            )
        ]

    def send_sib(b):
        return remote(p_sib, sib_o.at[b], core_p[0].at[b], core_p[1].at[b], s, f + 1 - 2 * (f % 2))

    for t in range(4):
        b = line_order(z, t)
        top = pltpu.make_async_copy(n_all.at[b, own], x.at[own], load.at[0])
        low_half = pltpu.make_async_copy(n_all.at[b, other], x.at[other], load.at[4])
        if t == 0:
            line_step(n_all, 0, z, s, f, line_n, own_n)
            core_copy(n_all, z, s, f, core_n, own_n).start()
            for copy, then in zip(first[:2], keep):
                copy.wait()
                then.start()
        else:
            line_arrive(n_all, t - 1, z, s, f, line_n)
            if t < 3:
                line_step(n_all, t, z, s, f, line_n)
            else:
                line_step(g_all, 0, z, s, f, line_g, own_g)
            new_blocks(t, z, lambda v: core_copy(n_all, v, s, f, core_n).start())
            top.start()
        core_copy(n_all, b, s, f, core_n).wait_recv()
        low_half.start()
        if t == 0:
            for copy in first[2:] + keep:
                copy.wait()
        else:
            top.wait()
            before = line_order(z, t - 1)
            for copy in outs(before):
                copy.wait()
            send_sib(before).wait_send()
        low_half.wait()

        @pl.loop(0, units // 256)
        def _(j):
            at = pl.ds(pl.multiple_of(j * 256, 256), 256)
            h = nt(x[...], w_in[at, :]) + bias[:, at]
            act[:, at], slope[:, at] = gelu_pair(h)

        @pl.loop(0, 2)
        def _(j):
            at = pl.ds(pl.multiple_of(units + j * 256, 256), 256)
            h = nt(x[...], w_in[at, :]) + bias[:, at]
            qkv[j] = turn(h, cos[b], sin[b]).astype(bf)

        at = pl.ds(units + 512, 256)
        qkv[2] = (nt(x[...], w_in[at, :]) + bias[:, at]).astype(bf)

        @pl.loop(0, TOK // 256)
        def _(i):
            rows = pl.ds(pl.multiple_of(i * 256, 256), 256)
            scores = nt(qkv[0, rows, :], qkv[1]) * (256 ** -0.5)
            scores = jnp.where(idr[b] <= idc[b, rows, :], scores, -1e30)
            top_score = jnp.max(scores, axis=1, keepdims=True)
            weights = jnp.exp(scores - top_score)
            total = jnp.sum(weights, axis=1, keepdims=True)
            probs = (weights / total).astype(bf)
            mixed[rows, :] = nn(probs, qkv[2]).astype(bf)
            lse[rows, :] = jnp.broadcast_to(top_score + jnp.log(total), (256, LANES))

        @pl.loop(0, p_own.shape[1] // 256)
        def _(j):
            at = pl.ds(pl.multiple_of(j * 256, 256), 256)
            out = nn(act[...], w_out[pl.ds(0, units), at]) + nn(mixed[...], w_out[pl.ds(units, 256), at])
            p_own[:, at] = out[:HALF].astype(bf)
            p_sib[:, at] = out[HALF:].astype(bf)

        for copy in outs(b):
            copy.start()
        send_sib(b).start()

    last = line_order(z, 3)
    for copy in outs(last):
        copy.wait()
    send_sib(last).wait_send()
    for b in range(4):
        core_copy(n_all, b, s, f, core_n).wait_send()
        send_sib(b).wait_recv()
    for k in range(3):
        line_sent(n_all, k, z, s, f, line_n)
    line_arrive(g_all, 0, z, s, f, line_g)
    line_sent(g_all, 0, z, s, f, line_g)


def forward_call(own_n, own_g, w_in, w_out, bias, cos, sin, ids_col, ids_row):
    width = own_n.shape[1]
    units = w_in.shape[0] - 768
    anys = pl.BlockSpec(memory_space=pl.ANY)
    vmem = pl.BlockSpec(memory_space=pltpu.VMEM)
    shape = jax.ShapeDtypeStruct
    dma = lambda n: pltpu.SemaphoreType.DMA((n,))
    return pl.pallas_call(
        forward_body,
        in_specs=[anys] * 4 + [vmem] * 5,
        out_specs=[anys] * 9,
        out_shape=[
            shape((4, TOK, width), bf), shape((4, TOK, width), bf),
            shape((4, TOK, units), bf), shape((4, TOK, units), bf), shape((4, 3, TOK, 256), bf),
            shape((4, TOK, 256), bf), shape((4, TOK, LANES), f32),
            shape((4, HALF, width), bf), shape((4, HALF, width), bf),
        ],
        scratch_shapes=[
            pltpu.VMEM(w_in.shape, bf), pltpu.VMEM(w_out.shape, bf), pltpu.VMEM((TOK, width), bf),
            pltpu.VMEM((TOK, units), bf), pltpu.VMEM((TOK, units), bf), pltpu.VMEM((3, TOK, 256), bf),
            pltpu.VMEM((TOK, 256), bf), pltpu.VMEM((TOK, LANES), f32),
            pltpu.VMEM((HALF, width), bf), pltpu.VMEM((HALF, width), bf),
            dma(5), dma(3), dma(3), dma(3), dma(3), dma(3), dma(3), dma(3), dma(3),
            dma(4), dma(4), dma(4), dma(4), dma(6),
        ],
        compiler_params=pltpu.CompilerParams(
            vmem_limit_bytes=60 * 1024 * 1024, collective_id=0, has_side_effects=True
        ),
        cost_estimate=cost(8 * TOK * width * (w_in.shape[0] + w_out.shape[0]), 200e6),
        name="forward",
    )(own_n, own_g, w_in, w_out, bias, cos, sin, ids_col, ids_row)


def sum_add(dst, parts):
    @pl.loop(0, HALF // 64)
    def _(i):
        rows = pl.ds(pl.multiple_of(i * 64, 64), 64)
        total = parts[0][rows, :].astype(f32)
        for part in parts[1:]:
            total = total + part[rows, :].astype(f32)
        dst[rows, :] = total.astype(bf)


def line_sum_step(k, z, s, f, own, sib, land, stage, out, loads, sends, recvs):
    for way in range(2):
        d = z - 3 + k if way == 0 else z + 3 - k
        valid = d >= 0 if way == 0 else d <= 3
        to = f - 2 if way == 0 else f + 2
        inner = z < 3 if way == 0 else z > 0
        was = z - 4 + k >= 0 if way == 0 else z + 4 - k <= 3

        @pl.when(valid)
        def _():
            terms = [
                pltpu.make_async_copy(own.at[d], stage.at[0], loads.at[0]),
                pltpu.make_async_copy(sib.at[d], stage.at[1], loads.at[1]),
            ]
            for copy in terms:
                copy.start()
            if k > 0:

                @pl.when(was)
                def _():
                    remote(out.at[way], land.at[way, k - 1], sends.at[way, k - 1], recvs.at[way, k - 1], s, to).wait_send()

                @pl.when(inner)
                def _():
                    remote(out.at[way], land.at[way, k - 1], sends.at[way, k - 1], recvs.at[way, k - 1], s, to).wait_recv()
                    came = pltpu.make_async_copy(land.at[way, k - 1], stage.at[2], loads.at[2])
                    came.start()
                    came.wait()

            for copy in terms:
                copy.wait()
            if k > 0:

                @pl.when(inner)
                def _():
                    sum_add(out.at[way], [stage.at[0], stage.at[1], stage.at[2]])

                @pl.when(jnp.logical_not(inner))
                def _():
                    sum_add(out.at[way], [stage.at[0], stage.at[1]])
            else:
                sum_add(out.at[way], [stage.at[0], stage.at[1]])
            remote(out.at[way], land.at[way, k], sends.at[way, k], recvs.at[way, k], s, to).start()


def line_sum_end(z, s, f, own, sib, land, stage, out, loads, sends, recvs, result):
    terms = [
        pltpu.make_async_copy(own.at[z], stage.at[0], loads.at[0]),
        pltpu.make_async_copy(sib.at[z], stage.at[1], loads.at[1]),
    ]
    for copy in terms:
        copy.start()
    for copy in terms:
        copy.wait()

    for way in range(2):
        to = f - 2 if way == 0 else f + 2
        sent = z > 0 if way == 0 else z < 3
        got = z < 3 if way == 0 else z > 0

        @pl.when(sent)
        def _():
            remote(out.at[way], land.at[way, 2], sends.at[way, 2], recvs.at[way, 2], s, to).wait_send()

        @pl.when(got)
        def _():
            remote(out.at[way], land.at[way, 2], sends.at[way, 2], recvs.at[way, 2], s, to).wait_recv()
            came = pltpu.make_async_copy(land.at[way, 2], stage.at[2], loads.at[2])
            came.start()
            came.wait()
            sum_add(stage.at[0], [stage.at[0], stage.at[2]])

    sum_add(stage.at[0], [stage.at[0], stage.at[1]])
    copy = pltpu.make_async_copy(stage.at[0], result, loads.at[0])
    copy.start()
    copy.wait()


def backward_body(
    g_part, w_in_h, w_out_h, slope_h, qkv_h, lse_h, p_own, p_sib, cos, sin, idc, idr,
    g_all, gh_o, gp_o, own_o, sib_o, branch, land, sums,
    w_in, w_out, x, slope, qkv, lse, gh, gmix, gp, acc_k, acc_v, u_own, u_sib, stage, rs_out,
    load, l0, l1, l2, l3, core_0, core_1, core_u0, core_u1, out_sems, rs_send, rs_recv,
):
    s, f = lax.axis_index("seq"), lax.axis_index("fsdp")
    z = f // 2
    line = (l0, l1, l2, l3)
    core = (core_0, core_1)
    own, other = pl.ds(0, HALF), pl.ds(HALF, HALF)
    units = gh.shape[1]
    scale = 256 ** -0.5
    first = [
        pltpu.make_async_copy(w_in_h, w_in, load.at[0]),
        pltpu.make_async_copy(w_out_h, w_out, load.at[1]),
    ]
    for copy in first:
        copy.start()
    line_barrier(s, f, z)
    swap = lambda b: core_copy(g_all, b, s, f, core)
    new_blocks(0, z, lambda b: swap(b).start())
    line_step(g_all, 1, z, s, f, line)
    new_blocks(1, z, lambda b: swap(b).start())
    reduce_args = (z, s, f, p_own, p_sib, land, stage, rs_out, load.at[pl.ds(8, 3)], rs_send, rs_recv)
    line_sum_step(0, *reduce_args)
    sums[...] = jnp.zeros_like(sums)

    def ins(b):
        return [
            pltpu.make_async_copy(src.at[b], dst, load.at[2 + i])
            for i, (src, dst) in enumerate([(slope_h, slope), (qkv_h, qkv), (lse_h, lse)])
        ]

    def outs(b):
        return [
            pltpu.make_async_copy(src, dst.at[b], out_sems.at[i])
            for i, (src, dst) in enumerate([(gh, gh_o), (gp, gp_o), (u_own, own_o)])
        ]

    def send_sib(b):
        return remote(u_sib, sib_o.at[b], core_u0.at[b], core_u1.at[b], s, f + 1 - 2 * (f % 2))

    for t in range(4):
        b = line_order(z, t)
        for copy in ins(b):
            copy.start()
        if t == 3:
            line_arrive(g_all, 2, z, s, f, line)
            new_blocks(3, z, lambda v: swap(v).start())
        top = pltpu.make_async_copy(g_all.at[b, own], x.at[own], load.at[5])
        top.start()
        swap(b).wait_recv()
        low_half = pltpu.make_async_copy(g_all.at[b, other], x.at[other], load.at[6])
        low_half.start()
        if t == 0:
            for copy in first:
                copy.wait()
        else:
            before = line_order(z, t - 1)
            for copy in outs(before):
                copy.wait()
            send_sib(before).wait_send()
        for copy in ins(b):
            copy.wait()
        top.wait()
        low_half.wait()

        @pl.loop(0, units // 256)
        def _(j):
            at = pl.ds(pl.multiple_of(j * 256, 256), 256)
            ga = nt(x[...], w_out[at, :]).astype(bf)
            gh[:, at] = (ga.astype(f32) * slope[:, at].astype(f32)).astype(bf)

        gmix[...] = nt(x[...], w_out[pl.ds(units, 256), :]).astype(bf)
        acc_k[...] = jnp.zeros_like(acc_k)
        acc_v[...] = jnp.zeros_like(acc_v)

        @pl.loop(0, TOK // 256)
        def _(i):
            rows = pl.ds(pl.multiple_of(i * 256, 256), 256)
            q, g = qkv[0, rows, :], gmix[rows, :]
            scores = nt(q, qkv[1]) * scale
            allowed = idr[b] <= idc[b, rows, :]
            probs = jnp.where(allowed, jnp.exp(scores - lse[rows, 0:1]), 0.0)
            grad_probs = nt(g, qkv[2])
            inner = jnp.sum(probs * grad_probs, axis=1, keepdims=True)
            gs = (probs * (grad_probs - inner)).astype(bf)
            gq = (nn(gs, qkv[1]) * scale).astype(bf).astype(f32)
            gq = turn(gq, cos[b, rows, :], -sin[b, rows, :])
            sums[0:1, :] += jnp.sum(gq, axis=0, keepdims=True)
            gp[0, rows, :] = gq.astype(bf)
            acc_k[...] += tn(gs, q)
            acc_v[...] += tn(probs.astype(bf), g)

        gk = (acc_k[...] * scale).astype(bf).astype(f32)
        gk = turn(gk, cos[b], -sin[b])
        sums[1:2, :] += jnp.sum(gk, axis=0, keepdims=True)
        gp[1] = gk.astype(bf)
        gv = acc_v[...].astype(bf)
        sums[2:3, :] += jnp.sum(gv.astype(f32), axis=0, keepdims=True)
        gp[2] = gv
        if t == 1:
            line_arrive(g_all, 1, z, s, f, line)
            line_step(g_all, 2, z, s, f, line)
            new_blocks(2, z, lambda v: swap(v).start())
            line_sum_step(1, *reduce_args)
        if t == 3:
            line_sum_step(2, *reduce_args)

        @pl.loop(0, u_own.shape[1] // 256)
        def _(j):
            at = pl.ds(pl.multiple_of(j * 256, 256), 256)
            out = nn(gh[...], w_in[pl.ds(0, units), at])
            for i in range(3):
                out = out + nn(gp[i], w_in[pl.ds(units + 256 * i, 256), at])
            u_own[:, at] = out[:HALF].astype(bf)
            u_sib[:, at] = out[HALF:].astype(bf)

        for copy in outs(b):
            copy.start()
        send_sib(b).start()

    line_sum_end(*reduce_args, branch)
    last = line_order(z, 3)
    for copy in outs(last):
        copy.wait()
    send_sib(last).wait_send()
    for b in range(4):
        swap(b).wait_send()
        send_sib(b).wait_recv()
    for k in (1, 2):
        line_sent(g_all, k, z, s, f, line)


def backward_call(g_part, w_in, w_out, slope, qkv, lse, p_own, p_sib, cos, sin, ids_col, ids_row):
    width = w_in.shape[1]
    units = w_in.shape[0] - 768
    anys = pl.BlockSpec(memory_space=pl.ANY)
    vmem = pl.BlockSpec(memory_space=pltpu.VMEM)
    shape = jax.ShapeDtypeStruct
    dma = lambda *n: pltpu.SemaphoreType.DMA(n)
    return pl.pallas_call(
        backward_body,
        in_specs=[anys] * 8 + [vmem] * 4,
        out_specs=[anys] * 7 + [vmem],
        out_shape=[
            shape((4, TOK, width), bf), shape((4, TOK, units), bf), shape((4, 3, TOK, 256), bf),
            shape((4, HALF, width), bf), shape((4, HALF, width), bf), shape((HALF, width), bf),
            shape((2, 3, HALF, width), bf), shape((8, 256), f32),
        ],
        input_output_aliases={0: 0},
        scratch_shapes=[
            pltpu.VMEM(w_in.shape, bf), pltpu.VMEM(w_out.shape, bf), pltpu.VMEM((TOK, width), bf),
            pltpu.VMEM((TOK, units), bf), pltpu.VMEM((3, TOK, 256), bf), pltpu.VMEM((TOK, LANES), f32),
            pltpu.VMEM((TOK, units), bf), pltpu.VMEM((TOK, 256), bf), pltpu.VMEM((3, TOK, 256), bf),
            pltpu.VMEM((TOK, 256), f32), pltpu.VMEM((TOK, 256), f32),
            pltpu.VMEM((HALF, width), bf), pltpu.VMEM((HALF, width), bf),
            pltpu.VMEM((3, HALF, width), bf), pltpu.VMEM((2, HALF, width), bf),
            dma(11), dma(3), dma(3), dma(3), dma(3), dma(4), dma(4), dma(4), dma(4), dma(3),
            dma(2, 3), dma(2, 3),
        ],
        compiler_params=pltpu.CompilerParams(
            vmem_limit_bytes=62 * 1024 * 1024, collective_id=1, has_side_effects=True
        ),
        cost_estimate=cost(8 * TOK * width * (w_in.shape[0] + w_out.shape[0]), 200e6),
        name="backward",
    )(g_part, w_in, w_out, slope, qkv, lse, p_own, p_sib, cos, sin, ids_col, ids_row)


def pick(slices, which):
    return lax.dynamic_index_in_dim(slices, which, 0, keepdims=False)


def swap_core(value):
    return lax.ppermute(value, "fsdp", [(i, i ^ 1) for i in range(8)])


def along_z(value, pairs):
    return lax.ppermute(value, "fsdp", [(2 * a + c, 2 * b + c) for a, b in pairs for c in range(2)])


def spread_pairs(step):
    pairs = []
    for source in range(4):
        part = (step + source) % 4
        for rank in range(8):
            pairs.append((source * 8 + rank, (2 * (rank % 2) + part // 2) * 8 + rank - rank % 2 + part % 2))
    return pairs


def gather_z(own, z):
    low_half = z < 2
    edge = (z == 0) | (z == 3)
    above = along_z(own, [(1, 0), (2, 1), (3, 2)])
    below = along_z(own, [(0, 1), (1, 2), (2, 3)])
    first = jnp.where(low_half, above, below)
    outer = jnp.where(low_half, below, above)
    inner = along_z(first, [(1, 0), (2, 3)])
    cross = along_z(outer, [(1, 2), (2, 1)])
    second = jnp.where(edge, inner, outer)
    third = jnp.where(edge, along_z(cross, [(1, 0), (2, 3)]), cross)
    return [own, first, second, third]


def scatter_z(parts, z):
    low = jnp.bfloat16
    low_half = z < 2
    far = along_z(parts[3].astype(low), [(0, 1), (3, 2)])
    cross = along_z((parts[3] + far.astype(jnp.float32)).astype(low), [(1, 2), (2, 1)])
    near = along_z(parts[2].astype(low), [(0, 1), (3, 2)])
    one = parts[1] + near.astype(jnp.float32)
    two = parts[2] + cross.astype(jnp.float32)
    up = jnp.where(low_half, one, two).astype(low)
    down = jnp.where(low_half, two, one).astype(low)
    from_below = along_z(up, [(0, 1), (1, 2), (2, 3)])
    from_above = along_z(down, [(1, 0), (2, 1), (3, 2)])
    return parts[0] + from_below.astype(jnp.float32) + from_above.astype(jnp.float32)


def swap_seq(value, bit):
    return lax.ppermute(value, "seq", [(i, i ^ bit) for i in range(4)])


def gather_small(value, f):
    gathered = value[None]
    for bit in (1, 2, 4):
        other = lax.ppermute(gathered, "fsdp", [(i, i ^ bit) for i in range(8)])
        low_side = (f // bit) % 2 == 0
        gathered = jnp.concatenate(
            [jnp.where(low_side, gathered, other), jnp.where(low_side, other, gathered)]
        )
    return gathered


def scatter_small(value, f):
    for bit in (4, 2, 1):
        half = value.shape[0] // 2
        low_side = (f // bit) % 2 == 0
        sent = jnp.where(low_side, value[half:], value[:half])
        kept = jnp.where(low_side, value[:half], value[half:])
        value = kept + lax.ppermute(sent, "fsdp", [(i, i ^ bit) for i in range(8)])
    return value[0]


def sum_small(value):
    for bit in (1, 2):
        value = value + swap_seq(value, bit)
    return value


def after(value, other):
    return lax.optimization_barrier((value, other))[0]


def sum_seq(part, x, y):
    rows, columns = part.shape
    halves = part.reshape(2, 2, 2, rows // 8, columns)
    low = jnp.bfloat16
    outs = []
    for half, (bit_a, at_a), (bit_b, at_b) in ((0, (1, x), (2, y)), (1, (2, y), (1, x))):
        mine = halves[half]
        sent = swap_seq(pick(mine, 1 - at_a).astype(low), bit_a)
        kept = pick(mine, at_a) + sent.astype(jnp.float32)
        sent = swap_seq(pick(kept, 1 - at_b).astype(low), bit_b)
        outs.append((pick(kept, at_b) + sent.astype(jnp.float32)).astype(low))
    return outs


def spread_seq(pieces, x, y):
    outs = []
    for piece, (bit_a, at_a), (bit_b, at_b) in ((pieces[0], (1, x), (2, y)), (pieces[1], (2, y), (1, x))):
        other = swap_seq(piece, bit_b)
        both = jnp.where(at_b == 0, jnp.stack([piece, other]), jnp.stack([other, piece]))
        other = swap_seq(both, bit_a)
        outs.append(jnp.where(at_a == 0, jnp.stack([both, other]), jnp.stack([other, both])))
    rows, columns = pieces[0].shape
    return jnp.stack(outs).reshape(8 * rows, columns).astype(jnp.float32)


def split_body(
    resid_in,
    qkv_weight,
    qkv_bias,
    out_weight,
    out_bias,
    up_weight,
    up_bias,
    down_weight,
    down_bias,
    attn_gain,
    attn_shift,
    mlp_gain,
    mlp_shift,
    block_ids,
    offsets,
    grad_out,
):
    low = jnp.bfloat16
    f32 = jnp.float32
    groups, piece, width = resid_in.shape
    tokens = groups * piece
    s = lax.axis_index("seq")
    f = lax.axis_index("fsdp")
    z, c = f // 2, f % 2
    x, y = s % 2, s // 2
    both_axes = ("seq", "fsdp")
    units = up_weight.shape[0]

    length = block_ids.shape[1]
    own_small = [attn_gain, attn_shift, mlp_gain, mlp_shift, out_bias + down_bias, qkv_bias]
    packed = jnp.concatenate(
        own_small + [block_ids.reshape(-1).astype(f32), offsets.reshape(-1).astype(f32)]
    )
    flat = resid_in.reshape(tokens, width)
    center = flat - jnp.mean(flat, axis=-1, keepdims=True)
    inv = lax.rsqrt(jnp.mean(center * center, axis=-1, keepdims=True) + EPS)
    normal = center * inv
    grad_flat = grad_out.reshape(tokens, width)
    small = gather_small(packed, f)
    gain_a, shift_a, gain_m, shift_m, bias_out = (
        small[:, i * 256 : (i + 1) * 256].reshape(width) for i in range(5)
    )
    head_bias = small[:, 1280:2048].reshape(3, HEADS, HEAD_DIM)
    head_bias = lax.dynamic_index_in_dim(head_bias, f, 1, keepdims=False).reshape(3 * HEAD_DIM)
    ids_all = small[:, 2048 : 2048 + groups * length].astype(jnp.int32).reshape(-1, 8, LANES)
    starts_all = small[:, 2048 + groups * length :].astype(jnp.int32).reshape(-1, offsets.shape[1])

    def plane_out(value):
        parts = value.reshape(4, tokens // 4, width)
        got = [
            lax.ppermute(pick(parts, (k + s) % 4), both_axes, spread_pairs(k)) for k in range(4)
        ]
        return jnp.concatenate(got, axis=0)

    def plane_back(value):
        parts = value.reshape(4, tokens // 4, width)
        got = jnp.stack(
            [
                lax.ppermute(parts[k], both_axes, [(b, a) for a, b in spread_pairs(k)])
                for k in range(4)
            ]
        )
        return jnp.concatenate([pick(got, (j - s + 4) % 4) for j in range(4)], axis=0)

    own_n = plane_out(normal.astype(low))
    own_g = plane_out(after(grad_flat.astype(low), own_n))

    quarter = HEAD_DIM // 4
    qkv_low = lax.dynamic_slice_in_dim(
        qkv_weight.reshape(3, HEAD_DIM, width), s * quarter, quarter, 1
    ).astype(low)
    came = jnp.stack(
        [
            lax.ppermute(qkv_low[i], "fsdp", [(r, (3 * r + i) % 8) for r in range(8)])
            for i in range(3)
        ]
    )

    def third_of(i):
        return (3 * ((3 * (f - i + 8)) % 8) + i) // 8

    slot_of = [
        sum(jnp.where(third_of(i) == kind, i, 0) for i in range(3)) for kind in range(3)
    ]
    came = jnp.stack([pick(came, slot_of[kind]) for kind in range(3)])
    got = jnp.stack([came] + [swap_seq(came, bit) for bit in (1, 2, 3)])
    head_w = jnp.stack([pick(got, s ^ q) for q in range(4)], axis=1).reshape(3 * HEAD_DIM, width)
    gain = jnp.stack([gain_m, gain_a])
    shift = jnp.stack([shift_m, shift_a])
    up_low = up_weight.astype(low).astype(f32)
    head32 = head_w.astype(f32)
    plain_w = jnp.concatenate([up_low, head32], axis=0).astype(low)
    w_up = (up_low * gain_m).astype(low)
    w_head = (head32 * gain_a).astype(low)
    w_in = jnp.concatenate([w_up, w_head], axis=0)
    bias_in = jnp.concatenate(
        [
            up_bias + jnp.sum(up_low * shift_m, axis=1),
            head_bias + jnp.sum(head32 * shift_a, axis=1),
        ]
    )[None]
    w_out = jnp.concatenate([down_weight.astype(low), out_weight.astype(low)], axis=0)

    halves = [(2 * (s % 2) + c, c), (2 * (s % 2) + 1 - c, 1 - c)]
    rows_at = [((part - k + 4) % 4) * 2 + core for part, core in halves for k in range(4)]
    ids_slots = [pick(ids_all, block * 4 + s) for block in range(4)]
    ids_here = jnp.stack(
        [jnp.concatenate([pick(row, at) for at in rows_at]) for row in ids_slots]
    ).reshape(4, 1024)
    starts_here = jnp.stack([pick(starts_all, block * 4 + s) for block in range(4)])
    pos = (jnp.stack(rows_at)[:, None] * LANES + jnp.arange(LANES)[None, :]).reshape(1024)
    positions = block_offset(ids_here, starts_here) + pos[None, :]
    lane = jnp.arange(LANES)
    inverse = jnp.exp(
        (lane % 32).astype(f32) * (-2.0 * math.log(10000.0) / ROT_DIM)
    )
    angles = jnp.where(lane < ROT_DIM, positions.astype(f32)[..., None] * inverse, 0.0)
    cosine = jnp.cos(angles)
    sine = jnp.sin(angles) * jnp.where(lane < ROT_DIM // 2, -1.0, 1.0)
    ids_col, ids_row = ids_here[:, :, None], ids_here[:, None, :]

    n_all, g_part, act_all, slope_all, qkv_all, mixed_all, lse_all, p_own, p_sib = forward_call(
        own_n, own_g, w_in, w_out, bias_in, cosine, sine, ids_col, ids_row
    )
    g_all, gh_all, gp_all, u_own, u_sib, branch, _, col_sums = backward_call(
        g_part, w_in, w_out, slope_all, qkv_all, lse_all, p_own, p_sib, cosine, sine, ids_col, ids_row
    )
    result = flat + plane_back(branch).astype(f32) + bias_out
    term_out = g2_call(act_all, mixed_all, g_all)
    down_out = lax.psum(term_out, "seq").astype(f32)
    blk = [line_order(z, t) for t in range(4)]
    parts = [pick(u_own, q).astype(f32) + pick(u_sib, q).astype(f32) for q in blk]
    u_sum = scatter_z(parts, z).astype(low)
    u = plane_back(u_sum).astype(f32)
    grad_input = grad_flat + inv * (
        u - jnp.mean(u, axis=-1, keepdims=True) - normal * jnp.mean(u * normal, axis=-1, keepdims=True)
    )
    term_in, sides, sums = g1_call(gh_all, gp_all, n_all, plain_w, gain, shift)
    qkv_sum = lax.psum(term_in[units:], "seq").reshape(3, HEAD_DIM, width)
    up_out = lax.psum(term_in[:units], "seq").astype(f32)
    kinds = [pick(qkv_sum, third_of(i)) for i in range(3)]
    qkv_back = [
        lax.ppermute(kinds[i], "fsdp", [((3 * r + i) % 8, r) for r in range(8)]) for i in range(3)
    ]
    qkv_out = jnp.concatenate(qkv_back).astype(f32)

    slots = jnp.zeros((16, HEAD_DIM), f32)
    slots = lax.dynamic_update_slice(slots, col_sums[0:1], (f, 0))
    slots = lax.dynamic_update_slice(slots, col_sums[1:2], (8 + f, 0))
    spread = jnp.concatenate([sides[:4], jnp.sum(grad_flat, axis=0)[None]])
    wide = jnp.concatenate(
        [spread.reshape(5, 8, 256).transpose(1, 0, 2).reshape(8, 5 * 256), slots.reshape(8, 512)], axis=1
    )
    wide = after(wide, u_sum)
    mine = sum_small(jnp.concatenate([scatter_small(wide, f), sums[:units, 0], col_sums[2]]))
    vectors = [mine[i * 256 : (i + 1) * 256] for i in range(5)]
    qk_grad = mine[1280:1792]
    up_bias_grad = mine[1792 : 1792 + units]
    value_grad = mine[1792 + units :]
    return (
        result.reshape(groups, piece, width),
        grad_input.reshape(groups, piece, width),
        qkv_out,
        qk_grad,
        value_grad,
        down_out[units:],
        vectors[4],
        up_out,
        up_bias_grad,
        down_out[:units],
        vectors[4],
        vectors[2],
        vectors[3],
        vectors[0],
        vectors[1],
    )


def solution(mesh):
    placed = (
        P("fsdp", "seq", None),
        P("fsdp", None),
        P("fsdp"),
        P("fsdp", None),
        P("fsdp"),
        P("fsdp", None),
        P("fsdp"),
        P("fsdp", None),
        P("fsdp"),
        P("fsdp"),
        P("fsdp"),
        P("fsdp"),
        P("fsdp"),
        P("fsdp", None),
        P("fsdp", None),
        P("fsdp", "seq", None),
    )
    return jax.shard_map(
        split_body if mesh.shape["fsdp"] == HEADS and mesh.shape["seq"] == 4 else body,
        mesh=mesh,
        in_specs=placed,
        out_specs=(
            P("fsdp", "seq", None),
            P("fsdp", "seq", None),
            P("fsdp", None),
            P("fsdp"),
            P("fsdp"),
            P("fsdp", None),
            P("fsdp"),
            P("fsdp", None),
            P("fsdp"),
            P("fsdp", None),
            P("fsdp"),
            P("fsdp"),
            P("fsdp"),
            P("fsdp"),
            P("fsdp"),
        ),
        check_vma=False,
    )
```

```python
import functools
import math

import jax
import jax.numpy as jnp
from jax import lax
from jax.experimental import pallas as pl
from jax.experimental.pallas import tpu as pltpu
from jax.sharding import PartitionSpec as P

HEADS = 8
HEAD_DIM = 256
ROT_DIM = 64


EPS = 1e-05
NEG_FILL = -1e30


def layer_norm(values, gain, shift):
    center = values - jnp.mean(values, axis=-1, keepdims=True)
    spread = jnp.mean(center * center, axis=-1, keepdims=True)
    return center * lax.rsqrt(spread + EPS) * gain + shift


def rotary_tables(positions):
    half = ROT_DIM // 2
    inverse = jnp.exp(jnp.arange(half, dtype=jnp.float32) * (-2.0 * math.log(10000.0) / ROT_DIM))
    angles = positions.astype(jnp.float32)[..., None] * inverse
    return (jnp.cos(angles), jnp.sin(angles))


def block_offset(ids, starts):
    numbers = jnp.arange(starts.shape[1], dtype=jnp.int32)
    match = (ids[:, :, None] == numbers[None, None, :]).astype(jnp.int32)
    return jnp.sum(match * starts[:, None, :], axis=-1)


def rotate(values, cosine, sine):
    half = ROT_DIM // 2
    cosine = cosine[..., None, :]
    sine = sine[..., None, :]
    first = values[..., :half]
    second = values[..., half:ROT_DIM]
    return jnp.concatenate(
        [first * cosine - second * sine, second * cosine + first * sine, values[..., ROT_DIM:]],
        axis=-1,
    )


def gelu_exact(values):
    return jax.nn.gelu(values, approximate=False)


def contract_lead(left, right):
    return lax.dot_general(
        left, right, (((0,), (0,)), ((), ())), preferred_element_type=jnp.float32
    )


def contract_last(left, right):
    return lax.dot_general(
        left, right, (((1,), (1,)), ((), ())), preferred_element_type=jnp.float32
    )


def attend_forward(items):
    query, keys, values, ids = items
    allowed = ids[None, :] <= ids[:, None]
    scores = jnp.where(allowed, contract_last(query, keys) * HEAD_DIM ** (-0.5), NEG_FILL)
    top = jnp.max(scores, axis=1, keepdims=True)
    weights = jnp.exp(scores - top)
    total = jnp.sum(weights, axis=1, keepdims=True)
    probs = (weights / total).astype(jnp.bfloat16)
    mixed = jnp.dot(probs, values, preferred_element_type=jnp.float32).astype(jnp.bfloat16)
    return (mixed, (top + jnp.log(total))[:, 0])


def attend_backward(items):
    query, keys, values, ids, lse_row, grad_mix = items
    scale = HEAD_DIM ** (-0.5)
    allowed = ids[None, :] <= ids[:, None]
    scores = contract_last(query, keys) * scale
    probs = jnp.where(allowed, jnp.exp(scores - lse_row[:, None]), 0.0)
    grad_probs = contract_last(grad_mix, values)
    inner = jnp.sum(probs * grad_probs, axis=1, keepdims=True)
    grad_scores = (probs * (grad_probs - inner)).astype(jnp.bfloat16)
    grad_query = (jnp.dot(grad_scores, keys, preferred_element_type=jnp.float32) * scale).astype(
        jnp.bfloat16
    )
    grad_keys = (contract_lead(grad_scores, query) * scale).astype(jnp.bfloat16)
    grad_values = contract_lead(probs.astype(jnp.bfloat16), grad_mix).astype(jnp.bfloat16)
    return (grad_query, grad_keys, grad_values)


def body(
    resid_in,
    qkv_weight,
    qkv_bias,
    out_weight,
    out_bias,
    up_weight,
    up_bias,
    down_weight,
    down_bias,
    attn_gain,
    attn_shift,
    mlp_gain,
    mlp_shift,
    block_ids,
    offsets,
    grad_out,
):
    groups, piece, width = resid_in.shape
    tokens = groups * piece
    pieces = lax.axis_size("seq")
    length = piece * pieces
    rank = lax.axis_index("fsdp")
    heads_here = HEADS // pieces
    pairs = groups * heads_here
    flat = resid_in.reshape(tokens, width)
    gain_a, shift_a, gain_m, shift_m, proj_bias, attn_bias, hidden_bias, mlp_bias = (
        lax.all_gather(attn_gain, "fsdp", axis=0, tiled=True),
        lax.all_gather(attn_shift, "fsdp", axis=0, tiled=True),
        lax.all_gather(mlp_gain, "fsdp", axis=0, tiled=True),
        lax.all_gather(mlp_shift, "fsdp", axis=0, tiled=True),
        lax.all_gather(qkv_bias, "fsdp", axis=0, tiled=True),
        lax.all_gather(out_bias, "fsdp", axis=0, tiled=True),
        lax.all_gather(up_bias, "fsdp", axis=0, tiled=True),
        lax.all_gather(down_bias, "fsdp", axis=0, tiled=True),
    )
    qkv_low = qkv_weight.astype(jnp.bfloat16)
    out_low = out_weight.astype(jnp.bfloat16)
    up_low = up_weight.astype(jnp.bfloat16)
    down_low = down_weight.astype(jnp.bfloat16)
    qkv_full, out_full = (
        lax.all_gather(qkv_low, "fsdp", axis=0, tiled=True),
        lax.all_gather(out_low, "fsdp", axis=0, tiled=True),
    )
    normed_a32, norm_back_a = jax.vjp(layer_norm, flat, gain_a, shift_a)
    normed_m32, norm_back_m = jax.vjp(layer_norm, flat, gain_m, shift_m)
    normed_attn = normed_a32.astype(jnp.bfloat16)
    normed_mlp = normed_m32.astype(jnp.bfloat16)
    projected = (contract_last(normed_attn, qkv_full) + proj_bias).reshape(
        groups, piece, 3, HEADS, HEAD_DIM
    )
    first_pos = lax.axis_index("seq") * piece
    ids_piece = lax.dynamic_slice_in_dim(block_ids, first_pos, piece, 1)
    positions = (
        block_offset(ids_piece, offsets) + first_pos + jnp.arange(piece, dtype=jnp.int32)[None, :]
    )
    cosine, sine = rotary_tables(positions)
    query = rotate(projected[:, :, 0], cosine, sine)
    keys = rotate(projected[:, :, 1], cosine, sine)
    packed = jnp.stack([query, keys, projected[:, :, 2]], axis=2).astype(jnp.bfloat16)
    heads = lax.all_to_all(packed, "seq", split_axis=3, concat_axis=1, tiled=True)
    stacked = heads.transpose(2, 0, 3, 1, 4).reshape(3, pairs, length, HEAD_DIM)
    ids_pairs = jnp.repeat(block_ids, heads_here, axis=0)
    mixed_pairs, lse_pairs = lax.map(
        attend_forward, (stacked[0], stacked[1], stacked[2], ids_pairs)
    )
    back_heads = mixed_pairs.reshape(groups, heads_here, length, HEAD_DIM).transpose(0, 2, 1, 3)
    mixed_tok = lax.all_to_all(back_heads, "seq", split_axis=1, concat_axis=2, tiled=True).reshape(
        tokens, width
    )
    attn_part = jnp.dot(mixed_tok, out_full, preferred_element_type=jnp.float32) + attn_bias
    units_here = up_weight.shape[0]
    group_rows = lax.all_gather(normed_mlp, "fsdp", axis=0, tiled=True)
    local_bias = lax.dynamic_slice_in_dim(hidden_bias, rank * units_here, units_here)
    hidden = contract_last(group_rows, up_low) + local_bias
    active, gelu_back = jax.vjp(gelu_exact, hidden)
    active_low = active.astype(jnp.bfloat16)
    branch = (
        lax.psum_scatter(
            jnp.dot(active_low, down_low, preferred_element_type=jnp.float32).astype(jnp.bfloat16),
            "fsdp",
            scatter_dimension=0,
            tiled=True,
        ).astype(jnp.float32)
        + mlp_bias
    )
    result = flat + attn_part + branch
    grad_flat = grad_out.reshape(tokens, width)
    grad_low = grad_flat.astype(jnp.bfloat16)
    bias_sum = jnp.sum(grad_flat, axis=0)
    group_grad = lax.all_gather(grad_low, "fsdp", axis=0, tiled=True)
    grad_active = contract_last(group_grad, down_low).astype(jnp.bfloat16)
    grad_hidden = gelu_back(grad_active.astype(jnp.float32))[0]
    grad_hidden_low = grad_hidden.astype(jnp.bfloat16)
    grad_normed_m = lax.psum_scatter(
        jnp.dot(grad_hidden_low, up_low, preferred_element_type=jnp.float32),
        "fsdp",
        scatter_dimension=0,
        tiled=True,
    )
    up_grad_shard = contract_lead(grad_hidden_low, group_rows)
    down_grad_shard = contract_lead(active_low, group_grad)
    local_sum = jnp.sum(grad_hidden, axis=0)
    up_bias_term = lax.dynamic_update_slice_in_dim(
        jnp.zeros((hidden_bias.shape[0],), jnp.float32), local_sum, rank * units_here, 0
    )
    grad_mixed = contract_last(grad_low, out_full).astype(jnp.bfloat16)
    grad_heads = lax.all_to_all(
        grad_mixed.reshape(groups, piece, HEADS, HEAD_DIM),
        "seq",
        split_axis=2,
        concat_axis=1,
        tiled=True,
    )
    grad_pairs = grad_heads.transpose(0, 2, 1, 3).reshape(pairs, length, HEAD_DIM)
    grad_query, grad_keys, grad_values = lax.map(
        attend_backward, (stacked[0], stacked[1], stacked[2], ids_pairs, lse_pairs, grad_pairs)
    )
    grads_stack = (
        jnp.stack([grad_query, grad_keys, grad_values], axis=0)
        .reshape(3, groups, heads_here, length, HEAD_DIM)
        .transpose(1, 3, 0, 2, 4)
    )
    returned = lax.all_to_all(grads_stack, "seq", split_axis=1, concat_axis=3, tiled=True).astype(
        jnp.float32
    )
    grad_projected = jnp.stack(
        [
            rotate(returned[:, :, 0], cosine, -sine),
            rotate(returned[:, :, 1], cosine, -sine),
            returned[:, :, 2],
        ],
        axis=2,
    ).reshape(tokens, 3 * width)
    grad_projected_low = grad_projected.astype(jnp.bfloat16)
    proj_bias_term = jnp.sum(grad_projected, axis=0)
    qk_bias_term = proj_bias_term[: 2 * width]
    value_bias_term = proj_bias_term[2 * width :]
    grad_normed_a = jnp.dot(grad_projected_low, qkv_full, preferred_element_type=jnp.float32)
    grad_from_a, gain_a_term, shift_a_term = norm_back_a(grad_normed_a)
    grad_from_m, gain_m_term, shift_m_term = norm_back_m(grad_normed_m)
    grad_input = grad_flat + grad_from_a + grad_from_m
    qkv_term = contract_lead(grad_projected_low, normed_attn)
    out_term = contract_lead(mixed_tok, grad_low)
    (
        qkv_shard,
        out_shard,
        qk_bias_shard,
        value_bias_shard,
        bias_shard,
        up_bias_shard,
        gain_a_shard,
        shift_a_shard,
        gain_m_shard,
        shift_m_shard,
    ) = (
        lax.psum_scatter(qkv_term, "fsdp", scatter_dimension=0, tiled=True),
        lax.psum_scatter(out_term, "fsdp", scatter_dimension=0, tiled=True),
        lax.psum_scatter(qk_bias_term, "fsdp", scatter_dimension=0, tiled=True),
        lax.psum_scatter(value_bias_term, "fsdp", scatter_dimension=0, tiled=True),
        lax.psum_scatter(bias_sum, "fsdp", scatter_dimension=0, tiled=True),
        lax.psum_scatter(up_bias_term, "fsdp", scatter_dimension=0, tiled=True),
        lax.psum_scatter(gain_a_term, "fsdp", scatter_dimension=0, tiled=True),
        lax.psum_scatter(shift_a_term, "fsdp", scatter_dimension=0, tiled=True),
        lax.psum_scatter(gain_m_term, "fsdp", scatter_dimension=0, tiled=True),
        lax.psum_scatter(shift_m_term, "fsdp", scatter_dimension=0, tiled=True),
    )
    totals = lax.psum(
        (
            qkv_shard,
            out_shard,
            up_grad_shard,
            down_grad_shard,
            qk_bias_shard,
            value_bias_shard,
            bias_shard,
            up_bias_shard,
            gain_a_shard,
            shift_a_shard,
            gain_m_shard,
            shift_m_shard,
        ),
        "seq",
    )
    return (
        result.reshape(groups, piece, width),
        grad_input.reshape(groups, piece, width),
        totals[0],
        totals[4],
        totals[5],
        totals[1],
        totals[6],
        totals[2],
        totals[7],
        totals[3],
        totals[6],
        totals[8],
        totals[9],
        totals[10],
        totals[11],
    )


bf, f32 = jnp.bfloat16, jnp.float32
TOK, HALF = 1024, 512
VM = 56 * 1024 * 1024


def nt(a, b):
    return lax.dot_general(a, b, (((1,), (1,)), ((), ())), preferred_element_type=f32)


def nn(a, b):
    return lax.dot_general(a, b, (((1,), (0,)), ((), ())), preferred_element_type=f32)


def tn(a, b):
    return lax.dot_general(a, b, (((0,), (0,)), ((), ())), preferred_element_type=f32)


def params(n=1, limit=VM):
    return pltpu.CompilerParams(dimension_semantics=("arbitrary",) * n, vmem_limit_bytes=limit)


def cost(flops, nbytes):
    return pl.CostEstimate(flops=int(flops), bytes_accessed=int(nbytes), transcendentals=0)


def turn(head, c, s):
    first = head[:, :128]
    lane = lax.broadcasted_iota(jnp.int32, first.shape, 1)
    partner = jnp.where(lane < 32, pltpu.roll(first, 96, 1), pltpu.roll(first, 32, 1))
    return jnp.concatenate([first * c + partner * s, head[:, 128:]], axis=1)


def gelu_pair(h):
    cdf = 0.5 * (1.0 + lax.erf(h * (0.5**0.5)))
    pdf = jnp.exp(-0.5 * (h * h)) * (1.0 / math.sqrt(2.0 * math.pi))
    return (h * cdf).astype(bf), (cdf + h * pdf).astype(bf)


def h_body(units_tiles, n0, n1, w, b, c, s, act, slope, qkv, x):
    j = pl.program_id(0)

    @pl.when(j == 0)
    def _():
        x[:HALF] = n0[...]
        x[HALF:] = n1[...]

    @pl.when(j < units_tiles)
    def _():
        act[...], slope[...] = gelu_pair(nt(x[...], w[...]) + b[...])

    @pl.when((j >= units_tiles) & (j < units_tiles + 2))
    def _():
        qkv[0] = turn(nt(x[...], w[...]) + b[...], c[0], s[0]).astype(bf)

    @pl.when(j == units_tiles + 2)
    def _():
        qkv[0] = (nt(x[...], w[...]) + b[...]).astype(bf)


def h_call(n0, n1, w, b, c, s, t):
    width = n0.shape[1]
    rows = w.shape[0]
    tile = 256
    units_tiles = (rows - 768) // tile
    full = lambda *shape: pl.BlockSpec(shape, lambda j: (0,) * len(shape))
    return pl.pallas_call(
        functools.partial(h_body, units_tiles),
        grid=(rows // tile,),
        in_specs=[
            full(HALF, width), full(HALF, width),
            pl.BlockSpec((tile, width), lambda j: (j, 0)),
            pl.BlockSpec((1, tile), lambda j: (0, j)),
            pl.BlockSpec((1, TOK, 128), lambda j: (t, 0, 0)), pl.BlockSpec((1, TOK, 128), lambda j: (t, 0, 0)),
        ],
        out_specs=[
            pl.BlockSpec((TOK, tile), lambda j: (0, jnp.minimum(j, units_tiles - 1))),
            pl.BlockSpec((TOK, tile), lambda j: (0, jnp.minimum(j, units_tiles - 1))),
            pl.BlockSpec((1, TOK, tile), lambda j: (jnp.maximum(j - units_tiles, 0), 0, 0)),
        ],
        out_shape=[
            jax.ShapeDtypeStruct((TOK, rows - 768), bf),
            jax.ShapeDtypeStruct((TOK, rows - 768), bf),
            jax.ShapeDtypeStruct((3, TOK, 256), bf),
        ],
        scratch_shapes=[pltpu.VMEM((TOK, width), bf)],
        compiler_params=params(),
        cost_estimate=cost(2 * TOK * width * rows, 24e6),
        name="project",
    )(n0, n1, w, b, c, s)


def attn_body(q, k, v, idq, idk, mixed, lse):
    scores = nt(q[0], k[0]) * (256 ** -0.5)
    allowed = idk[0] <= idq[0]
    scores = jnp.where(allowed, scores, -1e30)
    top = jnp.max(scores, axis=1, keepdims=True)
    weights = jnp.exp(scores - top)
    total = jnp.sum(weights, axis=1, keepdims=True)
    probs = (weights / total).astype(bf)
    mixed[...] = nn(probs, v[0]).astype(bf)
    lse[...] = top + jnp.log(total)


def attn_call(qkv, ids_col, ids_row, t):
    tile = 256
    return pl.pallas_call(
        attn_body,
        grid=(TOK // tile,),
        in_specs=[
            pl.BlockSpec((1, tile, 256), lambda i: (0, i, 0)),
            pl.BlockSpec((1, TOK, 256), lambda i: (1, 0, 0)),
            pl.BlockSpec((1, TOK, 256), lambda i: (2, 0, 0)),
            pl.BlockSpec((1, tile, 1), lambda i: (t, i, 0)),
            pl.BlockSpec((1, 1, TOK), lambda i: (t, 0, 0)),
        ],
        out_specs=[
            pl.BlockSpec((tile, 256), lambda i: (i, 0)),
            pl.BlockSpec((tile, 1), lambda i: (i, 0)),
        ],
        out_shape=[jax.ShapeDtypeStruct((TOK, 256), bf), jax.ShapeDtypeStruct((TOK, 1), f32)],
        compiler_params=params(),
        cost_estimate=cost(4 * TOK * TOK * 256, 4e6),
        name="attend",
    )(qkv, qkv, qkv, ids_col, ids_row)


def attn_back_body(q, k, v, g, idq, idk, lse, cq, sq, ck, sk, out_q, out_kv, sums, acc_k, acc_v, acc_s):
    i = pl.program_id(0)
    last = pl.num_programs(0) - 1
    scale = 256 ** -0.5

    @pl.when(i == 0)
    def _():
        acc_k[...] = jnp.zeros_like(acc_k)
        acc_v[...] = jnp.zeros_like(acc_v)
        acc_s[...] = jnp.zeros_like(acc_s)

    scores = nt(q[0], k[0]) * scale
    allowed = idk[0] <= idq[0]
    probs = jnp.where(allowed, jnp.exp(scores - lse[...]), 0.0)
    grad_probs = nt(g[...], v[0])
    inner = jnp.sum(probs * grad_probs, axis=1, keepdims=True)
    gs = (probs * (grad_probs - inner)).astype(bf)
    gq = (nn(gs, k[0]) * scale).astype(bf).astype(f32)
    gq = turn(gq, cq[0], -sq[0])
    acc_s[0:1, :] += jnp.sum(gq, axis=0, keepdims=True)
    out_q[0] = gq.astype(bf)
    acc_k[...] += tn(gs, q[0])
    acc_v[...] += tn(probs.astype(bf), g[...])

    @pl.when(i == last)
    def _():
        gk = (acc_k[...] * scale).astype(bf).astype(f32)
        gk = turn(gk, ck[0], -sk[0])
        out_kv[0] = gk.astype(bf)
        gv = acc_v[...].astype(bf)
        out_kv[1] = gv
        acc_s[1:2, :] = jnp.sum(gk, axis=0, keepdims=True)
        acc_s[2:3, :] = jnp.sum(gv.astype(f32), axis=0, keepdims=True)
        sums[...] = acc_s[...]


def attn_back_call(qkv, gmix, ids_col, ids_row, lse, c, s, t):
    tile = 256
    return pl.pallas_call(
        attn_back_body,
        grid=(TOK // tile,),
        in_specs=[
            pl.BlockSpec((1, tile, 256), lambda i: (0, i, 0)),
            pl.BlockSpec((1, TOK, 256), lambda i: (1, 0, 0)),
            pl.BlockSpec((1, TOK, 256), lambda i: (2, 0, 0)),
            pl.BlockSpec((tile, 256), lambda i: (i, 0)),
            pl.BlockSpec((1, tile, 1), lambda i: (t, i, 0)),
            pl.BlockSpec((1, 1, TOK), lambda i: (t, 0, 0)),
            pl.BlockSpec((tile, 1), lambda i: (i, 0)),
            pl.BlockSpec((1, tile, 128), lambda i: (t, i, 0)),
            pl.BlockSpec((1, tile, 128), lambda i: (t, i, 0)),
            pl.BlockSpec((1, TOK, 128), lambda i: (t, 0, 0)),
            pl.BlockSpec((1, TOK, 128), lambda i: (t, 0, 0)),
        ],
        out_specs=[
            pl.BlockSpec((1, tile, 256), lambda i: (0, i, 0)),
            pl.BlockSpec((2, TOK, 256), lambda i: (0, 0, 0)),
            pl.BlockSpec((8, 256), lambda i: (0, 0)),
        ],
        out_shape=[
            jax.ShapeDtypeStruct((1, TOK, 256), bf),
            jax.ShapeDtypeStruct((2, TOK, 256), bf),
            jax.ShapeDtypeStruct((8, 256), f32),
        ],
        scratch_shapes=[pltpu.VMEM((TOK, 256), f32), pltpu.VMEM((TOK, 256), f32), pltpu.VMEM((8, 256), f32)],
        compiler_params=params(),
        cost_estimate=cost(10 * TOK * TOK * 256, 6e6),
        name="attend_back",
    )(qkv, qkv, qkv, gmix, ids_col, ids_row, lse, c, s, c, s)


def p_body(act, mixed, wd, wo, own, sib):
    out = nn(act[...], wd[...]) + nn(mixed[...], wo[...])
    own[...] = out[:HALF]
    sib[...] = out[HALF:].astype(bf)


def p_call(act, mixed, w):
    units, width = act.shape[1], w.shape[1]
    tile = 256
    full = lambda *shape: pl.BlockSpec(shape, lambda j: (0,) * len(shape))
    return pl.pallas_call(
        p_body,
        grid=(width // tile,),
        in_specs=[
            full(TOK, units), full(TOK, 256),
            pl.BlockSpec((units, tile), lambda j: (0, j)),
            pl.BlockSpec((256, tile), lambda j: (units // 256, j)),
        ],
        out_specs=[pl.BlockSpec((HALF, tile), lambda j: (0, j))] * 2,
        out_shape=[jax.ShapeDtypeStruct((HALF, width), f32), jax.ShapeDtypeStruct((HALF, width), bf)],
        compiler_params=params(),
        cost_estimate=cost(2 * TOK * width * (units + 256), 16e6),
        name="combine",
    )(act, mixed, w, w)


def ga_body(units_tiles, g0, g1, w, slope, gh, gmix, x):
    j = pl.program_id(0)

    @pl.when(j == 0)
    def _():
        x[:HALF] = g0[...]
        x[HALF:] = g1[...]

    ga = nt(x[...], w[...]).astype(bf)

    @pl.when(j < units_tiles)
    def _():
        gh[...] = (ga.astype(f32) * slope[...].astype(f32)).astype(bf)

    @pl.when(j == units_tiles)
    def _():
        gmix[...] = ga


def ga_call(g0, g1, w, slope):
    width, rows = w.shape[1], w.shape[0]
    tile = 256
    units_tiles = rows // tile - 1
    full = lambda *shape: pl.BlockSpec(shape, lambda j: (0,) * len(shape))
    return pl.pallas_call(
        functools.partial(ga_body, units_tiles),
        grid=(rows // tile,),
        in_specs=[
            full(HALF, width), full(HALF, width),
            pl.BlockSpec((tile, width), lambda j: (j, 0)),
            pl.BlockSpec((TOK, tile), lambda j: (0, jnp.minimum(j, units_tiles - 1))),
        ],
        out_specs=[
            pl.BlockSpec((TOK, tile), lambda j: (0, jnp.minimum(j, units_tiles - 1))),
            full(TOK, 256),
        ],
        out_shape=[jax.ShapeDtypeStruct((TOK, rows - 256), bf), jax.ShapeDtypeStruct((TOK, 256), bf)],
        scratch_shapes=[pltpu.VMEM((TOK, width), bf)],
        compiler_params=params(),
        cost_estimate=cost(2 * TOK * width * rows, 16e6),
        name="pull",
    )(g0, g1, w, slope)


def u_body(gh, gq, gkv, wu, wq, own, sib):
    out = nn(gh[...], wu[...]) + nn(gq[0], wq[0:256]) + nn(gkv[0], wq[256:512]) + nn(gkv[1], wq[512:768])
    own[...] = out[:HALF]
    sib[...] = out[HALF:].astype(bf)


def u_call(gh, gq, gkv, w_up, w_qkv):
    units, width = gh.shape[1], w_up.shape[1]
    tile = 256
    full = lambda *shape: pl.BlockSpec(shape, lambda j: (0,) * len(shape))
    return pl.pallas_call(
        u_body,
        grid=(width // tile,),
        in_specs=[
            full(TOK, units), full(1, TOK, 256), full(2, TOK, 256),
            pl.BlockSpec((units, tile), lambda j: (0, j)),
            pl.BlockSpec((768, tile), lambda j: (0, j)),
        ],
        out_specs=[pl.BlockSpec((HALF, tile), lambda j: (0, j))] * 2,
        out_shape=[jax.ShapeDtypeStruct((HALF, width), f32), jax.ShapeDtypeStruct((HALF, width), bf)],
        compiler_params=params(),
        cost_estimate=cost(2 * TOK * width * (units + 768), 20e6),
        name="push",
    )(gh, gq, gkv, w_up, w_qkv)


LANES = 128


MESH = pl.DeviceIdType.MESH


def line_order(z, t):
    near = jnp.where(z < 2, z + 1, z - 1)
    mid = jnp.where(z == 0, 2, jnp.where(z == 1, 0, jnp.where(z == 2, 3, 1)))
    far = jnp.where(z < 2, 3, 0)
    return jnp.where(t == 0, z, jnp.where(t == 1, near, jnp.where(t == 2, mid, far)))


def remote(src, dst, send, recv, s, f):
    return pltpu.make_async_remote_copy(
        src_ref=src, dst_ref=dst, send_sem=send, recv_sem=recv, device_id=(s, f), device_id_type=MESH
    )


def line_barrier(s, f, z):
    barrier = pltpu.get_barrier_semaphore()

    @pl.when(z < 3)
    def _():
        pl.semaphore_signal(barrier, inc=1, device_id=(s, f + 2), device_id_type=MESH)

    @pl.when(z > 0)
    def _():
        pl.semaphore_signal(barrier, inc=1, device_id=(s, f - 2), device_id_type=MESH)

    pl.semaphore_signal(barrier, inc=1, device_id=(s, f + 1 - 2 * (f % 2)), device_id_type=MESH)

    @pl.when((z == 0) | (z == 3))
    def _():
        pl.semaphore_wait(barrier, 2)

    @pl.when((z == 1) | (z == 2))
    def _():
        pl.semaphore_wait(barrier, 3)


def near_barrier(s, f):
    barrier = pltpu.get_barrier_semaphore()
    c = f % 2
    for step in range(1, 8):
        pl.semaphore_signal(barrier, inc=1, device_id=(s, (f + step) % 8), device_id_type=MESH)
    for step in range(1, 4):
        for core in range(2):
            pl.semaphore_signal(
                barrier, inc=1, device_id=((s + step) % 4, f - c + core), device_id_type=MESH
            )
    pl.semaphore_wait(barrier, 13)


class PlaneBack:
    def __init__(self, src, dst, s, f, send, recv, own_sem):
        c = f % 2
        mine = 2 * (s % 2) + c
        self.parts = []
        for k in range(4):
            to_s, to_f = (mine - k + 4) % 4, f - c + s // 2
            piece = src.at[pl.ds(128 * k, 128)]
            place = dst.at[pl.ds(pl.multiple_of(128 * mine, 128), 128)]
            here = (to_s == s) & (to_f == f)
            self.parts.append(
                (
                    here,
                    pltpu.make_async_copy(piece, place, own_sem),
                    remote(piece, place, send.at[k], recv.at[mine], to_s, to_f),
                )
            )
        self.comes = []
        for part in range(4):
            from_s, from_f = 2 * c + part // 2, f - c + part % 2
            ref = dst.at[pl.ds(128 * part, 128)]
            away = jnp.logical_not((from_s == s) & (from_f == f))
            self.comes.append((away, remote(ref, ref, send.at[part], recv.at[part], from_s, from_f)))

    def start(self):
        for here, local, away in self.parts:
            pl.when(here)(local.start)
            pl.when(jnp.logical_not(here))(away.start)

    def wait(self):
        for here, local, away in self.parts:
            pl.when(here)(local.wait)
            pl.when(jnp.logical_not(here))(away.wait_send)
        for away, copy in self.comes:
            pl.when(away)(copy.wait_recv)


def line_step(buf, k, z, s, f, sems, held=None):
    send_up, recv_up, send_dn, recv_dn = sems
    own = pl.ds(0, HALF)

    @pl.when((z - k >= 0) & (z < 3))
    def _():
        ref = buf.at[z - k, own]
        remote(ref if held is None else held, ref, send_up.at[k], recv_up.at[k], s, f + 2).start()

    @pl.when((z + k <= 3) & (z > 0))
    def _():
        ref = buf.at[z + k, own]
        remote(ref if held is None else held, ref, send_dn.at[k], recv_dn.at[k], s, f - 2).start()


def line_arrive(buf, k, z, s, f, sems):
    send_up, recv_up, send_dn, recv_dn = sems
    own = pl.ds(0, HALF)

    @pl.when(z - 1 - k >= 0)
    def _():
        ref = buf.at[z - 1 - k, own]
        remote(ref, ref, send_up.at[k], recv_up.at[k], s, f - 2).wait_recv()

    @pl.when(z + 1 + k <= 3)
    def _():
        ref = buf.at[z + 1 + k, own]
        remote(ref, ref, send_dn.at[k], recv_dn.at[k], s, f + 2).wait_recv()


def line_sent(buf, k, z, s, f, sems):
    send_up, recv_up, send_dn, recv_dn = sems
    own = pl.ds(0, HALF)

    @pl.when((z - k >= 0) & (z < 3))
    def _():
        ref = buf.at[z - k, own]
        remote(ref, ref, send_up.at[k], recv_up.at[k], s, f + 2).wait_send()

    @pl.when((z + k <= 3) & (z > 0))
    def _():
        ref = buf.at[z + k, own]
        remote(ref, ref, send_dn.at[k], recv_dn.at[k], s, f - 2).wait_send()


def core_copy(buf, b, s, f, sems, held=None):
    send, recv = sems
    return remote(
        buf.at[b, pl.ds(0, HALF)] if held is None else held, buf.at[b, pl.ds(HALF, HALF)], send.at[b], recv.at[b], s, f + 1 - 2 * (f % 2)
    )


def new_blocks(k, z, act):
    if k == 0:
        act(z)
        return

    @pl.when(z - k >= 0)
    def _():
        act(z - k)

    @pl.when(z + k <= 3)
    def _():
        act(z + k)


def forward_body(
    own_n, own_g, w_in_h, w_out_h, bias, cos, sin, idc, idr,
    n_all, g_all, a_all, slope_o, qkv_o, lse_o, own_o, sib_o,
    w_in, w_out, x, act, slope, qkv, mixed, lse, p_own, p_sib,
    load, line_n0, line_n1, line_n2, line_n3, line_g0, line_g1, line_g2, line_g3,
    core_n0, core_n1, core_p0, core_p1, out_sems,
):
    s, f = lax.axis_index("seq"), lax.axis_index("fsdp")
    z = f // 2
    line_n, line_g = (line_n0, line_n1, line_n2, line_n3), (line_g0, line_g1, line_g2, line_g3)
    core_n, core_p = (core_n0, core_n1), (core_p0, core_p1)
    own, other = pl.ds(0, HALF), pl.ds(HALF, HALF)
    units = act.shape[1]
    first = [
        pltpu.make_async_copy(own_n, x.at[own], load.at[0]),
        pltpu.make_async_copy(own_g, p_sib, load.at[3]),
        pltpu.make_async_copy(w_in_h, w_in, load.at[1]),
        pltpu.make_async_copy(w_out_h, w_out, load.at[2]),
    ]
    keep = [
        pltpu.make_async_copy(x.at[own], n_all.at[z, own], load.at[0]),
        pltpu.make_async_copy(p_sib, g_all.at[z, own], load.at[3]),
    ]
    for copy in first:
        copy.start()
    line_barrier(s, f, z)

    def outs(b):
        pairs = [
            (act, a_all.at[b, :, pl.ds(0, units)]), (mixed, a_all.at[b, :, pl.ds(units, 256)]),
            (slope, slope_o.at[b]), (qkv, qkv_o.at[b]), (lse, lse_o.at[b]), (p_own, own_o.at[b]),
        ]
        return [pltpu.make_async_copy(src, dst, out_sems.at[i]) for i, (src, dst) in enumerate(pairs)]

    def send_sib(b):
        return remote(p_sib, sib_o.at[b], core_p[0].at[b], core_p[1].at[b], s, f + 1 - 2 * (f % 2))

    for t in range(4):
        b = line_order(z, t)
        low_half = pltpu.make_async_copy(n_all.at[b, other], x.at[other], load.at[4])
        if t == 0:
            line_step(n_all, 0, z, s, f, line_n, own_n)
            core_copy(n_all, z, s, f, core_n, own_n).start()
            for copy, then in zip(first[:2], keep):
                copy.wait()
                then.start()
        else:
            line_arrive(n_all, t - 1, z, s, f, line_n)
            if t < 3:
                line_step(n_all, t, z, s, f, line_n)
            else:
                line_step(g_all, 0, z, s, f, line_g, own_g)
            new_blocks(t, z, lambda v: core_copy(n_all, v, s, f, core_n).start())
            top = pltpu.make_async_copy(n_all.at[b, own], x.at[own], load.at[0])
            top.start()
        core_copy(n_all, b, s, f, core_n).wait_recv()
        low_half.start()
        if t == 0:
            for copy in first[2:] + keep:
                copy.wait()
        else:
            top.wait()
            before = line_order(z, t - 1)
            for copy in outs(before):
                copy.wait()
            send_sib(before).wait_send()
        low_half.wait()

        @pl.loop(0, units // 256)
        def _(j):
            at = pl.ds(pl.multiple_of(j * 256, 256), 256)
            h = nt(x[...], w_in[at, :]) + bias[:, at]
            act[:, at], slope[:, at] = gelu_pair(h)

        @pl.loop(0, 2)
        def _(j):
            at = pl.ds(pl.multiple_of(units + j * 256, 256), 256)
            h = nt(x[...], w_in[at, :]) + bias[:, at]
            qkv[j] = turn(h, cos[b], sin[b]).astype(bf)

        at = pl.ds(units + 512, 256)
        qkv[2] = (nt(x[...], w_in[at, :]) + bias[:, at]).astype(bf)

        @pl.loop(0, TOK // 256)
        def _(i):
            rows = pl.ds(pl.multiple_of(i * 256, 256), 256)
            scores = nt(qkv[0, rows, :], qkv[1]) * (256 ** -0.5)
            scores = jnp.where(idr[b] <= idc[b, rows, :], scores, -1e30)
            top_score = jnp.max(scores, axis=1, keepdims=True)
            weights = jnp.exp(scores - top_score)
            total = jnp.sum(weights, axis=1, keepdims=True)
            probs = (weights / total).astype(bf)
            mixed[rows, :] = nn(probs, qkv[2]).astype(bf)
            lse[rows, :] = jnp.broadcast_to(top_score + jnp.log(total), (256, LANES))

        @pl.loop(0, p_own.shape[1] // 256)
        def _(j):
            at = pl.ds(pl.multiple_of(j * 256, 256), 256)
            out = nn(act[...], w_out[pl.ds(0, units), at]) + nn(mixed[...], w_out[pl.ds(units, 256), at])
            p_own[:, at] = out[:HALF].astype(bf)
            p_sib[:, at] = out[HALF:].astype(bf)

        for copy in outs(b):
            copy.start()
        send_sib(b).start()

    last = line_order(z, 3)
    for copy in outs(last):
        copy.wait()
    send_sib(last).wait_send()
    for b in range(4):
        core_copy(n_all, b, s, f, core_n).wait_send()
        send_sib(b).wait_recv()
    for k in range(3):
        line_sent(n_all, k, z, s, f, line_n)
    line_arrive(g_all, 0, z, s, f, line_g)
    line_sent(g_all, 0, z, s, f, line_g)


def forward_call(own_n, own_g, w_in, w_out, bias, cos, sin, ids_col, ids_row):
    width = own_n.shape[1]
    units = w_in.shape[0] - 768
    anys = pl.BlockSpec(memory_space=pl.ANY)
    vmem = pl.BlockSpec(memory_space=pltpu.VMEM)
    shape = jax.ShapeDtypeStruct
    dma = lambda n: pltpu.SemaphoreType.DMA((n,))
    return pl.pallas_call(
        forward_body,
        in_specs=[anys] * 4 + [vmem] * 5,
        out_specs=[anys] * 8,
        out_shape=[
            shape((4, TOK, width), bf), shape((4, TOK, width), bf),
            shape((4, TOK, units + 256), bf), shape((4, TOK, units), bf), shape((4, 3, TOK, 256), bf),
            shape((4, TOK, LANES), f32),
            shape((4, HALF, width), bf), shape((4, HALF, width), bf),
        ],
        scratch_shapes=[
            pltpu.VMEM(w_in.shape, bf), pltpu.VMEM(w_out.shape, bf), pltpu.VMEM((TOK, width), bf),
            pltpu.VMEM((TOK, units), bf), pltpu.VMEM((TOK, units), bf), pltpu.VMEM((3, TOK, 256), bf),
            pltpu.VMEM((TOK, 256), bf), pltpu.VMEM((TOK, LANES), f32),
            pltpu.VMEM((HALF, width), bf), pltpu.VMEM((HALF, width), bf),
            dma(5), dma(3), dma(3), dma(3), dma(3), dma(3), dma(3), dma(3), dma(3),
            dma(4), dma(4), dma(4), dma(4), dma(6),
        ],
        compiler_params=pltpu.CompilerParams(
            vmem_limit_bytes=60 * 1024 * 1024, collective_id=0, has_side_effects=True
        ),
        cost_estimate=cost(8 * TOK * width * (w_in.shape[0] + w_out.shape[0]), 200e6),
        name="forward",
    )(own_n, own_g, w_in, w_out, bias, cos, sin, ids_col, ids_row)


def sum_add(dst, parts):
    @pl.loop(0, HALF // 64)
    def _(i):
        rows = pl.ds(pl.multiple_of(i * 64, 64), 64)
        total = parts[0][rows, :].astype(f32)
        for part in parts[1:]:
            total = total + part[rows, :].astype(f32)
        dst[rows, :] = total.astype(bf)


def line_sum_step(k, z, s, f, own, sib, land, stage, out, loads, sends, recvs):
    for way in range(2):
        d = z - 3 + k if way == 0 else z + 3 - k
        valid = d >= 0 if way == 0 else d <= 3
        to = f - 2 if way == 0 else f + 2
        inner = z < 3 if way == 0 else z > 0
        was = z - 4 + k >= 0 if way == 0 else z + 4 - k <= 3

        @pl.when(valid)
        def _():
            terms = [
                pltpu.make_async_copy(own.at[d], stage.at[0], loads.at[0]),
                pltpu.make_async_copy(sib.at[d], stage.at[1], loads.at[1]),
            ]
            for copy in terms:
                copy.start()
            if k > 0:

                @pl.when(was)
                def _():
                    remote(out.at[way], land.at[way, k - 1], sends.at[way, k - 1], recvs.at[way, k - 1], s, to).wait_send()

                @pl.when(inner)
                def _():
                    remote(out.at[way], land.at[way, k - 1], sends.at[way, k - 1], recvs.at[way, k - 1], s, to).wait_recv()
                    came = pltpu.make_async_copy(land.at[way, k - 1], stage.at[2], loads.at[2])
                    came.start()
                    came.wait()

            for copy in terms:
                copy.wait()
            if k > 0:

                @pl.when(inner)
                def _():
                    sum_add(out.at[way], [stage.at[0], stage.at[1], stage.at[2]])

                @pl.when(jnp.logical_not(inner))
                def _():
                    sum_add(out.at[way], [stage.at[0], stage.at[1]])
            else:
                sum_add(out.at[way], [stage.at[0], stage.at[1]])
            remote(out.at[way], land.at[way, k], sends.at[way, k], recvs.at[way, k], s, to).start()


def line_sum_end(z, s, f, own, sib, land, stage, out, loads, sends, recvs):
    terms = [
        pltpu.make_async_copy(own.at[z], stage.at[0], loads.at[0]),
        pltpu.make_async_copy(sib.at[z], stage.at[1], loads.at[1]),
    ]
    for copy in terms:
        copy.start()
    for copy in terms:
        copy.wait()

    for way in range(2):
        to = f - 2 if way == 0 else f + 2
        sent = z > 0 if way == 0 else z < 3
        got = z < 3 if way == 0 else z > 0

        @pl.when(sent)
        def _():
            remote(out.at[way], land.at[way, 2], sends.at[way, 2], recvs.at[way, 2], s, to).wait_send()

        @pl.when(got)
        def _():
            remote(out.at[way], land.at[way, 2], sends.at[way, 2], recvs.at[way, 2], s, to).wait_recv()
            came = pltpu.make_async_copy(land.at[way, 2], stage.at[2], loads.at[2])
            came.start()
            came.wait()
            sum_add(stage.at[0], [stage.at[0], stage.at[2]])

    sum_add(stage.at[0], [stage.at[0], stage.at[1]])


def backward_body(
    g_part, w_in_h, w_out_h, slope_h, qkv_h, lse_h, p_own, p_sib, cos, sin, idc, idr,
    g_all, b_all, own_o, sib_o, branch, land, sums,
    w_in, w_out, x, slope, qkv, lse, gh, gmix, gp, acc_k, acc_v, u_own, u_sib, stage, rs_out,
    load, l0, l1, l2, l3, core_0, core_1, core_u0, core_u1, out_sems, rs_send, rs_recv, pb_send, pb_recv,
):
    s, f = lax.axis_index("seq"), lax.axis_index("fsdp")
    z = f // 2
    line = (l0, l1, l2, l3)
    core = (core_0, core_1)
    own, other = pl.ds(0, HALF), pl.ds(HALF, HALF)
    units = gh.shape[1]
    scale = 256 ** -0.5
    first = [
        pltpu.make_async_copy(w_in_h, w_in, load.at[0]),
        pltpu.make_async_copy(w_out_h, w_out, load.at[1]),
    ]
    for copy in first:
        copy.start()
    near_barrier(s, f)
    swap = lambda b: core_copy(g_all, b, s, f, core)
    new_blocks(0, z, lambda b: swap(b).start())
    line_step(g_all, 1, z, s, f, line)
    new_blocks(1, z, lambda b: swap(b).start())
    reduce_args = (z, s, f, p_own, p_sib, land, stage, rs_out, load.at[pl.ds(8, 3)], rs_send, rs_recv)
    line_sum_step(0, *reduce_args)
    sums[...] = jnp.zeros_like(sums)
    back = PlaneBack(stage.at[0], branch, s, f, pb_send, pb_recv, load.at[7])

    def ins(b):
        return [
            pltpu.make_async_copy(src.at[b], dst, load.at[2 + i])
            for i, (src, dst) in enumerate([(slope_h, slope), (qkv_h, qkv), (lse_h, lse)])
        ]

    def outs(b):
        pairs = [(gh, b_all.at[b, :, pl.ds(0, units)]), (u_own, own_o.at[b])]
        pairs += [(gp.at[i], b_all.at[b, :, pl.ds(units + 256 * i, 256)]) for i in range(3)]
        return [pltpu.make_async_copy(src, dst, out_sems.at[i]) for i, (src, dst) in enumerate(pairs)]

    def send_sib(b):
        return remote(u_sib, sib_o.at[b], core_u0.at[b], core_u1.at[b], s, f + 1 - 2 * (f % 2))

    for t in range(4):
        b = line_order(z, t)
        for copy in ins(b):
            copy.start()
        if t == 3:
            line_arrive(g_all, 2, z, s, f, line)
            new_blocks(3, z, lambda v: swap(v).start())
        top = pltpu.make_async_copy(g_all.at[b, own], x.at[own], load.at[5])
        top.start()
        swap(b).wait_recv()
        low_half = pltpu.make_async_copy(g_all.at[b, other], x.at[other], load.at[6])
        low_half.start()
        if t == 0:
            for copy in first:
                copy.wait()
        else:
            before = line_order(z, t - 1)
            for copy in outs(before):
                copy.wait()
            send_sib(before).wait_send()
        for copy in ins(b):
            copy.wait()
        top.wait()
        low_half.wait()

        @pl.loop(0, units // 256)
        def _(j):
            at = pl.ds(pl.multiple_of(j * 256, 256), 256)
            ga = nt(x[...], w_out[at, :]).astype(bf)
            gh[:, at] = (ga.astype(f32) * slope[:, at].astype(f32)).astype(bf)

        gmix[...] = nt(x[...], w_out[pl.ds(units, 256), :]).astype(bf)
        acc_k[...] = jnp.zeros_like(acc_k)
        acc_v[...] = jnp.zeros_like(acc_v)

        @pl.loop(0, TOK // 256)
        def _(i):
            rows = pl.ds(pl.multiple_of(i * 256, 256), 256)
            q, g = qkv[0, rows, :], gmix[rows, :]
            scores = nt(q, qkv[1]) * scale
            allowed = idr[b] <= idc[b, rows, :]
            probs = jnp.where(allowed, jnp.exp(scores - lse[rows, 0:1]), 0.0)
            grad_probs = nt(g, qkv[2])
            inner = jnp.sum(probs * grad_probs, axis=1, keepdims=True)
            gs = (probs * (grad_probs - inner)).astype(bf)
            gq = (nn(gs, qkv[1]) * scale).astype(bf).astype(f32)
            gq = turn(gq, cos[b, rows, :], -sin[b, rows, :])
            sums[0:1, :] += jnp.sum(gq, axis=0, keepdims=True)
            gp[0, rows, :] = gq.astype(bf)
            acc_k[...] += tn(gs, q)
            acc_v[...] += tn(probs.astype(bf), g)

        gk = (acc_k[...] * scale).astype(bf).astype(f32)
        gk = turn(gk, cos[b], -sin[b])
        sums[1:2, :] += jnp.sum(gk, axis=0, keepdims=True)
        gp[1] = gk.astype(bf)
        gv = acc_v[...].astype(bf)
        sums[2:3, :] += jnp.sum(gv.astype(f32), axis=0, keepdims=True)
        gp[2] = gv
        if t == 1:
            line_arrive(g_all, 1, z, s, f, line)
            line_step(g_all, 2, z, s, f, line)
            new_blocks(2, z, lambda v: swap(v).start())
            line_sum_step(1, *reduce_args)
        if t == 2:
            line_sum_step(2, *reduce_args)
        if t == 3:
            line_sum_end(*reduce_args)
            back.start()

        @pl.loop(0, u_own.shape[1] // 256)
        def _(j):
            at = pl.ds(pl.multiple_of(j * 256, 256), 256)
            out = nn(gh[...], w_in[pl.ds(0, units), at])
            for i in range(3):
                out = out + nn(gp[i], w_in[pl.ds(units + 256 * i, 256), at])
            u_own[:, at] = out[:HALF].astype(bf)
            u_sib[:, at] = out[HALF:].astype(bf)

        for copy in outs(b):
            copy.start()
        send_sib(b).start()

    last = line_order(z, 3)
    for copy in outs(last):
        copy.wait()
    send_sib(last).wait_send()
    for b in range(4):
        swap(b).wait_send()
        send_sib(b).wait_recv()
    for k in (1, 2):
        line_sent(g_all, k, z, s, f, line)
    back.wait()


def backward_call(g_part, w_in, w_out, slope, qkv, lse, p_own, p_sib, cos, sin, ids_col, ids_row):
    width = w_in.shape[1]
    units = w_in.shape[0] - 768
    anys = pl.BlockSpec(memory_space=pl.ANY)
    vmem = pl.BlockSpec(memory_space=pltpu.VMEM)
    shape = jax.ShapeDtypeStruct
    dma = lambda *n: pltpu.SemaphoreType.DMA(n)
    return pl.pallas_call(
        backward_body,
        in_specs=[anys] * 8 + [vmem] * 4,
        out_specs=[anys] * 6 + [vmem],
        out_shape=[
            shape((4, TOK, width), bf), shape((4, TOK, units + 768), bf),
            shape((4, HALF, width), bf), shape((4, HALF, width), bf), shape((HALF, width), bf),
            shape((2, 3, HALF, width), bf), shape((8, 256), f32),
        ],
        input_output_aliases={0: 0},
        scratch_shapes=[
            pltpu.VMEM(w_in.shape, bf), pltpu.VMEM(w_out.shape, bf), pltpu.VMEM((TOK, width), bf),
            pltpu.VMEM((TOK, units), bf), pltpu.VMEM((3, TOK, 256), bf), pltpu.VMEM((TOK, LANES), f32),
            pltpu.VMEM((TOK, units), bf), pltpu.VMEM((TOK, 256), bf), pltpu.VMEM((3, TOK, 256), bf),
            pltpu.VMEM((TOK, 256), f32), pltpu.VMEM((TOK, 256), f32),
            pltpu.VMEM((HALF, width), bf), pltpu.VMEM((HALF, width), bf),
            pltpu.VMEM((3, HALF, width), bf), pltpu.VMEM((2, HALF, width), bf),
            dma(11), dma(3), dma(3), dma(3), dma(3), dma(4), dma(4), dma(4), dma(4), dma(5),
            dma(2, 3), dma(2, 3), dma(4), dma(4),
        ],
        compiler_params=pltpu.CompilerParams(
            vmem_limit_bytes=62 * 1024 * 1024, collective_id=1, has_side_effects=True
        ),
        cost_estimate=cost(8 * TOK * width * (w_in.shape[0] + w_out.shape[0]), 200e6),
        name="backward",
    )(g_part, w_in, w_out, slope, qkv, lse, p_own, p_sib, cos, sin, ids_col, ids_row)


PAIRS = 12


def tail_body(
    a_all, b_all, g_all, n_all, plain, u_own, u_sib, gain, shift, wide_in, more_in,
    fin_up, fin_out, fin_qkv, u_o, small_o, land,
    term, r1, r2, hop, stage, rs_out, left, right, acc, acc_s, weight, sides, wide, more, got, small,
    load, w_sem, r1_s, r1_r, r2_s, r2_r, hop_s, hop_r, r3_s, r3_r, r4_s, r4_r,
    rs_load, rs_send, rs_recv, pb_s, pb_r, sm_s, sm_r, sq_s, sq_r, own_sems, self_sem,
):
    s, f = lax.axis_index("seq"), lax.axis_index("fsdp")
    z = f // 2
    x, y = s % 2, s // 2
    across = (s + 1 - 2 * x, (s + 2) % 4)
    reduce_args = (z, s, f, u_own, u_sib, land, stage, rs_out, rs_load, rs_send, rs_recv)
    column = [4, 5, 6, 0, 1, 2, 3, 0, 1, 2, 3, 4]

    def loads(j, k):
        rows_of, right_of = (b_all, n_all) if j < 7 else (a_all, g_all)
        slot = k % 2
        return (
            pltpu.make_async_copy(rows_of.at[k, :, pl.ds(256 * column[j], 256)], left.at[slot], load.at[slot, 0]),
            pltpu.make_async_copy(right_of.at[k], right.at[slot], load.at[slot, 1]),
        )

    def weights(j):
        return pltpu.make_async_copy(plain.at[pl.ds(256 * column[j], 256)], weight, w_sem)

    for copy in loads(0, 0):
        copy.start()
    near_barrier(s, f)
    sides[...] = jnp.zeros_like(sides)
    wide[...] = wide_in[...]
    more[...] = more_in[...]

    def compute(j):
        if j < 7:
            weights(j).start()

        @pl.loop(0, 4)
        def _(k):
            slot = k % 2

            @pl.when(k < 3)
            def _():
                for copy in loads(j, k + 1):
                    copy.start()

            if j + 1 < PAIRS:

                @pl.when(k == 3)
                def _():
                    for copy in loads(j + 1, 0):
                        copy.start()

            for copy in loads(j, k):
                copy.wait()
            part = tn(left[slot], right[slot])

            @pl.when(k == 0)
            def _():
                acc[...] = part

            @pl.when(k > 0)
            def _():
                acc[...] += part

            if j < 7:
                part_s = tn(left[slot], jnp.ones((TOK, LANES), bf))

                @pl.when(k == 0)
                def _():
                    acc_s[...] = part_s

                @pl.when(k > 0)
                def _():
                    acc_s[...] += part_s

        if j < 7:
            which = 1 if j < 3 else 0
            weights(j).wait()
            raw, total = acc[...], acc_s[:, 0:1]
            term[j] = (raw * gain[which : which + 1, :] + total * shift[which : which + 1, :]).astype(bf)
            low_w = weight[...].astype(f32)
            sides[2 * which : 2 * which + 1, :] += jnp.sum(low_w * raw, axis=0, keepdims=True)
            sides[2 * which + 1 : 2 * which + 2, :] += jnp.sum(low_w * total, axis=0, keepdims=True)
            if j >= 3:
                row = jnp.transpose(acc_s[...])
                for half in range(2):
                    at = 2 * (j - 3) + half
                    more[at : at + 1, :] = row[0:1, 128 * half : 128 * half + 128]
        else:
            term[j] = acc[...].astype(bf)

    def rows(start, count):
        return pl.ds(pl.multiple_of(start, 32), count)

    ways = ((0, x, y), (1, y, x))

    def base(p, a, b):
        return 128 * p + 64 * a + 32 * b

    def result(i, start, count):
        if i < 4:
            return fin_up.at[rows(256 * i + start, count)]
        if i < 9:
            return fin_out.at[rows(256 * (i - 4) + start, count)]
        return fin_qkv.at[rows(256 * (i - 9) + start, count)]

    def send1(j, p, a):
        return remote(
            term.at[j, rows(128 * p + 64 * (1 - a), 64)], r1.at[j, p], r1_s.at[j, p], r1_r.at[j, p], across[p], f
        )

    def send2(j, p, a, b):
        return remote(
            term.at[j, rows(base(p, a, 1 - b), 32)], r2.at[j, p], r2_s.at[j, p], r2_r.at[j, p], across[1 - p], f
        )

    def keep3(i, p, a, b):
        return pltpu.make_async_copy(
            term.at[i + 3, rows(base(p, a, b), 32)], result(i, base(p, a, b), 32), own_sems.at[i, p]
        )

    def send3(i, p, a, b):
        ref = result(i, base(p, a, b), 32)
        src = term.at[i + 3, rows(base(p, a, b), 32)] if i < 9 else ref
        return remote(src, ref, r3_s.at[i, p], r3_r.at[i, p], across[1 - p], f)

    def send4(i, p, a):
        ref = result(i, 128 * p + 64 * a, 64)
        return remote(ref, ref, r4_s.at[i, p], r4_r.at[i, p], across[p], f)

    def owner(j):
        head = 8 * j + f
        return head // 3, head % 3

    def hop_place(i, p, a, b):
        return fin_qkv.at[rows(256 * i + base(p, a, b), 32)]

    def send_hop(j, p, a, b):
        to, i = owner(j)
        return remote(hop.at[j, p], hop_place(i, p, a, b), hop_s.at[j, p], hop_r.at[i, p], s, to)

    def keep_hop(j, p, a, b):
        return pltpu.make_async_copy(hop.at[j, p], hop_place(owner(j)[1], p, a, b), own_sems.at[9 + j, p])

    def step1(j):
        for p, a, b in ways:
            send1(j, p, a).start()

    def step2(j):
        for p, a, b in ways:
            send1(j, p, a).wait_recv()
            at = rows(128 * p + 64 * a, 64)
            term[j, at, :] = (term[j, at, :].astype(f32) + r1[j, p].astype(f32)).astype(bf)
            send2(j, p, a, b).start()

    def step3(j):
        for p, a, b in ways:
            send2(j, p, a, b).wait_recv()
            at = rows(base(p, a, b), 32)
            total = (term[j, at, :].astype(f32) + r2[j, p].astype(f32)).astype(bf)
            if j >= 3:
                term[j, at, :] = total
                send3(j - 3, p, a, b).start()
                keep3(j - 3, p, a, b).start()
            else:
                hop[j, p] = total
                here = owner(j)[0] == f
                pl.when(here)(keep_hop(j, p, a, b).start)
                pl.when(jnp.logical_not(here))(send_hop(j, p, a, b).start)

    def step3_own(i):
        head, kind = (3 * f + i) % 8, (3 * f + i) // 8
        for p, a, b in ways:
            ref = hop_place(i, p, a, b)
            coming = remote(ref, ref, hop_s.at[i, p], hop_r.at[i, p], s, head)
            staying = pltpu.make_async_copy(ref, ref, own_sems.at[9 + kind, p])
            pl.when(head != f)(coming.wait_recv)
            pl.when(head == f)(staying.wait)
            send3(9 + i, p, a, b).start()

    def step4(i):
        for p, a, b in ways:
            send3(i, p, a, b).wait_recv()
            if i < 9:
                keep3(i, p, a, b).wait()
            send4(i, p, a).start()

    def small_send(step):
        to = (f + step) % 8
        return remote(wide.at[to], got.at[step - 1], sm_s.at[step - 1], sm_r.at[step - 1], s, to)

    def small_one():
        for to in range(8):
            for v in range(4):
                for half in range(2):
                    at = 256 * to + 128 * half
                    wide[to, 2 * v + half : 2 * v + half + 1, :] = sides[v : v + 1, at : at + 128]
        for step in range(1, 8):
            small_send(step).start()

    def small_two():
        total = wide[f]
        for step in range(1, 8):
            small_send(step).wait_recv()
            total = total + got[step - 1]
        small[0, 0:16] = total
        small[0, 16:32] = more[...]
        small_seq(0).start()

    def small_seq(way):
        return remote(small.at[2 * way], small.at[2 * way + 1], sq_s.at[way], sq_r.at[way], across[way], f)

    def small_three():
        small_seq(0).wait_recv()
        small[2] = small[0] + small[1]
        small_seq(1).start()

    def small_four():
        small_seq(1).wait_recv()
        small_o[...] = small[2] + small[3]

    back = PlaneBack(stage.at[0], u_o, s, f, pb_s, pb_r, self_sem)
    compute(0)
    step1(0)
    line_sum_step(0, *reduce_args)
    compute(1)
    step1(1)
    for it in range(1, 16):
        if it + 1 < PAIRS:
            compute(it + 1)
            step1(it + 1)
        if it - 1 < PAIRS:
            step2(it - 1)
        if 0 <= it - 2 < PAIRS:
            step3(it - 2)
        if 5 <= it < 8:
            step3_own(it - 5)
        if 0 <= it - 6 < 9:
            step4(it - 6)
        if 6 <= it < 9:
            step4(9 + it - 6)
        if it == 4:
            line_sum_step(1, *reduce_args)
        if it == 7:
            line_sum_step(2, *reduce_args)
        if it == 8:
            small_one()
        if it == 10:
            small_two()
        if it == 11:
            line_sum_end(*reduce_args)
            back.start()
        if it == 12:
            small_three()
        if it == 14:
            small_four()

    back.wait()
    for j in range(PAIRS):
        for p, a, b in ways:
            send4(j, p, a).wait_recv()
            send1(j, p, a).wait_send()
            send2(j, p, a, b).wait_send()
            send3(j, p, a, b).wait_send()
            send4(j, p, a).wait_send()
            if j < 3:
                pl.when(owner(j)[0] != f)(send_hop(j, p, a, b).wait_send)

    for step in range(1, 8):
        small_send(step).wait_send()
    for way in range(2):
        small_seq(way).wait_send()


def tail_call(a_all, b_all, g_all, n_all, plain, u_own, u_sib, gain, shift, wide, more):
    width = plain.shape[1]
    anys = pl.BlockSpec(memory_space=pl.ANY)
    vmem = pl.BlockSpec(memory_space=pltpu.VMEM)
    shape = jax.ShapeDtypeStruct
    dma = lambda *n: pltpu.SemaphoreType.DMA(n)
    two = [dma(PAIRS, 2)] * 2
    return pl.pallas_call(
        tail_body,
        in_specs=[anys] * 7 + [vmem] * 4,
        out_specs=[anys] * 4 + [vmem, anys],
        out_shape=[
            shape((1024, width), bf), shape((1280, width), bf), shape((768, width), bf),
            shape((HALF, width), bf), shape((32, LANES), f32), shape((2, 3, HALF, width), bf),
        ],
        scratch_shapes=[
            pltpu.VMEM((PAIRS, 256, width), bf), pltpu.VMEM((PAIRS, 2, 64, width), bf),
            pltpu.VMEM((PAIRS, 2, 32, width), bf), pltpu.VMEM((3, 2, 32, width), bf),
            pltpu.VMEM((3, HALF, width), bf), pltpu.VMEM((2, HALF, width), bf),
            pltpu.VMEM((2, TOK, 256), bf), pltpu.VMEM((2, TOK, width), bf),
            pltpu.VMEM((256, width), f32), pltpu.VMEM((256, LANES), f32), pltpu.VMEM((256, width), bf),
            pltpu.VMEM((8, width), f32), pltpu.VMEM((8, 16, LANES), f32), pltpu.VMEM((16, LANES), f32),
            pltpu.VMEM((7, 16, LANES), f32), pltpu.VMEM((4, 32, LANES), f32),
            dma(2, 2), pltpu.SemaphoreType.DMA, *two, *two, dma(3, 2), dma(3, 2), *two, *two,
            dma(3), dma(2, 3), dma(2, 3), dma(4), dma(4), dma(7), dma(7), dma(2), dma(2), dma(PAIRS, 2),
            pltpu.SemaphoreType.DMA,
        ],
        compiler_params=pltpu.CompilerParams(
            vmem_limit_bytes=61 * 1024 * 1024, collective_id=2, has_side_effects=True
        ),
        cost_estimate=cost(1e11, 600e6),
        name="tail",
    )(a_all, b_all, g_all, n_all, plain, u_own, u_sib, gain, shift, wide, more)


def pick(slices, which):
    return lax.dynamic_index_in_dim(slices, which, 0, keepdims=False)


def swap_core(value):
    return lax.ppermute(value, "fsdp", [(i, i ^ 1) for i in range(8)])


def along_z(value, pairs):
    return lax.ppermute(value, "fsdp", [(2 * a + c, 2 * b + c) for a, b in pairs for c in range(2)])


def spread_pairs(step):
    pairs = []
    for source in range(4):
        part = (step + source) % 4
        for rank in range(8):
            pairs.append((source * 8 + rank, (2 * (rank % 2) + part // 2) * 8 + rank - rank % 2 + part % 2))
    return pairs


def gather_z(own, z):
    low_half = z < 2
    edge = (z == 0) | (z == 3)
    above = along_z(own, [(1, 0), (2, 1), (3, 2)])
    below = along_z(own, [(0, 1), (1, 2), (2, 3)])
    first = jnp.where(low_half, above, below)
    outer = jnp.where(low_half, below, above)
    inner = along_z(first, [(1, 0), (2, 3)])
    cross = along_z(outer, [(1, 2), (2, 1)])
    second = jnp.where(edge, inner, outer)
    third = jnp.where(edge, along_z(cross, [(1, 0), (2, 3)]), cross)
    return [own, first, second, third]


def scatter_z(parts, z):
    low = jnp.bfloat16
    low_half = z < 2
    far = along_z(parts[3].astype(low), [(0, 1), (3, 2)])
    cross = along_z((parts[3] + far.astype(jnp.float32)).astype(low), [(1, 2), (2, 1)])
    near = along_z(parts[2].astype(low), [(0, 1), (3, 2)])
    one = parts[1] + near.astype(jnp.float32)
    two = parts[2] + cross.astype(jnp.float32)
    up = jnp.where(low_half, one, two).astype(low)
    down = jnp.where(low_half, two, one).astype(low)
    from_below = along_z(up, [(0, 1), (1, 2), (2, 3)])
    from_above = along_z(down, [(1, 0), (2, 1), (3, 2)])
    return parts[0] + from_below.astype(jnp.float32) + from_above.astype(jnp.float32)


def swap_seq(value, bit):
    return lax.ppermute(value, "seq", [(i, i ^ bit) for i in range(4)])


def gather_small(value, f):
    gathered = value[None]
    for bit in (1, 2, 4):
        other = lax.ppermute(gathered, "fsdp", [(i, i ^ bit) for i in range(8)])
        low_side = (f // bit) % 2 == 0
        gathered = jnp.concatenate(
            [jnp.where(low_side, gathered, other), jnp.where(low_side, other, gathered)]
        )
    return gathered


def scatter_small(value, f):
    for bit in (4, 2, 1):
        half = value.shape[0] // 2
        low_side = (f // bit) % 2 == 0
        sent = jnp.where(low_side, value[half:], value[:half])
        kept = jnp.where(low_side, value[:half], value[half:])
        value = kept + lax.ppermute(sent, "fsdp", [(i, i ^ bit) for i in range(8)])
    return value[0]


def sum_small(value):
    for bit in (1, 2):
        value = value + swap_seq(value, bit)
    return value


def after(value, other):
    return lax.optimization_barrier((value, other))[0]


def sum_seq(part, x, y):
    rows, columns = part.shape
    halves = part.reshape(2, 2, 2, rows // 8, columns)
    low = jnp.bfloat16
    outs = []
    for half, (bit_a, at_a), (bit_b, at_b) in ((0, (1, x), (2, y)), (1, (2, y), (1, x))):
        mine = halves[half]
        sent = swap_seq(pick(mine, 1 - at_a).astype(low), bit_a)
        kept = pick(mine, at_a) + sent.astype(jnp.float32)
        sent = swap_seq(pick(kept, 1 - at_b).astype(low), bit_b)
        outs.append((pick(kept, at_b) + sent.astype(jnp.float32)).astype(low))
    return outs


def spread_seq(pieces, x, y):
    outs = []
    for piece, (bit_a, at_a), (bit_b, at_b) in ((pieces[0], (1, x), (2, y)), (pieces[1], (2, y), (1, x))):
        other = swap_seq(piece, bit_b)
        both = jnp.where(at_b == 0, jnp.stack([piece, other]), jnp.stack([other, piece]))
        other = swap_seq(both, bit_a)
        outs.append(jnp.where(at_a == 0, jnp.stack([both, other]), jnp.stack([other, both])))
    rows, columns = pieces[0].shape
    return jnp.stack(outs).reshape(8 * rows, columns).astype(jnp.float32)


def split_body(
    resid_in,
    qkv_weight,
    qkv_bias,
    out_weight,
    out_bias,
    up_weight,
    up_bias,
    down_weight,
    down_bias,
    attn_gain,
    attn_shift,
    mlp_gain,
    mlp_shift,
    block_ids,
    offsets,
    grad_out,
):
    low = jnp.bfloat16
    f32 = jnp.float32
    groups, piece, width = resid_in.shape
    tokens = groups * piece
    s = lax.axis_index("seq")
    f = lax.axis_index("fsdp")
    z, c = f // 2, f % 2
    x, y = s % 2, s // 2
    both_axes = ("seq", "fsdp")
    units = up_weight.shape[0]

    length = block_ids.shape[1]
    own_small = [attn_gain, attn_shift, mlp_gain, mlp_shift, out_bias + down_bias, qkv_bias]
    packed = jnp.concatenate(
        own_small + [block_ids.reshape(-1).astype(f32), offsets.reshape(-1).astype(f32)]
    )
    flat = resid_in.reshape(tokens, width)
    center = flat - jnp.mean(flat, axis=-1, keepdims=True)
    inv = lax.rsqrt(jnp.mean(center * center, axis=-1, keepdims=True) + EPS)
    normal = center * inv
    grad_flat = grad_out.reshape(tokens, width)
    small = gather_small(packed, f)
    gain_a, shift_a, gain_m, shift_m, bias_out = (
        small[:, i * 256 : (i + 1) * 256].reshape(width) for i in range(5)
    )
    head_bias = small[:, 1280:2048].reshape(3, HEADS, HEAD_DIM)
    head_bias = lax.dynamic_index_in_dim(head_bias, f, 1, keepdims=False).reshape(3 * HEAD_DIM)
    ids_all = small[:, 2048 : 2048 + groups * length].astype(jnp.int32).reshape(-1, 8, LANES)
    starts_all = small[:, 2048 + groups * length :].astype(jnp.int32).reshape(-1, offsets.shape[1])

    def plane_out(value):
        parts = value.reshape(4, tokens // 4, width)
        got = [
            lax.ppermute(pick(parts, (k + s) % 4), both_axes, spread_pairs(k)) for k in range(4)
        ]
        return jnp.concatenate(got, axis=0)

    def plane_back(value):
        parts = value.reshape(4, tokens // 4, width)
        got = jnp.stack(
            [
                lax.ppermute(parts[k], both_axes, [(b, a) for a, b in spread_pairs(k)])
                for k in range(4)
            ]
        )
        return jnp.concatenate([pick(got, (j - s + 4) % 4) for j in range(4)], axis=0)

    own_n = plane_out(normal.astype(low))
    own_g = plane_out(after(grad_flat.astype(low), own_n))

    quarter = HEAD_DIM // 4
    qkv_low = lax.dynamic_slice_in_dim(
        qkv_weight.reshape(3, HEAD_DIM, width), s * quarter, quarter, 1
    ).astype(low)
    came = jnp.stack(
        [
            lax.ppermute(qkv_low[i], "fsdp", [(r, (3 * r + i) % 8) for r in range(8)])
            for i in range(3)
        ]
    )

    def third_of(i):
        return (3 * ((3 * (f - i + 8)) % 8) + i) // 8

    slot_of = [
        sum(jnp.where(third_of(i) == kind, i, 0) for i in range(3)) for kind in range(3)
    ]
    came = jnp.stack([pick(came, slot_of[kind]) for kind in range(3)])
    got = jnp.stack([came] + [swap_seq(came, bit) for bit in (1, 2, 3)])
    head_w = jnp.stack([pick(got, s ^ q) for q in range(4)], axis=1).reshape(3 * HEAD_DIM, width)
    gain = jnp.stack([gain_m, gain_a])
    shift = jnp.stack([shift_m, shift_a])
    up_low = up_weight.astype(low).astype(f32)
    head32 = head_w.astype(f32)
    plain_w = jnp.concatenate([up_low, head32], axis=0).astype(low)
    w_up = (up_low * gain_m).astype(low)
    w_head = (head32 * gain_a).astype(low)
    w_in = jnp.concatenate([w_up, w_head], axis=0)
    bias_in = jnp.concatenate(
        [
            up_bias + jnp.sum(up_low * shift_m, axis=1),
            head_bias + jnp.sum(head32 * shift_a, axis=1),
        ]
    )[None]
    w_out = jnp.concatenate([down_weight.astype(low), out_weight.astype(low)], axis=0)

    halves = [(2 * (s % 2) + c, c), (2 * (s % 2) + 1 - c, 1 - c)]
    rows_at = [((part - k + 4) % 4) * 2 + core for part, core in halves for k in range(4)]
    ids_slots = [pick(ids_all, block * 4 + s) for block in range(4)]
    ids_here = jnp.stack(
        [jnp.concatenate([pick(row, at) for at in rows_at]) for row in ids_slots]
    ).reshape(4, 1024)
    starts_here = jnp.stack([pick(starts_all, block * 4 + s) for block in range(4)])
    pos = (jnp.stack(rows_at)[:, None] * LANES + jnp.arange(LANES)[None, :]).reshape(1024)
    positions = block_offset(ids_here, starts_here) + pos[None, :]
    lane = jnp.arange(LANES)
    inverse = jnp.exp(
        (lane % 32).astype(f32) * (-2.0 * math.log(10000.0) / ROT_DIM)
    )
    angles = jnp.where(lane < ROT_DIM, positions.astype(f32)[..., None] * inverse, 0.0)
    cosine = jnp.cos(angles)
    sine = jnp.sin(angles) * jnp.where(lane < ROT_DIM // 2, -1.0, 1.0)
    ids_col, ids_row = ids_here[:, :, None], ids_here[:, None, :]

    n_all, g_part, a_all, slope_all, qkv_all, lse_all, p_own, p_sib = forward_call(
        own_n, own_g, w_in, w_out, bias_in, cosine, sine, ids_col, ids_row
    )
    g_all, b_all, u_own, u_sib, branch, _, col_sums = backward_call(
        g_part, w_in, w_out, slope_all, qkv_all, lse_all, p_own, p_sib, cosine, sine, ids_col, ids_row
    )
    result = flat + branch.astype(f32) + bias_out

    slots = jnp.zeros((16, HEAD_DIM), f32)
    slots = lax.dynamic_update_slice(slots, col_sums[0:1], (f, 0))
    slots = lax.dynamic_update_slice(slots, col_sums[1:2], (8 + f, 0))
    spread = jnp.concatenate([jnp.zeros((4, width), f32), jnp.sum(grad_flat, axis=0)[None]])
    wide = jnp.concatenate(
        [spread.reshape(5, 8, 256).transpose(1, 0, 2).reshape(8, 5 * 256), slots.reshape(8, 512)], axis=1
    )
    wide = jnp.pad(wide, ((0, 0), (0, 256))).reshape(8, 16, LANES)
    more = jnp.pad(jnp.concatenate([jnp.zeros((units,), f32), col_sums[2]]), (0, 768)).reshape(16, LANES)
    up_low, out_low, qkv_low, u, small_sum, _ = tail_call(
        a_all, b_all, g_all, n_all, plain_w, u_own, u_sib, gain, shift, wide, more
    )
    u = u.astype(f32)
    grad_input = grad_flat + inv * (
        u - jnp.mean(u, axis=-1, keepdims=True) - normal * jnp.mean(u * normal, axis=-1, keepdims=True)
    )
    mine = small_sum.reshape(-1)
    vectors = [mine[i * 256 : (i + 1) * 256] for i in range(5)]
    qk_grad = mine[1280:1792]
    up_bias_grad = mine[2048 : 2048 + units]
    value_grad = mine[2048 + units : 2304 + units]
    return (
        result.reshape(groups, piece, width),
        grad_input.reshape(groups, piece, width),
        qkv_low.astype(f32),
        qk_grad,
        value_grad,
        out_low[units:].astype(f32),
        vectors[4],
        up_low.astype(f32),
        up_bias_grad,
        out_low[:units].astype(f32),
        vectors[4],
        vectors[2],
        vectors[3],
        vectors[0],
        vectors[1],
    )


def solution(mesh):
    placed = (
        P("fsdp", "seq", None),
        P("fsdp", None),
        P("fsdp"),
        P("fsdp", None),
        P("fsdp"),
        P("fsdp", None),
        P("fsdp"),
        P("fsdp", None),
        P("fsdp"),
        P("fsdp"),
        P("fsdp"),
        P("fsdp"),
        P("fsdp"),
        P("fsdp", None),
        P("fsdp", None),
        P("fsdp", "seq", None),
    )
    return jax.shard_map(
        split_body if mesh.shape["fsdp"] == HEADS and mesh.shape["seq"] == 4 else body,
        mesh=mesh,
        in_specs=placed,
        out_specs=(
            P("fsdp", "seq", None),
            P("fsdp", "seq", None),
            P("fsdp", None),
            P("fsdp"),
            P("fsdp"),
            P("fsdp", None),
            P("fsdp"),
            P("fsdp", None),
            P("fsdp"),
            P("fsdp", None),
            P("fsdp"),
            P("fsdp"),
            P("fsdp"),
            P("fsdp"),
            P("fsdp"),
        ),
        check_vma=False,
    )
```

```python
import functools
import math

import jax
import jax.numpy as jnp
from jax import lax
from jax.experimental import pallas as pl
from jax.experimental.pallas import tpu as pltpu
from jax.sharding import PartitionSpec as P

HEADS = 8
HEAD_DIM = 256
ROT_DIM = 64


EPS = 1e-05
NEG_FILL = -1e30


def layer_norm(values, gain, shift):
    center = values - jnp.mean(values, axis=-1, keepdims=True)
    spread = jnp.mean(center * center, axis=-1, keepdims=True)
    return center * lax.rsqrt(spread + EPS) * gain + shift


def rotary_tables(positions):
    half = ROT_DIM // 2
    inverse = jnp.exp(jnp.arange(half, dtype=jnp.float32) * (-2.0 * math.log(10000.0) / ROT_DIM))
    angles = positions.astype(jnp.float32)[..., None] * inverse
    return (jnp.cos(angles), jnp.sin(angles))


def block_offset(ids, starts):
    numbers = jnp.arange(starts.shape[1], dtype=jnp.int32)
    match = (ids[:, :, None] == numbers[None, None, :]).astype(jnp.int32)
    return jnp.sum(match * starts[:, None, :], axis=-1)


def rotate(values, cosine, sine):
    half = ROT_DIM // 2
    cosine = cosine[..., None, :]
    sine = sine[..., None, :]
    first = values[..., :half]
    second = values[..., half:ROT_DIM]
    return jnp.concatenate(
        [first * cosine - second * sine, second * cosine + first * sine, values[..., ROT_DIM:]],
        axis=-1,
    )


def gelu_exact(values):
    return jax.nn.gelu(values, approximate=False)


def contract_lead(left, right):
    return lax.dot_general(
        left, right, (((0,), (0,)), ((), ())), preferred_element_type=jnp.float32
    )


def contract_last(left, right):
    return lax.dot_general(
        left, right, (((1,), (1,)), ((), ())), preferred_element_type=jnp.float32
    )


def attend_forward(items):
    query, keys, values, ids = items
    allowed = ids[None, :] <= ids[:, None]
    scores = jnp.where(allowed, contract_last(query, keys) * HEAD_DIM ** (-0.5), NEG_FILL)
    top = jnp.max(scores, axis=1, keepdims=True)
    weights = jnp.exp(scores - top)
    total = jnp.sum(weights, axis=1, keepdims=True)
    probs = (weights / total).astype(jnp.bfloat16)
    mixed = jnp.dot(probs, values, preferred_element_type=jnp.float32).astype(jnp.bfloat16)
    return (mixed, (top + jnp.log(total))[:, 0])


def attend_backward(items):
    query, keys, values, ids, lse_row, grad_mix = items
    scale = HEAD_DIM ** (-0.5)
    allowed = ids[None, :] <= ids[:, None]
    scores = contract_last(query, keys) * scale
    probs = jnp.where(allowed, jnp.exp(scores - lse_row[:, None]), 0.0)
    grad_probs = contract_last(grad_mix, values)
    inner = jnp.sum(probs * grad_probs, axis=1, keepdims=True)
    grad_scores = (probs * (grad_probs - inner)).astype(jnp.bfloat16)
    grad_query = (jnp.dot(grad_scores, keys, preferred_element_type=jnp.float32) * scale).astype(
        jnp.bfloat16
    )
    grad_keys = (contract_lead(grad_scores, query) * scale).astype(jnp.bfloat16)
    grad_values = contract_lead(probs.astype(jnp.bfloat16), grad_mix).astype(jnp.bfloat16)
    return (grad_query, grad_keys, grad_values)


def body(
    resid_in,
    qkv_weight,
    qkv_bias,
    out_weight,
    out_bias,
    up_weight,
    up_bias,
    down_weight,
    down_bias,
    attn_gain,
    attn_shift,
    mlp_gain,
    mlp_shift,
    block_ids,
    offsets,
    grad_out,
):
    groups, piece, width = resid_in.shape
    tokens = groups * piece
    pieces = lax.axis_size("seq")
    length = piece * pieces
    rank = lax.axis_index("fsdp")
    heads_here = HEADS // pieces
    pairs = groups * heads_here
    flat = resid_in.reshape(tokens, width)
    gain_a, shift_a, gain_m, shift_m, proj_bias, attn_bias, hidden_bias, mlp_bias = (
        lax.all_gather(attn_gain, "fsdp", axis=0, tiled=True),
        lax.all_gather(attn_shift, "fsdp", axis=0, tiled=True),
        lax.all_gather(mlp_gain, "fsdp", axis=0, tiled=True),
        lax.all_gather(mlp_shift, "fsdp", axis=0, tiled=True),
        lax.all_gather(qkv_bias, "fsdp", axis=0, tiled=True),
        lax.all_gather(out_bias, "fsdp", axis=0, tiled=True),
        lax.all_gather(up_bias, "fsdp", axis=0, tiled=True),
        lax.all_gather(down_bias, "fsdp", axis=0, tiled=True),
    )
    qkv_low = qkv_weight.astype(jnp.bfloat16)
    out_low = out_weight.astype(jnp.bfloat16)
    up_low = up_weight.astype(jnp.bfloat16)
    down_low = down_weight.astype(jnp.bfloat16)
    qkv_full, out_full = (
        lax.all_gather(qkv_low, "fsdp", axis=0, tiled=True),
        lax.all_gather(out_low, "fsdp", axis=0, tiled=True),
    )
    normed_a32, norm_back_a = jax.vjp(layer_norm, flat, gain_a, shift_a)
    normed_m32, norm_back_m = jax.vjp(layer_norm, flat, gain_m, shift_m)
    normed_attn = normed_a32.astype(jnp.bfloat16)
    normed_mlp = normed_m32.astype(jnp.bfloat16)
    projected = (contract_last(normed_attn, qkv_full) + proj_bias).reshape(
        groups, piece, 3, HEADS, HEAD_DIM
    )
    first_pos = lax.axis_index("seq") * piece
    ids_piece = lax.dynamic_slice_in_dim(block_ids, first_pos, piece, 1)
    positions = (
        block_offset(ids_piece, offsets) + first_pos + jnp.arange(piece, dtype=jnp.int32)[None, :]
    )
    cosine, sine = rotary_tables(positions)
    query = rotate(projected[:, :, 0], cosine, sine)
    keys = rotate(projected[:, :, 1], cosine, sine)
    packed = jnp.stack([query, keys, projected[:, :, 2]], axis=2).astype(jnp.bfloat16)
    heads = lax.all_to_all(packed, "seq", split_axis=3, concat_axis=1, tiled=True)
    stacked = heads.transpose(2, 0, 3, 1, 4).reshape(3, pairs, length, HEAD_DIM)
    ids_pairs = jnp.repeat(block_ids, heads_here, axis=0)
    mixed_pairs, lse_pairs = lax.map(
        attend_forward, (stacked[0], stacked[1], stacked[2], ids_pairs)
    )
    back_heads = mixed_pairs.reshape(groups, heads_here, length, HEAD_DIM).transpose(0, 2, 1, 3)
    mixed_tok = lax.all_to_all(back_heads, "seq", split_axis=1, concat_axis=2, tiled=True).reshape(
        tokens, width
    )
    attn_part = jnp.dot(mixed_tok, out_full, preferred_element_type=jnp.float32) + attn_bias
    units_here = up_weight.shape[0]
    group_rows = lax.all_gather(normed_mlp, "fsdp", axis=0, tiled=True)
    local_bias = lax.dynamic_slice_in_dim(hidden_bias, rank * units_here, units_here)
    hidden = contract_last(group_rows, up_low) + local_bias
    active, gelu_back = jax.vjp(gelu_exact, hidden)
    active_low = active.astype(jnp.bfloat16)
    branch = (
        lax.psum_scatter(
            jnp.dot(active_low, down_low, preferred_element_type=jnp.float32).astype(jnp.bfloat16),
            "fsdp",
            scatter_dimension=0,
            tiled=True,
        ).astype(jnp.float32)
        + mlp_bias
    )
    result = flat + attn_part + branch
    grad_flat = grad_out.reshape(tokens, width)
    grad_low = grad_flat.astype(jnp.bfloat16)
    bias_sum = jnp.sum(grad_flat, axis=0)
    group_grad = lax.all_gather(grad_low, "fsdp", axis=0, tiled=True)
    grad_active = contract_last(group_grad, down_low).astype(jnp.bfloat16)
    grad_hidden = gelu_back(grad_active.astype(jnp.float32))[0]
    grad_hidden_low = grad_hidden.astype(jnp.bfloat16)
    grad_normed_m = lax.psum_scatter(
        jnp.dot(grad_hidden_low, up_low, preferred_element_type=jnp.float32),
        "fsdp",
        scatter_dimension=0,
        tiled=True,
    )
    up_grad_shard = contract_lead(grad_hidden_low, group_rows)
    down_grad_shard = contract_lead(active_low, group_grad)
    local_sum = jnp.sum(grad_hidden, axis=0)
    up_bias_term = lax.dynamic_update_slice_in_dim(
        jnp.zeros((hidden_bias.shape[0],), jnp.float32), local_sum, rank * units_here, 0
    )
    grad_mixed = contract_last(grad_low, out_full).astype(jnp.bfloat16)
    grad_heads = lax.all_to_all(
        grad_mixed.reshape(groups, piece, HEADS, HEAD_DIM),
        "seq",
        split_axis=2,
        concat_axis=1,
        tiled=True,
    )
    grad_pairs = grad_heads.transpose(0, 2, 1, 3).reshape(pairs, length, HEAD_DIM)
    grad_query, grad_keys, grad_values = lax.map(
        attend_backward, (stacked[0], stacked[1], stacked[2], ids_pairs, lse_pairs, grad_pairs)
    )
    grads_stack = (
        jnp.stack([grad_query, grad_keys, grad_values], axis=0)
        .reshape(3, groups, heads_here, length, HEAD_DIM)
        .transpose(1, 3, 0, 2, 4)
    )
    returned = lax.all_to_all(grads_stack, "seq", split_axis=1, concat_axis=3, tiled=True).astype(
        jnp.float32
    )
    grad_projected = jnp.stack(
        [
            rotate(returned[:, :, 0], cosine, -sine),
            rotate(returned[:, :, 1], cosine, -sine),
            returned[:, :, 2],
        ],
        axis=2,
    ).reshape(tokens, 3 * width)
    grad_projected_low = grad_projected.astype(jnp.bfloat16)
    proj_bias_term = jnp.sum(grad_projected, axis=0)
    qk_bias_term = proj_bias_term[: 2 * width]
    value_bias_term = proj_bias_term[2 * width :]
    grad_normed_a = jnp.dot(grad_projected_low, qkv_full, preferred_element_type=jnp.float32)
    grad_from_a, gain_a_term, shift_a_term = norm_back_a(grad_normed_a)
    grad_from_m, gain_m_term, shift_m_term = norm_back_m(grad_normed_m)
    grad_input = grad_flat + grad_from_a + grad_from_m
    qkv_term = contract_lead(grad_projected_low, normed_attn)
    out_term = contract_lead(mixed_tok, grad_low)
    (
        qkv_shard,
        out_shard,
        qk_bias_shard,
        value_bias_shard,
        bias_shard,
        up_bias_shard,
        gain_a_shard,
        shift_a_shard,
        gain_m_shard,
        shift_m_shard,
    ) = (
        lax.psum_scatter(qkv_term, "fsdp", scatter_dimension=0, tiled=True),
        lax.psum_scatter(out_term, "fsdp", scatter_dimension=0, tiled=True),
        lax.psum_scatter(qk_bias_term, "fsdp", scatter_dimension=0, tiled=True),
        lax.psum_scatter(value_bias_term, "fsdp", scatter_dimension=0, tiled=True),
        lax.psum_scatter(bias_sum, "fsdp", scatter_dimension=0, tiled=True),
        lax.psum_scatter(up_bias_term, "fsdp", scatter_dimension=0, tiled=True),
        lax.psum_scatter(gain_a_term, "fsdp", scatter_dimension=0, tiled=True),
        lax.psum_scatter(shift_a_term, "fsdp", scatter_dimension=0, tiled=True),
        lax.psum_scatter(gain_m_term, "fsdp", scatter_dimension=0, tiled=True),
        lax.psum_scatter(shift_m_term, "fsdp", scatter_dimension=0, tiled=True),
    )
    totals = lax.psum(
        (
            qkv_shard,
            out_shard,
            up_grad_shard,
            down_grad_shard,
            qk_bias_shard,
            value_bias_shard,
            bias_shard,
            up_bias_shard,
            gain_a_shard,
            shift_a_shard,
            gain_m_shard,
            shift_m_shard,
        ),
        "seq",
    )
    return (
        result.reshape(groups, piece, width),
        grad_input.reshape(groups, piece, width),
        totals[0],
        totals[4],
        totals[5],
        totals[1],
        totals[6],
        totals[2],
        totals[7],
        totals[3],
        totals[6],
        totals[8],
        totals[9],
        totals[10],
        totals[11],
    )


bf, f32 = jnp.bfloat16, jnp.float32
TOK, HALF = 1024, 512
VM = 56 * 1024 * 1024


def nt(a, b):
    return lax.dot_general(a, b, (((1,), (1,)), ((), ())), preferred_element_type=f32)


def nn(a, b):
    return lax.dot_general(a, b, (((1,), (0,)), ((), ())), preferred_element_type=f32)


def tn(a, b):
    return lax.dot_general(a, b, (((0,), (0,)), ((), ())), preferred_element_type=f32)


def params(n=1, limit=VM):
    return pltpu.CompilerParams(dimension_semantics=("arbitrary",) * n, vmem_limit_bytes=limit)


def cost(flops, nbytes):
    return pl.CostEstimate(flops=int(flops), bytes_accessed=int(nbytes), transcendentals=0)


def turn(head, c, s):
    first = head[:, :128]
    lane = lax.broadcasted_iota(jnp.int32, first.shape, 1)
    partner = jnp.where(lane < 32, pltpu.roll(first, 96, 1), pltpu.roll(first, 32, 1))
    return jnp.concatenate([first * c + partner * s, head[:, 128:]], axis=1)


def gelu_pair(h):
    cdf = 0.5 * (1.0 + lax.erf(h * (0.5**0.5)))
    pdf = jnp.exp(-0.5 * (h * h)) * (1.0 / math.sqrt(2.0 * math.pi))
    return (h * cdf).astype(bf), (cdf + h * pdf).astype(bf)


def h_body(units_tiles, n0, n1, w, b, c, s, act, slope, qkv, x):
    j = pl.program_id(0)

    @pl.when(j == 0)
    def _():
        x[:HALF] = n0[...]
        x[HALF:] = n1[...]

    @pl.when(j < units_tiles)
    def _():
        act[...], slope[...] = gelu_pair(nt(x[...], w[...]) + b[...])

    @pl.when((j >= units_tiles) & (j < units_tiles + 2))
    def _():
        qkv[0] = turn(nt(x[...], w[...]) + b[...], c[0], s[0]).astype(bf)

    @pl.when(j == units_tiles + 2)
    def _():
        qkv[0] = (nt(x[...], w[...]) + b[...]).astype(bf)


def h_call(n0, n1, w, b, c, s, t):
    width = n0.shape[1]
    rows = w.shape[0]
    tile = 256
    units_tiles = (rows - 768) // tile
    full = lambda *shape: pl.BlockSpec(shape, lambda j: (0,) * len(shape))
    return pl.pallas_call(
        functools.partial(h_body, units_tiles),
        grid=(rows // tile,),
        in_specs=[
            full(HALF, width), full(HALF, width),
            pl.BlockSpec((tile, width), lambda j: (j, 0)),
            pl.BlockSpec((1, tile), lambda j: (0, j)),
            pl.BlockSpec((1, TOK, 128), lambda j: (t, 0, 0)), pl.BlockSpec((1, TOK, 128), lambda j: (t, 0, 0)),
        ],
        out_specs=[
            pl.BlockSpec((TOK, tile), lambda j: (0, jnp.minimum(j, units_tiles - 1))),
            pl.BlockSpec((TOK, tile), lambda j: (0, jnp.minimum(j, units_tiles - 1))),
            pl.BlockSpec((1, TOK, tile), lambda j: (jnp.maximum(j - units_tiles, 0), 0, 0)),
        ],
        out_shape=[
            jax.ShapeDtypeStruct((TOK, rows - 768), bf),
            jax.ShapeDtypeStruct((TOK, rows - 768), bf),
            jax.ShapeDtypeStruct((3, TOK, 256), bf),
        ],
        scratch_shapes=[pltpu.VMEM((TOK, width), bf)],
        compiler_params=params(),
        cost_estimate=cost(2 * TOK * width * rows, 24e6),
        name="project",
    )(n0, n1, w, b, c, s)


def attn_body(q, k, v, idq, idk, mixed, lse):
    scores = nt(q[0], k[0]) * (256 ** -0.5)
    allowed = idk[0] <= idq[0]
    scores = jnp.where(allowed, scores, -1e30)
    top = jnp.max(scores, axis=1, keepdims=True)
    weights = jnp.exp(scores - top)
    total = jnp.sum(weights, axis=1, keepdims=True)
    probs = (weights / total).astype(bf)
    mixed[...] = nn(probs, v[0]).astype(bf)
    lse[...] = top + jnp.log(total)


def attn_call(qkv, ids_col, ids_row, t):
    tile = 256
    return pl.pallas_call(
        attn_body,
        grid=(TOK // tile,),
        in_specs=[
            pl.BlockSpec((1, tile, 256), lambda i: (0, i, 0)),
            pl.BlockSpec((1, TOK, 256), lambda i: (1, 0, 0)),
            pl.BlockSpec((1, TOK, 256), lambda i: (2, 0, 0)),
            pl.BlockSpec((1, tile, 1), lambda i: (t, i, 0)),
            pl.BlockSpec((1, 1, TOK), lambda i: (t, 0, 0)),
        ],
        out_specs=[
            pl.BlockSpec((tile, 256), lambda i: (i, 0)),
            pl.BlockSpec((tile, 1), lambda i: (i, 0)),
        ],
        out_shape=[jax.ShapeDtypeStruct((TOK, 256), bf), jax.ShapeDtypeStruct((TOK, 1), f32)],
        compiler_params=params(),
        cost_estimate=cost(4 * TOK * TOK * 256, 4e6),
        name="attend",
    )(qkv, qkv, qkv, ids_col, ids_row)


def attn_back_body(q, k, v, g, idq, idk, lse, cq, sq, ck, sk, out_q, out_kv, sums, acc_k, acc_v, acc_s):
    i = pl.program_id(0)
    last = pl.num_programs(0) - 1
    scale = 256 ** -0.5

    @pl.when(i == 0)
    def _():
        acc_k[...] = jnp.zeros_like(acc_k)
        acc_v[...] = jnp.zeros_like(acc_v)
        acc_s[...] = jnp.zeros_like(acc_s)

    scores = nt(q[0], k[0]) * scale
    allowed = idk[0] <= idq[0]
    probs = jnp.where(allowed, jnp.exp(scores - lse[...]), 0.0)
    grad_probs = nt(g[...], v[0])
    inner = jnp.sum(probs * grad_probs, axis=1, keepdims=True)
    gs = (probs * (grad_probs - inner)).astype(bf)
    gq = (nn(gs, k[0]) * scale).astype(bf).astype(f32)
    gq = turn(gq, cq[0], -sq[0])
    acc_s[0:1, :] += jnp.sum(gq, axis=0, keepdims=True)
    out_q[0] = gq.astype(bf)
    acc_k[...] += tn(gs, q[0])
    acc_v[...] += tn(probs.astype(bf), g[...])

    @pl.when(i == last)
    def _():
        gk = (acc_k[...] * scale).astype(bf).astype(f32)
        gk = turn(gk, ck[0], -sk[0])
        out_kv[0] = gk.astype(bf)
        gv = acc_v[...].astype(bf)
        out_kv[1] = gv
        acc_s[1:2, :] = jnp.sum(gk, axis=0, keepdims=True)
        acc_s[2:3, :] = jnp.sum(gv.astype(f32), axis=0, keepdims=True)
        sums[...] = acc_s[...]


def attn_back_call(qkv, gmix, ids_col, ids_row, lse, c, s, t):
    tile = 256
    return pl.pallas_call(
        attn_back_body,
        grid=(TOK // tile,),
        in_specs=[
            pl.BlockSpec((1, tile, 256), lambda i: (0, i, 0)),
            pl.BlockSpec((1, TOK, 256), lambda i: (1, 0, 0)),
            pl.BlockSpec((1, TOK, 256), lambda i: (2, 0, 0)),
            pl.BlockSpec((tile, 256), lambda i: (i, 0)),
            pl.BlockSpec((1, tile, 1), lambda i: (t, i, 0)),
            pl.BlockSpec((1, 1, TOK), lambda i: (t, 0, 0)),
            pl.BlockSpec((tile, 1), lambda i: (i, 0)),
            pl.BlockSpec((1, tile, 128), lambda i: (t, i, 0)),
            pl.BlockSpec((1, tile, 128), lambda i: (t, i, 0)),
            pl.BlockSpec((1, TOK, 128), lambda i: (t, 0, 0)),
            pl.BlockSpec((1, TOK, 128), lambda i: (t, 0, 0)),
        ],
        out_specs=[
            pl.BlockSpec((1, tile, 256), lambda i: (0, i, 0)),
            pl.BlockSpec((2, TOK, 256), lambda i: (0, 0, 0)),
            pl.BlockSpec((8, 256), lambda i: (0, 0)),
        ],
        out_shape=[
            jax.ShapeDtypeStruct((1, TOK, 256), bf),
            jax.ShapeDtypeStruct((2, TOK, 256), bf),
            jax.ShapeDtypeStruct((8, 256), f32),
        ],
        scratch_shapes=[pltpu.VMEM((TOK, 256), f32), pltpu.VMEM((TOK, 256), f32), pltpu.VMEM((8, 256), f32)],
        compiler_params=params(),
        cost_estimate=cost(10 * TOK * TOK * 256, 6e6),
        name="attend_back",
    )(qkv, qkv, qkv, gmix, ids_col, ids_row, lse, c, s, c, s)


def p_body(act, mixed, wd, wo, own, sib):
    out = nn(act[...], wd[...]) + nn(mixed[...], wo[...])
    own[...] = out[:HALF]
    sib[...] = out[HALF:].astype(bf)


def p_call(act, mixed, w):
    units, width = act.shape[1], w.shape[1]
    tile = 256
    full = lambda *shape: pl.BlockSpec(shape, lambda j: (0,) * len(shape))
    return pl.pallas_call(
        p_body,
        grid=(width // tile,),
        in_specs=[
            full(TOK, units), full(TOK, 256),
            pl.BlockSpec((units, tile), lambda j: (0, j)),
            pl.BlockSpec((256, tile), lambda j: (units // 256, j)),
        ],
        out_specs=[pl.BlockSpec((HALF, tile), lambda j: (0, j))] * 2,
        out_shape=[jax.ShapeDtypeStruct((HALF, width), f32), jax.ShapeDtypeStruct((HALF, width), bf)],
        compiler_params=params(),
        cost_estimate=cost(2 * TOK * width * (units + 256), 16e6),
        name="combine",
    )(act, mixed, w, w)


def ga_body(units_tiles, g0, g1, w, slope, gh, gmix, x):
    j = pl.program_id(0)

    @pl.when(j == 0)
    def _():
        x[:HALF] = g0[...]
        x[HALF:] = g1[...]

    ga = nt(x[...], w[...]).astype(bf)

    @pl.when(j < units_tiles)
    def _():
        gh[...] = (ga.astype(f32) * slope[...].astype(f32)).astype(bf)

    @pl.when(j == units_tiles)
    def _():
        gmix[...] = ga


def ga_call(g0, g1, w, slope):
    width, rows = w.shape[1], w.shape[0]
    tile = 256
    units_tiles = rows // tile - 1
    full = lambda *shape: pl.BlockSpec(shape, lambda j: (0,) * len(shape))
    return pl.pallas_call(
        functools.partial(ga_body, units_tiles),
        grid=(rows // tile,),
        in_specs=[
            full(HALF, width), full(HALF, width),
            pl.BlockSpec((tile, width), lambda j: (j, 0)),
            pl.BlockSpec((TOK, tile), lambda j: (0, jnp.minimum(j, units_tiles - 1))),
        ],
        out_specs=[
            pl.BlockSpec((TOK, tile), lambda j: (0, jnp.minimum(j, units_tiles - 1))),
            full(TOK, 256),
        ],
        out_shape=[jax.ShapeDtypeStruct((TOK, rows - 256), bf), jax.ShapeDtypeStruct((TOK, 256), bf)],
        scratch_shapes=[pltpu.VMEM((TOK, width), bf)],
        compiler_params=params(),
        cost_estimate=cost(2 * TOK * width * rows, 16e6),
        name="pull",
    )(g0, g1, w, slope)


def u_body(gh, gq, gkv, wu, wq, own, sib):
    out = nn(gh[...], wu[...]) + nn(gq[0], wq[0:256]) + nn(gkv[0], wq[256:512]) + nn(gkv[1], wq[512:768])
    own[...] = out[:HALF]
    sib[...] = out[HALF:].astype(bf)


def u_call(gh, gq, gkv, w_up, w_qkv):
    units, width = gh.shape[1], w_up.shape[1]
    tile = 256
    full = lambda *shape: pl.BlockSpec(shape, lambda j: (0,) * len(shape))
    return pl.pallas_call(
        u_body,
        grid=(width // tile,),
        in_specs=[
            full(TOK, units), full(1, TOK, 256), full(2, TOK, 256),
            pl.BlockSpec((units, tile), lambda j: (0, j)),
            pl.BlockSpec((768, tile), lambda j: (0, j)),
        ],
        out_specs=[pl.BlockSpec((HALF, tile), lambda j: (0, j))] * 2,
        out_shape=[jax.ShapeDtypeStruct((HALF, width), f32), jax.ShapeDtypeStruct((HALF, width), bf)],
        compiler_params=params(),
        cost_estimate=cost(2 * TOK * width * (units + 768), 20e6),
        name="push",
    )(gh, gq, gkv, w_up, w_qkv)


LANES = 128


MESH = pl.DeviceIdType.MESH


def line_order(z, t):
    near = jnp.where(z < 2, z + 1, z - 1)
    mid = jnp.where(z == 0, 2, jnp.where(z == 1, 0, jnp.where(z == 2, 3, 1)))
    far = jnp.where(z < 2, 3, 0)
    return jnp.where(t == 0, z, jnp.where(t == 1, near, jnp.where(t == 2, mid, far)))


def remote(src, dst, send, recv, s, f):
    return pltpu.make_async_remote_copy(
        src_ref=src, dst_ref=dst, send_sem=send, recv_sem=recv, device_id=(s, f), device_id_type=MESH
    )


def line_barrier(s, f, z):
    barrier = pltpu.get_barrier_semaphore()

    @pl.when(z < 3)
    def _():
        pl.semaphore_signal(barrier, inc=1, device_id=(s, f + 2), device_id_type=MESH)

    @pl.when(z > 0)
    def _():
        pl.semaphore_signal(barrier, inc=1, device_id=(s, f - 2), device_id_type=MESH)

    pl.semaphore_signal(barrier, inc=1, device_id=(s, f + 1 - 2 * (f % 2)), device_id_type=MESH)

    @pl.when((z == 0) | (z == 3))
    def _():
        pl.semaphore_wait(barrier, 2)

    @pl.when((z == 1) | (z == 2))
    def _():
        pl.semaphore_wait(barrier, 3)


def near_barrier(s, f):
    barrier = pltpu.get_barrier_semaphore()
    c = f % 2
    for step in range(1, 8):
        pl.semaphore_signal(barrier, inc=1, device_id=(s, (f + step) % 8), device_id_type=MESH)
    for step in range(1, 4):
        for core in range(2):
            pl.semaphore_signal(
                barrier, inc=1, device_id=((s + step) % 4, f - c + core), device_id_type=MESH
            )
    pl.semaphore_wait(barrier, 13)


class PlaneOut:
    def __init__(self, src, dst, s, f, send, recv, own_sem):
        c = f % 2
        mine = 2 * (s % 2) + c
        self.parts = []
        for j in range(4):
            k = (j - s + 4) % 4
            to_s, to_f = 2 * c + j // 2, f - c + j % 2
            place = dst.at[pl.ds(pl.multiple_of(128 * k, 128), 128)]
            here = (to_s == s) & (to_f == f)
            self.parts.append(
                (
                    here,
                    pltpu.make_async_copy(src.at[j], place, own_sem),
                    remote(src.at[j], place, send.at[j], recv.at[k], to_s, to_f),
                )
            )
        self.comes = []
        for k in range(4):
            from_s, from_f = (mine - k + 4) % 4, f - c + s // 2
            ref = dst.at[pl.ds(128 * k, 128)]
            away = jnp.logical_not((from_s == s) & (from_f == f))
            self.comes.append((away, remote(ref, ref, send.at[k], recv.at[k], from_s, from_f)))

    def start(self, j):
        here, local, away = self.parts[j]
        pl.when(here)(local.start)
        pl.when(jnp.logical_not(here))(away.start)

    def arrive(self):
        for here, local, away in self.parts:
            pl.when(here)(local.wait)
        for away, copy in self.comes:
            pl.when(away)(copy.wait_recv)

    def sent(self):
        for here, local, away in self.parts:
            pl.when(jnp.logical_not(here))(away.wait_send)

    def wait(self):
        self.arrive()
        self.sent()


def expand_tables(cos4, sin4, b, cos, sin):
    lane = lax.broadcasted_iota(jnp.int32, (256, LANES), 1)
    for q in range(4):
        at = pl.ds(256 * q, 256)
        c, s_ = cos4[b], sin4[b]
        if q > 0:
            c, s_ = pltpu.roll(c, 128 - 32 * q, 1), pltpu.roll(s_, 128 - 32 * q, 1)
        cos[at, :] = jnp.where(lane < 32, c, jnp.where(lane < 64, pltpu.roll(c, 32, 1), 1.0))
        sin[at, :] = jnp.where(lane < 32, -s_, jnp.where(lane < 64, pltpu.roll(s_, 32, 1), 0.0))


class PlaneBack:
    def __init__(self, src, dst, s, f, send, recv, own_sem):
        c = f % 2
        mine = 2 * (s % 2) + c
        self.parts = []
        for k in range(4):
            to_s, to_f = (mine - k + 4) % 4, f - c + s // 2
            piece = src.at[pl.ds(128 * k, 128)]
            place = dst.at[pl.ds(pl.multiple_of(128 * mine, 128), 128)]
            here = (to_s == s) & (to_f == f)
            self.parts.append(
                (
                    here,
                    pltpu.make_async_copy(piece, place, own_sem),
                    remote(piece, place, send.at[k], recv.at[mine], to_s, to_f),
                )
            )
        self.comes = []
        for part in range(4):
            from_s, from_f = 2 * c + part // 2, f - c + part % 2
            ref = dst.at[pl.ds(128 * part, 128)]
            away = jnp.logical_not((from_s == s) & (from_f == f))
            self.comes.append((away, remote(ref, ref, send.at[part], recv.at[part], from_s, from_f)))

    def start(self):
        for here, local, away in self.parts:
            pl.when(here)(local.start)
            pl.when(jnp.logical_not(here))(away.start)

    def wait(self):
        for here, local, away in self.parts:
            pl.when(here)(local.wait)
            pl.when(jnp.logical_not(here))(away.wait_send)
        for away, copy in self.comes:
            pl.when(away)(copy.wait_recv)


def line_step(buf, k, z, s, f, sems, held=None):
    send_up, recv_up, send_dn, recv_dn = sems
    own = pl.ds(0, HALF)

    @pl.when((z - k >= 0) & (z < 3))
    def _():
        ref = buf.at[z - k, own]
        remote(ref if held is None else held, ref, send_up.at[k], recv_up.at[k], s, f + 2).start()

    @pl.when((z + k <= 3) & (z > 0))
    def _():
        ref = buf.at[z + k, own]
        remote(ref if held is None else held, ref, send_dn.at[k], recv_dn.at[k], s, f - 2).start()


def line_arrive(buf, k, z, s, f, sems):
    send_up, recv_up, send_dn, recv_dn = sems
    own = pl.ds(0, HALF)

    @pl.when(z - 1 - k >= 0)
    def _():
        ref = buf.at[z - 1 - k, own]
        remote(ref, ref, send_up.at[k], recv_up.at[k], s, f - 2).wait_recv()

    @pl.when(z + 1 + k <= 3)
    def _():
        ref = buf.at[z + 1 + k, own]
        remote(ref, ref, send_dn.at[k], recv_dn.at[k], s, f + 2).wait_recv()


def line_sent(buf, k, z, s, f, sems):
    send_up, recv_up, send_dn, recv_dn = sems
    own = pl.ds(0, HALF)

    @pl.when((z - k >= 0) & (z < 3))
    def _():
        ref = buf.at[z - k, own]
        remote(ref, ref, send_up.at[k], recv_up.at[k], s, f + 2).wait_send()

    @pl.when((z + k <= 3) & (z > 0))
    def _():
        ref = buf.at[z + k, own]
        remote(ref, ref, send_dn.at[k], recv_dn.at[k], s, f - 2).wait_send()


def core_copy(buf, b, s, f, sems, held=None):
    send, recv = sems
    return remote(
        buf.at[b, pl.ds(0, HALF)] if held is None else held, buf.at[b, pl.ds(HALF, HALF)], send.at[b], recv.at[b], s, f + 1 - 2 * (f % 2)
    )


def new_blocks(k, z, act):
    if k == 0:
        act(z)
        return

    @pl.when(z - k >= 0)
    def _():
        act(z - k)

    @pl.when(z + k <= 3)
    def _():
        act(z + k)


def forward_body(
    own_n, g_low, heads, up_h, down_h, out_h, bias, gain, shift, cos4, sin4, idc, idr,
    n_all, g_all, w_in_o, w_out_o, a_all, slope_o, qkv_o, lse_o, own_o, sib_o,
    w_in, w_out, x, normed, act, slope, qkv, mixed, lse, p_own, p_sib, g_out, wide, cos, sin,
    load, w_load, w_store, line_n0, line_n1, line_n2, line_n3, line_g0, line_g1, line_g2, line_g3,
    core_n0, core_n1, core_p0, core_p1, out_sems, po_s, po_r, h_s, h_r,
):
    s, f = lax.axis_index("seq"), lax.axis_index("fsdp")
    z = f // 2
    line_n, line_g = (line_n0, line_n1, line_n2, line_n3), (line_g0, line_g1, line_g2, line_g3)
    core_n, core_p = (core_n0, core_n1), (core_p0, core_p1)
    own, other = pl.ds(0, HALF), pl.ds(HALF, HALF)
    units = act.shape[1]
    half = (s % 2 + s // 2) % 2
    across = (s + 1 - 2 * (s % 2), (s + 2) % 4)

    def head_rows(kind, which, count, start=0):
        return w_in.at[pl.ds(pl.multiple_of(units + 256 * kind + 128 * which + start, 64), count)]

    first = [pltpu.make_async_copy(own_n, x.at[own], load.at[0])] + [
        pltpu.make_async_copy(g_low.at[pl.ds(128 * j, 128)], g_out.at[j], load.at[1 + j]) for j in range(4)
    ]
    held = [pltpu.make_async_copy(heads.at[i], head_rows(i, half, 128), load.at[5 + i]) for i in range(3)]
    keep = pltpu.make_async_copy(x.at[own], n_all.at[z, own], load.at[0])
    chunks = [(up_h, w_in, i) for i in range(units // 256)]
    chunks += [(down_h, w_out, i) for i in range(units // 256)] + [(out_h, w_out, units // 256)]

    def chunk_load(i):
        src, dst, at = chunks[i]
        place = at if src is not out_h else 0
        return pltpu.make_async_copy(src.at[pl.ds(256 * place, 256)], wide.at[i % 2], w_load.at[i % 2])

    def send_head(kind, way):
        return remote(
            heads.at[kind, pl.ds(64 * way, 64)], head_rows(kind, half, 64, 64 * way),
            h_s.at[kind, way], h_r.at[kind, way], across[way], f,
        )

    def come_head(kind, way):
        ref = head_rows(kind, 1 - half, 64, 64 * way)
        return remote(ref, ref, h_s.at[kind, way], h_r.at[kind, way], across[way], f)

    for copy in first + held:
        copy.start()
    chunk_load(0).start()
    near_barrier(s, f)
    spread = PlaneOut(g_out, g_all.at[z, own], s, f, po_s, po_r, load.at[8])
    store = [pltpu.make_async_copy(w_in, w_in_o, w_store.at[0]), pltpu.make_async_copy(w_out, w_out_o, w_store.at[1])]

    def outs(b):
        pairs = [
            (act, a_all.at[b, :, pl.ds(0, units)]), (mixed, a_all.at[b, :, pl.ds(units, 256)]),
            (slope, slope_o.at[b]), (qkv, qkv_o.at[b]), (lse, lse_o.at[b]), (p_own, own_o.at[b]),
        ]
        return [pltpu.make_async_copy(src, dst, out_sems.at[i]) for i, (src, dst) in enumerate(pairs)]

    def send_sib(b):
        return remote(p_sib, sib_o.at[b], core_p[0].at[b], core_p[1].at[b], s, f + 1 - 2 * (f % 2))

    for t in range(4):
        b = line_order(z, t)
        low_half = pltpu.make_async_copy(n_all.at[b, other], x.at[other], load.at[9])
        if t == 0:
            line_step(n_all, 0, z, s, f, line_n, own_n)
            core_copy(n_all, z, s, f, core_n, own_n).start()
            for kind in range(3):
                for way in range(2):
                    send_head(kind, way).start()
            first[0].wait()
            keep.start()
            for i, (src, dst, at) in enumerate(chunks):
                if i + 1 < len(chunks):
                    chunk_load(i + 1).start()
                chunk_load(i).wait()
                dst[pl.ds(256 * at, 256), :] = wide[i % 2].astype(bf)
            for copy in first[1:]:
                copy.wait()
        else:
            line_arrive(n_all, t - 1, z, s, f, line_n)
            if t < 3:
                line_step(n_all, t, z, s, f, line_n)
            else:
                spread.arrive()
                line_step(g_all, 0, z, s, f, line_g)
            new_blocks(t, z, lambda v: core_copy(n_all, v, s, f, core_n).start())
            top = pltpu.make_async_copy(n_all.at[b, own], x.at[own], load.at[0])
            top.start()
        if t == 1:
            for j in range(4):
                spread.start(j)
        core_copy(n_all, b, s, f, core_n).wait_recv()
        low_half.start()
        expand_tables(cos4, sin4, b, cos, sin)
        if t == 0:
            keep.wait()
        else:
            top.wait()
            before = line_order(z, t - 1)
            for copy in outs(before):
                copy.wait()
            send_sib(before).wait_send()
        low_half.wait()

        def norm(which):
            @pl.loop(0, TOK // 64)
            def _(i):
                at = pl.ds(pl.multiple_of(i * 64, 64), 64)
                value = x[at, :].astype(f32) * gain[which : which + 1, :] + shift[which : which + 1, :]
                normed[at, :] = value.astype(bf)

        norm(0)

        @pl.loop(0, units // 256)
        def _(j):
            at = pl.ds(pl.multiple_of(j * 256, 256), 256)
            h = nt(normed[...], w_in[at, :]) + bias[:, at]
            act[:, at], slope[:, at] = gelu_pair(h)

        norm(1)
        if t == 0:
            for copy in held:
                copy.wait()
            for kind in range(3):
                for way in range(2):
                    come_head(kind, way).wait_recv()
            for copy in store:
                copy.start()

        @pl.loop(0, 2)
        def _(j):
            at = pl.ds(pl.multiple_of(units + j * 256, 256), 256)
            h = nt(normed[...], w_in[at, :]) + bias[:, at]
            qkv[j] = turn(h, cos[...], sin[...]).astype(bf)

        at = pl.ds(units + 512, 256)
        qkv[2] = (nt(normed[...], w_in[at, :]) + bias[:, at]).astype(bf)

        @pl.loop(0, TOK // 256)
        def _(i):
            rows = pl.ds(pl.multiple_of(i * 256, 256), 256)
            scores = nt(qkv[0, rows, :], qkv[1]) * (256 ** -0.5)
            scores = jnp.where(idr[b] <= idc[b, rows, :], scores, -1e30)
            top_score = jnp.max(scores, axis=1, keepdims=True)
            weights = jnp.exp(scores - top_score)
            total = jnp.sum(weights, axis=1, keepdims=True)
            probs = (weights / total).astype(bf)
            mixed[rows, :] = nn(probs, qkv[2]).astype(bf)
            lse[rows, :] = jnp.broadcast_to(top_score + jnp.log(total), (256, LANES))

        @pl.loop(0, p_own.shape[1] // 256)
        def _(j):
            at = pl.ds(pl.multiple_of(j * 256, 256), 256)
            out = nn(act[...], w_out[pl.ds(0, units), at]) + nn(mixed[...], w_out[pl.ds(units, 256), at])
            p_own[:, at] = out[:HALF].astype(bf)
            p_sib[:, at] = out[HALF:].astype(bf)

        for copy in outs(b):
            copy.start()
        send_sib(b).start()

    last = line_order(z, 3)
    for copy in outs(last):
        copy.wait()
    send_sib(last).wait_send()
    for b in range(4):
        core_copy(n_all, b, s, f, core_n).wait_send()
        send_sib(b).wait_recv()
    for k in range(3):
        line_sent(n_all, k, z, s, f, line_n)
    line_arrive(g_all, 0, z, s, f, line_g)
    line_sent(g_all, 0, z, s, f, line_g)
    spread.sent()
    for copy in store:
        copy.wait()
    for kind in range(3):
        for way in range(2):
            send_head(kind, way).wait_send()


def forward_call(own_n, g_low, heads, up, down, out, bias, gain, shift, cos4, sin4, ids_col, ids_row):
    width, units = up.shape[1], up.shape[0]
    anys = pl.BlockSpec(memory_space=pl.ANY)
    vmem = pl.BlockSpec(memory_space=pltpu.VMEM)
    shape = jax.ShapeDtypeStruct
    dma = lambda *n: pltpu.SemaphoreType.DMA(n)
    return pl.pallas_call(
        forward_body,
        in_specs=[anys] * 6 + [vmem] * 7,
        out_specs=[anys] * 10,
        out_shape=[
            shape((4, TOK, width), bf), shape((4, TOK, width), bf),
            shape((units + 768, width), bf), shape((units + 256, width), bf),
            shape((4, TOK, units + 256), bf), shape((4, TOK, units), bf), shape((4, 3, TOK, 256), bf),
            shape((4, TOK, LANES), f32), shape((4, HALF, width), bf), shape((4, HALF, width), bf),
        ],
        scratch_shapes=[
            pltpu.VMEM((units + 768, width), bf), pltpu.VMEM((units + 256, width), bf),
            pltpu.VMEM((TOK, width), bf), pltpu.VMEM((TOK, width), bf),
            pltpu.VMEM((TOK, units), bf), pltpu.VMEM((TOK, units), bf), pltpu.VMEM((3, TOK, 256), bf),
            pltpu.VMEM((TOK, 256), bf), pltpu.VMEM((TOK, LANES), f32),
            pltpu.VMEM((HALF, width), bf), pltpu.VMEM((HALF, width), bf),
            pltpu.VMEM((4, 128, width), bf), pltpu.VMEM((2, 256, width), f32),
            pltpu.VMEM((TOK, LANES), f32), pltpu.VMEM((TOK, LANES), f32),
            dma(10), dma(2), dma(2), dma(3), dma(3), dma(3), dma(3), dma(3), dma(3), dma(3), dma(3),
            dma(4), dma(4), dma(4), dma(4), dma(6), dma(4), dma(4), dma(3, 2), dma(3, 2),
        ],
        compiler_params=pltpu.CompilerParams(
            vmem_limit_bytes=60 * 1024 * 1024, collective_id=0, has_side_effects=True
        ),
        cost_estimate=cost(8 * TOK * width * (2 * units + 1024), 200e6),
        name="forward",
    )(own_n, g_low, heads, up, down, out, bias, gain, shift, cos4, sin4, ids_col, ids_row)


def entry_body(
    resid, grad, qkv, packed, own_n, g_low, heads, small_all,
    x_in, g_in, q_in, n_out, g_out, q_out,
    load, q_s, q_r, po_s, po_r, sm_s, sm_r, own_sems,
):
    s, f = lax.axis_index("seq"), lax.axis_index("fsdp")
    half = (s % 2 + s // 2) % 2
    width = resid.shape[1]
    parts = [pltpu.make_async_copy(resid.at[pl.ds(128 * j, 128)], x_in.at[j], load.at[j]) for j in range(4)]
    pulls = [pltpu.make_async_copy(grad.at[pl.ds(128 * j, 128)], g_in.at[j], load.at[4 + j]) for j in range(4)]
    rows = [
        pltpu.make_async_copy(
            qkv.at[pl.ds(pl.multiple_of(256 * i + 128 * half, 128), 128)], q_in.at[i], load.at[8 + i]
        )
        for i in range(3)
    ]
    for copy in rows + parts + pulls:
        copy.start()
    near_barrier(s, f)
    keep_small = pltpu.make_async_copy(packed, small_all.at[f], own_sems.at[0])
    keep_small.start()

    def send_small(step):
        to = (f + step) % 8
        return remote(packed, small_all.at[f], sm_s.at[step - 1], sm_r.at[step - 1], s, to)

    for step in range(1, 8):
        send_small(step).start()

    def hop(i):
        head = 3 * f + i
        return remote(q_out.at[i], heads.at[head // 8], q_s.at[i], q_r.at[head // 8], s, head % 8)

    def keep_hop(i):
        return pltpu.make_async_copy(q_out.at[i], heads.at[(3 * f + i) // 8], own_sems.at[1])

    for i in range(3):
        rows[i].wait()
        q_out[i] = q_in[i].astype(bf)
        here = (3 * f + i) % 8 == f
        pl.when(here)(keep_hop(i).start)
        pl.when(jnp.logical_not(here))(hop(i).start)

    out = PlaneOut(n_out, own_n, s, f, po_s, po_r, own_sems.at[2])
    for j in range(4):
        parts[j].wait()

        @pl.loop(0, 4)
        def _(i):
            at = pl.ds(pl.multiple_of(32 * i, 32), 32)
            value = x_in[j, at, :]
            center = value - jnp.sum(value, axis=1, keepdims=True) * (1.0 / width)
            spread = jnp.sum(center * center, axis=1, keepdims=True) * (1.0 / width)
            n_out[j, at, :] = (center * lax.rsqrt(spread + EPS)).astype(bf)

        out.start(j)
    for j in range(4):
        pulls[j].wait()
        g_out[j] = g_in[j].astype(bf)
    keep_g = [
        pltpu.make_async_copy(g_out.at[j], g_low.at[pl.ds(128 * j, 128)], load.at[j]) for j in range(4)
    ]
    for copy in keep_g:
        copy.start()
    keep_small.wait()
    for step in range(1, 8):
        send_small(step).wait_send()
        at = (f + 8 - step) % 8
        remote(packed, small_all.at[at], sm_s.at[step - 1], sm_r.at[step - 1], s, at).wait_recv()
    for kind in range(3):
        frm = (8 * kind + f) // 3
        ref = heads.at[kind]
        away = remote(ref, ref, q_s.at[kind], q_r.at[kind], s, frm)
        pl.when(frm != f)(away.wait_recv)
    for i in range(3):
        here = (3 * f + i) % 8 == f
        pl.when(here)(keep_hop(i).wait)
        pl.when(jnp.logical_not(here))(hop(i).wait_send)
    out.wait()
    for copy in keep_g:
        copy.wait()


def entry_call(resid, grad, qkv, packed):
    width = resid.shape[1]
    anys = pl.BlockSpec(memory_space=pl.ANY)
    vmem = pl.BlockSpec(memory_space=pltpu.VMEM)
    shape = jax.ShapeDtypeStruct
    dma = lambda n: pltpu.SemaphoreType.DMA((n,))
    return pl.pallas_call(
        entry_body,
        in_specs=[anys] * 3 + [vmem],
        out_specs=[anys] * 4,
        out_shape=[
            shape((HALF, width), bf), shape((HALF, width), bf), shape((3, 128, width), bf),
            shape((8,) + packed.shape, f32),
        ],
        scratch_shapes=[
            pltpu.VMEM((4, 128, width), f32), pltpu.VMEM((4, 128, width), f32), pltpu.VMEM((3, 128, width), f32),
            pltpu.VMEM((4, 128, width), bf), pltpu.VMEM((4, 128, width), bf), pltpu.VMEM((3, 128, width), bf),
            dma(11), dma(3), dma(3), dma(4), dma(4), dma(7), dma(7), dma(3),
        ],
        compiler_params=pltpu.CompilerParams(
            vmem_limit_bytes=40 * 1024 * 1024, collective_id=3, has_side_effects=True
        ),
        cost_estimate=cost(1e7, 20e6),
        name="entry",
    )(resid, grad, qkv, packed)


def sum_add(dst, parts):
    @pl.loop(0, HALF // 64)
    def _(i):
        rows = pl.ds(pl.multiple_of(i * 64, 64), 64)
        total = parts[0][rows, :].astype(f32)
        for part in parts[1:]:
            total = total + part[rows, :].astype(f32)
        dst[rows, :] = total.astype(bf)


def line_sum_step(k, z, s, f, own, sib, land, stage, out, loads, sends, recvs):
    for way in range(2):
        d = z - 3 + k if way == 0 else z + 3 - k
        valid = d >= 0 if way == 0 else d <= 3
        to = f - 2 if way == 0 else f + 2
        inner = z < 3 if way == 0 else z > 0
        was = z - 4 + k >= 0 if way == 0 else z + 4 - k <= 3

        @pl.when(valid)
        def _():
            terms = [
                pltpu.make_async_copy(own.at[d], stage.at[0], loads.at[0]),
                pltpu.make_async_copy(sib.at[d], stage.at[1], loads.at[1]),
            ]
            for copy in terms:
                copy.start()
            if k > 0:

                @pl.when(was)
                def _():
                    remote(out.at[way], land.at[way, k - 1], sends.at[way, k - 1], recvs.at[way, k - 1], s, to).wait_send()

                @pl.when(inner)
                def _():
                    remote(out.at[way], land.at[way, k - 1], sends.at[way, k - 1], recvs.at[way, k - 1], s, to).wait_recv()
                    came = pltpu.make_async_copy(land.at[way, k - 1], stage.at[2], loads.at[2])
                    came.start()
                    came.wait()

            for copy in terms:
                copy.wait()
            if k > 0:

                @pl.when(inner)
                def _():
                    sum_add(out.at[way], [stage.at[0], stage.at[1], stage.at[2]])

                @pl.when(jnp.logical_not(inner))
                def _():
                    sum_add(out.at[way], [stage.at[0], stage.at[1]])
            else:
                sum_add(out.at[way], [stage.at[0], stage.at[1]])
            remote(out.at[way], land.at[way, k], sends.at[way, k], recvs.at[way, k], s, to).start()


def line_sum_end(z, s, f, own, sib, land, stage, out, loads, sends, recvs):
    terms = [
        pltpu.make_async_copy(own.at[z], stage.at[0], loads.at[0]),
        pltpu.make_async_copy(sib.at[z], stage.at[1], loads.at[1]),
    ]
    for copy in terms:
        copy.start()
    for copy in terms:
        copy.wait()

    for way in range(2):
        to = f - 2 if way == 0 else f + 2
        sent = z > 0 if way == 0 else z < 3
        got = z < 3 if way == 0 else z > 0

        @pl.when(sent)
        def _():
            remote(out.at[way], land.at[way, 2], sends.at[way, 2], recvs.at[way, 2], s, to).wait_send()

        @pl.when(got)
        def _():
            remote(out.at[way], land.at[way, 2], sends.at[way, 2], recvs.at[way, 2], s, to).wait_recv()
            came = pltpu.make_async_copy(land.at[way, 2], stage.at[2], loads.at[2])
            came.start()
            came.wait()
            sum_add(stage.at[0], [stage.at[0], stage.at[2]])

    sum_add(stage.at[0], [stage.at[0], stage.at[1]])


def backward_body(
    g_part, w_in_h, w_out_h, slope_h, qkv_h, lse_h, p_own, p_sib, gain, cos4, sin4, idc, idr,
    g_all, b_all, own_o, sib_o, branch, land, sums,
    w_in, w_out, x, slope, qkv, lse, gh, gmix, gp, acc_k, acc_v, u_own, u_sib, stage, rs_out, cos, sin,
    load, l0, l1, l2, l3, core_0, core_1, core_u0, core_u1, out_sems, rs_send, rs_recv, pb_send, pb_recv,
):
    s, f = lax.axis_index("seq"), lax.axis_index("fsdp")
    z = f // 2
    line = (l0, l1, l2, l3)
    core = (core_0, core_1)
    own, other = pl.ds(0, HALF), pl.ds(HALF, HALF)
    units = gh.shape[1]
    scale = 256 ** -0.5
    first = [
        pltpu.make_async_copy(w_in_h, w_in, load.at[0]),
        pltpu.make_async_copy(w_out_h, w_out, load.at[1]),
    ]
    for copy in first:
        copy.start()
    near_barrier(s, f)
    swap = lambda b: core_copy(g_all, b, s, f, core)
    new_blocks(0, z, lambda b: swap(b).start())
    line_step(g_all, 1, z, s, f, line)
    new_blocks(1, z, lambda b: swap(b).start())
    reduce_args = (z, s, f, p_own, p_sib, land, stage, rs_out, load.at[pl.ds(8, 3)], rs_send, rs_recv)
    line_sum_step(0, *reduce_args)
    sums[...] = jnp.zeros_like(sums)
    back = PlaneBack(stage.at[0], branch, s, f, pb_send, pb_recv, load.at[7])

    def ins(b):
        return [
            pltpu.make_async_copy(src.at[b], dst, load.at[2 + i])
            for i, (src, dst) in enumerate([(slope_h, slope), (qkv_h, qkv), (lse_h, lse)])
        ]

    def outs(b):
        pairs = [(gh, b_all.at[b, :, pl.ds(0, units)]), (u_own, own_o.at[b])]
        pairs += [(gp.at[i], b_all.at[b, :, pl.ds(units + 256 * i, 256)]) for i in range(3)]
        return [pltpu.make_async_copy(src, dst, out_sems.at[i]) for i, (src, dst) in enumerate(pairs)]

    def send_sib(b):
        return remote(u_sib, sib_o.at[b], core_u0.at[b], core_u1.at[b], s, f + 1 - 2 * (f % 2))

    for t in range(4):
        b = line_order(z, t)
        for copy in ins(b):
            copy.start()
        expand_tables(cos4, sin4, b, cos, sin)
        if t == 3:
            line_arrive(g_all, 2, z, s, f, line)
            new_blocks(3, z, lambda v: swap(v).start())
        top = pltpu.make_async_copy(g_all.at[b, own], x.at[own], load.at[5])
        top.start()
        swap(b).wait_recv()
        low_half = pltpu.make_async_copy(g_all.at[b, other], x.at[other], load.at[6])
        low_half.start()
        if t == 0:
            for copy in first:
                copy.wait()
        else:
            before = line_order(z, t - 1)
            for copy in outs(before):
                copy.wait()
            send_sib(before).wait_send()
        for copy in ins(b):
            copy.wait()
        top.wait()
        low_half.wait()

        @pl.loop(0, units // 256)
        def _(j):
            at = pl.ds(pl.multiple_of(j * 256, 256), 256)
            ga = nt(x[...], w_out[at, :]).astype(bf)
            gh[:, at] = (ga.astype(f32) * slope[:, at].astype(f32)).astype(bf)

        gmix[...] = nt(x[...], w_out[pl.ds(units, 256), :]).astype(bf)
        acc_k[...] = jnp.zeros_like(acc_k)
        acc_v[...] = jnp.zeros_like(acc_v)

        @pl.loop(0, TOK // 256)
        def _(i):
            rows = pl.ds(pl.multiple_of(i * 256, 256), 256)
            q, g = qkv[0, rows, :], gmix[rows, :]
            scores = nt(q, qkv[1]) * scale
            allowed = idr[b] <= idc[b, rows, :]
            probs = jnp.where(allowed, jnp.exp(scores - lse[rows, 0:1]), 0.0)
            grad_probs = nt(g, qkv[2])
            inner = jnp.sum(probs * grad_probs, axis=1, keepdims=True)
            gs = (probs * (grad_probs - inner)).astype(bf)
            gq = (nn(gs, qkv[1]) * scale).astype(bf).astype(f32)
            gq = turn(gq, cos[rows, :], -sin[rows, :])
            sums[0:1, :] += jnp.sum(gq, axis=0, keepdims=True)
            gp[0, rows, :] = gq.astype(bf)
            acc_k[...] += tn(gs, q)
            acc_v[...] += tn(probs.astype(bf), g)

        gk = (acc_k[...] * scale).astype(bf).astype(f32)
        gk = turn(gk, cos[...], -sin[...])
        sums[1:2, :] += jnp.sum(gk, axis=0, keepdims=True)
        gp[1] = gk.astype(bf)
        gv = acc_v[...].astype(bf)
        sums[2:3, :] += jnp.sum(gv.astype(f32), axis=0, keepdims=True)
        gp[2] = gv
        if t == 1:
            line_arrive(g_all, 1, z, s, f, line)
            line_step(g_all, 2, z, s, f, line)
            new_blocks(2, z, lambda v: swap(v).start())
            line_sum_step(1, *reduce_args)
        if t == 2:
            line_sum_step(2, *reduce_args)
        if t == 3:
            line_sum_end(*reduce_args)
            back.start()

        @pl.loop(0, u_own.shape[1] // 256)
        def _(j):
            at = pl.ds(pl.multiple_of(j * 256, 256), 256)
            from_mlp = nn(gh[...], w_in[pl.ds(0, units), at])
            from_attn = nn(gp[0], w_in[pl.ds(units, 256), at])
            for i in range(1, 3):
                from_attn = from_attn + nn(gp[i], w_in[pl.ds(units + 256 * i, 256), at])
            out = from_mlp * gain[0:1, at] + from_attn * gain[1:2, at]
            u_own[:, at] = out[:HALF].astype(bf)
            u_sib[:, at] = out[HALF:].astype(bf)

        for copy in outs(b):
            copy.start()
        send_sib(b).start()

    last = line_order(z, 3)
    for copy in outs(last):
        copy.wait()
    send_sib(last).wait_send()
    for b in range(4):
        swap(b).wait_send()
        send_sib(b).wait_recv()
    for k in (1, 2):
        line_sent(g_all, k, z, s, f, line)
    back.wait()


def backward_call(g_part, w_in, w_out, slope, qkv, lse, p_own, p_sib, gain, cos4, sin4, ids_col, ids_row):
    width = w_in.shape[1]
    units = w_in.shape[0] - 768
    anys = pl.BlockSpec(memory_space=pl.ANY)
    vmem = pl.BlockSpec(memory_space=pltpu.VMEM)
    shape = jax.ShapeDtypeStruct
    dma = lambda *n: pltpu.SemaphoreType.DMA(n)
    return pl.pallas_call(
        backward_body,
        in_specs=[anys] * 8 + [vmem] * 5,
        out_specs=[anys] * 6 + [vmem],
        out_shape=[
            shape((4, TOK, width), bf), shape((4, TOK, units + 768), bf),
            shape((4, HALF, width), bf), shape((4, HALF, width), bf), shape((HALF, width), bf),
            shape((2, 3, HALF, width), bf), shape((8, 256), f32),
        ],
        input_output_aliases={0: 0},
        scratch_shapes=[
            pltpu.VMEM(w_in.shape, bf), pltpu.VMEM(w_out.shape, bf), pltpu.VMEM((TOK, width), bf),
            pltpu.VMEM((TOK, units), bf), pltpu.VMEM((3, TOK, 256), bf), pltpu.VMEM((TOK, LANES), f32),
            pltpu.VMEM((TOK, units), bf), pltpu.VMEM((TOK, 256), bf), pltpu.VMEM((3, TOK, 256), bf),
            pltpu.VMEM((TOK, 256), f32), pltpu.VMEM((TOK, 256), f32),
            pltpu.VMEM((HALF, width), bf), pltpu.VMEM((HALF, width), bf),
            pltpu.VMEM((3, HALF, width), bf), pltpu.VMEM((2, HALF, width), bf),
            pltpu.VMEM((TOK, LANES), f32), pltpu.VMEM((TOK, LANES), f32),
            dma(11), dma(3), dma(3), dma(3), dma(3), dma(4), dma(4), dma(4), dma(4), dma(5),
            dma(2, 3), dma(2, 3), dma(4), dma(4),
        ],
        compiler_params=pltpu.CompilerParams(
            vmem_limit_bytes=62 * 1024 * 1024, collective_id=1, has_side_effects=True
        ),
        cost_estimate=cost(8 * TOK * width * (w_in.shape[0] + w_out.shape[0]), 200e6),
        name="backward",
    )(g_part, w_in, w_out, slope, qkv, lse, p_own, p_sib, gain, cos4, sin4, ids_col, ids_row)


PAIRS = 12


def tail_body(
    a_all, b_all, g_all, n_all, plain, u_own, u_sib, gain, shift, wide_in, more_in,
    fin_up, fin_down, fin_out, fin_qkv, u_o, small_o, land,
    term, r1, r2, hop, stage, rs_out, left, right, acc, acc_s, weight, sides, wide, more, got, small,
    load, w_sem, r1_s, r1_r, r2_s, r2_r, hop_s, hop_r, r3_s, r3_r, r4_s, r4_r,
    rs_load, rs_send, rs_recv, pb_s, pb_r, sm_s, sm_r, sq_s, sq_r, own_sems, self_sem,
):
    s, f = lax.axis_index("seq"), lax.axis_index("fsdp")
    z = f // 2
    x, y = s % 2, s // 2
    across = (s + 1 - 2 * x, (s + 2) % 4)
    reduce_args = (z, s, f, u_own, u_sib, land, stage, rs_out, rs_load, rs_send, rs_recv)
    column = [4, 5, 6, 0, 1, 2, 3, 0, 1, 2, 3, 4]

    def loads(j, k):
        rows_of, right_of = (b_all, n_all) if j < 7 else (a_all, g_all)
        slot = k % 2
        return (
            pltpu.make_async_copy(rows_of.at[k, :, pl.ds(256 * column[j], 256)], left.at[slot], load.at[slot, 0]),
            pltpu.make_async_copy(right_of.at[k], right.at[slot], load.at[slot, 1]),
        )

    def weights(j):
        return pltpu.make_async_copy(plain.at[pl.ds(256 * column[j], 256)], weight, w_sem)

    for copy in loads(0, 0):
        copy.start()
    near_barrier(s, f)
    sides[...] = jnp.zeros_like(sides)
    wide[...] = wide_in[...]
    more[...] = more_in[...]

    def compute(j):
        if j < 7:
            weights(j).start()

        @pl.loop(0, 4)
        def _(k):
            slot = k % 2

            @pl.when(k < 3)
            def _():
                for copy in loads(j, k + 1):
                    copy.start()

            if j + 1 < PAIRS:

                @pl.when(k == 3)
                def _():
                    for copy in loads(j + 1, 0):
                        copy.start()

            for copy in loads(j, k):
                copy.wait()
            part = tn(left[slot], right[slot])

            @pl.when(k == 0)
            def _():
                acc[...] = part

            @pl.when(k > 0)
            def _():
                acc[...] += part

            if j < 7:
                part_s = tn(left[slot], jnp.ones((TOK, LANES), bf))

                @pl.when(k == 0)
                def _():
                    acc_s[...] = part_s

                @pl.when(k > 0)
                def _():
                    acc_s[...] += part_s

        if j < 7:
            which = 1 if j < 3 else 0
            weights(j).wait()
            raw, total = acc[...], acc_s[:, 0:1]
            term[j] = (raw * gain[which : which + 1, :] + total * shift[which : which + 1, :]).astype(bf)
            low_w = weight[...].astype(f32)
            sides[2 * which : 2 * which + 1, :] += jnp.sum(low_w * raw, axis=0, keepdims=True)
            sides[2 * which + 1 : 2 * which + 2, :] += jnp.sum(low_w * total, axis=0, keepdims=True)
            if j >= 3:
                row = jnp.transpose(acc_s[...])
                for half in range(2):
                    at = 2 * (j - 3) + half
                    more[at : at + 1, :] = row[0:1, 128 * half : 128 * half + 128]
        else:
            term[j] = acc[...].astype(bf)

    def rows(start, count):
        return pl.ds(pl.multiple_of(start, 32), count)

    ways = ((0, x, y), (1, y, x))

    def base(p, a, b):
        return 128 * p + 64 * a + 32 * b

    def result(i, start, count):
        if i < 4:
            return fin_up.at[rows(256 * i + start, count)]
        if i < 8:
            return fin_down.at[rows(256 * (i - 4) + start, count)]
        if i < 9:
            return fin_out.at[rows(start, count)]
        return fin_qkv.at[rows(256 * (i - 9) + start, count)]

    def send1(j, p, a):
        return remote(
            term.at[j, rows(128 * p + 64 * (1 - a), 64)], r1.at[j, p], r1_s.at[j, p], r1_r.at[j, p], across[p], f
        )

    def send2(j, p, a, b):
        return remote(
            term.at[j, rows(base(p, a, 1 - b), 32)], r2.at[j, p], r2_s.at[j, p], r2_r.at[j, p], across[1 - p], f
        )

    def keep3(i, p, a, b):
        return pltpu.make_async_copy(
            term.at[i + 3, rows(base(p, a, b), 32)], result(i, base(p, a, b), 32), own_sems.at[i, p]
        )

    def send3(i, p, a, b):
        ref = result(i, base(p, a, b), 32)
        src = term.at[i + 3, rows(base(p, a, b), 32)] if i < 9 else ref
        return remote(src, ref, r3_s.at[i, p], r3_r.at[i, p], across[1 - p], f)

    def send4(i, p, a):
        ref = result(i, 128 * p + 64 * a, 64)
        return remote(ref, ref, r4_s.at[i, p], r4_r.at[i, p], across[p], f)

    def owner(j):
        head = 8 * j + f
        return head // 3, head % 3

    def hop_place(i, p, a, b):
        return fin_qkv.at[rows(256 * i + base(p, a, b), 32)]

    def send_hop(j, p, a, b):
        to, i = owner(j)
        return remote(hop.at[j, p], hop_place(i, p, a, b), hop_s.at[j, p], hop_r.at[i, p], s, to)

    def keep_hop(j, p, a, b):
        return pltpu.make_async_copy(hop.at[j, p], hop_place(owner(j)[1], p, a, b), own_sems.at[9 + j, p])

    def step1(j):
        for p, a, b in ways:
            send1(j, p, a).start()

    def step2(j):
        for p, a, b in ways:
            send1(j, p, a).wait_recv()
            at = rows(128 * p + 64 * a, 64)
            term[j, at, :] = (term[j, at, :].astype(f32) + r1[j, p].astype(f32)).astype(bf)
            send2(j, p, a, b).start()

    def step3(j):
        for p, a, b in ways:
            send2(j, p, a, b).wait_recv()
            at = rows(base(p, a, b), 32)
            total = (term[j, at, :].astype(f32) + r2[j, p].astype(f32)).astype(bf)
            if j >= 3:
                term[j, at, :] = total
                send3(j - 3, p, a, b).start()
                keep3(j - 3, p, a, b).start()
            else:
                hop[j, p] = total
                here = owner(j)[0] == f
                pl.when(here)(keep_hop(j, p, a, b).start)
                pl.when(jnp.logical_not(here))(send_hop(j, p, a, b).start)

    def step3_own(i):
        head, kind = (3 * f + i) % 8, (3 * f + i) // 8
        for p, a, b in ways:
            ref = hop_place(i, p, a, b)
            coming = remote(ref, ref, hop_s.at[i, p], hop_r.at[i, p], s, head)
            staying = pltpu.make_async_copy(ref, ref, own_sems.at[9 + kind, p])
            pl.when(head != f)(coming.wait_recv)
            pl.when(head == f)(staying.wait)
            send3(9 + i, p, a, b).start()

    def step4(i):
        for p, a, b in ways:
            send3(i, p, a, b).wait_recv()
            if i < 9:
                keep3(i, p, a, b).wait()
            send4(i, p, a).start()

    def small_send(step):
        to = (f + step) % 8
        return remote(wide.at[to], got.at[step - 1], sm_s.at[step - 1], sm_r.at[step - 1], s, to)

    def small_one():
        for to in range(8):
            for v in range(4):
                for half in range(2):
                    at = 256 * to + 128 * half
                    wide[to, 2 * v + half : 2 * v + half + 1, :] = sides[v : v + 1, at : at + 128]
        for step in range(1, 8):
            small_send(step).start()

    def small_two():
        total = wide[f]
        for step in range(1, 8):
            small_send(step).wait_recv()
            total = total + got[step - 1]
        small[0, 0:16] = total
        small[0, 16:32] = more[...]
        small_seq(0).start()

    def small_seq(way):
        return remote(small.at[2 * way], small.at[2 * way + 1], sq_s.at[way], sq_r.at[way], across[way], f)

    def small_three():
        small_seq(0).wait_recv()
        small[2] = small[0] + small[1]
        small_seq(1).start()

    def small_four():
        small_seq(1).wait_recv()
        small_o[...] = small[2] + small[3]

    back = PlaneBack(stage.at[0], u_o, s, f, pb_s, pb_r, self_sem)
    compute(0)
    step1(0)
    line_sum_step(0, *reduce_args)
    compute(1)
    step1(1)
    for it in range(1, 16):
        if it + 1 < PAIRS:
            compute(it + 1)
            step1(it + 1)
        if it - 1 < PAIRS:
            step2(it - 1)
        if 0 <= it - 2 < PAIRS:
            step3(it - 2)
        if 5 <= it < 8:
            step3_own(it - 5)
        if 0 <= it - 6 < 9:
            step4(it - 6)
        if 6 <= it < 9:
            step4(9 + it - 6)
        if it == 4:
            line_sum_step(1, *reduce_args)
        if it == 7:
            line_sum_step(2, *reduce_args)
        if it == 8:
            small_one()
        if it == 10:
            small_two()
        if it == 11:
            line_sum_end(*reduce_args)
            back.start()
        if it == 12:
            small_three()
        if it == 14:
            small_four()

    back.wait()
    for j in range(PAIRS):
        for p, a, b in ways:
            send4(j, p, a).wait_recv()
            send1(j, p, a).wait_send()
            send2(j, p, a, b).wait_send()
            send3(j, p, a, b).wait_send()
            send4(j, p, a).wait_send()
            if j < 3:
                pl.when(owner(j)[0] != f)(send_hop(j, p, a, b).wait_send)

    for step in range(1, 8):
        small_send(step).wait_send()
    for way in range(2):
        small_seq(way).wait_send()


def tail_call(a_all, b_all, g_all, n_all, plain, u_own, u_sib, gain, shift, wide, more):
    width = plain.shape[1]
    anys = pl.BlockSpec(memory_space=pl.ANY)
    vmem = pl.BlockSpec(memory_space=pltpu.VMEM)
    shape = jax.ShapeDtypeStruct
    dma = lambda *n: pltpu.SemaphoreType.DMA(n)
    two = [dma(PAIRS, 2)] * 2
    return pl.pallas_call(
        tail_body,
        in_specs=[anys] * 7 + [vmem] * 4,
        out_specs=[anys] * 5 + [vmem, anys],
        out_shape=[
            shape((1024, width), bf), shape((1024, width), bf), shape((256, width), bf), shape((768, width), bf),
            shape((HALF, width), bf), shape((32, LANES), f32), shape((2, 3, HALF, width), bf),
        ],
        scratch_shapes=[
            pltpu.VMEM((PAIRS, 256, width), bf), pltpu.VMEM((PAIRS, 2, 64, width), bf),
            pltpu.VMEM((PAIRS, 2, 32, width), bf), pltpu.VMEM((3, 2, 32, width), bf),
            pltpu.VMEM((3, HALF, width), bf), pltpu.VMEM((2, HALF, width), bf),
            pltpu.VMEM((2, TOK, 256), bf), pltpu.VMEM((2, TOK, width), bf),
            pltpu.VMEM((256, width), f32), pltpu.VMEM((256, LANES), f32), pltpu.VMEM((256, width), bf),
            pltpu.VMEM((8, width), f32), pltpu.VMEM((8, 16, LANES), f32), pltpu.VMEM((16, LANES), f32),
            pltpu.VMEM((7, 16, LANES), f32), pltpu.VMEM((4, 32, LANES), f32),
            dma(2, 2), pltpu.SemaphoreType.DMA, *two, *two, dma(3, 2), dma(3, 2), *two, *two,
            dma(3), dma(2, 3), dma(2, 3), dma(4), dma(4), dma(7), dma(7), dma(2), dma(2), dma(PAIRS, 2),
            pltpu.SemaphoreType.DMA,
        ],
        compiler_params=pltpu.CompilerParams(
            vmem_limit_bytes=61 * 1024 * 1024, collective_id=2, has_side_effects=True
        ),
        cost_estimate=cost(1e11, 600e6),
        name="tail",
    )(a_all, b_all, g_all, n_all, plain, u_own, u_sib, gain, shift, wide, more)


def pick(slices, which):
    return lax.dynamic_index_in_dim(slices, which, 0, keepdims=False)


def split_body(
    resid_in,
    qkv_weight,
    qkv_bias,
    out_weight,
    out_bias,
    up_weight,
    up_bias,
    down_weight,
    down_bias,
    attn_gain,
    attn_shift,
    mlp_gain,
    mlp_shift,
    block_ids,
    offsets,
    grad_out,
):
    low = jnp.bfloat16
    f32 = jnp.float32
    groups, piece, width = resid_in.shape
    tokens = groups * piece
    s = lax.axis_index("seq")
    f = lax.axis_index("fsdp")
    z, c = f // 2, f % 2
    units = up_weight.shape[0]

    length = block_ids.shape[1]
    own_small = [attn_gain, attn_shift, mlp_gain, mlp_shift, out_bias + down_bias, qkv_bias]
    packed = jnp.concatenate(
        own_small + [block_ids.reshape(-1).astype(f32), offsets.reshape(-1).astype(f32)]
    )
    packed = jnp.pad(packed, (0, 40 * LANES - packed.shape[0])).reshape(40, LANES)
    flat = resid_in.reshape(tokens, width)
    grad_flat = grad_out.reshape(tokens, width)
    own_n, g_low, head_half, small = entry_call(flat, grad_flat, qkv_weight, packed)
    small = small.reshape(8, 40 * LANES)
    gain_a, shift_a, gain_m, shift_m, bias_out = (
        small[:, i * 256 : (i + 1) * 256].reshape(width) for i in range(5)
    )
    head_bias = small[:, 1280:2048].reshape(3, HEADS, HEAD_DIM)
    head_bias = lax.dynamic_index_in_dim(head_bias, f, 1, keepdims=False).reshape(3 * HEAD_DIM)
    ids_end = 2048 + groups * length
    ids_all = small[:, 2048:ids_end].astype(jnp.int32).reshape(-1, 8, LANES)
    starts_all = small[:, ids_end : ids_end + groups * offsets.shape[1]].astype(jnp.int32)
    starts_all = starts_all.reshape(-1, offsets.shape[1])
    gain = jnp.stack([gain_m, gain_a])
    shift = jnp.stack([shift_m, shift_a])
    bias_in = jnp.concatenate([up_bias, head_bias])[None]

    halves = [(2 * (s % 2) + c, c), (2 * (s % 2) + 1 - c, 1 - c)]
    rows_at = [((part - k + 4) % 4) * 2 + core for part, core in halves for k in range(4)]
    ids_slots = [pick(ids_all, block * 4 + s) for block in range(4)]
    ids_here = jnp.stack(
        [jnp.concatenate([pick(row, at) for at in rows_at]) for row in ids_slots]
    ).reshape(4, 1024)
    starts_here = jnp.stack([pick(starts_all, block * 4 + s) for block in range(4)])
    pos = (jnp.stack(rows_at)[:, None] * LANES + jnp.arange(LANES)[None, :]).reshape(1024)
    positions = block_offset(ids_here, starts_here) + pos[None, :]
    lane = jnp.arange(LANES)
    inverse = jnp.exp((lane % 32).astype(f32) * (-2.0 * math.log(10000.0) / ROT_DIM))
    grouped = positions.astype(f32).reshape(4, 4, 256, 1)
    spot = sum(jnp.where(lane // 32 == q, grouped[:, q], 0.0) for q in range(4))
    angles = spot * inverse
    cosine, sine = jnp.cos(angles), jnp.sin(angles)
    ids_col, ids_row = ids_here[:, :, None], ids_here[:, None, :]

    n_all, g_part, w_in, w_out, a_all, slope_all, qkv_all, lse_all, p_own, p_sib = forward_call(
        own_n, g_low, head_half, up_weight, down_weight, out_weight, bias_in, gain, shift,
        cosine, sine, ids_col, ids_row,
    )
    g_all, b_all, u_own, u_sib, branch, _, col_sums = backward_call(
        g_part, w_in, w_out, slope_all, qkv_all, lse_all, p_own, p_sib, gain, cosine, sine, ids_col, ids_row
    )
    result = flat + branch.astype(f32) + bias_out

    slots = jnp.zeros((16, HEAD_DIM), f32)
    slots = lax.dynamic_update_slice(slots, col_sums[0:1], (f, 0))
    slots = lax.dynamic_update_slice(slots, col_sums[1:2], (8 + f, 0))
    spread = jnp.concatenate([jnp.zeros((4, width), f32), jnp.sum(grad_flat, axis=0)[None]])
    wide = jnp.concatenate(
        [spread.reshape(5, 8, 256).transpose(1, 0, 2).reshape(8, 5 * 256), slots.reshape(8, 512)], axis=1
    )
    wide = jnp.pad(wide, ((0, 0), (0, 256))).reshape(8, 16, LANES)
    more = jnp.pad(jnp.concatenate([jnp.zeros((units,), f32), col_sums[2]]), (0, 768)).reshape(16, LANES)
    up_low, down_low, out_low, qkv_low, u, small_sum, _ = tail_call(
        a_all, b_all, g_all, n_all, w_in, u_own, u_sib, gain, shift, wide, more
    )
    u = u.astype(f32)
    center = flat - jnp.mean(flat, axis=-1, keepdims=True)
    inv = lax.rsqrt(jnp.mean(center * center, axis=-1, keepdims=True) + EPS)
    normal = center * inv
    grad_input = grad_flat + inv * (
        u - jnp.mean(u, axis=-1, keepdims=True) - normal * jnp.mean(u * normal, axis=-1, keepdims=True)
    )
    mine = small_sum.reshape(-1)
    vectors = [mine[i * 256 : (i + 1) * 256] for i in range(5)]
    qk_grad = mine[1280:1792]
    up_bias_grad = mine[2048 : 2048 + units]
    value_grad = mine[2048 + units : 2304 + units]
    return (
        result.reshape(groups, piece, width),
        grad_input.reshape(groups, piece, width),
        qkv_low.astype(f32),
        qk_grad,
        value_grad,
        out_low.astype(f32),
        vectors[4],
        up_low.astype(f32),
        up_bias_grad,
        down_low.astype(f32),
        vectors[4],
        vectors[2],
        vectors[3],
        vectors[0],
        vectors[1],
    )


def solution(mesh):
    placed = (
        P("fsdp", "seq", None),
        P("fsdp", None),
        P("fsdp"),
        P("fsdp", None),
        P("fsdp"),
        P("fsdp", None),
        P("fsdp"),
        P("fsdp", None),
        P("fsdp"),
        P("fsdp"),
        P("fsdp"),
        P("fsdp"),
        P("fsdp"),
        P("fsdp", None),
        P("fsdp", None),
        P("fsdp", "seq", None),
    )
    return jax.shard_map(
        split_body if mesh.shape["fsdp"] == HEADS and mesh.shape["seq"] == 4 else body,
        mesh=mesh,
        in_specs=placed,
        out_specs=(
            P("fsdp", "seq", None),
            P("fsdp", "seq", None),
            P("fsdp", None),
            P("fsdp"),
            P("fsdp"),
            P("fsdp", None),
            P("fsdp"),
            P("fsdp", None),
            P("fsdp"),
            P("fsdp", None),
            P("fsdp"),
            P("fsdp"),
            P("fsdp"),
            P("fsdp"),
            P("fsdp"),
        ),
        check_vma=False,
    )
```

```python
import functools
import math

import jax
import jax.numpy as jnp
from jax import lax
from jax.experimental import pallas as pl
from jax.experimental.pallas import tpu as pltpu
from jax.sharding import PartitionSpec as P

HEADS = 8
HEAD_DIM = 256
ROT_DIM = 64


EPS = 1e-05
NEG_FILL = -1e30


def layer_norm(values, gain, shift):
    center = values - jnp.mean(values, axis=-1, keepdims=True)
    spread = jnp.mean(center * center, axis=-1, keepdims=True)
    return center * lax.rsqrt(spread + EPS) * gain + shift


def rotary_tables(positions):
    half = ROT_DIM // 2
    inverse = jnp.exp(jnp.arange(half, dtype=jnp.float32) * (-2.0 * math.log(10000.0) / ROT_DIM))
    angles = positions.astype(jnp.float32)[..., None] * inverse
    return (jnp.cos(angles), jnp.sin(angles))


def block_offset(ids, starts):
    numbers = jnp.arange(starts.shape[1], dtype=jnp.int32)
    match = (ids[:, :, None] == numbers[None, None, :]).astype(jnp.int32)
    return jnp.sum(match * starts[:, None, :], axis=-1)


def rotate(values, cosine, sine):
    half = ROT_DIM // 2
    cosine = cosine[..., None, :]
    sine = sine[..., None, :]
    first = values[..., :half]
    second = values[..., half:ROT_DIM]
    return jnp.concatenate(
        [first * cosine - second * sine, second * cosine + first * sine, values[..., ROT_DIM:]],
        axis=-1,
    )


def gelu_exact(values):
    return jax.nn.gelu(values, approximate=False)


def contract_lead(left, right):
    return lax.dot_general(
        left, right, (((0,), (0,)), ((), ())), preferred_element_type=jnp.float32
    )


def contract_last(left, right):
    return lax.dot_general(
        left, right, (((1,), (1,)), ((), ())), preferred_element_type=jnp.float32
    )


def attend_forward(items):
    query, keys, values, ids = items
    allowed = ids[None, :] <= ids[:, None]
    scores = jnp.where(allowed, contract_last(query, keys) * HEAD_DIM ** (-0.5), NEG_FILL)
    top = jnp.max(scores, axis=1, keepdims=True)
    weights = jnp.exp(scores - top)
    total = jnp.sum(weights, axis=1, keepdims=True)
    probs = (weights / total).astype(jnp.bfloat16)
    mixed = jnp.dot(probs, values, preferred_element_type=jnp.float32).astype(jnp.bfloat16)
    return (mixed, (top + jnp.log(total))[:, 0])


def attend_backward(items):
    query, keys, values, ids, lse_row, grad_mix = items
    scale = HEAD_DIM ** (-0.5)
    allowed = ids[None, :] <= ids[:, None]
    scores = contract_last(query, keys) * scale
    probs = jnp.where(allowed, jnp.exp(scores - lse_row[:, None]), 0.0)
    grad_probs = contract_last(grad_mix, values)
    inner = jnp.sum(probs * grad_probs, axis=1, keepdims=True)
    grad_scores = (probs * (grad_probs - inner)).astype(jnp.bfloat16)
    grad_query = (jnp.dot(grad_scores, keys, preferred_element_type=jnp.float32) * scale).astype(
        jnp.bfloat16
    )
    grad_keys = (contract_lead(grad_scores, query) * scale).astype(jnp.bfloat16)
    grad_values = contract_lead(probs.astype(jnp.bfloat16), grad_mix).astype(jnp.bfloat16)
    return (grad_query, grad_keys, grad_values)


def body(
    resid_in,
    qkv_weight,
    qkv_bias,
    out_weight,
    out_bias,
    up_weight,
    up_bias,
    down_weight,
    down_bias,
    attn_gain,
    attn_shift,
    mlp_gain,
    mlp_shift,
    block_ids,
    offsets,
    grad_out,
):
    groups, piece, width = resid_in.shape
    tokens = groups * piece
    pieces = lax.axis_size("seq")
    length = piece * pieces
    rank = lax.axis_index("fsdp")
    heads_here = HEADS // pieces
    pairs = groups * heads_here
    flat = resid_in.reshape(tokens, width)
    gain_a, shift_a, gain_m, shift_m, proj_bias, attn_bias, hidden_bias, mlp_bias = (
        lax.all_gather(attn_gain, "fsdp", axis=0, tiled=True),
        lax.all_gather(attn_shift, "fsdp", axis=0, tiled=True),
        lax.all_gather(mlp_gain, "fsdp", axis=0, tiled=True),
        lax.all_gather(mlp_shift, "fsdp", axis=0, tiled=True),
        lax.all_gather(qkv_bias, "fsdp", axis=0, tiled=True),
        lax.all_gather(out_bias, "fsdp", axis=0, tiled=True),
        lax.all_gather(up_bias, "fsdp", axis=0, tiled=True),
        lax.all_gather(down_bias, "fsdp", axis=0, tiled=True),
    )
    qkv_low = qkv_weight.astype(jnp.bfloat16)
    out_low = out_weight.astype(jnp.bfloat16)
    up_low = up_weight.astype(jnp.bfloat16)
    down_low = down_weight.astype(jnp.bfloat16)
    qkv_full, out_full = (
        lax.all_gather(qkv_low, "fsdp", axis=0, tiled=True),
        lax.all_gather(out_low, "fsdp", axis=0, tiled=True),
    )
    normed_a32, norm_back_a = jax.vjp(layer_norm, flat, gain_a, shift_a)
    normed_m32, norm_back_m = jax.vjp(layer_norm, flat, gain_m, shift_m)
    normed_attn = normed_a32.astype(jnp.bfloat16)
    normed_mlp = normed_m32.astype(jnp.bfloat16)
    projected = (contract_last(normed_attn, qkv_full) + proj_bias).reshape(
        groups, piece, 3, HEADS, HEAD_DIM
    )
    first_pos = lax.axis_index("seq") * piece
    ids_piece = lax.dynamic_slice_in_dim(block_ids, first_pos, piece, 1)
    positions = (
        block_offset(ids_piece, offsets) + first_pos + jnp.arange(piece, dtype=jnp.int32)[None, :]
    )
    cosine, sine = rotary_tables(positions)
    query = rotate(projected[:, :, 0], cosine, sine)
    keys = rotate(projected[:, :, 1], cosine, sine)
    packed = jnp.stack([query, keys, projected[:, :, 2]], axis=2).astype(jnp.bfloat16)
    heads = lax.all_to_all(packed, "seq", split_axis=3, concat_axis=1, tiled=True)
    stacked = heads.transpose(2, 0, 3, 1, 4).reshape(3, pairs, length, HEAD_DIM)
    ids_pairs = jnp.repeat(block_ids, heads_here, axis=0)
    mixed_pairs, lse_pairs = lax.map(
        attend_forward, (stacked[0], stacked[1], stacked[2], ids_pairs)
    )
    back_heads = mixed_pairs.reshape(groups, heads_here, length, HEAD_DIM).transpose(0, 2, 1, 3)
    mixed_tok = lax.all_to_all(back_heads, "seq", split_axis=1, concat_axis=2, tiled=True).reshape(
        tokens, width
    )
    attn_part = jnp.dot(mixed_tok, out_full, preferred_element_type=jnp.float32) + attn_bias
    units_here = up_weight.shape[0]
    group_rows = lax.all_gather(normed_mlp, "fsdp", axis=0, tiled=True)
    local_bias = lax.dynamic_slice_in_dim(hidden_bias, rank * units_here, units_here)
    hidden = contract_last(group_rows, up_low) + local_bias
    active, gelu_back = jax.vjp(gelu_exact, hidden)
    active_low = active.astype(jnp.bfloat16)
    branch = (
        lax.psum_scatter(
            jnp.dot(active_low, down_low, preferred_element_type=jnp.float32).astype(jnp.bfloat16),
            "fsdp",
            scatter_dimension=0,
            tiled=True,
        ).astype(jnp.float32)
        + mlp_bias
    )
    result = flat + attn_part + branch
    grad_flat = grad_out.reshape(tokens, width)
    grad_low = grad_flat.astype(jnp.bfloat16)
    bias_sum = jnp.sum(grad_flat, axis=0)
    group_grad = lax.all_gather(grad_low, "fsdp", axis=0, tiled=True)
    grad_active = contract_last(group_grad, down_low).astype(jnp.bfloat16)
    grad_hidden = gelu_back(grad_active.astype(jnp.float32))[0]
    grad_hidden_low = grad_hidden.astype(jnp.bfloat16)
    grad_normed_m = lax.psum_scatter(
        jnp.dot(grad_hidden_low, up_low, preferred_element_type=jnp.float32),
        "fsdp",
        scatter_dimension=0,
        tiled=True,
    )
    up_grad_shard = contract_lead(grad_hidden_low, group_rows)
    down_grad_shard = contract_lead(active_low, group_grad)
    local_sum = jnp.sum(grad_hidden, axis=0)
    up_bias_term = lax.dynamic_update_slice_in_dim(
        jnp.zeros((hidden_bias.shape[0],), jnp.float32), local_sum, rank * units_here, 0
    )
    grad_mixed = contract_last(grad_low, out_full).astype(jnp.bfloat16)
    grad_heads = lax.all_to_all(
        grad_mixed.reshape(groups, piece, HEADS, HEAD_DIM),
        "seq",
        split_axis=2,
        concat_axis=1,
        tiled=True,
    )
    grad_pairs = grad_heads.transpose(0, 2, 1, 3).reshape(pairs, length, HEAD_DIM)
    grad_query, grad_keys, grad_values = lax.map(
        attend_backward, (stacked[0], stacked[1], stacked[2], ids_pairs, lse_pairs, grad_pairs)
    )
    grads_stack = (
        jnp.stack([grad_query, grad_keys, grad_values], axis=0)
        .reshape(3, groups, heads_here, length, HEAD_DIM)
        .transpose(1, 3, 0, 2, 4)
    )
    returned = lax.all_to_all(grads_stack, "seq", split_axis=1, concat_axis=3, tiled=True).astype(
        jnp.float32
    )
    grad_projected = jnp.stack(
        [
            rotate(returned[:, :, 0], cosine, -sine),
            rotate(returned[:, :, 1], cosine, -sine),
            returned[:, :, 2],
        ],
        axis=2,
    ).reshape(tokens, 3 * width)
    grad_projected_low = grad_projected.astype(jnp.bfloat16)
    proj_bias_term = jnp.sum(grad_projected, axis=0)
    qk_bias_term = proj_bias_term[: 2 * width]
    value_bias_term = proj_bias_term[2 * width :]
    grad_normed_a = jnp.dot(grad_projected_low, qkv_full, preferred_element_type=jnp.float32)
    grad_from_a, gain_a_term, shift_a_term = norm_back_a(grad_normed_a)
    grad_from_m, gain_m_term, shift_m_term = norm_back_m(grad_normed_m)
    grad_input = grad_flat + grad_from_a + grad_from_m
    qkv_term = contract_lead(grad_projected_low, normed_attn)
    out_term = contract_lead(mixed_tok, grad_low)
    (
        qkv_shard,
        out_shard,
        qk_bias_shard,
        value_bias_shard,
        bias_shard,
        up_bias_shard,
        gain_a_shard,
        shift_a_shard,
        gain_m_shard,
        shift_m_shard,
    ) = (
        lax.psum_scatter(qkv_term, "fsdp", scatter_dimension=0, tiled=True),
        lax.psum_scatter(out_term, "fsdp", scatter_dimension=0, tiled=True),
        lax.psum_scatter(qk_bias_term, "fsdp", scatter_dimension=0, tiled=True),
        lax.psum_scatter(value_bias_term, "fsdp", scatter_dimension=0, tiled=True),
        lax.psum_scatter(bias_sum, "fsdp", scatter_dimension=0, tiled=True),
        lax.psum_scatter(up_bias_term, "fsdp", scatter_dimension=0, tiled=True),
        lax.psum_scatter(gain_a_term, "fsdp", scatter_dimension=0, tiled=True),
        lax.psum_scatter(shift_a_term, "fsdp", scatter_dimension=0, tiled=True),
        lax.psum_scatter(gain_m_term, "fsdp", scatter_dimension=0, tiled=True),
        lax.psum_scatter(shift_m_term, "fsdp", scatter_dimension=0, tiled=True),
    )
    totals = lax.psum(
        (
            qkv_shard,
            out_shard,
            up_grad_shard,
            down_grad_shard,
            qk_bias_shard,
            value_bias_shard,
            bias_shard,
            up_bias_shard,
            gain_a_shard,
            shift_a_shard,
            gain_m_shard,
            shift_m_shard,
        ),
        "seq",
    )
    return (
        result.reshape(groups, piece, width),
        grad_input.reshape(groups, piece, width),
        totals[0],
        totals[4],
        totals[5],
        totals[1],
        totals[6],
        totals[2],
        totals[7],
        totals[3],
        totals[6],
        totals[8],
        totals[9],
        totals[10],
        totals[11],
    )


bf, f32 = jnp.bfloat16, jnp.float32
TOK, HALF = 1024, 512
VM = 56 * 1024 * 1024


def nt(a, b):
    return lax.dot_general(a, b, (((1,), (1,)), ((), ())), preferred_element_type=f32)


def nn(a, b):
    return lax.dot_general(a, b, (((1,), (0,)), ((), ())), preferred_element_type=f32)


def tn(a, b):
    return lax.dot_general(a, b, (((0,), (0,)), ((), ())), preferred_element_type=f32)


def params(n=1, limit=VM):
    return pltpu.CompilerParams(dimension_semantics=("arbitrary",) * n, vmem_limit_bytes=limit)


def cost(flops, nbytes):
    return pl.CostEstimate(flops=int(flops), bytes_accessed=int(nbytes), transcendentals=0)


def turn(head, c, s):
    first = head[:, :128]
    lane = lax.broadcasted_iota(jnp.int32, first.shape, 1)
    partner = jnp.where(lane < 32, pltpu.roll(first, 96, 1), pltpu.roll(first, 32, 1))
    return jnp.concatenate([first * c + partner * s, head[:, 128:]], axis=1)


def gelu_pair(h):
    cdf = 0.5 * (1.0 + lax.erf(h * (0.5**0.5)))
    pdf = jnp.exp(-0.5 * (h * h)) * (1.0 / math.sqrt(2.0 * math.pi))
    return (h * cdf).astype(bf), (cdf + h * pdf).astype(bf)


def h_body(units_tiles, n0, n1, w, b, c, s, act, slope, qkv, x):
    j = pl.program_id(0)

    @pl.when(j == 0)
    def _():
        x[:HALF] = n0[...]
        x[HALF:] = n1[...]

    @pl.when(j < units_tiles)
    def _():
        act[...], slope[...] = gelu_pair(nt(x[...], w[...]) + b[...])

    @pl.when((j >= units_tiles) & (j < units_tiles + 2))
    def _():
        qkv[0] = turn(nt(x[...], w[...]) + b[...], c[0], s[0]).astype(bf)

    @pl.when(j == units_tiles + 2)
    def _():
        qkv[0] = (nt(x[...], w[...]) + b[...]).astype(bf)


def h_call(n0, n1, w, b, c, s, t):
    width = n0.shape[1]
    rows = w.shape[0]
    tile = 256
    units_tiles = (rows - 768) // tile
    full = lambda *shape: pl.BlockSpec(shape, lambda j: (0,) * len(shape))
    return pl.pallas_call(
        functools.partial(h_body, units_tiles),
        grid=(rows // tile,),
        in_specs=[
            full(HALF, width), full(HALF, width),
            pl.BlockSpec((tile, width), lambda j: (j, 0)),
            pl.BlockSpec((1, tile), lambda j: (0, j)),
            pl.BlockSpec((1, TOK, 128), lambda j: (t, 0, 0)), pl.BlockSpec((1, TOK, 128), lambda j: (t, 0, 0)),
        ],
        out_specs=[
            pl.BlockSpec((TOK, tile), lambda j: (0, jnp.minimum(j, units_tiles - 1))),
            pl.BlockSpec((TOK, tile), lambda j: (0, jnp.minimum(j, units_tiles - 1))),
            pl.BlockSpec((1, TOK, tile), lambda j: (jnp.maximum(j - units_tiles, 0), 0, 0)),
        ],
        out_shape=[
            jax.ShapeDtypeStruct((TOK, rows - 768), bf),
            jax.ShapeDtypeStruct((TOK, rows - 768), bf),
            jax.ShapeDtypeStruct((3, TOK, 256), bf),
        ],
        scratch_shapes=[pltpu.VMEM((TOK, width), bf)],
        compiler_params=params(),
        cost_estimate=cost(2 * TOK * width * rows, 24e6),
        name="project",
    )(n0, n1, w, b, c, s)


def attn_body(q, k, v, idq, idk, mixed, lse):
    scores = nt(q[0], k[0]) * (256 ** -0.5)
    allowed = idk[0] <= idq[0]
    scores = jnp.where(allowed, scores, -1e30)
    top = jnp.max(scores, axis=1, keepdims=True)
    weights = jnp.exp(scores - top)
    total = jnp.sum(weights, axis=1, keepdims=True)
    probs = (weights / total).astype(bf)
    mixed[...] = nn(probs, v[0]).astype(bf)
    lse[...] = top + jnp.log(total)


def attn_call(qkv, ids_col, ids_row, t):
    tile = 256
    return pl.pallas_call(
        attn_body,
        grid=(TOK // tile,),
        in_specs=[
            pl.BlockSpec((1, tile, 256), lambda i: (0, i, 0)),
            pl.BlockSpec((1, TOK, 256), lambda i: (1, 0, 0)),
            pl.BlockSpec((1, TOK, 256), lambda i: (2, 0, 0)),
            pl.BlockSpec((1, tile, 1), lambda i: (t, i, 0)),
            pl.BlockSpec((1, 1, TOK), lambda i: (t, 0, 0)),
        ],
        out_specs=[
            pl.BlockSpec((tile, 256), lambda i: (i, 0)),
            pl.BlockSpec((tile, 1), lambda i: (i, 0)),
        ],
        out_shape=[jax.ShapeDtypeStruct((TOK, 256), bf), jax.ShapeDtypeStruct((TOK, 1), f32)],
        compiler_params=params(),
        cost_estimate=cost(4 * TOK * TOK * 256, 4e6),
        name="attend",
    )(qkv, qkv, qkv, ids_col, ids_row)


def attn_back_body(q, k, v, g, idq, idk, lse, cq, sq, ck, sk, out_q, out_kv, sums, acc_k, acc_v, acc_s):
    i = pl.program_id(0)
    last = pl.num_programs(0) - 1
    scale = 256 ** -0.5

    @pl.when(i == 0)
    def _():
        acc_k[...] = jnp.zeros_like(acc_k)
        acc_v[...] = jnp.zeros_like(acc_v)
        acc_s[...] = jnp.zeros_like(acc_s)

    scores = nt(q[0], k[0]) * scale
    allowed = idk[0] <= idq[0]
    probs = jnp.where(allowed, jnp.exp(scores - lse[...]), 0.0)
    grad_probs = nt(g[...], v[0])
    inner = jnp.sum(probs * grad_probs, axis=1, keepdims=True)
    gs = (probs * (grad_probs - inner)).astype(bf)
    gq = (nn(gs, k[0]) * scale).astype(bf).astype(f32)
    gq = turn(gq, cq[0], -sq[0])
    acc_s[0:1, :] += jnp.sum(gq, axis=0, keepdims=True)
    out_q[0] = gq.astype(bf)
    acc_k[...] += tn(gs, q[0])
    acc_v[...] += tn(probs.astype(bf), g[...])

    @pl.when(i == last)
    def _():
        gk = (acc_k[...] * scale).astype(bf).astype(f32)
        gk = turn(gk, ck[0], -sk[0])
        out_kv[0] = gk.astype(bf)
        gv = acc_v[...].astype(bf)
        out_kv[1] = gv
        acc_s[1:2, :] = jnp.sum(gk, axis=0, keepdims=True)
        acc_s[2:3, :] = jnp.sum(gv.astype(f32), axis=0, keepdims=True)
        sums[...] = acc_s[...]


def attn_back_call(qkv, gmix, ids_col, ids_row, lse, c, s, t):
    tile = 256
    return pl.pallas_call(
        attn_back_body,
        grid=(TOK // tile,),
        in_specs=[
            pl.BlockSpec((1, tile, 256), lambda i: (0, i, 0)),
            pl.BlockSpec((1, TOK, 256), lambda i: (1, 0, 0)),
            pl.BlockSpec((1, TOK, 256), lambda i: (2, 0, 0)),
            pl.BlockSpec((tile, 256), lambda i: (i, 0)),
            pl.BlockSpec((1, tile, 1), lambda i: (t, i, 0)),
            pl.BlockSpec((1, 1, TOK), lambda i: (t, 0, 0)),
            pl.BlockSpec((tile, 1), lambda i: (i, 0)),
            pl.BlockSpec((1, tile, 128), lambda i: (t, i, 0)),
            pl.BlockSpec((1, tile, 128), lambda i: (t, i, 0)),
            pl.BlockSpec((1, TOK, 128), lambda i: (t, 0, 0)),
            pl.BlockSpec((1, TOK, 128), lambda i: (t, 0, 0)),
        ],
        out_specs=[
            pl.BlockSpec((1, tile, 256), lambda i: (0, i, 0)),
            pl.BlockSpec((2, TOK, 256), lambda i: (0, 0, 0)),
            pl.BlockSpec((8, 256), lambda i: (0, 0)),
        ],
        out_shape=[
            jax.ShapeDtypeStruct((1, TOK, 256), bf),
            jax.ShapeDtypeStruct((2, TOK, 256), bf),
            jax.ShapeDtypeStruct((8, 256), f32),
        ],
        scratch_shapes=[pltpu.VMEM((TOK, 256), f32), pltpu.VMEM((TOK, 256), f32), pltpu.VMEM((8, 256), f32)],
        compiler_params=params(),
        cost_estimate=cost(10 * TOK * TOK * 256, 6e6),
        name="attend_back",
    )(qkv, qkv, qkv, gmix, ids_col, ids_row, lse, c, s, c, s)


def p_body(act, mixed, wd, wo, own, sib):
    out = nn(act[...], wd[...]) + nn(mixed[...], wo[...])
    own[...] = out[:HALF]
    sib[...] = out[HALF:].astype(bf)


def p_call(act, mixed, w):
    units, width = act.shape[1], w.shape[1]
    tile = 256
    full = lambda *shape: pl.BlockSpec(shape, lambda j: (0,) * len(shape))
    return pl.pallas_call(
        p_body,
        grid=(width // tile,),
        in_specs=[
            full(TOK, units), full(TOK, 256),
            pl.BlockSpec((units, tile), lambda j: (0, j)),
            pl.BlockSpec((256, tile), lambda j: (units // 256, j)),
        ],
        out_specs=[pl.BlockSpec((HALF, tile), lambda j: (0, j))] * 2,
        out_shape=[jax.ShapeDtypeStruct((HALF, width), f32), jax.ShapeDtypeStruct((HALF, width), bf)],
        compiler_params=params(),
        cost_estimate=cost(2 * TOK * width * (units + 256), 16e6),
        name="combine",
    )(act, mixed, w, w)


def ga_body(units_tiles, g0, g1, w, slope, gh, gmix, x):
    j = pl.program_id(0)

    @pl.when(j == 0)
    def _():
        x[:HALF] = g0[...]
        x[HALF:] = g1[...]

    ga = nt(x[...], w[...]).astype(bf)

    @pl.when(j < units_tiles)
    def _():
        gh[...] = (ga.astype(f32) * slope[...].astype(f32)).astype(bf)

    @pl.when(j == units_tiles)
    def _():
        gmix[...] = ga


def ga_call(g0, g1, w, slope):
    width, rows = w.shape[1], w.shape[0]
    tile = 256
    units_tiles = rows // tile - 1
    full = lambda *shape: pl.BlockSpec(shape, lambda j: (0,) * len(shape))
    return pl.pallas_call(
        functools.partial(ga_body, units_tiles),
        grid=(rows // tile,),
        in_specs=[
            full(HALF, width), full(HALF, width),
            pl.BlockSpec((tile, width), lambda j: (j, 0)),
            pl.BlockSpec((TOK, tile), lambda j: (0, jnp.minimum(j, units_tiles - 1))),
        ],
        out_specs=[
            pl.BlockSpec((TOK, tile), lambda j: (0, jnp.minimum(j, units_tiles - 1))),
            full(TOK, 256),
        ],
        out_shape=[jax.ShapeDtypeStruct((TOK, rows - 256), bf), jax.ShapeDtypeStruct((TOK, 256), bf)],
        scratch_shapes=[pltpu.VMEM((TOK, width), bf)],
        compiler_params=params(),
        cost_estimate=cost(2 * TOK * width * rows, 16e6),
        name="pull",
    )(g0, g1, w, slope)


def u_body(gh, gq, gkv, wu, wq, own, sib):
    out = nn(gh[...], wu[...]) + nn(gq[0], wq[0:256]) + nn(gkv[0], wq[256:512]) + nn(gkv[1], wq[512:768])
    own[...] = out[:HALF]
    sib[...] = out[HALF:].astype(bf)


def u_call(gh, gq, gkv, w_up, w_qkv):
    units, width = gh.shape[1], w_up.shape[1]
    tile = 256
    full = lambda *shape: pl.BlockSpec(shape, lambda j: (0,) * len(shape))
    return pl.pallas_call(
        u_body,
        grid=(width // tile,),
        in_specs=[
            full(TOK, units), full(1, TOK, 256), full(2, TOK, 256),
            pl.BlockSpec((units, tile), lambda j: (0, j)),
            pl.BlockSpec((768, tile), lambda j: (0, j)),
        ],
        out_specs=[pl.BlockSpec((HALF, tile), lambda j: (0, j))] * 2,
        out_shape=[jax.ShapeDtypeStruct((HALF, width), f32), jax.ShapeDtypeStruct((HALF, width), bf)],
        compiler_params=params(),
        cost_estimate=cost(2 * TOK * width * (units + 768), 20e6),
        name="push",
    )(gh, gq, gkv, w_up, w_qkv)


LANES = 128


MESH = pl.DeviceIdType.MESH


def line_order(z, t):
    near = jnp.where(z < 2, z + 1, z - 1)
    mid = jnp.where(z == 0, 2, jnp.where(z == 1, 0, jnp.where(z == 2, 3, 1)))
    far = jnp.where(z < 2, 3, 0)
    return jnp.where(t == 0, z, jnp.where(t == 1, near, jnp.where(t == 2, mid, far)))


def remote(src, dst, send, recv, s, f):
    return pltpu.make_async_remote_copy(
        src_ref=src, dst_ref=dst, send_sem=send, recv_sem=recv, device_id=(s, f), device_id_type=MESH
    )


def line_barrier(s, f, z):
    barrier = pltpu.get_barrier_semaphore()

    @pl.when(z < 3)
    def _():
        pl.semaphore_signal(barrier, inc=1, device_id=(s, f + 2), device_id_type=MESH)

    @pl.when(z > 0)
    def _():
        pl.semaphore_signal(barrier, inc=1, device_id=(s, f - 2), device_id_type=MESH)

    pl.semaphore_signal(barrier, inc=1, device_id=(s, f + 1 - 2 * (f % 2)), device_id_type=MESH)

    @pl.when((z == 0) | (z == 3))
    def _():
        pl.semaphore_wait(barrier, 2)

    @pl.when((z == 1) | (z == 2))
    def _():
        pl.semaphore_wait(barrier, 3)


def near_barrier(s, f):
    barrier = pltpu.get_barrier_semaphore()
    c = f % 2
    for step in range(1, 8):
        pl.semaphore_signal(barrier, inc=1, device_id=(s, (f + step) % 8), device_id_type=MESH)
    for step in range(1, 4):
        for core in range(2):
            pl.semaphore_signal(
                barrier, inc=1, device_id=((s + step) % 4, f - c + core), device_id_type=MESH
            )
    pl.semaphore_wait(barrier, 13)


class PlaneOut:
    def __init__(self, src, dst, s, f, send, recv, own_sem):
        c = f % 2
        mine = 2 * (s % 2) + c
        self.parts = []
        for j in range(4):
            k = (j - s + 4) % 4
            to_s, to_f = 2 * c + j // 2, f - c + j % 2
            place = dst.at[pl.ds(pl.multiple_of(128 * k, 128), 128)]
            here = (to_s == s) & (to_f == f)
            self.parts.append(
                (
                    here,
                    pltpu.make_async_copy(src.at[j], place, own_sem),
                    remote(src.at[j], place, send.at[j], recv.at[k], to_s, to_f),
                )
            )
        self.comes = []
        for k in range(4):
            from_s, from_f = (mine - k + 4) % 4, f - c + s // 2
            ref = dst.at[pl.ds(128 * k, 128)]
            away = jnp.logical_not((from_s == s) & (from_f == f))
            self.comes.append((away, remote(ref, ref, send.at[k], recv.at[k], from_s, from_f)))

    def start(self, j):
        here, local, away = self.parts[j]
        pl.when(here)(local.start)
        pl.when(jnp.logical_not(here))(away.start)

    def arrive(self):
        for here, local, away in self.parts:
            pl.when(here)(local.wait)
        for away, copy in self.comes:
            pl.when(away)(copy.wait_recv)

    def sent(self):
        for here, local, away in self.parts:
            pl.when(jnp.logical_not(here))(away.wait_send)

    def wait(self):
        self.arrive()
        self.sent()


def expand_tables(cos4, sin4, b, cos, sin):
    lane = lax.broadcasted_iota(jnp.int32, (256, LANES), 1)
    for q in range(4):
        at = pl.ds(256 * q, 256)
        c, s_ = cos4[b], sin4[b]
        if q > 0:
            c, s_ = pltpu.roll(c, 128 - 32 * q, 1), pltpu.roll(s_, 128 - 32 * q, 1)
        cos[at, :] = jnp.where(lane < 32, c, jnp.where(lane < 64, pltpu.roll(c, 32, 1), 1.0))
        sin[at, :] = jnp.where(lane < 32, -s_, jnp.where(lane < 64, pltpu.roll(s_, 32, 1), 0.0))


class PlaneBack:
    def __init__(self, src, dst, s, f, send, recv, own_sem):
        c = f % 2
        mine = 2 * (s % 2) + c
        self.parts = []
        for k in range(4):
            to_s, to_f = (mine - k + 4) % 4, f - c + s // 2
            piece = src.at[pl.ds(128 * k, 128)]
            place = dst.at[pl.ds(pl.multiple_of(128 * mine, 128), 128)]
            here = (to_s == s) & (to_f == f)
            self.parts.append(
                (
                    here,
                    pltpu.make_async_copy(piece, place, own_sem),
                    remote(piece, place, send.at[k], recv.at[mine], to_s, to_f),
                )
            )
        self.comes = []
        for part in range(4):
            from_s, from_f = 2 * c + part // 2, f - c + part % 2
            ref = dst.at[pl.ds(128 * part, 128)]
            away = jnp.logical_not((from_s == s) & (from_f == f))
            self.comes.append((away, remote(ref, ref, send.at[part], recv.at[part], from_s, from_f)))

    def start(self):
        for here, local, away in self.parts:
            pl.when(here)(local.start)
            pl.when(jnp.logical_not(here))(away.start)

    def wait(self):
        for here, local, away in self.parts:
            pl.when(here)(local.wait)
            pl.when(jnp.logical_not(here))(away.wait_send)
        for away, copy in self.comes:
            pl.when(away)(copy.wait_recv)


def line_step(buf, k, z, s, f, sems, held=None):
    send_up, recv_up, send_dn, recv_dn = sems
    own = pl.ds(0, HALF)

    @pl.when((z - k >= 0) & (z < 3))
    def _():
        ref = buf.at[z - k, own]
        remote(ref if held is None else held, ref, send_up.at[k], recv_up.at[k], s, f + 2).start()

    @pl.when((z + k <= 3) & (z > 0))
    def _():
        ref = buf.at[z + k, own]
        remote(ref if held is None else held, ref, send_dn.at[k], recv_dn.at[k], s, f - 2).start()


def line_arrive(buf, k, z, s, f, sems):
    send_up, recv_up, send_dn, recv_dn = sems
    own = pl.ds(0, HALF)

    @pl.when(z - 1 - k >= 0)
    def _():
        ref = buf.at[z - 1 - k, own]
        remote(ref, ref, send_up.at[k], recv_up.at[k], s, f - 2).wait_recv()

    @pl.when(z + 1 + k <= 3)
    def _():
        ref = buf.at[z + 1 + k, own]
        remote(ref, ref, send_dn.at[k], recv_dn.at[k], s, f + 2).wait_recv()


def line_sent(buf, k, z, s, f, sems):
    send_up, recv_up, send_dn, recv_dn = sems
    own = pl.ds(0, HALF)

    @pl.when((z - k >= 0) & (z < 3))
    def _():
        ref = buf.at[z - k, own]
        remote(ref, ref, send_up.at[k], recv_up.at[k], s, f + 2).wait_send()

    @pl.when((z + k <= 3) & (z > 0))
    def _():
        ref = buf.at[z + k, own]
        remote(ref, ref, send_dn.at[k], recv_dn.at[k], s, f - 2).wait_send()


def core_copy(buf, b, s, f, sems, held=None):
    send, recv = sems
    return remote(
        buf.at[b, pl.ds(0, HALF)] if held is None else held, buf.at[b, pl.ds(HALF, HALF)], send.at[b], recv.at[b], s, f + 1 - 2 * (f % 2)
    )


def new_blocks(k, z, act):
    if k == 0:
        act(z)
        return

    @pl.when(z - k >= 0)
    def _():
        act(z - k)

    @pl.when(z + k <= 3)
    def _():
        act(z + k)


def forward_body(
    own_n, g_low, heads, up_h, down_h, out_h, bias, gain, shift, cos4, sin4, idc, idr,
    n_all, g_all, w_in_o, w_out_o, a_all, slope_o, qkv_o, lse_o, own_o, sib_o,
    w_in, w_out, x, normed, act, slope, qkv, mixed, lse, p_own, p_sib, g_out, wide, cos, sin,
    load, w_load, w_store, line_n0, line_n1, line_n2, line_n3, line_g0, line_g1, line_g2, line_g3,
    core_n0, core_n1, core_p0, core_p1, out_sems, po_s, po_r, h_s, h_r,
):
    s, f = lax.axis_index("seq"), lax.axis_index("fsdp")
    z = f // 2
    line_n, line_g = (line_n0, line_n1, line_n2, line_n3), (line_g0, line_g1, line_g2, line_g3)
    core_n, core_p = (core_n0, core_n1), (core_p0, core_p1)
    own, other = pl.ds(0, HALF), pl.ds(HALF, HALF)
    units = act.shape[1]
    half = (s % 2 + s // 2) % 2
    across = (s + 1 - 2 * (s % 2), (s + 2) % 4)

    def head_rows(kind, which, count, start=0):
        return w_in.at[pl.ds(pl.multiple_of(units + 256 * kind + 128 * which + start, 64), count)]

    first = [pltpu.make_async_copy(own_n, x.at[own], load.at[0])] + [
        pltpu.make_async_copy(g_low.at[pl.ds(128 * j, 128)], g_out.at[j], load.at[1 + j]) for j in range(4)
    ]
    held = [pltpu.make_async_copy(heads.at[i], head_rows(i, half, 128), load.at[5 + i]) for i in range(3)]
    keep = pltpu.make_async_copy(x.at[own], n_all.at[z, own], load.at[0])
    chunks = [(up_h, w_in, i) for i in range(units // 256)]
    chunks += [(down_h, w_out, i) for i in range(units // 256)] + [(out_h, w_out, units // 256)]

    def chunk_load(i):
        src, dst, at = chunks[i]
        place = at if src is not out_h else 0
        return pltpu.make_async_copy(src.at[pl.ds(256 * place, 256)], wide.at[i % 2], w_load.at[i % 2])

    def send_head(kind, way):
        return remote(
            heads.at[kind, pl.ds(64 * way, 64)], head_rows(kind, half, 64, 64 * way),
            h_s.at[kind, way], h_r.at[kind, way], across[way], f,
        )

    def come_head(kind, way):
        ref = head_rows(kind, 1 - half, 64, 64 * way)
        return remote(ref, ref, h_s.at[kind, way], h_r.at[kind, way], across[way], f)

    for copy in first + held:
        copy.start()
    chunk_load(0).start()
    near_barrier(s, f)
    spread = PlaneOut(g_out, g_all.at[z, own], s, f, po_s, po_r, load.at[8])
    store = [pltpu.make_async_copy(w_in, w_in_o, w_store.at[0]), pltpu.make_async_copy(w_out, w_out_o, w_store.at[1])]

    def outs(b):
        pairs = [
            (act, a_all.at[b, :, pl.ds(0, units)]), (mixed, a_all.at[b, :, pl.ds(units, 256)]),
            (slope, slope_o.at[b]), (qkv, qkv_o.at[b]), (lse, lse_o.at[b]), (p_own, own_o.at[b]),
        ]
        return [pltpu.make_async_copy(src, dst, out_sems.at[i]) for i, (src, dst) in enumerate(pairs)]

    def send_sib(b):
        return remote(p_sib, sib_o.at[b], core_p[0].at[b], core_p[1].at[b], s, f + 1 - 2 * (f % 2))

    for t in range(4):
        b = line_order(z, t)
        low_half = pltpu.make_async_copy(n_all.at[b, other], x.at[other], load.at[9])
        if t == 0:
            line_step(n_all, 0, z, s, f, line_n, own_n)
            core_copy(n_all, z, s, f, core_n, own_n).start()
            for kind in range(3):
                for way in range(2):
                    send_head(kind, way).start()
            first[0].wait()
            keep.start()
            for i, (src, dst, at) in enumerate(chunks):
                if i + 1 < len(chunks):
                    chunk_load(i + 1).start()
                chunk_load(i).wait()
                dst[pl.ds(256 * at, 256), :] = wide[i % 2].astype(bf)
            for copy in first[1:]:
                copy.wait()
        else:
            line_arrive(n_all, t - 1, z, s, f, line_n)
            if t < 3:
                line_step(n_all, t, z, s, f, line_n)
            else:
                spread.arrive()
                line_step(g_all, 0, z, s, f, line_g)
            new_blocks(t, z, lambda v: core_copy(n_all, v, s, f, core_n).start())
            top = pltpu.make_async_copy(n_all.at[b, own], x.at[own], load.at[0])
            top.start()
        if t == 1:
            for j in range(4):
                spread.start(j)
        core_copy(n_all, b, s, f, core_n).wait_recv()
        low_half.start()
        expand_tables(cos4, sin4, b, cos, sin)
        if t == 0:
            keep.wait()
        else:
            top.wait()
            before = line_order(z, t - 1)
            for copy in outs(before):
                copy.wait()
            send_sib(before).wait_send()
        low_half.wait()

        def norm(which):
            @pl.loop(0, TOK // 64)
            def _(i):
                at = pl.ds(pl.multiple_of(i * 64, 64), 64)
                value = x[at, :].astype(f32) * gain[which : which + 1, :] + shift[which : which + 1, :]
                normed[at, :] = value.astype(bf)

        norm(0)

        @pl.loop(0, units // 256)
        def _(j):
            at = pl.ds(pl.multiple_of(j * 256, 256), 256)
            h = nt(normed[...], w_in[at, :]) + bias[:, at]
            act[:, at], slope[:, at] = gelu_pair(h)

        norm(1)
        if t == 0:
            for copy in held:
                copy.wait()
            for kind in range(3):
                for way in range(2):
                    come_head(kind, way).wait_recv()
            for copy in store:
                copy.start()

        @pl.loop(0, 2)
        def _(j):
            at = pl.ds(pl.multiple_of(units + j * 256, 256), 256)
            h = nt(normed[...], w_in[at, :]) + bias[:, at]
            qkv[j] = turn(h, cos[...], sin[...]).astype(bf)

        at = pl.ds(units + 512, 256)
        qkv[2] = (nt(normed[...], w_in[at, :]) + bias[:, at]).astype(bf)

        @pl.loop(0, TOK // 256)
        def _(i):
            rows = pl.ds(pl.multiple_of(i * 256, 256), 256)
            scores = nt(qkv[0, rows, :], qkv[1]) * (256 ** -0.5)
            scores = jnp.where(idr[b] <= idc[b, rows, :], scores, -1e30)
            top_score = jnp.max(scores, axis=1, keepdims=True)
            weights = jnp.exp(scores - top_score)
            total = jnp.sum(weights, axis=1, keepdims=True)
            probs = (weights / total).astype(bf)
            mixed[rows, :] = nn(probs, qkv[2]).astype(bf)
            lse[rows, :] = jnp.broadcast_to(top_score + jnp.log(total), (256, LANES))

        @pl.loop(0, p_own.shape[1] // 256)
        def _(j):
            at = pl.ds(pl.multiple_of(j * 256, 256), 256)
            out = nn(act[...], w_out[pl.ds(0, units), at]) + nn(mixed[...], w_out[pl.ds(units, 256), at])
            p_own[:, at] = out[:HALF].astype(bf)
            p_sib[:, at] = out[HALF:].astype(bf)

        for copy in outs(b):
            copy.start()
        send_sib(b).start()

    last = line_order(z, 3)
    for copy in outs(last):
        copy.wait()
    send_sib(last).wait_send()
    for b in range(4):
        core_copy(n_all, b, s, f, core_n).wait_send()
        send_sib(b).wait_recv()
    for k in range(3):
        line_sent(n_all, k, z, s, f, line_n)
    line_arrive(g_all, 0, z, s, f, line_g)
    line_sent(g_all, 0, z, s, f, line_g)
    spread.sent()
    for copy in store:
        copy.wait()
    for kind in range(3):
        for way in range(2):
            send_head(kind, way).wait_send()


def forward_call(own_n, g_low, heads, up, down, out, bias, gain, shift, cos4, sin4, ids_col, ids_row):
    width, units = up.shape[1], up.shape[0]
    anys = pl.BlockSpec(memory_space=pl.ANY)
    vmem = pl.BlockSpec(memory_space=pltpu.VMEM)
    shape = jax.ShapeDtypeStruct
    dma = lambda *n: pltpu.SemaphoreType.DMA(n)
    return pl.pallas_call(
        forward_body,
        in_specs=[anys] * 6 + [vmem] * 7,
        out_specs=[anys] * 10,
        out_shape=[
            shape((4, TOK, width), bf), shape((4, TOK, width), bf),
            shape((units + 768, width), bf), shape((units + 256, width), bf),
            shape((4, TOK, units + 256), bf), shape((4, TOK, units), bf), shape((4, 3, TOK, 256), bf),
            shape((4, TOK, LANES), f32), shape((4, HALF, width), bf), shape((4, HALF, width), bf),
        ],
        scratch_shapes=[
            pltpu.VMEM((units + 768, width), bf), pltpu.VMEM((units + 256, width), bf),
            pltpu.VMEM((TOK, width), bf), pltpu.VMEM((TOK, width), bf),
            pltpu.VMEM((TOK, units), bf), pltpu.VMEM((TOK, units), bf), pltpu.VMEM((3, TOK, 256), bf),
            pltpu.VMEM((TOK, 256), bf), pltpu.VMEM((TOK, LANES), f32),
            pltpu.VMEM((HALF, width), bf), pltpu.VMEM((HALF, width), bf),
            pltpu.VMEM((4, 128, width), bf), pltpu.VMEM((2, 256, width), f32),
            pltpu.VMEM((TOK, LANES), f32), pltpu.VMEM((TOK, LANES), f32),
            dma(10), dma(2), dma(2), dma(3), dma(3), dma(3), dma(3), dma(3), dma(3), dma(3), dma(3),
            dma(4), dma(4), dma(4), dma(4), dma(6), dma(4), dma(4), dma(3, 2), dma(3, 2),
        ],
        compiler_params=pltpu.CompilerParams(
            vmem_limit_bytes=60 * 1024 * 1024, collective_id=0, has_side_effects=True
        ),
        cost_estimate=cost(8 * TOK * width * (2 * units + 1024), 200e6),
        name="forward",
    )(own_n, g_low, heads, up, down, out, bias, gain, shift, cos4, sin4, ids_col, ids_row)


def entry_body(
    resid, grad, qkv, packed, own_n, g_low, heads, small_all, bias_sum,
    x_in, g_in, q_in, n_out, g_out, q_out,
    load, q_s, q_r, po_s, po_r, sm_s, sm_r, own_sems,
):
    s, f = lax.axis_index("seq"), lax.axis_index("fsdp")
    half = (s % 2 + s // 2) % 2
    width = resid.shape[1]
    parts = [pltpu.make_async_copy(resid.at[pl.ds(128 * j, 128)], x_in.at[j], load.at[j]) for j in range(4)]
    pulls = [pltpu.make_async_copy(grad.at[pl.ds(128 * j, 128)], g_in.at[j], load.at[4 + j]) for j in range(4)]
    rows = [
        pltpu.make_async_copy(
            qkv.at[pl.ds(pl.multiple_of(256 * i + 128 * half, 128), 128)], q_in.at[i], load.at[8 + i]
        )
        for i in range(3)
    ]
    for copy in rows + parts + pulls:
        copy.start()
    near_barrier(s, f)
    keep_small = pltpu.make_async_copy(packed, small_all.at[f], own_sems.at[0])
    keep_small.start()

    def send_small(step):
        to = (f + step) % 8
        return remote(packed, small_all.at[f], sm_s.at[step - 1], sm_r.at[step - 1], s, to)

    for step in range(1, 8):
        send_small(step).start()

    def hop(i):
        head = 3 * f + i
        return remote(q_out.at[i], heads.at[head // 8], q_s.at[i], q_r.at[head // 8], s, head % 8)

    def keep_hop(i):
        return pltpu.make_async_copy(q_out.at[i], heads.at[(3 * f + i) // 8], own_sems.at[1])

    for i in range(3):
        rows[i].wait()
        q_out[i] = q_in[i].astype(bf)
        here = (3 * f + i) % 8 == f
        pl.when(here)(keep_hop(i).start)
        pl.when(jnp.logical_not(here))(hop(i).start)

    out = PlaneOut(n_out, own_n, s, f, po_s, po_r, own_sems.at[2])
    for j in range(4):
        parts[j].wait()

        @pl.loop(0, 4)
        def _(i):
            at = pl.ds(pl.multiple_of(32 * i, 32), 32)
            value = x_in[j, at, :]
            mean = jnp.sum(value, axis=1, keepdims=True) * (1.0 / width)
            center = value - mean
            spread = jnp.sum(center * center, axis=1, keepdims=True) * (1.0 / width)
            inv = lax.rsqrt(spread + EPS)
            n_out[j, at, :] = (center * inv).astype(bf)

        out.start(j)
    for j in range(4):
        pulls[j].wait()
        g_out[j] = g_in[j].astype(bf)
        part = jnp.sum(g_in[j], axis=0, keepdims=True)
        bias_sum[...] = part if j == 0 else bias_sum[...] + part
    keep_g = [
        pltpu.make_async_copy(g_out.at[j], g_low.at[pl.ds(128 * j, 128)], load.at[j]) for j in range(4)
    ]
    for copy in keep_g:
        copy.start()
    keep_small.wait()
    for step in range(1, 8):
        send_small(step).wait_send()
        at = (f + 8 - step) % 8
        remote(packed, small_all.at[at], sm_s.at[step - 1], sm_r.at[step - 1], s, at).wait_recv()
    for kind in range(3):
        frm = (8 * kind + f) // 3
        ref = heads.at[kind]
        away = remote(ref, ref, q_s.at[kind], q_r.at[kind], s, frm)
        pl.when(frm != f)(away.wait_recv)
    for i in range(3):
        here = (3 * f + i) % 8 == f
        pl.when(here)(keep_hop(i).wait)
        pl.when(jnp.logical_not(here))(hop(i).wait_send)
    out.wait()
    for copy in keep_g:
        copy.wait()


def entry_call(resid, grad, qkv, packed):
    width = resid.shape[1]
    anys = pl.BlockSpec(memory_space=pl.ANY)
    vmem = pl.BlockSpec(memory_space=pltpu.VMEM)
    shape = jax.ShapeDtypeStruct
    dma = lambda n: pltpu.SemaphoreType.DMA((n,))
    return pl.pallas_call(
        entry_body,
        in_specs=[anys] * 3 + [vmem],
        out_specs=[anys] * 4 + [vmem],
        out_shape=[
            shape((HALF, width), bf), shape((HALF, width), bf), shape((3, 128, width), bf),
            shape((8,) + packed.shape, f32), shape((1, width), f32),
        ],
        scratch_shapes=[
            pltpu.VMEM((4, 128, width), f32), pltpu.VMEM((4, 128, width), f32), pltpu.VMEM((3, 128, width), f32),
            pltpu.VMEM((4, 128, width), bf), pltpu.VMEM((4, 128, width), bf), pltpu.VMEM((3, 128, width), bf),
            dma(11), dma(3), dma(3), dma(4), dma(4), dma(7), dma(7), dma(3),
        ],
        compiler_params=pltpu.CompilerParams(
            vmem_limit_bytes=60 * 1024 * 1024, collective_id=3, has_side_effects=True
        ),
        cost_estimate=cost(1e7, 20e6),
        name="entry",
    )(resid, grad, qkv, packed)


class SeqSum:
    def __init__(self, term, r1, r2, sems, own_sems, result, s, f):
        self.term, self.r1, self.r2, self.own_sems, self.result, self.f = term, r1, r2, own_sems, result, f
        self.sems = sems
        x, y = s % 2, s // 2
        self.across = (s + 1 - 2 * x, (s + 2) % 4)
        self.ways = ((0, x, y), (1, y, x))

    @staticmethod
    def rows(start, count):
        return pl.ds(pl.multiple_of(start, 32), count)

    @staticmethod
    def base(p, a, b):
        return 128 * p + 64 * a + 32 * b

    def copy(self, step, src, dst, j, p):
        to = self.across[p if step in (1, 4) else 1 - p]
        send, recv = self.sems[2 * step - 2 : 2 * step]
        return remote(src, dst, send.at[j, p], recv.at[j, p], to, self.f)

    def send1(self, j, p, a):
        return self.copy(1, self.term.at[j, self.rows(128 * p + 64 * (1 - a), 64)], self.r1.at[j, p], j, p)

    def send2(self, j, p, a, b):
        return self.copy(2, self.term.at[j, self.rows(self.base(p, a, 1 - b), 32)], self.r2.at[j, p], j, p)

    def keep3(self, j, p, a, b):
        at = self.base(p, a, b)
        return pltpu.make_async_copy(self.term.at[j, self.rows(at, 32)], self.result(j, at, 32), self.own_sems.at[j, p])

    def send3(self, j, p, a, b, held=True):
        at = self.base(p, a, b)
        ref = self.result(j, at, 32)
        return self.copy(3, self.term.at[j, self.rows(at, 32)] if held else ref, ref, j, p)

    def send4(self, j, p, a):
        ref = self.result(j, 128 * p + 64 * a, 64)
        return self.copy(4, ref, ref, j, p)

    def step1(self, j):
        for p, a, b in self.ways:
            self.send1(j, p, a).start()

    def step2(self, j):
        for p, a, b in self.ways:
            self.send1(j, p, a).wait_recv()
            at = self.rows(128 * p + 64 * a, 64)
            self.term[j, at, :] = (self.term[j, at, :].astype(f32) + self.r1[j, p].astype(f32)).astype(bf)
            self.send2(j, p, a, b).start()

    def total(self, j, p, a, b):
        self.send2(j, p, a, b).wait_recv()
        at = self.rows(self.base(p, a, b), 32)
        return (self.term[j, at, :].astype(f32) + self.r2[j, p].astype(f32)).astype(bf)

    def step3(self, j):
        for p, a, b in self.ways:
            self.term[j, self.rows(self.base(p, a, b), 32), :] = self.total(j, p, a, b)
            self.send3(j, p, a, b).start()
            self.keep3(j, p, a, b).start()

    def step4(self, j, held=True):
        for p, a, b in self.ways:
            self.send3(j, p, a, b, held).wait_recv()
            if held:
                self.keep3(j, p, a, b).wait()
            self.send4(j, p, a).start()

    def finish(self, j):
        for p, a, b in self.ways:
            self.send4(j, p, a).wait_recv()
            self.send1(j, p, a).wait_send()
            self.send2(j, p, a, b).wait_send()
            self.send3(j, p, a, b).wait_send()
            self.send4(j, p, a).wait_send()


def sum_add(dst, parts):
    @pl.loop(0, HALF // 64)
    def _(i):
        rows = pl.ds(pl.multiple_of(i * 64, 64), 64)
        total = parts[0][rows, :].astype(f32)
        for part in parts[1:]:
            total = total + part[rows, :].astype(f32)
        dst[rows, :] = total.astype(bf)


def line_sum_step(k, z, s, f, own, sib, land, stage, out, loads, sends, recvs, early=None):
    for way in range(2):
        d = z - 3 + k if way == 0 else z + 3 - k
        valid = d >= 0 if way == 0 else d <= 3
        to = f - 2 if way == 0 else f + 2
        inner = z < 3 if way == 0 else z > 0
        was = z - 4 + k >= 0 if way == 0 else z + 4 - k <= 3

        @pl.when(valid)
        def _():
            terms = [
                pltpu.make_async_copy(own.at[d], stage.at[0], loads.at[0]),
                pltpu.make_async_copy(sib.at[d], stage.at[1], loads.at[1]),
            ]
            for copy in terms:
                copy.start()
            if k == 1 and early is not None:

                @pl.when(inner)
                def _():
                    came = pltpu.make_async_copy(early.at[way], stage.at[2], loads.at[2])
                    came.start()
                    came.wait()

            elif k > 0:

                @pl.when(was)
                def _():
                    remote(out.at[way], land.at[way, k - 1], sends.at[way, k - 1], recvs.at[way, k - 1], s, to).wait_send()

                @pl.when(inner)
                def _():
                    remote(out.at[way], land.at[way, k - 1], sends.at[way, k - 1], recvs.at[way, k - 1], s, to).wait_recv()
                    came = pltpu.make_async_copy(land.at[way, k - 1], stage.at[2], loads.at[2])
                    came.start()
                    came.wait()

            for copy in terms:
                copy.wait()
            if k > 0:

                @pl.when(inner)
                def _():
                    sum_add(out.at[way], [stage.at[0], stage.at[1], stage.at[2]])

                @pl.when(jnp.logical_not(inner))
                def _():
                    sum_add(out.at[way], [stage.at[0], stage.at[1]])
            else:
                sum_add(out.at[way], [stage.at[0], stage.at[1]])
            remote(out.at[way], land.at[way, k], sends.at[way, k], recvs.at[way, k], s, to).start()


def line_sum_end(z, s, f, own, sib, land, stage, out, loads, sends, recvs):
    terms = [
        pltpu.make_async_copy(own.at[z], stage.at[0], loads.at[0]),
        pltpu.make_async_copy(sib.at[z], stage.at[1], loads.at[1]),
    ]
    for copy in terms:
        copy.start()
    for copy in terms:
        copy.wait()

    for way in range(2):
        to = f - 2 if way == 0 else f + 2
        sent = z > 0 if way == 0 else z < 3
        got = z < 3 if way == 0 else z > 0

        @pl.when(sent)
        def _():
            remote(out.at[way], land.at[way, 2], sends.at[way, 2], recvs.at[way, 2], s, to).wait_send()

        @pl.when(got)
        def _():
            remote(out.at[way], land.at[way, 2], sends.at[way, 2], recvs.at[way, 2], s, to).wait_recv()
            came = pltpu.make_async_copy(land.at[way, 2], stage.at[2], loads.at[2])
            came.start()
            came.wait()
            sum_add(stage.at[0], [stage.at[0], stage.at[2]])

    sum_add(stage.at[2], [stage.at[0], stage.at[1]])


def backward_body(
    g_part, a_all, w_in_h, w_out_h, slope_h, qkv_h, lse_h, p_own, p_sib, gain, cos4, sin4, idc, idr,
    g_all, b_all, own_o, sib_o, branch, land, land_u, fin_down, fin_out, sums,
    w_in, w_out, x, slope, qkv, lse, gh, gmix, gp, acc_k, acc_v, u_own, u_sib, stage, rs_out, cos, sin, term, r1, r2, left, acc,
    load, l0, l1, l2, l3, core_0, core_1, core_u0, core_u1, out_sems, rs_send, rs_recv, pb_send, pb_recv,
    t_load, r1_s, r1_r, r2_s, r2_r, r3_s, r3_r, r4_s, r4_r, own_sems, u_send, u_recv,
):
    s, f = lax.axis_index("seq"), lax.axis_index("fsdp")
    z = f // 2
    line = (l0, l1, l2, l3)
    core = (core_0, core_1)
    own, other = pl.ds(0, HALF), pl.ds(HALF, HALF)
    units = gh.shape[1]
    scale = 256 ** -0.5
    first = [
        pltpu.make_async_copy(w_in_h, w_in, load.at[0]),
        pltpu.make_async_copy(w_out_h, w_out, load.at[1]),
    ]
    for copy in first:
        copy.start()
    near_barrier(s, f)
    swap = lambda b: core_copy(g_all, b, s, f, core)
    new_blocks(0, z, lambda b: swap(b).start())
    line_step(g_all, 1, z, s, f, line)
    new_blocks(1, z, lambda b: swap(b).start())
    reduce_args = (z, s, f, p_own, p_sib, land, stage, rs_out, load.at[pl.ds(8, 3)], rs_send, rs_recv)
    line_sum_step(0, *reduce_args)
    sums[...] = jnp.zeros_like(sums)
    back = PlaneBack(stage.at[2], branch, s, f, pb_send, pb_recv, load.at[7])

    def ins(b, which=(0, 1, 2)):
        pairs = [(slope_h, slope), (qkv_h, qkv), (lse_h, lse)]
        return [pltpu.make_async_copy(pairs[i][0].at[b], pairs[i][1], load.at[2 + i]) for i in which]

    def outs(b):
        pairs = [(gh, b_all.at[b, :, pl.ds(0, units)]), (u_own, own_o.at[b])]
        pairs += [(gp.at[i], b_all.at[b, :, pl.ds(units + 256 * i, 256)]) for i in range(3)]
        return [pltpu.make_async_copy(src, dst, out_sems.at[i]) for i, (src, dst) in enumerate(pairs)]

    def send_sib(b):
        return remote(u_sib, sib_o.at[b], core_u0.at[b], core_u1.at[b], s, f + 1 - 2 * (f % 2))

    def result(j, start, count):
        if j < 4:
            return fin_down.at[SeqSum.rows(256 * j + start, count)]
        return fin_out.at[SeqSum.rows(start, count)]

    row_sums = SeqSum(
        term, r1, r2, (r1_s, r1_r, r2_s, r2_r, r3_s, r3_r, r4_s, r4_r), own_sems, result, s, f
    )

    def term_loads(j, k):
        slot = (8 * j + k) % 3
        at = pl.ds(pl.multiple_of(HALF * (k % 2), HALF), HALF)
        return (
            pltpu.make_async_copy(a_all.at[k // 2, at, pl.ds(256 * j, 256)], left.at[slot], t_load.at[slot, 0]),
            pltpu.make_async_copy(g_all.at[k // 2, at], stage.at[slot], t_load.at[slot, 1]),
        )

    def compute_term(j):
        @pl.loop(0, 8)
        def _(k):
            @pl.when(k < 6)
            def _():
                for copy in term_loads(j, k + 2):
                    copy.start()

            if j < 4:

                @pl.when(k >= 6)
                def _():
                    for copy in term_loads(j + 1, k - 6):
                        copy.start()

            for copy in term_loads(j, k):
                copy.wait()
            slot = (8 * j + k) % 3
            part = tn(left[slot], stage[slot])

            @pl.when(k == 0)
            def _():
                acc[...] = part

            @pl.when((k > 0) & (k < 7))
            def _():
                acc[...] += part

            @pl.when(k == 7)
            def _():
                term[j] = (acc[...] + part).astype(bf)

    def load_x(b):
        return [
            pltpu.make_async_copy(g_all.at[b, own], x.at[own], load.at[5]),
            pltpu.make_async_copy(g_all.at[b, other], x.at[other], load.at[6]),
        ]

    for copy in ins(z):
        copy.start()
    swap(z).wait_recv()
    for copy in load_x(z):
        copy.start()
    for copy in first:
        copy.wait()

    for t in range(4):
        b = line_order(z, t)
        expand_tables(cos4, sin4, b, cos, sin)
        if t == 3:
            line_arrive(g_all, 2, z, s, f, line)
            new_blocks(3, z, lambda v: swap(v).start())
            line_sum_step(2, *reduce_args)
            swap(b).wait_recv()
            for copy in term_loads(0, 0) + term_loads(0, 1) + tuple(load_x(b)):
                copy.start()
            for j in range(5):
                compute_term(j)
                row_sums.step1(j)
                if j >= 2:
                    row_sums.step2(j - 2)
                if j >= 3:
                    row_sums.step3(j - 3)
        if t > 0:
            before = line_order(z, t - 1)
            for copy in outs(before):
                copy.wait()
            send_sib(before).wait_send()
        for copy in ins(b) + load_x(b):
            copy.wait()

        @pl.loop(0, units // 256)
        def _(j):
            at = pl.ds(pl.multiple_of(j * 256, 256), 256)
            ga = nt(x[...], w_out[at, :]).astype(bf)
            gh[:, at] = (ga.astype(f32) * slope[:, at].astype(f32)).astype(bf)

        gmix[...] = nt(x[...], w_out[pl.ds(units, 256), :]).astype(bf)
        after = line_order(z, t + 1)
        if t < 3:
            ins(after, (0,))[0].start()
        else:
            row_sums.step2(3)
            row_sums.step3(2)
            row_sums.step4(0)
        acc_k[...] = jnp.zeros_like(acc_k)
        acc_v[...] = jnp.zeros_like(acc_v)

        @pl.loop(0, TOK // 256)
        def _(i):
            rows = pl.ds(pl.multiple_of(i * 256, 256), 256)
            q, g = qkv[0, rows, :], gmix[rows, :]
            scores = nt(q, qkv[1]) * scale
            allowed = idr[b] <= idc[b, rows, :]
            probs = jnp.where(allowed, jnp.exp(scores - lse[rows, 0:1]), 0.0)
            grad_probs = nt(g, qkv[2])
            inner = jnp.sum(probs * grad_probs, axis=1, keepdims=True)
            gs = (probs * (grad_probs - inner)).astype(bf)
            gq = (nn(gs, qkv[1]) * scale).astype(bf).astype(f32)
            gq = turn(gq, cos[rows, :], -sin[rows, :])
            sums[0:1, :] += jnp.sum(gq, axis=0, keepdims=True)
            gp[0, rows, :] = gq.astype(bf)
            acc_k[...] += tn(gs, q)
            acc_v[...] += tn(probs.astype(bf), g)

        gk = (acc_k[...] * scale).astype(bf).astype(f32)
        gk = turn(gk, cos[...], -sin[...])
        sums[1:2, :] += jnp.sum(gk, axis=0, keepdims=True)
        gp[1] = gk.astype(bf)
        gv = acc_v[...].astype(bf)
        sums[2:3, :] += jnp.sum(gv.astype(f32), axis=0, keepdims=True)
        gp[2] = gv
        if t < 3:
            for copy in ins(after, (1, 2)):
                copy.start()
        if t == 1:
            line_arrive(g_all, 1, z, s, f, line)
            line_step(g_all, 2, z, s, f, line)
            new_blocks(2, z, lambda v: swap(v).start())
        if t < 2:
            swap(after).wait_recv()
            for copy in load_x(after):
                copy.start()
        if t == 1:
            line_sum_step(1, *reduce_args)
        if t == 3:
            row_sums.step2(4)
            row_sums.step3(3)
            row_sums.step4(1)
            line_sum_end(*reduce_args)
            back.start()

        @pl.loop(0, u_own.shape[1] // 256)
        def _(j):
            at = pl.ds(pl.multiple_of(j * 256, 256), 256)
            from_mlp = nn(gh[...], w_in[pl.ds(0, units), at])
            from_attn = nn(gp[0], w_in[pl.ds(units, 256), at])
            for i in range(1, 3):
                from_attn = from_attn + nn(gp[i], w_in[pl.ds(units + 256 * i, 256), at])
            out = from_mlp * gain[0:1, at] + from_attn * gain[1:2, at]
            u_own[:, at] = out[:HALF].astype(bf)
            u_sib[:, at] = out[HALF:].astype(bf)

        for copy in outs(b):
            copy.start()
        send_sib(b).start()

    last = line_order(z, 3)
    for copy in outs(last):
        copy.wait()
    send_sib(last).wait_send()
    for b in range(4):
        swap(b).wait_send()
        send_sib(b).wait_recv()
    line_sum_step(0, z, s, f, own_o, sib_o, land_u, stage, rs_out, load.at[pl.ds(8, 3)], u_send, u_recv)
    row_sums.step3(4)
    row_sums.step4(2)
    row_sums.step4(3)
    row_sums.step4(4)
    back.wait()
    for k in (1, 2):
        line_sent(g_all, k, z, s, f, line)
    for j in range(5):
        row_sums.finish(j)
    for way in range(2):
        to = f - 2 if way == 0 else f + 2
        copy = remote(rs_out.at[way], land_u.at[way, 0], u_send.at[way, 0], u_recv.at[way, 0], s, to)
        pl.when(z == (3 if way == 0 else 0))(copy.wait_send)
        pl.when(z == (2 if way == 0 else 1))(copy.wait_recv)


def backward_call(g_part, a_all, w_in, w_out, slope, qkv, lse, p_own, p_sib, gain, cos4, sin4, ids_col, ids_row):
    width = w_in.shape[1]
    units = w_in.shape[0] - 768
    anys = pl.BlockSpec(memory_space=pl.ANY)
    vmem = pl.BlockSpec(memory_space=pltpu.VMEM)
    shape = jax.ShapeDtypeStruct
    dma = lambda *n: pltpu.SemaphoreType.DMA(n)
    return pl.pallas_call(
        backward_body,
        in_specs=[anys] * 9 + [vmem] * 5,
        out_specs=[anys] * 9 + [vmem],
        out_shape=[
            shape((4, TOK, width), bf), shape((4, TOK, units + 768), bf),
            shape((4, HALF, width), bf), shape((4, HALF, width), bf), shape((HALF, width), bf),
            shape((2, 3, HALF, width), bf), shape((2, 1, HALF, width), bf), shape((1024, width), bf),
            shape((256, width), bf), shape((8, 256), f32),
        ],
        input_output_aliases={0: 0},
        scratch_shapes=[
            pltpu.VMEM(w_in.shape, bf), pltpu.VMEM(w_out.shape, bf), pltpu.VMEM((TOK, width), bf),
            pltpu.VMEM((TOK, units), bf), pltpu.VMEM((3, TOK, 256), bf), pltpu.VMEM((TOK, LANES), f32),
            pltpu.VMEM((TOK, units), bf), pltpu.VMEM((TOK, 256), bf), pltpu.VMEM((3, TOK, 256), bf),
            pltpu.VMEM((TOK, 256), f32), pltpu.VMEM((TOK, 256), f32),
            pltpu.VMEM((HALF, width), bf), pltpu.VMEM((HALF, width), bf),
            pltpu.VMEM((3, HALF, width), bf), pltpu.VMEM((2, HALF, width), bf),
            pltpu.VMEM((TOK, LANES), f32), pltpu.VMEM((TOK, LANES), f32),
            pltpu.VMEM((5, 256, width), bf), pltpu.VMEM((5, 2, 64, width), bf), pltpu.VMEM((5, 2, 32, width), bf),
            pltpu.VMEM((3, HALF, 256), bf), pltpu.VMEM((256, width), f32),
            dma(11), dma(3), dma(3), dma(3), dma(3), dma(4), dma(4), dma(4), dma(4), dma(5),
            dma(2, 3), dma(2, 3), dma(4), dma(4), dma(3, 2), *[dma(5, 2)] * 9, dma(2, 3), dma(2, 3),
        ],
        compiler_params=pltpu.CompilerParams(
            vmem_limit_bytes=63 * 1024 * 1024, collective_id=1, has_side_effects=True
        ),
        cost_estimate=cost(8 * TOK * width * (w_in.shape[0] + w_out.shape[0]), 200e6),
        name="backward",
    )(g_part, a_all, w_in, w_out, slope, qkv, lse, p_own, p_sib, gain, cos4, sin4, ids_col, ids_row)


PAIRS = 7


def tail_body(
    b_all, n_all, plain, u_own, u_sib, early, gain, shift, wide_in, more_in,
    fin_up, fin_qkv, u_o, small_o, land,
    term, r1, r2, hop, stage, rs_out, left, right, acc, acc_s, weight, sides, wide, more, got, small,
    load, w_sem, r1_s, r1_r, r2_s, r2_r, hop_s, hop_r, r3_s, r3_r, r4_s, r4_r,
    rs_load, rs_send, rs_recv, pb_s, pb_r, sm_s, sm_r, sq_s, sq_r, own_sems, self_sem,
):
    s, f = lax.axis_index("seq"), lax.axis_index("fsdp")
    z = f // 2
    reduce_args = (z, s, f, u_own, u_sib, land, stage, rs_out, rs_load, rs_send, rs_recv)
    column = [4, 5, 6, 0, 1, 2, 3]

    def result(j, start, count):
        if j < 3:
            return fin_qkv.at[SeqSum.rows(256 * j + start, count)]
        return fin_up.at[SeqSum.rows(256 * (j - 3) + start, count)]

    sums = SeqSum(
        term, r1, r2, (r1_s, r1_r, r2_s, r2_r, r3_s, r3_r, r4_s, r4_r), own_sems, result, s, f
    )
    across = sums.across

    def loads(j, k):
        slot = k % 2
        return (
            pltpu.make_async_copy(b_all.at[k, :, pl.ds(256 * column[j], 256)], left.at[slot], load.at[slot, 0]),
            pltpu.make_async_copy(n_all.at[k], right.at[slot], load.at[slot, 1]),
        )

    def weights(j):
        return pltpu.make_async_copy(plain.at[pl.ds(256 * column[j], 256)], weight, w_sem)

    for copy in loads(0, 0):
        copy.start()
    near_barrier(s, f)
    sides[...] = jnp.zeros_like(sides)
    wide[...] = wide_in[...]
    more[...] = more_in[...]

    def compute(j):
        weights(j).start()

        @pl.loop(0, 4)
        def _(k):
            slot = k % 2

            @pl.when(k < 3)
            def _():
                for copy in loads(j, k + 1):
                    copy.start()

            if j + 1 < PAIRS:

                @pl.when(k == 3)
                def _():
                    for copy in loads(j + 1, 0):
                        copy.start()

            for copy in loads(j, k):
                copy.wait()
            part = tn(left[slot], right[slot])
            part_s = tn(left[slot], jnp.ones((TOK, LANES), bf))

            @pl.when(k == 0)
            def _():
                acc[...] = part
                acc_s[...] = part_s

            @pl.when(k > 0)
            def _():
                acc[...] += part
                acc_s[...] += part_s

        which = 1 if j < 3 else 0
        weights(j).wait()
        raw, total = acc[...], acc_s[:, 0:1]
        term[j] = (raw * gain[which : which + 1, :] + total * shift[which : which + 1, :]).astype(bf)
        low_w = weight[...].astype(f32)
        sides[2 * which : 2 * which + 1, :] += jnp.sum(low_w * raw, axis=0, keepdims=True)
        sides[2 * which + 1 : 2 * which + 2, :] += jnp.sum(low_w * total, axis=0, keepdims=True)
        if j >= 3:
            row = jnp.transpose(acc_s[...])
            for half in range(2):
                at = 2 * (j - 3) + half
                more[at : at + 1, :] = row[0:1, 128 * half : 128 * half + 128]

    def owner(j):
        head = 8 * j + f
        return head // 3, head % 3

    def hop_place(i, p, a, b):
        return fin_qkv.at[SeqSum.rows(256 * i + SeqSum.base(p, a, b), 32)]

    def send_hop(j, p, a, b):
        to, i = owner(j)
        return remote(hop.at[j, p], hop_place(i, p, a, b), hop_s.at[j, p], hop_r.at[i, p], s, to)

    def keep_hop(j, p, a, b):
        return pltpu.make_async_copy(hop.at[j, p], hop_place(owner(j)[1], p, a, b), own_sems.at[j, p])

    def step3(j):
        if j >= 3:
            sums.step3(j)
            return
        for p, a, b in sums.ways:
            hop[j, p] = sums.total(j, p, a, b)
            here = owner(j)[0] == f
            pl.when(here)(keep_hop(j, p, a, b).start)
            pl.when(jnp.logical_not(here))(send_hop(j, p, a, b).start)

    def step3_own(i):
        head, kind = (3 * f + i) % 8, (3 * f + i) // 8
        for p, a, b in sums.ways:
            ref = hop_place(i, p, a, b)
            coming = remote(ref, ref, hop_s.at[i, p], hop_r.at[i, p], s, head)
            staying = pltpu.make_async_copy(ref, ref, own_sems.at[kind, p])
            pl.when(head != f)(coming.wait_recv)
            pl.when(head == f)(staying.wait)
            sums.send3(i, p, a, b, False).start()

    def small_send(step):
        to = (f + step) % 8
        return remote(wide.at[to], got.at[step - 1], sm_s.at[step - 1], sm_r.at[step - 1], s, to)

    def small_one():
        for to in range(8):
            for v in range(4):
                for half in range(2):
                    at = 256 * to + 128 * half
                    wide[to, 2 * v + half : 2 * v + half + 1, :] = sides[v : v + 1, at : at + 128]
        for step in range(1, 8):
            small_send(step).start()

    def small_two():
        total = wide[f]
        for step in range(1, 8):
            small_send(step).wait_recv()
            total = total + got[step - 1]
        small[0, 0:16] = total
        small[0, 16:32] = more[...]
        small_seq(0).start()

    def small_seq(way):
        return remote(small.at[2 * way], small.at[2 * way + 1], sq_s.at[way], sq_r.at[way], across[way], f)

    def small_three():
        small_seq(0).wait_recv()
        small[2] = small[0] + small[1]
        small_seq(1).start()

    def small_four():
        small_seq(1).wait_recv()
        small_o[...] = small[2] + small[3]

    back = PlaneBack(stage.at[2], u_o, s, f, pb_s, pb_r, self_sem)
    line_sum_step(1, *reduce_args, early.at[:, 0])
    compute(0)
    sums.step1(0)
    compute(1)
    sums.step1(1)
    for it in range(1, 10):
        if it + 1 < PAIRS:
            compute(it + 1)
            sums.step1(it + 1)
        if it - 1 < PAIRS:
            sums.step2(it - 1)
        if 0 <= it - 2 < PAIRS:
            step3(it - 2)
        if it == 4:
            line_sum_step(2, *reduce_args)
        if 5 <= it < 8:
            step3_own(it - 5)
        if 3 <= it - 3 < PAIRS:
            sums.step4(it - 3)
        if 6 <= it < 9:
            sums.step4(it - 6, False)
        if it == 6:
            small_one()
        if it == 7:
            small_two()
        if it == 8:
            small_three()
            line_sum_end(*reduce_args)
            back.start()

    small_four()
    for j in range(PAIRS):
        sums.finish(j)
    for j in range(3):
        for p, a, b in sums.ways:
            pl.when(owner(j)[0] != f)(send_hop(j, p, a, b).wait_send)

    for step in range(1, 8):
        small_send(step).wait_send()
    for way in range(2):
        small_seq(way).wait_send()
    back.wait()


def tail_call(b_all, n_all, plain, u_own, u_sib, early, gain, shift, wide, more):
    width = plain.shape[1]
    anys = pl.BlockSpec(memory_space=pl.ANY)
    vmem = pl.BlockSpec(memory_space=pltpu.VMEM)
    shape = jax.ShapeDtypeStruct
    dma = lambda *n: pltpu.SemaphoreType.DMA(n)
    two = [dma(PAIRS, 2)] * 2
    return pl.pallas_call(
        tail_body,
        in_specs=[anys] * 6 + [vmem] * 4,
        out_specs=[anys] * 3 + [vmem, anys],
        out_shape=[
            shape((1024, width), bf), shape((768, width), bf),
            shape((HALF, width), bf), shape((32, LANES), f32), shape((2, 3, HALF, width), bf),
        ],
        scratch_shapes=[
            pltpu.VMEM((PAIRS, 256, width), bf), pltpu.VMEM((PAIRS, 2, 64, width), bf),
            pltpu.VMEM((PAIRS, 2, 32, width), bf), pltpu.VMEM((3, 2, 32, width), bf),
            pltpu.VMEM((3, HALF, width), bf), pltpu.VMEM((2, HALF, width), bf),
            pltpu.VMEM((2, TOK, 256), bf), pltpu.VMEM((2, TOK, width), bf),
            pltpu.VMEM((256, width), f32), pltpu.VMEM((256, LANES), f32), pltpu.VMEM((256, width), bf),
            pltpu.VMEM((8, width), f32), pltpu.VMEM((8, 16, LANES), f32), pltpu.VMEM((16, LANES), f32),
            pltpu.VMEM((7, 16, LANES), f32), pltpu.VMEM((4, 32, LANES), f32),
            dma(2, 2), pltpu.SemaphoreType.DMA, *two, *two, dma(3, 2), dma(3, 2), *two, *two,
            dma(3), dma(2, 3), dma(2, 3), dma(4), dma(4), dma(7), dma(7), dma(2), dma(2), dma(PAIRS, 2),
            pltpu.SemaphoreType.DMA,
        ],
        compiler_params=pltpu.CompilerParams(
            vmem_limit_bytes=61 * 1024 * 1024, collective_id=2, has_side_effects=True
        ),
        cost_estimate=cost(1e11, 600e6),
        name="tail",
    )(b_all, n_all, plain, u_own, u_sib, early, gain, shift, wide, more)


def pick(slices, which):
    return lax.dynamic_index_in_dim(slices, which, 0, keepdims=False)


def split_body(
    resid_in,
    qkv_weight,
    qkv_bias,
    out_weight,
    out_bias,
    up_weight,
    up_bias,
    down_weight,
    down_bias,
    attn_gain,
    attn_shift,
    mlp_gain,
    mlp_shift,
    block_ids,
    offsets,
    grad_out,
):
    low = jnp.bfloat16
    f32 = jnp.float32
    groups, piece, width = resid_in.shape
    tokens = groups * piece
    s = lax.axis_index("seq")
    f = lax.axis_index("fsdp")
    z, c = f // 2, f % 2
    units = up_weight.shape[0]

    length = block_ids.shape[1]
    own_small = [attn_gain, attn_shift, mlp_gain, mlp_shift, out_bias + down_bias, qkv_bias]
    packed = jnp.concatenate(
        own_small + [block_ids.reshape(-1).astype(f32), offsets.reshape(-1).astype(f32)]
    )
    packed = jnp.pad(packed, (0, 40 * LANES - packed.shape[0])).reshape(40, LANES)
    flat = resid_in.reshape(tokens, width)
    grad_flat = grad_out.reshape(tokens, width)
    own_n, g_low, head_half, small, bias_sum = entry_call(flat, grad_flat, qkv_weight, packed)
    small = small.reshape(8, 40 * LANES)
    gain_a, shift_a, gain_m, shift_m, bias_out = (
        small[:, i * 256 : (i + 1) * 256].reshape(width) for i in range(5)
    )
    head_bias = small[:, 1280:2048].reshape(3, HEADS, HEAD_DIM)
    head_bias = lax.dynamic_index_in_dim(head_bias, f, 1, keepdims=False).reshape(3 * HEAD_DIM)
    ids_end = 2048 + groups * length
    ids_all = small[:, 2048:ids_end].astype(jnp.int32).reshape(-1, 8, LANES)
    starts_all = small[:, ids_end : ids_end + groups * offsets.shape[1]].astype(jnp.int32)
    starts_all = starts_all.reshape(-1, offsets.shape[1])
    gain = jnp.stack([gain_m, gain_a])
    shift = jnp.stack([shift_m, shift_a])
    bias_in = jnp.concatenate([up_bias, head_bias])[None]

    halves = [(2 * (s % 2) + c, c), (2 * (s % 2) + 1 - c, 1 - c)]
    rows_at = [((part - k + 4) % 4) * 2 + core for part, core in halves for k in range(4)]
    ids_slots = [pick(ids_all, block * 4 + s) for block in range(4)]
    ids_here = jnp.stack(
        [jnp.concatenate([pick(row, at) for at in rows_at]) for row in ids_slots]
    ).reshape(4, 1024)
    starts_here = jnp.stack([pick(starts_all, block * 4 + s) for block in range(4)])
    pos = (jnp.stack(rows_at)[:, None] * LANES + jnp.arange(LANES)[None, :]).reshape(1024)
    positions = block_offset(ids_here, starts_here) + pos[None, :]
    lane = jnp.arange(LANES)
    inverse = jnp.exp((lane % 32).astype(f32) * (-2.0 * math.log(10000.0) / ROT_DIM))
    grouped = positions.astype(f32).reshape(4, 4, 256, 1)
    spot = sum(jnp.where(lane // 32 == q, grouped[:, q], 0.0) for q in range(4))
    angles = spot * inverse
    cosine, sine = jnp.cos(angles), jnp.sin(angles)
    ids_col, ids_row = ids_here[:, :, None], ids_here[:, None, :]

    n_all, g_part, w_in, w_out, a_all, slope_all, qkv_all, lse_all, p_own, p_sib = forward_call(
        own_n, g_low, head_half, up_weight, down_weight, out_weight, bias_in, gain, shift,
        cosine, sine, ids_col, ids_row,
    )
    _, b_all, u_own, u_sib, branch, _, early, down_low, out_low, col_sums = backward_call(
        g_part, a_all, w_in, w_out, slope_all, qkv_all, lse_all, p_own, p_sib, gain, cosine, sine, ids_col, ids_row
    )
    result = flat + branch.astype(f32) + bias_out

    slots = jnp.zeros((16, HEAD_DIM), f32)
    slots = lax.dynamic_update_slice(slots, col_sums[0:1], (f, 0))
    slots = lax.dynamic_update_slice(slots, col_sums[1:2], (8 + f, 0))
    spread = jnp.concatenate([jnp.zeros((4, width), f32), bias_sum])
    wide = jnp.concatenate(
        [spread.reshape(5, 8, 256).transpose(1, 0, 2).reshape(8, 5 * 256), slots.reshape(8, 512)], axis=1
    )
    wide = jnp.pad(wide, ((0, 0), (0, 256))).reshape(8, 16, LANES)
    more = jnp.pad(jnp.concatenate([jnp.zeros((units,), f32), col_sums[2]]), (0, 768)).reshape(16, LANES)
    up_low, qkv_low, u, small_sum, _ = tail_call(
        b_all, n_all, w_in, u_own, u_sib, early, gain, shift, wide, more
    )
    u = u.astype(f32)
    center = flat - jnp.mean(flat, axis=-1, keepdims=True)
    inv = lax.rsqrt(jnp.mean(center * center, axis=-1, keepdims=True) + EPS)
    normal = center * inv
    grad_input = grad_flat + inv * (
        u - jnp.mean(u, axis=-1, keepdims=True) - normal * jnp.mean(u * normal, axis=-1, keepdims=True)
    )
    mine = small_sum.reshape(-1)
    vectors = [mine[i * 256 : (i + 1) * 256] for i in range(5)]
    qk_grad = mine[1280:1792]
    up_bias_grad = mine[2048 : 2048 + units]
    value_grad = mine[2048 + units : 2304 + units]
    return (
        result.reshape(groups, piece, width),
        grad_input.reshape(groups, piece, width),
        qkv_low.astype(f32),
        qk_grad,
        value_grad,
        out_low.astype(f32),
        vectors[4],
        up_low.astype(f32),
        up_bias_grad,
        down_low.astype(f32),
        vectors[4],
        vectors[2],
        vectors[3],
        vectors[0],
        vectors[1],
    )


def solution(mesh):
    placed = (
        P("fsdp", "seq", None),
        P("fsdp", None),
        P("fsdp"),
        P("fsdp", None),
        P("fsdp"),
        P("fsdp", None),
        P("fsdp"),
        P("fsdp", None),
        P("fsdp"),
        P("fsdp"),
        P("fsdp"),
        P("fsdp"),
        P("fsdp"),
        P("fsdp", None),
        P("fsdp", None),
        P("fsdp", "seq", None),
    )
    return jax.shard_map(
        split_body if mesh.shape["fsdp"] == HEADS and mesh.shape["seq"] == 4 else body,
        mesh=mesh,
        in_specs=placed,
        out_specs=(
            P("fsdp", "seq", None),
            P("fsdp", "seq", None),
            P("fsdp", None),
            P("fsdp"),
            P("fsdp"),
            P("fsdp", None),
            P("fsdp"),
            P("fsdp", None),
            P("fsdp"),
            P("fsdp", None),
            P("fsdp"),
            P("fsdp"),
            P("fsdp"),
            P("fsdp"),
            P("fsdp"),
        ),
        check_vma=False,
    )
```

```python
import functools
import math

import jax
import jax.numpy as jnp
from jax import lax
from jax.experimental import pallas as pl
from jax.experimental.pallas import tpu as pltpu
from jax.sharding import PartitionSpec as P

HEADS = 8
HEAD_DIM = 256
ROT_DIM = 64


EPS = 1e-05
NEG_FILL = -1e30


def layer_norm(values, gain, shift):
    center = values - jnp.mean(values, axis=-1, keepdims=True)
    spread = jnp.mean(center * center, axis=-1, keepdims=True)
    return center * lax.rsqrt(spread + EPS) * gain + shift


def rotary_tables(positions):
    half = ROT_DIM // 2
    inverse = jnp.exp(jnp.arange(half, dtype=jnp.float32) * (-2.0 * math.log(10000.0) / ROT_DIM))
    angles = positions.astype(jnp.float32)[..., None] * inverse
    return (jnp.cos(angles), jnp.sin(angles))


def block_offset(ids, starts):
    numbers = jnp.arange(starts.shape[1], dtype=jnp.int32)
    match = (ids[:, :, None] == numbers[None, None, :]).astype(jnp.int32)
    return jnp.sum(match * starts[:, None, :], axis=-1)


def rotate(values, cosine, sine):
    half = ROT_DIM // 2
    cosine = cosine[..., None, :]
    sine = sine[..., None, :]
    first = values[..., :half]
    second = values[..., half:ROT_DIM]
    return jnp.concatenate(
        [first * cosine - second * sine, second * cosine + first * sine, values[..., ROT_DIM:]],
        axis=-1,
    )


def gelu_exact(values):
    return jax.nn.gelu(values, approximate=False)


def contract_lead(left, right):
    return lax.dot_general(
        left, right, (((0,), (0,)), ((), ())), preferred_element_type=jnp.float32
    )


def contract_last(left, right):
    return lax.dot_general(
        left, right, (((1,), (1,)), ((), ())), preferred_element_type=jnp.float32
    )


def attend_forward(items):
    query, keys, values, ids = items
    allowed = ids[None, :] <= ids[:, None]
    scores = jnp.where(allowed, contract_last(query, keys) * HEAD_DIM ** (-0.5), NEG_FILL)
    top = jnp.max(scores, axis=1, keepdims=True)
    weights = jnp.exp(scores - top)
    total = jnp.sum(weights, axis=1, keepdims=True)
    probs = (weights / total).astype(jnp.bfloat16)
    mixed = jnp.dot(probs, values, preferred_element_type=jnp.float32).astype(jnp.bfloat16)
    return (mixed, (top + jnp.log(total))[:, 0])


def attend_backward(items):
    query, keys, values, ids, lse_row, grad_mix = items
    scale = HEAD_DIM ** (-0.5)
    allowed = ids[None, :] <= ids[:, None]
    scores = contract_last(query, keys) * scale
    probs = jnp.where(allowed, jnp.exp(scores - lse_row[:, None]), 0.0)
    grad_probs = contract_last(grad_mix, values)
    inner = jnp.sum(probs * grad_probs, axis=1, keepdims=True)
    grad_scores = (probs * (grad_probs - inner)).astype(jnp.bfloat16)
    grad_query = (jnp.dot(grad_scores, keys, preferred_element_type=jnp.float32) * scale).astype(
        jnp.bfloat16
    )
    grad_keys = (contract_lead(grad_scores, query) * scale).astype(jnp.bfloat16)
    grad_values = contract_lead(probs.astype(jnp.bfloat16), grad_mix).astype(jnp.bfloat16)
    return (grad_query, grad_keys, grad_values)


def body(
    resid_in,
    qkv_weight,
    qkv_bias,
    out_weight,
    out_bias,
    up_weight,
    up_bias,
    down_weight,
    down_bias,
    attn_gain,
    attn_shift,
    mlp_gain,
    mlp_shift,
    block_ids,
    offsets,
    grad_out,
):
    groups, piece, width = resid_in.shape
    tokens = groups * piece
    pieces = lax.axis_size("seq")
    length = piece * pieces
    rank = lax.axis_index("fsdp")
    heads_here = HEADS // pieces
    pairs = groups * heads_here
    flat = resid_in.reshape(tokens, width)
    gain_a, shift_a, gain_m, shift_m, proj_bias, attn_bias, hidden_bias, mlp_bias = (
        lax.all_gather(attn_gain, "fsdp", axis=0, tiled=True),
        lax.all_gather(attn_shift, "fsdp", axis=0, tiled=True),
        lax.all_gather(mlp_gain, "fsdp", axis=0, tiled=True),
        lax.all_gather(mlp_shift, "fsdp", axis=0, tiled=True),
        lax.all_gather(qkv_bias, "fsdp", axis=0, tiled=True),
        lax.all_gather(out_bias, "fsdp", axis=0, tiled=True),
        lax.all_gather(up_bias, "fsdp", axis=0, tiled=True),
        lax.all_gather(down_bias, "fsdp", axis=0, tiled=True),
    )
    qkv_low = qkv_weight.astype(jnp.bfloat16)
    out_low = out_weight.astype(jnp.bfloat16)
    up_low = up_weight.astype(jnp.bfloat16)
    down_low = down_weight.astype(jnp.bfloat16)
    qkv_full, out_full = (
        lax.all_gather(qkv_low, "fsdp", axis=0, tiled=True),
        lax.all_gather(out_low, "fsdp", axis=0, tiled=True),
    )
    normed_a32, norm_back_a = jax.vjp(layer_norm, flat, gain_a, shift_a)
    normed_m32, norm_back_m = jax.vjp(layer_norm, flat, gain_m, shift_m)
    normed_attn = normed_a32.astype(jnp.bfloat16)
    normed_mlp = normed_m32.astype(jnp.bfloat16)
    projected = (contract_last(normed_attn, qkv_full) + proj_bias).reshape(
        groups, piece, 3, HEADS, HEAD_DIM
    )
    first_pos = lax.axis_index("seq") * piece
    ids_piece = lax.dynamic_slice_in_dim(block_ids, first_pos, piece, 1)
    positions = (
        block_offset(ids_piece, offsets) + first_pos + jnp.arange(piece, dtype=jnp.int32)[None, :]
    )
    cosine, sine = rotary_tables(positions)
    query = rotate(projected[:, :, 0], cosine, sine)
    keys = rotate(projected[:, :, 1], cosine, sine)
    packed = jnp.stack([query, keys, projected[:, :, 2]], axis=2).astype(jnp.bfloat16)
    heads = lax.all_to_all(packed, "seq", split_axis=3, concat_axis=1, tiled=True)
    stacked = heads.transpose(2, 0, 3, 1, 4).reshape(3, pairs, length, HEAD_DIM)
    ids_pairs = jnp.repeat(block_ids, heads_here, axis=0)
    mixed_pairs, lse_pairs = lax.map(
        attend_forward, (stacked[0], stacked[1], stacked[2], ids_pairs)
    )
    back_heads = mixed_pairs.reshape(groups, heads_here, length, HEAD_DIM).transpose(0, 2, 1, 3)
    mixed_tok = lax.all_to_all(back_heads, "seq", split_axis=1, concat_axis=2, tiled=True).reshape(
        tokens, width
    )
    attn_part = jnp.dot(mixed_tok, out_full, preferred_element_type=jnp.float32) + attn_bias
    units_here = up_weight.shape[0]
    group_rows = lax.all_gather(normed_mlp, "fsdp", axis=0, tiled=True)
    local_bias = lax.dynamic_slice_in_dim(hidden_bias, rank * units_here, units_here)
    hidden = contract_last(group_rows, up_low) + local_bias
    active, gelu_back = jax.vjp(gelu_exact, hidden)
    active_low = active.astype(jnp.bfloat16)
    branch = (
        lax.psum_scatter(
            jnp.dot(active_low, down_low, preferred_element_type=jnp.float32).astype(jnp.bfloat16),
            "fsdp",
            scatter_dimension=0,
            tiled=True,
        ).astype(jnp.float32)
        + mlp_bias
    )
    result = flat + attn_part + branch
    grad_flat = grad_out.reshape(tokens, width)
    grad_low = grad_flat.astype(jnp.bfloat16)
    bias_sum = jnp.sum(grad_flat, axis=0)
    group_grad = lax.all_gather(grad_low, "fsdp", axis=0, tiled=True)
    grad_active = contract_last(group_grad, down_low).astype(jnp.bfloat16)
    grad_hidden = gelu_back(grad_active.astype(jnp.float32))[0]
    grad_hidden_low = grad_hidden.astype(jnp.bfloat16)
    grad_normed_m = lax.psum_scatter(
        jnp.dot(grad_hidden_low, up_low, preferred_element_type=jnp.float32),
        "fsdp",
        scatter_dimension=0,
        tiled=True,
    )
    up_grad_shard = contract_lead(grad_hidden_low, group_rows)
    down_grad_shard = contract_lead(active_low, group_grad)
    local_sum = jnp.sum(grad_hidden, axis=0)
    up_bias_term = lax.dynamic_update_slice_in_dim(
        jnp.zeros((hidden_bias.shape[0],), jnp.float32), local_sum, rank * units_here, 0
    )
    grad_mixed = contract_last(grad_low, out_full).astype(jnp.bfloat16)
    grad_heads = lax.all_to_all(
        grad_mixed.reshape(groups, piece, HEADS, HEAD_DIM),
        "seq",
        split_axis=2,
        concat_axis=1,
        tiled=True,
    )
    grad_pairs = grad_heads.transpose(0, 2, 1, 3).reshape(pairs, length, HEAD_DIM)
    grad_query, grad_keys, grad_values = lax.map(
        attend_backward, (stacked[0], stacked[1], stacked[2], ids_pairs, lse_pairs, grad_pairs)
    )
    grads_stack = (
        jnp.stack([grad_query, grad_keys, grad_values], axis=0)
        .reshape(3, groups, heads_here, length, HEAD_DIM)
        .transpose(1, 3, 0, 2, 4)
    )
    returned = lax.all_to_all(grads_stack, "seq", split_axis=1, concat_axis=3, tiled=True).astype(
        jnp.float32
    )
    grad_projected = jnp.stack(
        [
            rotate(returned[:, :, 0], cosine, -sine),
            rotate(returned[:, :, 1], cosine, -sine),
            returned[:, :, 2],
        ],
        axis=2,
    ).reshape(tokens, 3 * width)
    grad_projected_low = grad_projected.astype(jnp.bfloat16)
    proj_bias_term = jnp.sum(grad_projected, axis=0)
    qk_bias_term = proj_bias_term[: 2 * width]
    value_bias_term = proj_bias_term[2 * width :]
    grad_normed_a = jnp.dot(grad_projected_low, qkv_full, preferred_element_type=jnp.float32)
    grad_from_a, gain_a_term, shift_a_term = norm_back_a(grad_normed_a)
    grad_from_m, gain_m_term, shift_m_term = norm_back_m(grad_normed_m)
    grad_input = grad_flat + grad_from_a + grad_from_m
    qkv_term = contract_lead(grad_projected_low, normed_attn)
    out_term = contract_lead(mixed_tok, grad_low)
    (
        qkv_shard,
        out_shard,
        qk_bias_shard,
        value_bias_shard,
        bias_shard,
        up_bias_shard,
        gain_a_shard,
        shift_a_shard,
        gain_m_shard,
        shift_m_shard,
    ) = (
        lax.psum_scatter(qkv_term, "fsdp", scatter_dimension=0, tiled=True),
        lax.psum_scatter(out_term, "fsdp", scatter_dimension=0, tiled=True),
        lax.psum_scatter(qk_bias_term, "fsdp", scatter_dimension=0, tiled=True),
        lax.psum_scatter(value_bias_term, "fsdp", scatter_dimension=0, tiled=True),
        lax.psum_scatter(bias_sum, "fsdp", scatter_dimension=0, tiled=True),
        lax.psum_scatter(up_bias_term, "fsdp", scatter_dimension=0, tiled=True),
        lax.psum_scatter(gain_a_term, "fsdp", scatter_dimension=0, tiled=True),
        lax.psum_scatter(shift_a_term, "fsdp", scatter_dimension=0, tiled=True),
        lax.psum_scatter(gain_m_term, "fsdp", scatter_dimension=0, tiled=True),
        lax.psum_scatter(shift_m_term, "fsdp", scatter_dimension=0, tiled=True),
    )
    totals = lax.psum(
        (
            qkv_shard,
            out_shard,
            up_grad_shard,
            down_grad_shard,
            qk_bias_shard,
            value_bias_shard,
            bias_shard,
            up_bias_shard,
            gain_a_shard,
            shift_a_shard,
            gain_m_shard,
            shift_m_shard,
        ),
        "seq",
    )
    return (
        result.reshape(groups, piece, width),
        grad_input.reshape(groups, piece, width),
        totals[0],
        totals[4],
        totals[5],
        totals[1],
        totals[6],
        totals[2],
        totals[7],
        totals[3],
        totals[6],
        totals[8],
        totals[9],
        totals[10],
        totals[11],
    )


bf, f32 = jnp.bfloat16, jnp.float32
TOK, HALF = 1024, 512
VM = 56 * 1024 * 1024


def nt(a, b):
    return lax.dot_general(a, b, (((1,), (1,)), ((), ())), preferred_element_type=f32)


def nn(a, b):
    return lax.dot_general(a, b, (((1,), (0,)), ((), ())), preferred_element_type=f32)


def tn(a, b):
    return lax.dot_general(a, b, (((0,), (0,)), ((), ())), preferred_element_type=f32)


def params(n=1, limit=VM):
    return pltpu.CompilerParams(dimension_semantics=("arbitrary",) * n, vmem_limit_bytes=limit)


def cost(flops, nbytes):
    return pl.CostEstimate(flops=int(flops), bytes_accessed=int(nbytes), transcendentals=0)


def turn(head, c, s):
    first = head[:, :128]
    lane = lax.broadcasted_iota(jnp.int32, first.shape, 1)
    partner = jnp.where(lane < 32, pltpu.roll(first, 96, 1), pltpu.roll(first, 32, 1))
    return jnp.concatenate([first * c + partner * s, head[:, 128:]], axis=1)


def gelu_pair(h):
    cdf = 0.5 * (1.0 + lax.erf(h * (0.5**0.5)))
    pdf = jnp.exp(-0.5 * (h * h)) * (1.0 / math.sqrt(2.0 * math.pi))
    return (h * cdf).astype(bf), (cdf + h * pdf).astype(bf)


def h_body(units_tiles, n0, n1, w, b, c, s, act, slope, qkv, x):
    j = pl.program_id(0)

    @pl.when(j == 0)
    def _():
        x[:HALF] = n0[...]
        x[HALF:] = n1[...]

    @pl.when(j < units_tiles)
    def _():
        act[...], slope[...] = gelu_pair(nt(x[...], w[...]) + b[...])

    @pl.when((j >= units_tiles) & (j < units_tiles + 2))
    def _():
        qkv[0] = turn(nt(x[...], w[...]) + b[...], c[0], s[0]).astype(bf)

    @pl.when(j == units_tiles + 2)
    def _():
        qkv[0] = (nt(x[...], w[...]) + b[...]).astype(bf)


def h_call(n0, n1, w, b, c, s, t):
    width = n0.shape[1]
    rows = w.shape[0]
    tile = 256
    units_tiles = (rows - 768) // tile
    full = lambda *shape: pl.BlockSpec(shape, lambda j: (0,) * len(shape))
    return pl.pallas_call(
        functools.partial(h_body, units_tiles),
        grid=(rows // tile,),
        in_specs=[
            full(HALF, width), full(HALF, width),
            pl.BlockSpec((tile, width), lambda j: (j, 0)),
            pl.BlockSpec((1, tile), lambda j: (0, j)),
            pl.BlockSpec((1, TOK, 128), lambda j: (t, 0, 0)), pl.BlockSpec((1, TOK, 128), lambda j: (t, 0, 0)),
        ],
        out_specs=[
            pl.BlockSpec((TOK, tile), lambda j: (0, jnp.minimum(j, units_tiles - 1))),
            pl.BlockSpec((TOK, tile), lambda j: (0, jnp.minimum(j, units_tiles - 1))),
            pl.BlockSpec((1, TOK, tile), lambda j: (jnp.maximum(j - units_tiles, 0), 0, 0)),
        ],
        out_shape=[
            jax.ShapeDtypeStruct((TOK, rows - 768), bf),
            jax.ShapeDtypeStruct((TOK, rows - 768), bf),
            jax.ShapeDtypeStruct((3, TOK, 256), bf),
        ],
        scratch_shapes=[pltpu.VMEM((TOK, width), bf)],
        compiler_params=params(),
        cost_estimate=cost(2 * TOK * width * rows, 24e6),
        name="project",
    )(n0, n1, w, b, c, s)


def attn_body(q, k, v, idq, idk, mixed, lse):
    scores = nt(q[0], k[0]) * (256 ** -0.5)
    allowed = idk[0] <= idq[0]
    scores = jnp.where(allowed, scores, -1e30)
    top = jnp.max(scores, axis=1, keepdims=True)
    weights = jnp.exp(scores - top)
    total = jnp.sum(weights, axis=1, keepdims=True)
    probs = (weights / total).astype(bf)
    mixed[...] = nn(probs, v[0]).astype(bf)
    lse[...] = top + jnp.log(total)


def attn_call(qkv, ids_col, ids_row, t):
    tile = 256
    return pl.pallas_call(
        attn_body,
        grid=(TOK // tile,),
        in_specs=[
            pl.BlockSpec((1, tile, 256), lambda i: (0, i, 0)),
            pl.BlockSpec((1, TOK, 256), lambda i: (1, 0, 0)),
            pl.BlockSpec((1, TOK, 256), lambda i: (2, 0, 0)),
            pl.BlockSpec((1, tile, 1), lambda i: (t, i, 0)),
            pl.BlockSpec((1, 1, TOK), lambda i: (t, 0, 0)),
        ],
        out_specs=[
            pl.BlockSpec((tile, 256), lambda i: (i, 0)),
            pl.BlockSpec((tile, 1), lambda i: (i, 0)),
        ],
        out_shape=[jax.ShapeDtypeStruct((TOK, 256), bf), jax.ShapeDtypeStruct((TOK, 1), f32)],
        compiler_params=params(),
        cost_estimate=cost(4 * TOK * TOK * 256, 4e6),
        name="attend",
    )(qkv, qkv, qkv, ids_col, ids_row)


def attn_back_body(q, k, v, g, idq, idk, lse, cq, sq, ck, sk, out_q, out_kv, sums, acc_k, acc_v, acc_s):
    i = pl.program_id(0)
    last = pl.num_programs(0) - 1
    scale = 256 ** -0.5

    @pl.when(i == 0)
    def _():
        acc_k[...] = jnp.zeros_like(acc_k)
        acc_v[...] = jnp.zeros_like(acc_v)
        acc_s[...] = jnp.zeros_like(acc_s)

    scores = nt(q[0], k[0]) * scale
    allowed = idk[0] <= idq[0]
    probs = jnp.where(allowed, jnp.exp(scores - lse[...]), 0.0)
    grad_probs = nt(g[...], v[0])
    inner = jnp.sum(probs * grad_probs, axis=1, keepdims=True)
    gs = (probs * (grad_probs - inner)).astype(bf)
    gq = (nn(gs, k[0]) * scale).astype(bf).astype(f32)
    gq = turn(gq, cq[0], -sq[0])
    acc_s[0:1, :] += jnp.sum(gq, axis=0, keepdims=True)
    out_q[0] = gq.astype(bf)
    acc_k[...] += tn(gs, q[0])
    acc_v[...] += tn(probs.astype(bf), g[...])

    @pl.when(i == last)
    def _():
        gk = (acc_k[...] * scale).astype(bf).astype(f32)
        gk = turn(gk, ck[0], -sk[0])
        out_kv[0] = gk.astype(bf)
        gv = acc_v[...].astype(bf)
        out_kv[1] = gv
        acc_s[1:2, :] = jnp.sum(gk, axis=0, keepdims=True)
        acc_s[2:3, :] = jnp.sum(gv.astype(f32), axis=0, keepdims=True)
        sums[...] = acc_s[...]


def attn_back_call(qkv, gmix, ids_col, ids_row, lse, c, s, t):
    tile = 256
    return pl.pallas_call(
        attn_back_body,
        grid=(TOK // tile,),
        in_specs=[
            pl.BlockSpec((1, tile, 256), lambda i: (0, i, 0)),
            pl.BlockSpec((1, TOK, 256), lambda i: (1, 0, 0)),
            pl.BlockSpec((1, TOK, 256), lambda i: (2, 0, 0)),
            pl.BlockSpec((tile, 256), lambda i: (i, 0)),
            pl.BlockSpec((1, tile, 1), lambda i: (t, i, 0)),
            pl.BlockSpec((1, 1, TOK), lambda i: (t, 0, 0)),
            pl.BlockSpec((tile, 1), lambda i: (i, 0)),
            pl.BlockSpec((1, tile, 128), lambda i: (t, i, 0)),
            pl.BlockSpec((1, tile, 128), lambda i: (t, i, 0)),
            pl.BlockSpec((1, TOK, 128), lambda i: (t, 0, 0)),
            pl.BlockSpec((1, TOK, 128), lambda i: (t, 0, 0)),
        ],
        out_specs=[
            pl.BlockSpec((1, tile, 256), lambda i: (0, i, 0)),
            pl.BlockSpec((2, TOK, 256), lambda i: (0, 0, 0)),
            pl.BlockSpec((8, 256), lambda i: (0, 0)),
        ],
        out_shape=[
            jax.ShapeDtypeStruct((1, TOK, 256), bf),
            jax.ShapeDtypeStruct((2, TOK, 256), bf),
            jax.ShapeDtypeStruct((8, 256), f32),
        ],
        scratch_shapes=[pltpu.VMEM((TOK, 256), f32), pltpu.VMEM((TOK, 256), f32), pltpu.VMEM((8, 256), f32)],
        compiler_params=params(),
        cost_estimate=cost(10 * TOK * TOK * 256, 6e6),
        name="attend_back",
    )(qkv, qkv, qkv, gmix, ids_col, ids_row, lse, c, s, c, s)


def p_body(act, mixed, wd, wo, own, sib):
    out = nn(act[...], wd[...]) + nn(mixed[...], wo[...])
    own[...] = out[:HALF]
    sib[...] = out[HALF:].astype(bf)


def p_call(act, mixed, w):
    units, width = act.shape[1], w.shape[1]
    tile = 256
    full = lambda *shape: pl.BlockSpec(shape, lambda j: (0,) * len(shape))
    return pl.pallas_call(
        p_body,
        grid=(width // tile,),
        in_specs=[
            full(TOK, units), full(TOK, 256),
            pl.BlockSpec((units, tile), lambda j: (0, j)),
            pl.BlockSpec((256, tile), lambda j: (units // 256, j)),
        ],
        out_specs=[pl.BlockSpec((HALF, tile), lambda j: (0, j))] * 2,
        out_shape=[jax.ShapeDtypeStruct((HALF, width), f32), jax.ShapeDtypeStruct((HALF, width), bf)],
        compiler_params=params(),
        cost_estimate=cost(2 * TOK * width * (units + 256), 16e6),
        name="combine",
    )(act, mixed, w, w)


def ga_body(units_tiles, g0, g1, w, slope, gh, gmix, x):
    j = pl.program_id(0)

    @pl.when(j == 0)
    def _():
        x[:HALF] = g0[...]
        x[HALF:] = g1[...]

    ga = nt(x[...], w[...]).astype(bf)

    @pl.when(j < units_tiles)
    def _():
        gh[...] = (ga.astype(f32) * slope[...].astype(f32)).astype(bf)

    @pl.when(j == units_tiles)
    def _():
        gmix[...] = ga


def ga_call(g0, g1, w, slope):
    width, rows = w.shape[1], w.shape[0]
    tile = 256
    units_tiles = rows // tile - 1
    full = lambda *shape: pl.BlockSpec(shape, lambda j: (0,) * len(shape))
    return pl.pallas_call(
        functools.partial(ga_body, units_tiles),
        grid=(rows // tile,),
        in_specs=[
            full(HALF, width), full(HALF, width),
            pl.BlockSpec((tile, width), lambda j: (j, 0)),
            pl.BlockSpec((TOK, tile), lambda j: (0, jnp.minimum(j, units_tiles - 1))),
        ],
        out_specs=[
            pl.BlockSpec((TOK, tile), lambda j: (0, jnp.minimum(j, units_tiles - 1))),
            full(TOK, 256),
        ],
        out_shape=[jax.ShapeDtypeStruct((TOK, rows - 256), bf), jax.ShapeDtypeStruct((TOK, 256), bf)],
        scratch_shapes=[pltpu.VMEM((TOK, width), bf)],
        compiler_params=params(),
        cost_estimate=cost(2 * TOK * width * rows, 16e6),
        name="pull",
    )(g0, g1, w, slope)


def u_body(gh, gq, gkv, wu, wq, own, sib):
    out = nn(gh[...], wu[...]) + nn(gq[0], wq[0:256]) + nn(gkv[0], wq[256:512]) + nn(gkv[1], wq[512:768])
    own[...] = out[:HALF]
    sib[...] = out[HALF:].astype(bf)


def u_call(gh, gq, gkv, w_up, w_qkv):
    units, width = gh.shape[1], w_up.shape[1]
    tile = 256
    full = lambda *shape: pl.BlockSpec(shape, lambda j: (0,) * len(shape))
    return pl.pallas_call(
        u_body,
        grid=(width // tile,),
        in_specs=[
            full(TOK, units), full(1, TOK, 256), full(2, TOK, 256),
            pl.BlockSpec((units, tile), lambda j: (0, j)),
            pl.BlockSpec((768, tile), lambda j: (0, j)),
        ],
        out_specs=[pl.BlockSpec((HALF, tile), lambda j: (0, j))] * 2,
        out_shape=[jax.ShapeDtypeStruct((HALF, width), f32), jax.ShapeDtypeStruct((HALF, width), bf)],
        compiler_params=params(),
        cost_estimate=cost(2 * TOK * width * (units + 768), 20e6),
        name="push",
    )(gh, gq, gkv, w_up, w_qkv)


LANES = 128


MESH = pl.DeviceIdType.MESH


def line_order(z, t):
    near = jnp.where(z < 2, z + 1, z - 1)
    mid = jnp.where(z == 0, 2, jnp.where(z == 1, 0, jnp.where(z == 2, 3, 1)))
    far = jnp.where(z < 2, 3, 0)
    return jnp.where(t == 0, z, jnp.where(t == 1, near, jnp.where(t == 2, mid, far)))


def remote(src, dst, send, recv, s, f):
    return pltpu.make_async_remote_copy(
        src_ref=src, dst_ref=dst, send_sem=send, recv_sem=recv, device_id=(s, f), device_id_type=MESH
    )


def line_barrier(s, f, z):
    barrier = pltpu.get_barrier_semaphore()

    @pl.when(z < 3)
    def _():
        pl.semaphore_signal(barrier, inc=1, device_id=(s, f + 2), device_id_type=MESH)

    @pl.when(z > 0)
    def _():
        pl.semaphore_signal(barrier, inc=1, device_id=(s, f - 2), device_id_type=MESH)

    pl.semaphore_signal(barrier, inc=1, device_id=(s, f + 1 - 2 * (f % 2)), device_id_type=MESH)

    @pl.when((z == 0) | (z == 3))
    def _():
        pl.semaphore_wait(barrier, 2)

    @pl.when((z == 1) | (z == 2))
    def _():
        pl.semaphore_wait(barrier, 3)


def near_barrier(s, f):
    barrier = pltpu.get_barrier_semaphore()
    c = f % 2
    for step in range(1, 8):
        pl.semaphore_signal(barrier, inc=1, device_id=(s, (f + step) % 8), device_id_type=MESH)
    for step in range(1, 4):
        for core in range(2):
            pl.semaphore_signal(
                barrier, inc=1, device_id=((s + step) % 4, f - c + core), device_id_type=MESH
            )
    pl.semaphore_wait(barrier, 13)


class PlaneOut:
    def __init__(self, src, dst, s, f, send, recv, own_sem):
        c = f % 2
        mine = 2 * (s % 2) + c
        self.parts = []
        for j in range(4):
            k = (j - s + 4) % 4
            to_s, to_f = 2 * c + j // 2, f - c + j % 2
            place = dst.at[pl.ds(pl.multiple_of(128 * k, 128), 128)]
            here = (to_s == s) & (to_f == f)
            self.parts.append(
                (
                    here,
                    pltpu.make_async_copy(src.at[j], place, own_sem),
                    remote(src.at[j], place, send.at[j], recv.at[k], to_s, to_f),
                )
            )
        self.comes = []
        for k in range(4):
            from_s, from_f = (mine - k + 4) % 4, f - c + s // 2
            ref = dst.at[pl.ds(128 * k, 128)]
            away = jnp.logical_not((from_s == s) & (from_f == f))
            self.comes.append((away, remote(ref, ref, send.at[k], recv.at[k], from_s, from_f)))

    def start(self, j):
        here, local, away = self.parts[j]
        pl.when(here)(local.start)
        pl.when(jnp.logical_not(here))(away.start)

    def arrive(self):
        for here, local, away in self.parts:
            pl.when(here)(local.wait)
        for away, copy in self.comes:
            pl.when(away)(copy.wait_recv)

    def sent(self):
        for here, local, away in self.parts:
            pl.when(jnp.logical_not(here))(away.wait_send)

    def wait(self):
        self.arrive()
        self.sent()


def expand_tables(cos4, sin4, b, cos, sin):
    lane = lax.broadcasted_iota(jnp.int32, (256, LANES), 1)
    for q in range(4):
        at = pl.ds(256 * q, 256)
        c, s_ = cos4[b], sin4[b]
        if q > 0:
            c, s_ = pltpu.roll(c, 128 - 32 * q, 1), pltpu.roll(s_, 128 - 32 * q, 1)
        cos[at, :] = jnp.where(lane < 32, c, jnp.where(lane < 64, pltpu.roll(c, 32, 1), 1.0))
        sin[at, :] = jnp.where(lane < 32, -s_, jnp.where(lane < 64, pltpu.roll(s_, 32, 1), 0.0))


class PlaneBack:
    def __init__(self, src, dst, s, f, send, recv, own_sem):
        c = f % 2
        mine = 2 * (s % 2) + c
        self.parts = []
        for k in range(4):
            to_s, to_f = (mine - k + 4) % 4, f - c + s // 2
            piece = src.at[pl.ds(128 * k, 128)]
            place = dst.at[pl.ds(pl.multiple_of(128 * mine, 128), 128)]
            here = (to_s == s) & (to_f == f)
            self.parts.append(
                (
                    here,
                    pltpu.make_async_copy(piece, place, own_sem),
                    remote(piece, place, send.at[k], recv.at[mine], to_s, to_f),
                )
            )
        self.comes = []
        for part in range(4):
            from_s, from_f = 2 * c + part // 2, f - c + part % 2
            ref = dst.at[pl.ds(128 * part, 128)]
            away = jnp.logical_not((from_s == s) & (from_f == f))
            self.comes.append((away, remote(ref, ref, send.at[part], recv.at[part], from_s, from_f)))

    def start(self):
        for here, local, away in self.parts:
            pl.when(here)(local.start)
            pl.when(jnp.logical_not(here))(away.start)

    def wait(self):
        for here, local, away in self.parts:
            pl.when(here)(local.wait)
            pl.when(jnp.logical_not(here))(away.wait_send)
        for away, copy in self.comes:
            pl.when(away)(copy.wait_recv)


def line_step(buf, k, z, s, f, sems, held=None):
    send_up, recv_up, send_dn, recv_dn = sems
    own = pl.ds(0, HALF)

    @pl.when((z - k >= 0) & (z < 3))
    def _():
        ref = buf.at[z - k, own]
        remote(ref if held is None else held, ref, send_up.at[k], recv_up.at[k], s, f + 2).start()

    @pl.when((z + k <= 3) & (z > 0))
    def _():
        ref = buf.at[z + k, own]
        remote(ref if held is None else held, ref, send_dn.at[k], recv_dn.at[k], s, f - 2).start()


def line_arrive(buf, k, z, s, f, sems):
    send_up, recv_up, send_dn, recv_dn = sems
    own = pl.ds(0, HALF)

    @pl.when(z - 1 - k >= 0)
    def _():
        ref = buf.at[z - 1 - k, own]
        remote(ref, ref, send_up.at[k], recv_up.at[k], s, f - 2).wait_recv()

    @pl.when(z + 1 + k <= 3)
    def _():
        ref = buf.at[z + 1 + k, own]
        remote(ref, ref, send_dn.at[k], recv_dn.at[k], s, f + 2).wait_recv()


def line_sent(buf, k, z, s, f, sems):
    send_up, recv_up, send_dn, recv_dn = sems
    own = pl.ds(0, HALF)

    @pl.when((z - k >= 0) & (z < 3))
    def _():
        ref = buf.at[z - k, own]
        remote(ref, ref, send_up.at[k], recv_up.at[k], s, f + 2).wait_send()

    @pl.when((z + k <= 3) & (z > 0))
    def _():
        ref = buf.at[z + k, own]
        remote(ref, ref, send_dn.at[k], recv_dn.at[k], s, f - 2).wait_send()


def core_copy(buf, b, s, f, sems, held=None):
    send, recv = sems
    return remote(
        buf.at[b, pl.ds(0, HALF)] if held is None else held, buf.at[b, pl.ds(HALF, HALF)], send.at[b], recv.at[b], s, f + 1 - 2 * (f % 2)
    )


def new_blocks(k, z, act):
    if k == 0:
        act(z)
        return

    @pl.when(z - k >= 0)
    def _():
        act(z - k)

    @pl.when(z + k <= 3)
    def _():
        act(z + k)


def forward_body(
    own_n, g_low, heads, up_h, down_h, out_h, bias, gain, shift, cos4, sin4, idc, idr,
    n_all, g_all, w_in_o, w_out_o, a_all, slope_o, qkv_o, lse_o, own_o, sib_o,
    w_in, w_out, x, normed, act, slope, qkv, mixed, lse, p_own, p_sib, g_out, wide, cos, sin,
    load, w_load, w_store, line_n0, line_n1, line_n2, line_n3, line_g0, line_g1, line_g2, line_g3,
    core_n0, core_n1, core_p0, core_p1, out_sems, po_s, po_r, h_s, h_r,
):
    s, f = lax.axis_index("seq"), lax.axis_index("fsdp")
    z = f // 2
    line_n, line_g = (line_n0, line_n1, line_n2, line_n3), (line_g0, line_g1, line_g2, line_g3)
    core_n, core_p = (core_n0, core_n1), (core_p0, core_p1)
    own, other = pl.ds(0, HALF), pl.ds(HALF, HALF)
    units = act.shape[1]
    half = (s % 2 + s // 2) % 2
    across = (s + 1 - 2 * (s % 2), (s + 2) % 4)

    def head_rows(kind, which, count, start=0):
        return w_in.at[pl.ds(pl.multiple_of(units + 256 * kind + 128 * which + start, 64), count)]

    first = [pltpu.make_async_copy(own_n, x.at[own], load.at[0])] + [
        pltpu.make_async_copy(g_low.at[pl.ds(128 * j, 128)], g_out.at[j], load.at[1 + j]) for j in range(4)
    ]
    held = [pltpu.make_async_copy(heads.at[i], head_rows(i, half, 128), load.at[5 + i]) for i in range(3)]
    keep = pltpu.make_async_copy(x.at[own], n_all.at[z, own], load.at[0])
    chunks = [(up_h, w_in, i) for i in range(units // 256)]
    chunks += [(down_h, w_out, i) for i in range(units // 256)] + [(out_h, w_out, units // 256)]

    def chunk_load(i):
        src, dst, at = chunks[i]
        place = at if src is not out_h else 0
        return pltpu.make_async_copy(src.at[pl.ds(256 * place, 256)], wide.at[i % 2], w_load.at[i % 2])

    def send_head(kind, way):
        return remote(
            heads.at[kind, pl.ds(64 * way, 64)], head_rows(kind, half, 64, 64 * way),
            h_s.at[kind, way], h_r.at[kind, way], across[way], f,
        )

    def come_head(kind, way):
        ref = head_rows(kind, 1 - half, 64, 64 * way)
        return remote(ref, ref, h_s.at[kind, way], h_r.at[kind, way], across[way], f)

    for copy in first + held:
        copy.start()
    chunk_load(0).start()
    near_barrier(s, f)
    spread = PlaneOut(g_out, g_all.at[z, own], s, f, po_s, po_r, load.at[8])
    store = [pltpu.make_async_copy(w_in, w_in_o, w_store.at[0]), pltpu.make_async_copy(w_out, w_out_o, w_store.at[1])]

    def outs(b):
        pairs = [
            (act, a_all.at[b, :, pl.ds(0, units)]), (mixed, a_all.at[b, :, pl.ds(units, 256)]),
            (slope, slope_o.at[b]), (qkv, qkv_o.at[b]), (lse, lse_o.at[b]), (p_own, own_o.at[b]),
        ]
        return [pltpu.make_async_copy(src, dst, out_sems.at[i]) for i, (src, dst) in enumerate(pairs)]

    def send_sib(b):
        return remote(p_sib, sib_o.at[b], core_p[0].at[b], core_p[1].at[b], s, f + 1 - 2 * (f % 2))

    def pass_on(t):
        line_arrive(n_all, t - 1, z, s, f, line_n)
        if t < 3:
            line_step(n_all, t, z, s, f, line_n)
        else:
            spread.arrive()
            line_step(g_all, 0, z, s, f, line_g)
        new_blocks(t, z, lambda v: core_copy(n_all, v, s, f, core_n).start())

    for t in range(4):
        b = line_order(z, t)
        low_half = pltpu.make_async_copy(n_all.at[b, other], x.at[other], load.at[9])
        if t == 0:
            line_step(n_all, 0, z, s, f, line_n, own_n)
            core_copy(n_all, z, s, f, core_n, own_n).start()
            for kind in range(3):
                for way in range(2):
                    send_head(kind, way).start()
            first[0].wait()
            keep.start()
            for i, (src, dst, at) in enumerate(chunks):
                if i + 1 < len(chunks):
                    chunk_load(i + 1).start()
                chunk_load(i).wait()
                dst[pl.ds(256 * at, 256), :] = wide[i % 2].astype(bf)
            for copy in first[1:]:
                copy.wait()
        else:
            if t > 1:
                pass_on(t)
            top = pltpu.make_async_copy(n_all.at[b, own], x.at[own], load.at[0])
            top.start()
        if t == 1:
            for j in range(4):
                spread.start(j)
        core_copy(n_all, b, s, f, core_n).wait_recv()
        low_half.start()
        expand_tables(cos4, sin4, b, cos, sin)
        if t == 0:
            keep.wait()
        else:
            top.wait()
            before = line_order(z, t - 1)
            for copy in outs(before):
                copy.wait()
            send_sib(before).wait_send()
        low_half.wait()

        def norm(which):
            @pl.loop(0, TOK // 64)
            def _(i):
                at = pl.ds(pl.multiple_of(i * 64, 64), 64)
                value = x[at, :].astype(f32) * gain[which : which + 1, :] + shift[which : which + 1, :]
                normed[at, :] = value.astype(bf)

        norm(0)

        @pl.loop(0, units // 256)
        def _(j):
            at = pl.ds(pl.multiple_of(j * 256, 256), 256)
            h = nt(normed[...], w_in[at, :]) + bias[:, at]
            act[:, at], slope[:, at] = gelu_pair(h)

        norm(1)
        if t == 0:
            for copy in held:
                copy.wait()
            for kind in range(3):
                for way in range(2):
                    come_head(kind, way).wait_recv()
            for copy in store:
                copy.start()

        @pl.loop(0, 2)
        def _(j):
            at = pl.ds(pl.multiple_of(units + j * 256, 256), 256)
            h = nt(normed[...], w_in[at, :]) + bias[:, at]
            qkv[j] = turn(h, cos[...], sin[...]).astype(bf)

        at = pl.ds(units + 512, 256)
        qkv[2] = (nt(normed[...], w_in[at, :]) + bias[:, at]).astype(bf)

        @pl.loop(0, TOK // 256)
        def _(i):
            rows = pl.ds(pl.multiple_of(i * 256, 256), 256)
            scores = nt(qkv[0, rows, :], qkv[1]) * (256 ** -0.5)
            scores = jnp.where(idr[b] <= idc[b, rows, :], scores, -1e30)
            top_score = jnp.max(scores, axis=1, keepdims=True)
            weights = jnp.exp(scores - top_score)
            total = jnp.sum(weights, axis=1, keepdims=True)
            probs = (weights / total).astype(bf)
            mixed[rows, :] = nn(probs, qkv[2]).astype(bf)
            lse[rows, :] = jnp.broadcast_to(top_score + jnp.log(total), (256, LANES))

        if t == 0:
            pass_on(1)

        @pl.loop(0, p_own.shape[1] // 256)
        def _(j):
            at = pl.ds(pl.multiple_of(j * 256, 256), 256)
            out = nn(act[...], w_out[pl.ds(0, units), at]) + nn(mixed[...], w_out[pl.ds(units, 256), at])
            p_own[:, at] = out[:HALF].astype(bf)
            p_sib[:, at] = out[HALF:].astype(bf)

        for copy in outs(b):
            copy.start()
        send_sib(b).start()

    last = line_order(z, 3)
    for copy in outs(last):
        copy.wait()
    send_sib(last).wait_send()
    for b in range(4):
        core_copy(n_all, b, s, f, core_n).wait_send()
        send_sib(b).wait_recv()
    for k in range(3):
        line_sent(n_all, k, z, s, f, line_n)
    line_arrive(g_all, 0, z, s, f, line_g)
    line_sent(g_all, 0, z, s, f, line_g)
    spread.sent()
    for copy in store:
        copy.wait()
    for kind in range(3):
        for way in range(2):
            send_head(kind, way).wait_send()


def forward_call(own_n, g_low, heads, up, down, out, bias, gain, shift, cos4, sin4, ids_col, ids_row):
    width, units = up.shape[1], up.shape[0]
    anys = pl.BlockSpec(memory_space=pl.ANY)
    vmem = pl.BlockSpec(memory_space=pltpu.VMEM)
    shape = jax.ShapeDtypeStruct
    dma = lambda *n: pltpu.SemaphoreType.DMA(n)
    return pl.pallas_call(
        forward_body,
        in_specs=[anys] * 6 + [vmem] * 7,
        out_specs=[anys] * 10,
        out_shape=[
            shape((4, TOK, width), bf), shape((4, TOK, width), bf),
            shape((units + 768, width), bf), shape((units + 256, width), bf),
            shape((4, TOK, units + 256), bf), shape((4, TOK, units), bf), shape((4, 3, TOK, 256), bf),
            shape((4, TOK, LANES), f32), shape((4, HALF, width), bf), shape((4, HALF, width), bf),
        ],
        scratch_shapes=[
            pltpu.VMEM((units + 768, width), bf), pltpu.VMEM((units + 256, width), bf),
            pltpu.VMEM((TOK, width), bf), pltpu.VMEM((TOK, width), bf),
            pltpu.VMEM((TOK, units), bf), pltpu.VMEM((TOK, units), bf), pltpu.VMEM((3, TOK, 256), bf),
            pltpu.VMEM((TOK, 256), bf), pltpu.VMEM((TOK, LANES), f32),
            pltpu.VMEM((HALF, width), bf), pltpu.VMEM((HALF, width), bf),
            pltpu.VMEM((4, 128, width), bf), pltpu.VMEM((2, 256, width), f32),
            pltpu.VMEM((TOK, LANES), f32), pltpu.VMEM((TOK, LANES), f32),
            dma(10), dma(2), dma(2), dma(3), dma(3), dma(3), dma(3), dma(3), dma(3), dma(3), dma(3),
            dma(4), dma(4), dma(4), dma(4), dma(6), dma(4), dma(4), dma(3, 2), dma(3, 2),
        ],
        compiler_params=pltpu.CompilerParams(
            vmem_limit_bytes=60 * 1024 * 1024, collective_id=0, has_side_effects=True
        ),
        cost_estimate=cost(8 * TOK * width * (2 * units + 1024), 200e6),
        name="forward",
    )(own_n, g_low, heads, up, down, out, bias, gain, shift, cos4, sin4, ids_col, ids_row)


def entry_body(
    resid, grad, qkv, packed, own_n, g_low, heads, small_all, bias_sum,
    x_in, g_in, q_in, n_out, g_out, q_out,
    load, q_s, q_r, po_s, po_r, sm_s, sm_r, own_sems,
):
    s, f = lax.axis_index("seq"), lax.axis_index("fsdp")
    half = (s % 2 + s // 2) % 2
    width = resid.shape[1]
    parts = [pltpu.make_async_copy(resid.at[pl.ds(128 * j, 128)], x_in.at[j], load.at[j]) for j in range(4)]
    pulls = [pltpu.make_async_copy(grad.at[pl.ds(128 * j, 128)], g_in.at[j], load.at[4 + j]) for j in range(4)]
    rows = [
        pltpu.make_async_copy(
            qkv.at[pl.ds(pl.multiple_of(256 * i + 128 * half, 128), 128)], q_in.at[i], load.at[8 + i]
        )
        for i in range(3)
    ]
    for copy in rows + parts + pulls:
        copy.start()
    near_barrier(s, f)
    keep_small = pltpu.make_async_copy(packed, small_all.at[f], own_sems.at[0])
    keep_small.start()

    def send_small(step):
        to = (f + step) % 8
        return remote(packed, small_all.at[f], sm_s.at[step - 1], sm_r.at[step - 1], s, to)

    for step in range(1, 8):
        send_small(step).start()

    def hop(i):
        head = 3 * f + i
        return remote(q_out.at[i], heads.at[head // 8], q_s.at[i], q_r.at[head // 8], s, head % 8)

    def keep_hop(i):
        return pltpu.make_async_copy(q_out.at[i], heads.at[(3 * f + i) // 8], own_sems.at[1])

    for i in range(3):
        rows[i].wait()
        q_out[i] = q_in[i].astype(bf)
        here = (3 * f + i) % 8 == f
        pl.when(here)(keep_hop(i).start)
        pl.when(jnp.logical_not(here))(hop(i).start)

    out = PlaneOut(n_out, own_n, s, f, po_s, po_r, own_sems.at[2])
    for j in range(4):
        parts[j].wait()

        @pl.loop(0, 4)
        def _(i):
            at = pl.ds(pl.multiple_of(32 * i, 32), 32)
            value = x_in[j, at, :]
            mean = jnp.sum(value, axis=1, keepdims=True) * (1.0 / width)
            center = value - mean
            spread = jnp.sum(center * center, axis=1, keepdims=True) * (1.0 / width)
            inv = lax.rsqrt(spread + EPS)
            n_out[j, at, :] = (center * inv).astype(bf)

        out.start(j)
    for j in range(4):
        pulls[j].wait()
        g_out[j] = g_in[j].astype(bf)
        part = jnp.sum(g_in[j], axis=0, keepdims=True)
        bias_sum[...] = part if j == 0 else bias_sum[...] + part
    keep_g = [
        pltpu.make_async_copy(g_out.at[j], g_low.at[pl.ds(128 * j, 128)], load.at[j]) for j in range(4)
    ]
    for copy in keep_g:
        copy.start()
    keep_small.wait()
    for step in range(1, 8):
        send_small(step).wait_send()
        at = (f + 8 - step) % 8
        remote(packed, small_all.at[at], sm_s.at[step - 1], sm_r.at[step - 1], s, at).wait_recv()
    for kind in range(3):
        frm = (8 * kind + f) // 3
        ref = heads.at[kind]
        away = remote(ref, ref, q_s.at[kind], q_r.at[kind], s, frm)
        pl.when(frm != f)(away.wait_recv)
    for i in range(3):
        here = (3 * f + i) % 8 == f
        pl.when(here)(keep_hop(i).wait)
        pl.when(jnp.logical_not(here))(hop(i).wait_send)
    out.wait()
    for copy in keep_g:
        copy.wait()


def entry_call(resid, grad, qkv, packed):
    width = resid.shape[1]
    anys = pl.BlockSpec(memory_space=pl.ANY)
    vmem = pl.BlockSpec(memory_space=pltpu.VMEM)
    shape = jax.ShapeDtypeStruct
    dma = lambda n: pltpu.SemaphoreType.DMA((n,))
    return pl.pallas_call(
        entry_body,
        in_specs=[anys] * 3 + [vmem],
        out_specs=[anys] * 4 + [vmem],
        out_shape=[
            shape((HALF, width), bf), shape((HALF, width), bf), shape((3, 128, width), bf),
            shape((8,) + packed.shape, f32), shape((1, width), f32),
        ],
        scratch_shapes=[
            pltpu.VMEM((4, 128, width), f32), pltpu.VMEM((4, 128, width), f32), pltpu.VMEM((3, 128, width), f32),
            pltpu.VMEM((4, 128, width), bf), pltpu.VMEM((4, 128, width), bf), pltpu.VMEM((3, 128, width), bf),
            dma(11), dma(3), dma(3), dma(4), dma(4), dma(7), dma(7), dma(3),
        ],
        compiler_params=pltpu.CompilerParams(
            vmem_limit_bytes=60 * 1024 * 1024, collective_id=3, has_side_effects=True
        ),
        cost_estimate=cost(1e7, 20e6),
        name="entry",
    )(resid, grad, qkv, packed)


class SeqSum:
    def __init__(self, term, r1, r2, sems, own_sems, result, s, f):
        self.term, self.r1, self.r2, self.own_sems, self.result, self.f = term, r1, r2, own_sems, result, f
        self.sems = sems
        x, y = s % 2, s // 2
        self.across = (s + 1 - 2 * x, (s + 2) % 4)
        self.ways = ((0, x, y), (1, y, x))

    @staticmethod
    def rows(start, count):
        return pl.ds(pl.multiple_of(start, 32), count)

    @staticmethod
    def base(p, a, b):
        return 128 * p + 64 * a + 32 * b

    def copy(self, step, src, dst, j, p):
        to = self.across[p if step in (1, 4) else 1 - p]
        send, recv = self.sems[2 * step - 2 : 2 * step]
        return remote(src, dst, send.at[j, p], recv.at[j, p], to, self.f)

    def send1(self, j, p, a):
        return self.copy(1, self.term.at[j, self.rows(128 * p + 64 * (1 - a), 64)], self.r1.at[j, p], j, p)

    def send2(self, j, p, a, b):
        return self.copy(2, self.term.at[j, self.rows(self.base(p, a, 1 - b), 32)], self.r2.at[j, p], j, p)

    def keep3(self, j, p, a, b):
        at = self.base(p, a, b)
        return pltpu.make_async_copy(self.term.at[j, self.rows(at, 32)], self.result(j, at, 32), self.own_sems.at[j, p])

    def send3(self, j, p, a, b, held=True):
        at = self.base(p, a, b)
        ref = self.result(j, at, 32)
        return self.copy(3, self.term.at[j, self.rows(at, 32)] if held else ref, ref, j, p)

    def send4(self, j, p, a):
        ref = self.result(j, 128 * p + 64 * a, 64)
        return self.copy(4, ref, ref, j, p)

    def step1(self, j):
        for p, a, b in self.ways:
            self.send1(j, p, a).start()

    def step2(self, j):
        for p, a, b in self.ways:
            self.send1(j, p, a).wait_recv()
            at = self.rows(128 * p + 64 * a, 64)
            self.term[j, at, :] = (self.term[j, at, :].astype(f32) + self.r1[j, p].astype(f32)).astype(bf)
            self.send2(j, p, a, b).start()

    def total(self, j, p, a, b):
        self.send2(j, p, a, b).wait_recv()
        at = self.rows(self.base(p, a, b), 32)
        return (self.term[j, at, :].astype(f32) + self.r2[j, p].astype(f32)).astype(bf)

    def step3(self, j):
        for p, a, b in self.ways:
            self.term[j, self.rows(self.base(p, a, b), 32), :] = self.total(j, p, a, b)
            self.send3(j, p, a, b).start()
            self.keep3(j, p, a, b).start()

    def step4(self, j, held=True):
        for p, a, b in self.ways:
            self.send3(j, p, a, b, held).wait_recv()
            if held:
                self.keep3(j, p, a, b).wait()
            self.send4(j, p, a).start()

    def finish(self, j):
        for p, a, b in self.ways:
            self.send4(j, p, a).wait_recv()
            self.send1(j, p, a).wait_send()
            self.send2(j, p, a, b).wait_send()
            self.send3(j, p, a, b).wait_send()
            self.send4(j, p, a).wait_send()


def sum_add(dst, parts):
    @pl.loop(0, HALF // 64)
    def _(i):
        rows = pl.ds(pl.multiple_of(i * 64, 64), 64)
        total = parts[0][rows, :].astype(f32)
        for part in parts[1:]:
            total = total + part[rows, :].astype(f32)
        dst[rows, :] = total.astype(bf)


def line_sum_step(k, z, s, f, own, sib, land, stage, out, loads, sends, recvs, early=None):
    for way in range(2):
        d = z - 3 + k if way == 0 else z + 3 - k
        valid = d >= 0 if way == 0 else d <= 3
        to = f - 2 if way == 0 else f + 2
        inner = z < 3 if way == 0 else z > 0
        was = z - 4 + k >= 0 if way == 0 else z + 4 - k <= 3

        @pl.when(valid)
        def _():
            terms = [
                pltpu.make_async_copy(own.at[d], stage.at[0], loads.at[0]),
                pltpu.make_async_copy(sib.at[d], stage.at[1], loads.at[1]),
            ]
            for copy in terms:
                copy.start()
            if k == 1 and early is not None:

                @pl.when(inner)
                def _():
                    came = pltpu.make_async_copy(early.at[way], stage.at[2], loads.at[2])
                    came.start()
                    came.wait()

            elif k > 0:

                @pl.when(was)
                def _():
                    remote(out.at[way], land.at[way, k - 1], sends.at[way, k - 1], recvs.at[way, k - 1], s, to).wait_send()

                @pl.when(inner)
                def _():
                    remote(out.at[way], land.at[way, k - 1], sends.at[way, k - 1], recvs.at[way, k - 1], s, to).wait_recv()
                    came = pltpu.make_async_copy(land.at[way, k - 1], stage.at[2], loads.at[2])
                    came.start()
                    came.wait()

            for copy in terms:
                copy.wait()
            if k > 0:

                @pl.when(inner)
                def _():
                    sum_add(out.at[way], [stage.at[0], stage.at[1], stage.at[2]])

                @pl.when(jnp.logical_not(inner))
                def _():
                    sum_add(out.at[way], [stage.at[0], stage.at[1]])
            else:
                sum_add(out.at[way], [stage.at[0], stage.at[1]])
            remote(out.at[way], land.at[way, k], sends.at[way, k], recvs.at[way, k], s, to).start()


def line_sum_end(z, s, f, own, sib, land, stage, out, loads, sends, recvs):
    terms = [
        pltpu.make_async_copy(own.at[z], stage.at[0], loads.at[0]),
        pltpu.make_async_copy(sib.at[z], stage.at[1], loads.at[1]),
    ]
    for copy in terms:
        copy.start()
    for copy in terms:
        copy.wait()

    for way in range(2):
        to = f - 2 if way == 0 else f + 2
        sent = z > 0 if way == 0 else z < 3
        got = z < 3 if way == 0 else z > 0

        @pl.when(sent)
        def _():
            remote(out.at[way], land.at[way, 2], sends.at[way, 2], recvs.at[way, 2], s, to).wait_send()

        @pl.when(got)
        def _():
            remote(out.at[way], land.at[way, 2], sends.at[way, 2], recvs.at[way, 2], s, to).wait_recv()
            came = pltpu.make_async_copy(land.at[way, 2], stage.at[2], loads.at[2])
            came.start()
            came.wait()
            sum_add(stage.at[0], [stage.at[0], stage.at[2]])

    sum_add(stage.at[2], [stage.at[0], stage.at[1]])


def backward_body(
    g_part, a_all, w_in_h, w_out_h, slope_h, qkv_h, lse_h, p_own, p_sib, gain, cos4, sin4, idc, idr,
    g_all, b_all, own_o, sib_o, branch, land, land_u, fin_down, fin_out, sums,
    w_in, w_out, x, slope, qkv, lse, gh, gmix, gp, acc_k, acc_v, u_own, u_sib, stage, rs_out, cos, sin, term, r1, r2, left, acc,
    load, l0, l1, l2, l3, core_0, core_1, core_u0, core_u1, out_sems, rs_send, rs_recv, pb_send, pb_recv,
    t_load, r1_s, r1_r, r2_s, r2_r, r3_s, r3_r, r4_s, r4_r, own_sems, u_send, u_recv,
):
    s, f = lax.axis_index("seq"), lax.axis_index("fsdp")
    z = f // 2
    line = (l0, l1, l2, l3)
    core = (core_0, core_1)
    own, other = pl.ds(0, HALF), pl.ds(HALF, HALF)
    units = gh.shape[1]
    scale = 256 ** -0.5
    first = [
        pltpu.make_async_copy(w_in_h, w_in, load.at[0]),
        pltpu.make_async_copy(w_out_h, w_out, load.at[1]),
    ]
    for copy in first:
        copy.start()
    near_barrier(s, f)
    swap = lambda b: core_copy(g_all, b, s, f, core)
    new_blocks(0, z, lambda b: swap(b).start())
    line_step(g_all, 1, z, s, f, line)
    new_blocks(1, z, lambda b: swap(b).start())
    reduce_args = (z, s, f, p_own, p_sib, land, stage, rs_out, load.at[pl.ds(8, 3)], rs_send, rs_recv)
    line_sum_step(0, *reduce_args)
    sums[...] = jnp.zeros_like(sums)
    back = PlaneBack(stage.at[2], branch, s, f, pb_send, pb_recv, load.at[7])

    def ins(b, which=(0, 1, 2)):
        pairs = [(slope_h, slope), (qkv_h, qkv), (lse_h, lse)]
        return [pltpu.make_async_copy(pairs[i][0].at[b], pairs[i][1], load.at[2 + i]) for i in which]

    def outs(b):
        pairs = [(gh, b_all.at[b, :, pl.ds(0, units)]), (u_own, own_o.at[b])]
        pairs += [(gp.at[i], b_all.at[b, :, pl.ds(units + 256 * i, 256)]) for i in range(3)]
        return [pltpu.make_async_copy(src, dst, out_sems.at[i]) for i, (src, dst) in enumerate(pairs)]

    def send_sib(b):
        return remote(u_sib, sib_o.at[b], core_u0.at[b], core_u1.at[b], s, f + 1 - 2 * (f % 2))

    def result(j, start, count):
        if j < 4:
            return fin_down.at[SeqSum.rows(256 * j + start, count)]
        return fin_out.at[SeqSum.rows(start, count)]

    row_sums = SeqSum(
        term, r1, r2, (r1_s, r1_r, r2_s, r2_r, r3_s, r3_r, r4_s, r4_r), own_sems, result, s, f
    )

    def term_loads(j, k):
        slot = (8 * j + k) % 3
        at = pl.ds(pl.multiple_of(HALF * (k % 2), HALF), HALF)
        return (
            pltpu.make_async_copy(a_all.at[k // 2, at, pl.ds(256 * j, 256)], left.at[slot], t_load.at[slot, 0]),
            pltpu.make_async_copy(g_all.at[k // 2, at], stage.at[slot], t_load.at[slot, 1]),
        )

    def compute_term(j):
        @pl.loop(0, 8)
        def _(k):
            @pl.when(k < 6)
            def _():
                for copy in term_loads(j, k + 2):
                    copy.start()

            if j < 4:

                @pl.when(k >= 6)
                def _():
                    for copy in term_loads(j + 1, k - 6):
                        copy.start()

            for copy in term_loads(j, k):
                copy.wait()
            slot = (8 * j + k) % 3
            part = tn(left[slot], stage[slot])

            @pl.when(k == 0)
            def _():
                acc[...] = part

            @pl.when((k > 0) & (k < 7))
            def _():
                acc[...] += part

            @pl.when(k == 7)
            def _():
                term[j] = (acc[...] + part).astype(bf)

    def load_x(b):
        return [
            pltpu.make_async_copy(g_all.at[b, own], x.at[own], load.at[5]),
            pltpu.make_async_copy(g_all.at[b, other], x.at[other], load.at[6]),
        ]

    for copy in ins(z):
        copy.start()
    swap(z).wait_recv()
    for copy in load_x(z):
        copy.start()
    for copy in first:
        copy.wait()

    for t in range(4):
        b = line_order(z, t)
        expand_tables(cos4, sin4, b, cos, sin)
        if t == 3:
            line_arrive(g_all, 2, z, s, f, line)
            new_blocks(3, z, lambda v: swap(v).start())
            line_sum_step(2, *reduce_args)
            swap(b).wait_recv()
            for copy in term_loads(0, 0) + term_loads(0, 1) + tuple(load_x(b)):
                copy.start()
            for j in range(5):
                compute_term(j)
                row_sums.step1(j)
                if j >= 2:
                    row_sums.step2(j - 2)
                if j >= 3:
                    row_sums.step3(j - 3)
        if t > 0:
            before = line_order(z, t - 1)
            for copy in outs(before):
                copy.wait()
            send_sib(before).wait_send()
        for copy in ins(b) + load_x(b):
            copy.wait()

        @pl.loop(0, units // 256)
        def _(j):
            at = pl.ds(pl.multiple_of(j * 256, 256), 256)
            ga = nt(x[...], w_out[at, :]).astype(bf)
            gh[:, at] = (ga.astype(f32) * slope[:, at].astype(f32)).astype(bf)

        gmix[...] = nt(x[...], w_out[pl.ds(units, 256), :]).astype(bf)
        after = line_order(z, t + 1)
        if t < 3:
            ins(after, (0,))[0].start()
        else:
            row_sums.step2(3)
            row_sums.step3(2)
            row_sums.step4(0)
        acc_k[...] = jnp.zeros_like(acc_k)
        acc_v[...] = jnp.zeros_like(acc_v)

        @pl.loop(0, TOK // 256)
        def _(i):
            rows = pl.ds(pl.multiple_of(i * 256, 256), 256)
            q, g = qkv[0, rows, :], gmix[rows, :]
            scores = nt(q, qkv[1]) * scale
            allowed = idr[b] <= idc[b, rows, :]
            probs = jnp.where(allowed, jnp.exp(scores - lse[rows, 0:1]), 0.0)
            grad_probs = nt(g, qkv[2])
            inner = jnp.sum(probs * grad_probs, axis=1, keepdims=True)
            gs = (probs * (grad_probs - inner)).astype(bf)
            gq = (nn(gs, qkv[1]) * scale).astype(bf).astype(f32)
            gq = turn(gq, cos[rows, :], -sin[rows, :])
            sums[0:1, :] += jnp.sum(gq, axis=0, keepdims=True)
            gp[0, rows, :] = gq.astype(bf)
            acc_k[...] += tn(gs, q)
            acc_v[...] += tn(probs.astype(bf), g)

        gk = (acc_k[...] * scale).astype(bf).astype(f32)
        gk = turn(gk, cos[...], -sin[...])
        sums[1:2, :] += jnp.sum(gk, axis=0, keepdims=True)
        gp[1] = gk.astype(bf)
        gv = acc_v[...].astype(bf)
        sums[2:3, :] += jnp.sum(gv.astype(f32), axis=0, keepdims=True)
        gp[2] = gv
        if t < 3:
            for copy in ins(after, (1, 2)):
                copy.start()
        if t == 1:
            line_arrive(g_all, 1, z, s, f, line)
            line_step(g_all, 2, z, s, f, line)
            new_blocks(2, z, lambda v: swap(v).start())
        if t < 2:
            swap(after).wait_recv()
            for copy in load_x(after):
                copy.start()
        if t == 1:
            line_sum_step(1, *reduce_args)
        if t == 3:
            row_sums.step2(4)
            row_sums.step3(3)
            row_sums.step4(1)
            line_sum_end(*reduce_args)
            back.start()

        @pl.loop(0, u_own.shape[1] // 256)
        def _(j):
            at = pl.ds(pl.multiple_of(j * 256, 256), 256)
            from_mlp = nn(gh[...], w_in[pl.ds(0, units), at])
            from_attn = nn(gp[0], w_in[pl.ds(units, 256), at])
            for i in range(1, 3):
                from_attn = from_attn + nn(gp[i], w_in[pl.ds(units + 256 * i, 256), at])
            out = from_mlp * gain[0:1, at] + from_attn * gain[1:2, at]
            u_own[:, at] = out[:HALF].astype(bf)
            u_sib[:, at] = out[HALF:].astype(bf)

        for copy in outs(b):
            copy.start()
        send_sib(b).start()

    last = line_order(z, 3)
    for copy in outs(last):
        copy.wait()
    send_sib(last).wait_send()
    for b in range(4):
        swap(b).wait_send()
        send_sib(b).wait_recv()
    line_sum_step(0, z, s, f, own_o, sib_o, land_u, stage, rs_out, load.at[pl.ds(8, 3)], u_send, u_recv)
    row_sums.step3(4)
    row_sums.step4(2)
    row_sums.step4(3)
    row_sums.step4(4)
    back.wait()
    for k in (1, 2):
        line_sent(g_all, k, z, s, f, line)
    for j in range(5):
        row_sums.finish(j)
    for way in range(2):
        to = f - 2 if way == 0 else f + 2
        copy = remote(rs_out.at[way], land_u.at[way, 0], u_send.at[way, 0], u_recv.at[way, 0], s, to)
        pl.when(z == (3 if way == 0 else 0))(copy.wait_send)
        pl.when(z == (2 if way == 0 else 1))(copy.wait_recv)


def backward_call(g_part, a_all, w_in, w_out, slope, qkv, lse, p_own, p_sib, gain, cos4, sin4, ids_col, ids_row):
    width = w_in.shape[1]
    units = w_in.shape[0] - 768
    anys = pl.BlockSpec(memory_space=pl.ANY)
    vmem = pl.BlockSpec(memory_space=pltpu.VMEM)
    shape = jax.ShapeDtypeStruct
    dma = lambda *n: pltpu.SemaphoreType.DMA(n)
    return pl.pallas_call(
        backward_body,
        in_specs=[anys] * 9 + [vmem] * 5,
        out_specs=[anys] * 9 + [vmem],
        out_shape=[
            shape((4, TOK, width), bf), shape((4, TOK, units + 768), bf),
            shape((4, HALF, width), bf), shape((4, HALF, width), bf), shape((HALF, width), bf),
            shape((2, 3, HALF, width), bf), shape((2, 1, HALF, width), bf), shape((1024, width), bf),
            shape((256, width), bf), shape((8, 256), f32),
        ],
        input_output_aliases={0: 0},
        scratch_shapes=[
            pltpu.VMEM(w_in.shape, bf), pltpu.VMEM(w_out.shape, bf), pltpu.VMEM((TOK, width), bf),
            pltpu.VMEM((TOK, units), bf), pltpu.VMEM((3, TOK, 256), bf), pltpu.VMEM((TOK, LANES), f32),
            pltpu.VMEM((TOK, units), bf), pltpu.VMEM((TOK, 256), bf), pltpu.VMEM((3, TOK, 256), bf),
            pltpu.VMEM((TOK, 256), f32), pltpu.VMEM((TOK, 256), f32),
            pltpu.VMEM((HALF, width), bf), pltpu.VMEM((HALF, width), bf),
            pltpu.VMEM((3, HALF, width), bf), pltpu.VMEM((2, HALF, width), bf),
            pltpu.VMEM((TOK, LANES), f32), pltpu.VMEM((TOK, LANES), f32),
            pltpu.VMEM((5, 256, width), bf), pltpu.VMEM((5, 2, 64, width), bf), pltpu.VMEM((5, 2, 32, width), bf),
            pltpu.VMEM((3, HALF, 256), bf), pltpu.VMEM((256, width), f32),
            dma(11), dma(3), dma(3), dma(3), dma(3), dma(4), dma(4), dma(4), dma(4), dma(5),
            dma(2, 3), dma(2, 3), dma(4), dma(4), dma(3, 2), *[dma(5, 2)] * 9, dma(2, 3), dma(2, 3),
        ],
        compiler_params=pltpu.CompilerParams(
            vmem_limit_bytes=63 * 1024 * 1024, collective_id=1, has_side_effects=True
        ),
        cost_estimate=cost(8 * TOK * width * (w_in.shape[0] + w_out.shape[0]), 200e6),
        name="backward",
    )(g_part, a_all, w_in, w_out, slope, qkv, lse, p_own, p_sib, gain, cos4, sin4, ids_col, ids_row)


PAIRS = 7


def tail_body(
    b_all, n_all, plain, u_own, u_sib, early, gain, shift, wide_in, more_in,
    fin_up, fin_qkv, u_o, small_o, land,
    term, r1, r2, hop, stage, rs_out, left, right, acc, acc_s, weight, sides, wide, more, got, small,
    load, w_sem, r1_s, r1_r, r2_s, r2_r, hop_s, hop_r, r3_s, r3_r, r4_s, r4_r,
    rs_load, rs_send, rs_recv, pb_s, pb_r, sm_s, sm_r, sq_s, sq_r, own_sems, self_sem,
):
    s, f = lax.axis_index("seq"), lax.axis_index("fsdp")
    z = f // 2
    reduce_args = (z, s, f, u_own, u_sib, land, stage, rs_out, rs_load, rs_send, rs_recv)
    column = [4, 5, 6, 0, 1, 2, 3]

    def result(j, start, count):
        if j < 3:
            return fin_qkv.at[SeqSum.rows(256 * j + start, count)]
        return fin_up.at[SeqSum.rows(256 * (j - 3) + start, count)]

    sums = SeqSum(
        term, r1, r2, (r1_s, r1_r, r2_s, r2_r, r3_s, r3_r, r4_s, r4_r), own_sems, result, s, f
    )
    across = sums.across

    def loads(j, k):
        slot = k % 2
        return (
            pltpu.make_async_copy(b_all.at[k, :, pl.ds(256 * column[j], 256)], left.at[slot], load.at[slot, 0]),
            pltpu.make_async_copy(n_all.at[k], right.at[slot], load.at[slot, 1]),
        )

    def weights(j):
        return pltpu.make_async_copy(plain.at[pl.ds(256 * column[j], 256)], weight, w_sem)

    for copy in loads(0, 0):
        copy.start()
    near_barrier(s, f)
    sides[...] = jnp.zeros_like(sides)
    wide[...] = wide_in[...]
    more[...] = more_in[...]

    def compute(j):
        weights(j).start()

        @pl.loop(0, 4)
        def _(k):
            slot = k % 2

            @pl.when(k < 3)
            def _():
                for copy in loads(j, k + 1):
                    copy.start()

            if j + 1 < PAIRS:

                @pl.when(k == 3)
                def _():
                    for copy in loads(j + 1, 0):
                        copy.start()

            for copy in loads(j, k):
                copy.wait()
            part = tn(left[slot], right[slot])
            part_s = tn(left[slot], jnp.ones((TOK, LANES), bf))

            @pl.when(k == 0)
            def _():
                acc[...] = part
                acc_s[...] = part_s

            @pl.when(k > 0)
            def _():
                acc[...] += part
                acc_s[...] += part_s

        which = 1 if j < 3 else 0
        weights(j).wait()
        raw, total = acc[...], acc_s[:, 0:1]
        term[j] = (raw * gain[which : which + 1, :] + total * shift[which : which + 1, :]).astype(bf)
        low_w = weight[...].astype(f32)
        sides[2 * which : 2 * which + 1, :] += jnp.sum(low_w * raw, axis=0, keepdims=True)
        sides[2 * which + 1 : 2 * which + 2, :] += jnp.sum(low_w * total, axis=0, keepdims=True)
        if j >= 3:
            row = jnp.transpose(acc_s[...])
            for half in range(2):
                at = 2 * (j - 3) + half
                more[at : at + 1, :] = row[0:1, 128 * half : 128 * half + 128]

    def owner(j):
        head = 8 * j + f
        return head // 3, head % 3

    def hop_place(i, p, a, b):
        return fin_qkv.at[SeqSum.rows(256 * i + SeqSum.base(p, a, b), 32)]

    def send_hop(j, p, a, b):
        to, i = owner(j)
        return remote(hop.at[j, p], hop_place(i, p, a, b), hop_s.at[j, p], hop_r.at[i, p], s, to)

    def keep_hop(j, p, a, b):
        return pltpu.make_async_copy(hop.at[j, p], hop_place(owner(j)[1], p, a, b), own_sems.at[j, p])

    def step3(j):
        if j >= 3:
            sums.step3(j)
            return
        for p, a, b in sums.ways:
            hop[j, p] = sums.total(j, p, a, b)
            here = owner(j)[0] == f
            pl.when(here)(keep_hop(j, p, a, b).start)
            pl.when(jnp.logical_not(here))(send_hop(j, p, a, b).start)

    def step3_own(i):
        head, kind = (3 * f + i) % 8, (3 * f + i) // 8
        for p, a, b in sums.ways:
            ref = hop_place(i, p, a, b)
            coming = remote(ref, ref, hop_s.at[i, p], hop_r.at[i, p], s, head)
            staying = pltpu.make_async_copy(ref, ref, own_sems.at[kind, p])
            pl.when(head != f)(coming.wait_recv)
            pl.when(head == f)(staying.wait)
            sums.send3(i, p, a, b, False).start()

    def small_send(step):
        to = (f + step) % 8
        return remote(wide.at[to], got.at[step - 1], sm_s.at[step - 1], sm_r.at[step - 1], s, to)

    def small_one():
        for to in range(8):
            for v in range(4):
                for half in range(2):
                    at = 256 * to + 128 * half
                    wide[to, 2 * v + half : 2 * v + half + 1, :] = sides[v : v + 1, at : at + 128]
        for step in range(1, 8):
            small_send(step).start()

    def small_two():
        total = wide[f]
        for step in range(1, 8):
            small_send(step).wait_recv()
            total = total + got[step - 1]
        small[0, 0:16] = total
        small[0, 16:32] = more[...]
        small_seq(0).start()

    def small_seq(way):
        return remote(small.at[2 * way], small.at[2 * way + 1], sq_s.at[way], sq_r.at[way], across[way], f)

    def small_three():
        small_seq(0).wait_recv()
        small[2] = small[0] + small[1]
        small_seq(1).start()

    def small_four():
        small_seq(1).wait_recv()
        small_o[...] = small[2] + small[3]

    back = PlaneBack(stage.at[2], u_o, s, f, pb_s, pb_r, self_sem)
    line_sum_step(1, *reduce_args, early.at[:, 0])
    compute(0)
    sums.step1(0)
    compute(1)
    sums.step1(1)
    for it in range(1, 10):
        if it + 1 < PAIRS:
            compute(it + 1)
            sums.step1(it + 1)
        if it - 1 < PAIRS:
            sums.step2(it - 1)
        if 0 <= it - 2 < PAIRS:
            step3(it - 2)
        if it == 4:
            line_sum_step(2, *reduce_args)
        if 5 <= it < 8:
            step3_own(it - 5)
        if 3 <= it - 3 < PAIRS:
            sums.step4(it - 3)
        if 6 <= it < 9:
            sums.step4(it - 6, False)
        if it == 6:
            small_one()
        if it == 7:
            small_two()
        if it == 8:
            small_three()
            line_sum_end(*reduce_args)
            back.start()

    small_four()
    for j in range(PAIRS):
        sums.finish(j)
    for j in range(3):
        for p, a, b in sums.ways:
            pl.when(owner(j)[0] != f)(send_hop(j, p, a, b).wait_send)

    for step in range(1, 8):
        small_send(step).wait_send()
    for way in range(2):
        small_seq(way).wait_send()
    back.wait()


def tail_call(b_all, n_all, plain, u_own, u_sib, early, gain, shift, wide, more):
    width = plain.shape[1]
    anys = pl.BlockSpec(memory_space=pl.ANY)
    vmem = pl.BlockSpec(memory_space=pltpu.VMEM)
    shape = jax.ShapeDtypeStruct
    dma = lambda *n: pltpu.SemaphoreType.DMA(n)
    two = [dma(PAIRS, 2)] * 2
    return pl.pallas_call(
        tail_body,
        in_specs=[anys] * 6 + [vmem] * 4,
        out_specs=[anys] * 3 + [vmem, anys],
        out_shape=[
            shape((1024, width), bf), shape((768, width), bf),
            shape((HALF, width), bf), shape((32, LANES), f32), shape((2, 3, HALF, width), bf),
        ],
        scratch_shapes=[
            pltpu.VMEM((PAIRS, 256, width), bf), pltpu.VMEM((PAIRS, 2, 64, width), bf),
            pltpu.VMEM((PAIRS, 2, 32, width), bf), pltpu.VMEM((3, 2, 32, width), bf),
            pltpu.VMEM((3, HALF, width), bf), pltpu.VMEM((2, HALF, width), bf),
            pltpu.VMEM((2, TOK, 256), bf), pltpu.VMEM((2, TOK, width), bf),
            pltpu.VMEM((256, width), f32), pltpu.VMEM((256, LANES), f32), pltpu.VMEM((256, width), bf),
            pltpu.VMEM((8, width), f32), pltpu.VMEM((8, 16, LANES), f32), pltpu.VMEM((16, LANES), f32),
            pltpu.VMEM((7, 16, LANES), f32), pltpu.VMEM((4, 32, LANES), f32),
            dma(2, 2), pltpu.SemaphoreType.DMA, *two, *two, dma(3, 2), dma(3, 2), *two, *two,
            dma(3), dma(2, 3), dma(2, 3), dma(4), dma(4), dma(7), dma(7), dma(2), dma(2), dma(PAIRS, 2),
            pltpu.SemaphoreType.DMA,
        ],
        compiler_params=pltpu.CompilerParams(
            vmem_limit_bytes=61 * 1024 * 1024, collective_id=2, has_side_effects=True
        ),
        cost_estimate=cost(1e11, 600e6),
        name="tail",
    )(b_all, n_all, plain, u_own, u_sib, early, gain, shift, wide, more)


def pick(slices, which):
    return lax.dynamic_index_in_dim(slices, which, 0, keepdims=False)


def split_body(
    resid_in,
    qkv_weight,
    qkv_bias,
    out_weight,
    out_bias,
    up_weight,
    up_bias,
    down_weight,
    down_bias,
    attn_gain,
    attn_shift,
    mlp_gain,
    mlp_shift,
    block_ids,
    offsets,
    grad_out,
):
    low = jnp.bfloat16
    f32 = jnp.float32
    groups, piece, width = resid_in.shape
    tokens = groups * piece
    s = lax.axis_index("seq")
    f = lax.axis_index("fsdp")
    z, c = f // 2, f % 2
    units = up_weight.shape[0]

    length = block_ids.shape[1]
    own_small = [attn_gain, attn_shift, mlp_gain, mlp_shift, out_bias + down_bias, qkv_bias]
    packed = jnp.concatenate(
        own_small + [block_ids.reshape(-1).astype(f32), offsets.reshape(-1).astype(f32)]
    )
    packed = jnp.pad(packed, (0, 40 * LANES - packed.shape[0])).reshape(40, LANES)
    flat = resid_in.reshape(tokens, width)
    grad_flat = grad_out.reshape(tokens, width)
    own_n, g_low, head_half, small, bias_sum = entry_call(flat, grad_flat, qkv_weight, packed)
    small = small.reshape(8, 40 * LANES)
    gain_a, shift_a, gain_m, shift_m, bias_out = (
        small[:, i * 256 : (i + 1) * 256].reshape(width) for i in range(5)
    )
    head_bias = small[:, 1280:2048].reshape(3, HEADS, HEAD_DIM)
    head_bias = lax.dynamic_index_in_dim(head_bias, f, 1, keepdims=False).reshape(3 * HEAD_DIM)
    ids_end = 2048 + groups * length
    ids_all = small[:, 2048:ids_end].astype(jnp.int32).reshape(-1, 8, LANES)
    starts_all = small[:, ids_end : ids_end + groups * offsets.shape[1]].astype(jnp.int32)
    starts_all = starts_all.reshape(-1, offsets.shape[1])
    gain = jnp.stack([gain_m, gain_a])
    shift = jnp.stack([shift_m, shift_a])
    bias_in = jnp.concatenate([up_bias, head_bias])[None]

    halves = [(2 * (s % 2) + c, c), (2 * (s % 2) + 1 - c, 1 - c)]
    rows_at = [((part - k + 4) % 4) * 2 + core for part, core in halves for k in range(4)]
    ids_slots = [pick(ids_all, block * 4 + s) for block in range(4)]
    ids_here = jnp.stack(
        [jnp.concatenate([pick(row, at) for at in rows_at]) for row in ids_slots]
    ).reshape(4, 1024)
    starts_here = jnp.stack([pick(starts_all, block * 4 + s) for block in range(4)])
    pos = (jnp.stack(rows_at)[:, None] * LANES + jnp.arange(LANES)[None, :]).reshape(1024)
    positions = block_offset(ids_here, starts_here) + pos[None, :]
    lane = jnp.arange(LANES)
    inverse = jnp.exp((lane % 32).astype(f32) * (-2.0 * math.log(10000.0) / ROT_DIM))
    grouped = positions.astype(f32).reshape(4, 4, 256, 1)
    spot = sum(jnp.where(lane // 32 == q, grouped[:, q], 0.0) for q in range(4))
    angles = spot * inverse
    cosine, sine = jnp.cos(angles), jnp.sin(angles)
    ids_col, ids_row = ids_here[:, :, None], ids_here[:, None, :]

    n_all, g_part, w_in, w_out, a_all, slope_all, qkv_all, lse_all, p_own, p_sib = forward_call(
        own_n, g_low, head_half, up_weight, down_weight, out_weight, bias_in, gain, shift,
        cosine, sine, ids_col, ids_row,
    )
    _, b_all, u_own, u_sib, branch, _, early, down_low, out_low, col_sums = backward_call(
        g_part, a_all, w_in, w_out, slope_all, qkv_all, lse_all, p_own, p_sib, gain, cosine, sine, ids_col, ids_row
    )
    result = flat + branch.astype(f32) + bias_out

    slots = jnp.zeros((16, HEAD_DIM), f32)
    slots = lax.dynamic_update_slice(slots, col_sums[0:1], (f, 0))
    slots = lax.dynamic_update_slice(slots, col_sums[1:2], (8 + f, 0))
    spread = jnp.concatenate([jnp.zeros((4, width), f32), bias_sum])
    wide = jnp.concatenate(
        [spread.reshape(5, 8, 256).transpose(1, 0, 2).reshape(8, 5 * 256), slots.reshape(8, 512)], axis=1
    )
    wide = jnp.pad(wide, ((0, 0), (0, 256))).reshape(8, 16, LANES)
    more = jnp.pad(jnp.concatenate([jnp.zeros((units,), f32), col_sums[2]]), (0, 768)).reshape(16, LANES)
    up_low, qkv_low, u, small_sum, _ = tail_call(
        b_all, n_all, w_in, u_own, u_sib, early, gain, shift, wide, more
    )
    u = u.astype(f32)
    center = flat - jnp.mean(flat, axis=-1, keepdims=True)
    inv = lax.rsqrt(jnp.mean(center * center, axis=-1, keepdims=True) + EPS)
    normal = center * inv
    grad_input = grad_flat + inv * (
        u - jnp.mean(u, axis=-1, keepdims=True) - normal * jnp.mean(u * normal, axis=-1, keepdims=True)
    )
    mine = small_sum.reshape(-1)
    vectors = [mine[i * 256 : (i + 1) * 256] for i in range(5)]
    qk_grad = mine[1280:1792]
    up_bias_grad = mine[2048 : 2048 + units]
    value_grad = mine[2048 + units : 2304 + units]
    return (
        result.reshape(groups, piece, width),
        grad_input.reshape(groups, piece, width),
        qkv_low.astype(f32),
        qk_grad,
        value_grad,
        out_low.astype(f32),
        vectors[4],
        up_low.astype(f32),
        up_bias_grad,
        down_low.astype(f32),
        vectors[4],
        vectors[2],
        vectors[3],
        vectors[0],
        vectors[1],
    )


def solution(mesh):
    placed = (
        P("fsdp", "seq", None),
        P("fsdp", None),
        P("fsdp"),
        P("fsdp", None),
        P("fsdp"),
        P("fsdp", None),
        P("fsdp"),
        P("fsdp", None),
        P("fsdp"),
        P("fsdp"),
        P("fsdp"),
        P("fsdp"),
        P("fsdp"),
        P("fsdp", None),
        P("fsdp", None),
        P("fsdp", "seq", None),
    )
    return jax.shard_map(
        split_body if mesh.shape["fsdp"] == HEADS and mesh.shape["seq"] == 4 else body,
        mesh=mesh,
        in_specs=placed,
        out_specs=(
            P("fsdp", "seq", None),
            P("fsdp", "seq", None),
            P("fsdp", None),
            P("fsdp"),
            P("fsdp"),
            P("fsdp", None),
            P("fsdp"),
            P("fsdp", None),
            P("fsdp"),
            P("fsdp", None),
            P("fsdp"),
            P("fsdp"),
            P("fsdp"),
            P("fsdp"),
            P("fsdp"),
        ),
        check_vma=False,
    )
```
